32 devices in a mesh: grp: 4 (over y, x), brick: 8 (over z, core).
Axes of the slice: x: 2, y: 2, z: 4, core: 2. Of those that a mesh axis runs over, the one named last changes fastest.
Arguments:
- positions: float32 [3, 1048576], P(None, ('grp', 'brick')), may hold values from -4 to 4
- charges: float32 [1048576], P(('grp', 'brick')), may hold values from -5 to 5
- cluster_fill: int32 [8192], P(('grp', 'brick')), may hold values from 1 to 128, as said below
- cluster_cell: int32 [8192], P(('grp', 'brick')), may hold values from 0 to 131071
- send_index: int32 [224, 32], P(('grp', 'brick')), may hold values from 0 to 255
- send_count: int32 [32, 7], P(('grp', 'brick')), may hold values from 1 to 32, as said below
- pair_local: int32 [32768], P(('grp', 'brick')), may hold values from 0 to 255
- pair_dir: int32 [32768], P(('grp', 'brick')), may hold values from 0 to 6, as said below
- pair_slot: int32 [32768], P(('grp', 'brick')), may hold values from 0 to 31
- ion_density: float32 [64, 256, 256], P('grp', 'brick'), may hold values from 0.2 to 2
- potential_prev: float32 [64, 256, 256], P('grp', 'brick'), may hold values from -6 to 6
- screening: float32 [64, 256, 256], P('grp', 'brick'), may hold values from 0.05 to 0.5
Outputs:
- forces: float32 [3, 1048576], P(None, ('grp', 'brick'))
- potential: float32 [64, 256, 256], P('grp', 'brick')
- ion_next: float32 [64, 256, 256], P('grp', 'brick')
The draws below stay inside these ranges and needn't reach their ends.
Inputs may be any that keep to these rules, and one draw needn't show every extreme that they name: `cluster_fill`: live particles of a cluster; later slots are padding; some cluster is full. `send_count`: every device sends 32 live slots in some direction. `send_index`: local cluster indices; row e * 7 + k lists what device e sends to the device at minus the offset of direction k. `pair_local`: local cluster indices. `pair_dir`: a direction never names a device outside the room. `pair_slot`: slot indices; a slot at or past the sender's count carries no charge. `cluster_cell`: cell indices within a device's block.
All inputs are finite; a program needn't handle non-finite values.
Results may differ from the reference program's by a relative error of at most 0.0001.
Values sent between devices are 32-bit elements; how exact they have to be, the bound alone decides.
No kernel may reach another device: no remote copies, remote signals or barrier semaphores. Data moves between devices by JAX's collectives and lax.ppermute only.
A program may use at most 192 MiB of HBM per device.

```python
import math
import jax
import jax.numpy as jnp
from jax import lax

CL_DEV = 256
PSIZE = 128
DIRS = 7
SLOTS = 32
PAIRS_DEV = 1024
GX = 16
GY = 32
GZ = 256
SWEEPS = 4
NX = 64
NY = 256
CLUSTERS = 8192
PARTICLES = 1048576
PAIRS = 32768
N_GRP = 4
N_BRICK = 8
DEVICES = 32


def draw_cluster_fill(key, part):
    fill = jax.random.randint(key, (DEVICES * CL_DEV,), 1, PSIZE + 1, dtype=jnp.int32)
    return fill.at[0].set(PSIZE)


def draw_send_count(key, part):
    key_count, key_pick = jax.random.split(key)
    counts = jax.random.randint(key_count, (DEVICES, DIRS), 1, SLOTS + 1, dtype=jnp.int32)
    pick = jax.random.randint(key_pick, (DEVICES, 1), 0, DIRS, dtype=jnp.int32)
    columns = jnp.arange(DIRS, dtype=jnp.int32)[None, :]
    return jnp.where(columns == pick, SLOTS, counts)


def draw_pair_dir(key, part):
    raw = jax.random.randint(key, (DEVICES * PAIRS_DEV,), 0, DIRS, dtype=jnp.int32)
    device = jnp.arange(DEVICES * PAIRS_DEV, dtype=jnp.int32) // PAIRS_DEV
    slab = device // N_BRICK
    column = device % N_BRICK
    step_g = jnp.where(raw == 5, -1, jnp.where(raw == 6, 1, 0))
    step_b = jnp.where(raw == 1, -1, jnp.where(raw == 2, 1, jnp.where(raw == 3, -2, jnp.where(raw == 4, 2, 0))))
    valid = (slab + step_g >= 0) & (slab + step_g < N_GRP) & (column + step_b >= 0) & (column + step_b < N_BRICK)
    return jnp.where(valid, raw, 0).astype(jnp.int32)


def touch_ends(values, own_key, smallest, largest):
    longest = values.shape.index(max(values.shape))
    spots = []
    for shift in (0, 1):
        where = [jax.random.randint(jax.random.fold_in(own_key, axis), (), 0, length) for axis, length in enumerate(values.shape)]
        where[longest] = (where[longest] + shift) % values.shape[longest]
        spots.append(tuple(where))
    return values.at[spots[0]].set(smallest).at[spots[1]].set(largest)


def steps_of(key, extent, shards, smallest, high):
    gain, own = 1.0, jax.random.fold_in(key, 6)
    for dim, parts in shards:
        heights = jnp.exp(jax.random.uniform(jax.random.fold_in(own, dim), (parts,), jnp.float32, smallest / len(shards), high / len(shards)))
        gain = gain * jnp.repeat(heights, extent[dim] // parts).reshape([-1 if axis == dim else 1 for axis in range(len(extent))])
    return gain


def bell_draw(key, dims, deviation, limit, cuts=(), held_as=jnp.bfloat16):
    factor_of = steps_of(key, dims, cuts, -0.22, 0.18) if cuts else 1.0
    drawn = jax.random.normal(key, dims, jnp.float32) * deviation * factor_of
    return jnp.minimum(jnp.maximum(drawn, -limit), limit).astype(held_as)


def setup_inputs(seed: int = 0) -> dict:
    key_list = jax.random.split(jax.random.key(seed), 13)
    return {
        "positions": bell_draw(key_list[0], (3, PARTICLES), 1.0, 4.0, ((1, 32),), jnp.float32),
        "charges": bell_draw(key_list[1], (PARTICLES,), 1.0, 5.0, ((0, 32),), jnp.float32),
        "cluster_fill": draw_cluster_fill(jax.random.fold_in(key_list[12], 71), 0),
        "cluster_cell": touch_ends(jax.random.randint(key_list[3], (CLUSTERS,), 0, GX * GY * GZ), jax.random.fold_in(key_list[3], 1), 0, (GX * GY * GZ) - 1).astype(jnp.int32),
        "send_index": touch_ends(jax.random.randint(key_list[4], (DEVICES * DIRS, SLOTS), 0, CL_DEV), jax.random.fold_in(key_list[4], 1), 0, CL_DEV - 1).astype(jnp.int32),
        "send_count": draw_send_count(jax.random.fold_in(key_list[12], 71), 0),
        "pair_local": touch_ends(jax.random.randint(key_list[6], (PAIRS,), 0, CL_DEV), jax.random.fold_in(key_list[6], 1), 0, CL_DEV - 1).astype(jnp.int32),
        "pair_dir": draw_pair_dir(jax.random.fold_in(key_list[12], 71), 0),
        "pair_slot": touch_ends(jax.random.randint(key_list[8], (PAIRS,), 0, SLOTS), jax.random.fold_in(key_list[8], 1), 0, SLOTS - 1).astype(jnp.int32),
        "ion_density": jnp.clip(jnp.exp(math.log(2.0) - 2.3025851 * jax.random.uniform(key_list[9], (NX, NY, GZ), jnp.float32) ** steps_of(key_list[9], (NX, NY, GZ), ((0, 4), (1, 8)), -0.2, 0.2)), 0.2, 2.0),
        "potential_prev": bell_draw(key_list[10], (NX, NY, GZ), 1.0, 6.0, ((0, 4), (1, 8)), jnp.float32),
        "screening": jnp.clip(jnp.exp(math.log(0.5) - 2.3025851 * jax.random.uniform(key_list[11], (NX, NY, GZ), jnp.float32) ** steps_of(key_list[11], (NX, NY, GZ), ((0, 4), (1, 8)), -0.2, 0.2)), 0.05, 0.5),
    }


coulomb_scale = 0.02
softening = 0.1
field_scale = 0.5
deposit_scale = 0.2
lowest_eig = 0.01
highest_eig = 1.99
mobility = 0.3
diffusion = 0.2
time_step = 0.2

def offsets_of(dirs):
    step_g = jnp.where(dirs == 5, -1, jnp.where(dirs == 6, 1, 0)).astype(jnp.int32)
    step_b = jnp.where(dirs == 1, -1, jnp.where(dirs == 2, 1, jnp.where(dirs == 3, -2, jnp.where(dirs == 4, 2, 0)))).astype(jnp.int32)
    return (step_g, step_b)

def stencil_core(padded, center, screen):
    beside = padded[2:, 1:-1, 1:-1] + padded[:-2, 1:-1, 1:-1]
    beside = beside + padded[1:-1, 2:, 1:-1] + padded[1:-1, :-2, 1:-1]
    beside = beside + padded[1:-1, 1:-1, 2:] + padded[1:-1, 1:-1, :-2]
    return (6.0 + screen) * center - beside

def operate_plain(field, screen):
    return stencil_core(jnp.pad(field, 1), field, screen)

def chebyshev(start, rhs, screen):
    middle = 0.5 * (highest_eig + lowest_eig)
    spread = 0.5 * (highest_eig - lowest_eig)
    ratio_ms = middle / spread
    weight_now = 1.0 / ratio_ms
    inverse = 1.0 / (6.0 + screen)
    solution = start
    resid = rhs - operate_plain(solution, screen)
    update = inverse * resid / middle
    for turn in range(SWEEPS):
        solution = solution + update
        if turn + 1 < SWEEPS:
            resid = resid - operate_plain(update, screen)
            weight_next = 1.0 / (2.0 * ratio_ms - weight_now)
            update = weight_next * weight_now * update + 2.0 * weight_next / spread * (inverse * resid)
            weight_now = weight_next
    return solution

def tile_forces(own, other):
    diff = own[:, :3, :, None] - other[:, :3, None, :]
    dist = lax.optimization_barrier(jnp.sum(diff * diff, axis=1)) + softening
    weight = coulomb_scale * own[:, 3, :, None] * other[:, 3, None, :] / (dist * jnp.sqrt(dist))
    pull = diff * weight[:, None]
    return (lax.optimization_barrier(jnp.sum(pull, axis=3)), lax.optimization_barrier(jnp.sum(pull, axis=2)))

def face_div(pot, ions, axis):
    inner = [slice(1, -1), slice(1, -1), slice(1, -1)]
    inner[axis] = slice(None)
    pot = pot[tuple(inner)]
    ions = ions[tuple(inner)]

    def upper(arr):
        return lax.slice_in_dim(arr, 1, arr.shape[axis], axis=axis)

    def lower(arr):
        return lax.slice_in_dim(arr, 0, arr.shape[axis] - 1, axis=axis)
    speed = -mobility * (upper(pot) - lower(pot))
    flux = jnp.maximum(speed, 0.0) * lower(ions) + jnp.minimum(speed, 0.0) * upper(ions) - diffusion * (upper(ions) - lower(ions))
    return upper(flux) - lower(flux)

def field_of(padded):
    along_x = -(padded[2:, 1:-1, 1:-1] - padded[:-2, 1:-1, 1:-1]) * 0.5
    along_y = -(padded[1:-1, 2:, 1:-1] - padded[1:-1, :-2, 1:-1]) * 0.5
    along_z = -(padded[1:-1, 1:-1, 2:] - padded[1:-1, 1:-1, :-2]) * 0.5
    return jnp.stack([along_x, along_y, along_z])

def reference(positions, charges, cluster_fill, cluster_cell, send_index, send_count, pair_local, pair_dir, pair_slot, ion_density, potential_prev, screening):
    total = cluster_fill.shape[0]
    lanes = jnp.arange(PSIZE, dtype=jnp.int32)
    qmask = charges.reshape(total, PSIZE) * (lanes[None, :] < cluster_fill[:, None]).astype(jnp.float32)
    cluster_data = jnp.concatenate([positions.reshape(3, total, PSIZE).transpose(1, 0, 2), qmask[:, None, :]], axis=1)
    cluster_ids = jnp.arange(total, dtype=jnp.int32)
    owner = cluster_ids // CL_DEV
    grp_of = owner // N_BRICK
    brick_of = owner % N_BRICK
    cell_i = cluster_cell // (GY * GZ)
    cell_j = cluster_cell // GZ % GY
    cell_k = cluster_cell % GZ
    width_y = GY * N_BRICK
    flat = ((grp_of * GX + cell_i) * width_y + brick_of * GY + cell_j) * GZ + cell_k
    length_x = GX * N_GRP
    deposit = jnp.zeros(length_x * width_y * GZ, jnp.float32).at[flat].add(lax.optimization_barrier(jnp.sum(qmask, axis=1))).reshape(length_x, width_y, GZ)
    rhs = ion_density + deposit_scale * deposit
    pair_ids = jnp.arange(pair_local.shape[0], dtype=jnp.int32)
    device = pair_ids // PAIRS_DEV
    step_g, step_b = offsets_of(pair_dir)
    source = (device // N_BRICK + step_g) * N_BRICK + device % N_BRICK + step_b
    partner = source * CL_DEV + send_index[source * DIRS + pair_dir, pair_slot]
    alive = (pair_slot < send_count[source, pair_dir]).astype(jnp.float32)
    own_ids = device * CL_DEV + pair_local
    block = math.gcd(pair_local.shape[0], 256)

    def visit(accum, items):
        own_rows, other_rows, live_rows = items
        own = cluster_data[own_rows]
        other = cluster_data[other_rows]
        other = jnp.concatenate([other[:, :3], (other[:, 3] * live_rows[:, None])[:, None]], axis=1)
        pull_own, pull_other = tile_forces(own, other)
        accum = accum.at[own_rows].add(pull_own).at[other_rows].add(-pull_other)
        return (accum, None)
    coulomb, _ = lax.scan(visit, jnp.zeros((total, 3, PSIZE), jnp.float32), (own_ids.reshape(-1, block), partner.reshape(-1, block), alive.reshape(-1, block)))
    potential = chebyshev(potential_prev, rhs, screening)
    padded_pot = jnp.pad(potential, 1)
    padded_ion = jnp.pad(ion_density, 1)
    ion_next = ion_density - time_step * (face_div(padded_pot, padded_ion, 0) + face_div(padded_pot, padded_ion, 1) + face_div(padded_pot, padded_ion, 2))
    ecell = field_of(padded_pot).reshape(3, -1)[:, flat]
    forces = coulomb.transpose(1, 0, 2) + field_scale * qmask[None] * ecell[:, :, None]
    return (forces.reshape(3, -1), potential, ion_next)
```

```python
import jax
import jax.numpy as jnp
from jax import lax
from jax.experimental import pallas as pl
from jax.experimental.pallas import tpu as pltpu
from jax.sharding import PartitionSpec as P

SWEEPS = 4
UNROLL = 4


coulomb_scale = 0.02
softening = 0.1
field_scale = 0.5
deposit_scale = 0.2
lowest_eig = 0.01
highest_eig = 1.99
mobility = 0.3
diffusion = 0.2
time_step = 0.2


def extended(shard, sides, width):
    for axis, dim in sides:
        devices, length = (lax.axis_size(axis), shard.shape[dim])
        up = [(i, (i + 1) % devices) for i in range(devices - 1)]
        down = [(j, i) for i, j in up]
        last = lax.slice_in_dim(shard, length - width, length, axis=dim)
        initial = lax.slice_in_dim(shard, 0, width, axis=dim)
        before = lax.ppermute(last, axis, up)
        after = lax.ppermute(initial, axis, down)
        shard = jnp.concatenate([before, shard, after], axis=dim)
    return shard


def passed_along(shard, axis, by):
    devices = lax.axis_size(axis)
    pairs = [(i, i + by) for i in range(devices) if 0 <= i + by < devices]
    return lax.ppermute(shard, axis, pairs)


def stencil_core(padded, center, screen):
    beside = padded[2:, 1:-1, 1:-1] + padded[:-2, 1:-1, 1:-1]
    beside = beside + padded[1:-1, 2:, 1:-1] + padded[1:-1, :-2, 1:-1]
    beside = beside + padded[1:-1, 1:-1, 2:] + padded[1:-1, 1:-1, :-2]
    return (6.0 + screen) * center - beside


def operate_rim(field, screen):
    rimmed = extended(field, (("grp", 0), ("brick", 1)), 1)
    padded = jnp.pad(rimmed, ((0, 0), (0, 0), (1, 1)))
    return stencil_core(padded, field, screen)


def chebyshev(start, rhs, screen, operate, inside):
    middle = 0.5 * (highest_eig + lowest_eig)
    spread = 0.5 * (highest_eig - lowest_eig)
    ratio_ms = middle / spread
    weight_now = 1.0 / ratio_ms
    inverse = 1.0 / (6.0 + screen)
    solution = start
    resid = rhs - operate(solution, screen)
    update = inside * (inverse * resid / middle)
    for turn in range(SWEEPS):
        solution = solution + update
        if turn + 1 < SWEEPS:
            resid = resid - operate(update, screen)
            weight_next = 1.0 / (2.0 * ratio_ms - weight_now)
            update = inside * (
                weight_next * weight_now * update + 2.0 * weight_next / spread * (inverse * resid)
            )
            weight_now = weight_next
    return solution


def split3(value):
    first = value.astype(jnp.bfloat16).astype(jnp.float32)
    rest = value - first
    second = rest.astype(jnp.bfloat16).astype(jnp.float32)
    third = (rest - second).astype(jnp.bfloat16).astype(jnp.float32)
    return (first, second, third)


def moment_rows(comps, charge, rows_ref, base):
    for part, charged in enumerate((*comps, None)):
        pieces = split3(charge if charged is None else charge * charged)
        for level, piece in enumerate(pieces):
            rows_ref[pl.ds(base + 4 * level + part, 8, stride=16), :] = piece


def pair_kernel(
    own_rows_ref,
    other_rows_ref,
    own_ref,
    other_ref,
    own_out_ref,
    other_out_ref,
    near_ref,
    far_ref,
    own_moment_ref,
    other_moment_ref,
    own_sum_ref,
    other_sum_ref,
    stage_ref,
):
    clusters = own_ref.shape[0] // 4
    others = other_ref.shape[0] // 4
    pairs = own_rows_ref.shape[0]
    ones = jnp.ones((8, 128), jnp.float32)
    zeros = jnp.zeros((8, 128), jnp.float32)

    def components(data_ref, start):
        return [data_ref[pl.ds(4 * start + part, 8, stride=4), :] for part in range(4)]

    def put(rows, base, stride):
        for index, row in enumerate(rows):
            stage_ref[pl.ds(base + index, 8, stride=stride), :] = row

    stage_ref[...] = jnp.zeros_like(stage_ref)

    def near_rows(step, _):
        start = pl.multiple_of(step * 8, 8)
        *comps, charge = components(own_ref, start)
        moment_rows(comps, charge, stage_ref, 0)
        own_moment_ref[pl.ds(pl.multiple_of(start * 16, 128), 128), :] = stage_ref[0:128, :].astype(
            jnp.bfloat16
        )
        rows = []
        square = zeros
        for comp in comps:
            first, second, third = split3(comp)
            square = square + comp * comp
            rows += [first, first, first, second, second, third]
        rows += [*split3(square), ones, ones, ones]
        rows += [zeros] * (32 - len(rows))
        put(rows, 0, 32)
        for half in range(2):
            block = stage_ref[128 * half : 128 * half + 128, :]
            near_ref[pl.ds(pl.multiple_of(step * 256 + half * 128, 128), 128), :] = block.T.astype(
                jnp.bfloat16
            )
        return 0

    def far_rows(step, _):
        start = pl.multiple_of(step * 8, 8)
        *comps, charge = components(other_ref, start)
        moment_rows(comps, charge, stage_ref, 0)
        other_moment_ref[pl.ds(pl.multiple_of(start * 16, 128), 128), :] = stage_ref[
            0:128, :
        ].astype(jnp.bfloat16)
        rows = []
        square = zeros
        for comp in comps:
            first, second, third = split3(-2.0 * comp)
            square = square + comp * comp
            rows += [first, second, third, first, second, first]
        rows += [ones, ones, ones, *split3(square + softening)]
        rows += [zeros] * (32 - len(rows))
        put(rows, 0, 32)
        for index in range(8):
            target = pl.multiple_of((start + index) * 128, 128)
            far_ref[pl.ds(target, 96), :] = jnp.zeros((96, 128), jnp.bfloat16)
            far_ref[pl.ds(target + 96, 32), :] = stage_ref[32 * index : 32 * index + 32, :].astype(
                jnp.bfloat16
            )
        return 0

    lax.fori_loop(0, clusters // 8, near_rows, 0)
    lax.fori_loop(0, others // 8, far_rows, 0)
    far_ref[pl.ds(others * 128, 128), :] = jnp.zeros((128, 128), jnp.bfloat16)
    own_sum_ref[...] = jnp.zeros_like(own_sum_ref)
    other_sum_ref[...] = jnp.zeros_like(other_sum_ref)

    def pull(pair):
        own = own_rows_ref[pair]
        other = other_rows_ref[pair]
        group = lax.shift_right_logical(own, 2)
        member = lax.bitwise_and(own, 3)
        near = near_ref[pl.ds(pl.multiple_of(group * 128, 128), 128), :]
        far = far_ref[pl.ds(pl.multiple_of(other * 128 + 96 - member * 32, 32), 128), :]
        dist = jnp.dot(near, far, preferred_element_type=jnp.float32)
        root = lax.rsqrt(dist)
        weight = root * root * root
        high = weight.astype(jnp.bfloat16)
        low = (weight - high.astype(jnp.float32)).astype(jnp.bfloat16)
        both = jnp.concatenate([high, low], axis=1)
        own_at = pl.ds(pl.multiple_of(own * 16, 16), 16)
        other_at = pl.ds(pl.multiple_of(other * 16, 16), 16)
        own_moment = own_moment_ref[own_at, :]
        other_moment = other_moment_ref[other_at, :]
        to_own = lax.dot_general(
            jnp.concatenate([other_moment, other_moment], axis=1),
            both,
            (((1,), (1,)), ((), ())),
            preferred_element_type=jnp.float32,
        )
        to_other = jnp.dot(own_moment, both, preferred_element_type=jnp.float32)
        return (own_at, other_at, to_own, to_other[:, :128] + to_other[:, 128:])

    def visit(step, _):
        results = [pull(step * UNROLL + turn) for turn in range(UNROLL)]
        for own_at, other_at, to_own, to_other in results:
            own_sum_ref[own_at, :] += to_own
            other_sum_ref[other_at, :] += to_other
        return 0

    lax.fori_loop(0, pairs // UNROLL, visit, 0)

    def finish(data_ref, sum_ref, out_ref):
        def body(step, _):
            start = pl.multiple_of(step * 8, 8)
            *comps, charge = components(data_ref, start)

            def total(part):
                terms = [
                    sum_ref[pl.ds(start * 16 + 4 * level + part, 8, stride=16), :]
                    for level in range(3)
                ]
                return terms[0] + (terms[1] + terms[2])

            weight = total(3)
            scale = coulomb_scale * charge
            for part, comp in enumerate(comps):
                out_ref[pl.ds(4 * start + part, 8, stride=4), :] = scale * (
                    comp * weight - total(part)
                )
            out_ref[pl.ds(4 * start + 3, 8, stride=4), :] = zeros
            return 0

        lax.fori_loop(0, data_ref.shape[0] // 32, body, 0)

    finish(own_ref, own_sum_ref, own_out_ref)
    finish(other_ref, other_sum_ref, other_out_ref)


def pair_forces(own_rows, other_rows, own, other):
    clusters = own.shape[0] // 4
    others = other.shape[0] // 4
    pairs = own_rows.shape[0]
    smem = pl.BlockSpec(memory_space=pltpu.SMEM)
    vmem = pl.BlockSpec(memory_space=pltpu.VMEM)
    return pl.pallas_call(
        pair_kernel,
        out_shape=(
            jax.ShapeDtypeStruct(own.shape, jnp.float32),
            jax.ShapeDtypeStruct(other.shape, jnp.float32),
        ),
        in_specs=[smem, smem, vmem, vmem],
        out_specs=(vmem, vmem),
        scratch_shapes=[
            pltpu.VMEM((clusters * 32, 128), jnp.bfloat16),
            pltpu.VMEM(((others + 1) * 128, 128), jnp.bfloat16),
            pltpu.VMEM((clusters * 16, 128), jnp.bfloat16),
            pltpu.VMEM((others * 16, 128), jnp.bfloat16),
            pltpu.VMEM((clusters * 16, 128), jnp.float32),
            pltpu.VMEM((others * 16, 128), jnp.float32),
            pltpu.VMEM((256, 128), jnp.float32),
        ],
        compiler_params=pltpu.CompilerParams(vmem_limit_bytes=40 * 1024 * 1024),
        cost_estimate=pl.CostEstimate(
            flops=pairs * 128 * 128 * 20, bytes_accessed=4 * 1024 * 1024, transcendentals=0
        ),
        name="pair_forces",
    )(own_rows, other_rows, own, other)


def face_div(pot, ions, axis):
    inner = [slice(1, -1), slice(1, -1), slice(1, -1)]
    inner[axis] = slice(None)
    pot = pot[tuple(inner)]
    ions = ions[tuple(inner)]

    def upper(arr):
        return lax.slice_in_dim(arr, 1, arr.shape[axis], axis=axis)

    def lower(arr):
        return lax.slice_in_dim(arr, 0, arr.shape[axis] - 1, axis=axis)

    speed = -mobility * (upper(pot) - lower(pot))
    flux = (
        jnp.maximum(speed, 0.0) * lower(ions)
        + jnp.minimum(speed, 0.0) * upper(ions)
        - diffusion * (upper(ions) - lower(ions))
    )
    return upper(flux) - lower(flux)


def field_of(padded):
    along_x = -(padded[2:, 1:-1, 1:-1] - padded[:-2, 1:-1, 1:-1]) * 0.5
    along_y = -(padded[1:-1, 2:, 1:-1] - padded[1:-1, :-2, 1:-1]) * 0.5
    along_z = -(padded[1:-1, 1:-1, 2:] - padded[1:-1, 1:-1, :-2]) * 0.5
    return jnp.stack([along_x, along_y, along_z])


def shards(
    positions,
    charges,
    cluster_fill,
    cluster_cell,
    send_index,
    send_count,
    pair_local,
    pair_dir,
    pair_slot,
    ion_density,
    potential_prev,
    screening,
):
    clusters = cluster_fill.shape[0]
    psize = charges.shape[0] // clusters
    directions = send_index.shape[0]
    slots = send_index.shape[1]
    lanes = jnp.arange(psize, dtype=jnp.int32)
    qmask = charges.reshape(clusters, psize) * (lanes[None, :] < cluster_fill[:, None]).astype(
        jnp.float32
    )
    cluster_data = jnp.concatenate(
        [positions.reshape(3, clusters, psize).transpose(1, 0, 2), qmask[:, None, :]], axis=1
    )
    cells_x, cells_y, cells_z = ion_density.shape
    deposit = (
        jnp.zeros(cells_x * cells_y * cells_z, jnp.float32)
        .at[cluster_cell]
        .add(jnp.sum(qmask, axis=1))
    )
    rhs = ion_density + deposit_scale * deposit.reshape(cells_x, cells_y, cells_z)
    slot_ids = jnp.arange(slots, dtype=jnp.int32)
    slot_live = (slot_ids[None, :] < send_count.reshape(directions, 1)).astype(jnp.float32)
    outgoing = cluster_data[send_index]
    outgoing = jnp.concatenate(
        [outgoing[:, :, :3], (outgoing[:, :, 3] * slot_live[:, :, None])[:, :, None]], axis=2
    )
    pieces = [outgoing[0]]
    for offset in (-1, 1, -2, 2):
        pieces.append(passed_along(outgoing[len(pieces)], "brick", -offset))
    for offset in (-1, 1):
        pieces.append(passed_along(outgoing[len(pieces)], "grp", -offset))
    arrived = jnp.stack(pieces).reshape(directions * slots, 4, psize)
    partner_row = pair_dir * slots + pair_slot

    own_force, react = pair_forces(
        pair_local, partner_row, cluster_data.reshape(-1, psize), arrived.reshape(-1, psize)
    )
    own_force = own_force.reshape(clusters, 4, psize)[:, :3]
    react = react.reshape(directions, slots, 4, psize)[:, :, :3]
    backs = [react[0]]
    for offset in (-1, 1, -2, 2):
        backs.append(passed_along(react[len(backs)], "brick", offset))
    for offset in (-1, 1):
        backs.append(passed_along(react[len(backs)], "grp", offset))
    returned = jnp.stack(backs).reshape(directions * slots, 3, psize)
    coulomb = own_force.at[send_index.reshape(-1)].add(returned)
    potential = chebyshev(potential_prev, rhs, screening, operate_rim, 1.0)
    rimmed = extended(jnp.stack([potential, ion_density]), (("grp", 1), ("brick", 2)), 1)
    rimmed = jnp.pad(rimmed, ((0, 0), (0, 0), (0, 0), (1, 1)))
    padded_pot = rimmed[0]
    padded_ion = rimmed[1]
    ion_next = ion_density - time_step * (
        face_div(padded_pot, padded_ion, 0)
        + face_div(padded_pot, padded_ion, 1)
        + face_div(padded_pot, padded_ion, 2)
    )
    ecell = field_of(padded_pot).reshape(3, -1)[:, cluster_cell]
    forces = coulomb.transpose(1, 0, 2) + field_scale * qmask[None] * ecell[:, :, None]
    return (forces.reshape(3, -1), potential, ion_next)


def solution(mesh):
    in_specs = (
        P(None, ("grp", "brick")),
        P(("grp", "brick")),
        P(("grp", "brick")),
        P(("grp", "brick")),
        P(("grp", "brick"), None),
        P(("grp", "brick"), None),
        P(("grp", "brick")),
        P(("grp", "brick")),
        P(("grp", "brick")),
        P("grp", "brick", None),
        P("grp", "brick", None),
        P("grp", "brick", None),
    )
    out_specs = (P(None, ("grp", "brick")), P("grp", "brick", None), P("grp", "brick", None))
    return jax.shard_map(shards, mesh=mesh, in_specs=in_specs, out_specs=out_specs, check_vma=False)
```

```python
import jax
import jax.numpy as jnp
from jax import lax
from jax.experimental import pallas as pl
from jax.experimental.pallas import tpu as pltpu
from jax.sharding import PartitionSpec as P

SWEEPS = 4
UNROLL = 4


coulomb_scale = 0.02
softening = 0.1
field_scale = 0.5
deposit_scale = 0.2
lowest_eig = 0.01
highest_eig = 1.99
mobility = 0.3
diffusion = 0.2
time_step = 0.2


def extended(shard, sides, width):
    for axis, dim in sides:
        devices, length = (lax.axis_size(axis), shard.shape[dim])
        up = [(i, (i + 1) % devices) for i in range(devices - 1)]
        down = [(j, i) for i, j in up]
        last = lax.slice_in_dim(shard, length - width, length, axis=dim)
        initial = lax.slice_in_dim(shard, 0, width, axis=dim)
        before = lax.ppermute(last, axis, up)
        after = lax.ppermute(initial, axis, down)
        shard = jnp.concatenate([before, shard, after], axis=dim)
    return shard


def passed_along(shard, axis, by):
    devices = lax.axis_size(axis)
    pairs = [(i, i + by) for i in range(devices) if 0 <= i + by < devices]
    return lax.ppermute(shard, axis, pairs)


def stencil_core(padded, center, screen):
    beside = padded[2:, 1:-1, 1:-1] + padded[:-2, 1:-1, 1:-1]
    beside = beside + padded[1:-1, 2:, 1:-1] + padded[1:-1, :-2, 1:-1]
    beside = beside + padded[1:-1, 1:-1, 2:] + padded[1:-1, 1:-1, :-2]
    return (6.0 + screen) * center - beside


def operate_rim(field, screen):
    rimmed = extended(field, (("grp", 0), ("brick", 1)), 1)
    padded = jnp.pad(rimmed, ((0, 0), (0, 0), (1, 1)))
    return stencil_core(padded, field, screen)


def chebyshev(start, rhs, screen, operate, inside):
    middle = 0.5 * (highest_eig + lowest_eig)
    spread = 0.5 * (highest_eig - lowest_eig)
    ratio_ms = middle / spread
    weight_now = 1.0 / ratio_ms
    inverse = 1.0 / (6.0 + screen)
    solution = start
    resid = rhs - operate(solution, screen)
    update = inside * (inverse * resid / middle)
    for turn in range(SWEEPS):
        solution = solution + update
        if turn + 1 < SWEEPS:
            resid = resid - operate(update, screen)
            weight_next = 1.0 / (2.0 * ratio_ms - weight_now)
            update = inside * (
                weight_next * weight_now * update + 2.0 * weight_next / spread * (inverse * resid)
            )
            weight_now = weight_next
    return solution


def split3(value):
    first = value.astype(jnp.bfloat16).astype(jnp.float32)
    rest = value - first
    second = rest.astype(jnp.bfloat16).astype(jnp.float32)
    third = (rest - second).astype(jnp.bfloat16).astype(jnp.float32)
    return (first, second, third)


def moment_rows(comps, charge, rows_ref, base):
    for part, charged in enumerate((*comps, None)):
        pieces = split3(charge if charged is None else charge * charged)
        for level, piece in enumerate(pieces):
            rows_ref[pl.ds(base + 4 * level + part, 8, stride=16), :] = piece


def pair_kernel(
    own_rows_ref,
    other_rows_ref,
    own_ref,
    other_ref,
    own_out_ref,
    other_out_ref,
    near_ref,
    far_ref,
    own_moment_ref,
    other_moment_ref,
    own_sum_ref,
    other_sum_ref,
    stage_ref,
    dist_ref,
    weight_ref,
):
    clusters = own_ref.shape[0] // 4
    others = other_ref.shape[0] // 4
    groups = own_rows_ref.shape[0] // UNROLL
    ones = jnp.ones((8, 128), jnp.float32)
    zeros = jnp.zeros((8, 128), jnp.float32)
    stage_ref[...] = jnp.zeros_like(stage_ref)

    def components(data_ref, start):
        return [data_ref[pl.ds(4 * start + part, 8, stride=4), :] for part in range(4)]

    def put(rows, base, stride):
        for index, row in enumerate(rows):
            stage_ref[pl.ds(base + index, 8, stride=stride), :] = row

    def near_rows(step, _):
        start = pl.multiple_of(step * 8, 8)
        *comps, charge = components(own_ref, start)
        moment_rows(comps, charge, stage_ref, 0)
        own_moment_ref[pl.ds(pl.multiple_of(start * 16, 128), 128), :] = stage_ref[0:128, :].astype(
            jnp.bfloat16
        )
        rows = []
        square = zeros
        for comp in comps:
            first, second, third = split3(comp)
            square = square + comp * comp
            rows += [first, first, first, second, second, third]
        rows += [*split3(square), ones, ones, ones]
        rows += [zeros] * (32 - len(rows))
        put(rows, 0, 32)
        for half in range(2):
            block = stage_ref[128 * half : 128 * half + 128, :]
            near_ref[pl.ds(pl.multiple_of(step * 256 + half * 128, 128), 128), :] = block.T.astype(
                jnp.bfloat16
            )
        for index in range(8):
            own_sum_ref[pl.ds(pl.multiple_of((start + index) * 128, 128), 128), :] = jnp.zeros(
                (128, 128), jnp.float32
            )
        return 0

    def far_rows(step, _):
        start = pl.multiple_of(step * 8, 8)
        *comps, charge = components(other_ref, start)
        moment_rows(comps, charge, stage_ref, 0)
        columns = stage_ref[0:128, :].T
        rows = []
        square = zeros
        for comp in comps:
            first, second, third = split3(-2.0 * comp)
            square = square + comp * comp
            rows += [first, second, third, first, second, first]
        rows += [ones, ones, ones, *split3(square + softening)]
        rows += [zeros] * (32 - len(rows))
        put(rows, 0, 32)
        for index in range(8):
            target = pl.multiple_of((start + index) * 128, 128)
            far_ref[pl.ds(target, 96), :] = jnp.zeros((96, 128), jnp.bfloat16)
            far_ref[pl.ds(target + 96, 32), :] = stage_ref[32 * index : 32 * index + 32, :].astype(
                jnp.bfloat16
            )
            rolled = columns if index == 0 else pltpu.roll(columns, 128 - 16 * index, 1)
            other_moment_ref[pl.ds(target, 128), :] = rolled.astype(jnp.bfloat16)
        return 0

    lax.fori_loop(0, clusters // 8, near_rows, 0)
    lax.fori_loop(0, others // 8, far_rows, 0)
    far_ref[pl.ds(others * 128, 128), :] = jnp.zeros((128, 128), jnp.bfloat16)
    other_sum_ref[...] = jnp.zeros_like(other_sum_ref)
    dist_ref[...] = jnp.full(dist_ref.shape, 1e38, jnp.float32)
    weight_ref[...] = jnp.zeros_like(weight_ref)

    def distances(pair, turn):
        own = own_rows_ref[pair]
        other = other_rows_ref[pair]
        group = lax.shift_right_logical(own, 2)
        member = lax.bitwise_and(own, 3)
        near = near_ref[pl.ds(pl.multiple_of(group * 128, 128), 128), :]
        far = far_ref[pl.ds(pl.multiple_of(other * 128 + 96 - member * 32, 32), 128), :]
        dist_ref[turn] = jnp.dot(near, far, preferred_element_type=jnp.float32)

    def weights(turn):
        root = lax.rsqrt(dist_ref[turn])
        weight = root * root * root
        high = weight.astype(jnp.bfloat16)
        weight_ref[turn, :, :128] = high
        weight_ref[turn, :, 128:] = (weight - high.astype(jnp.float32)).astype(jnp.bfloat16)

    def products(pair, turn):
        own = own_rows_ref[pair]
        other = other_rows_ref[pair]
        both = weight_ref[turn]
        moment = other_moment_ref[pl.ds(pl.multiple_of(other * 128, 128), 128), :]
        to_own = jnp.dot(
            both,
            jnp.concatenate([moment, moment], axis=0),
            preferred_element_type=jnp.float32,
        )
        to_other = jnp.dot(
            own_moment_ref[pl.ds(pl.multiple_of(own * 16, 16), 16), :],
            both,
            preferred_element_type=jnp.float32,
        )
        return (own, other, to_own, to_other[:, :128] + to_other[:, 128:])

    def visit(step, _):
        last = jnp.maximum(step - 2, 0) * UNROLL
        first = jnp.minimum(step, groups - 1) * UNROLL
        results = [products(last + turn, turn) for turn in range(UNROLL)]
        for turn in range(UNROLL):
            weights(turn)
        for turn in range(UNROLL):
            distances(first + turn, turn)
        for own, other, to_own, to_other in results:
            own_sum_ref[pl.ds(pl.multiple_of(own * 128, 128), 128), :] += to_own
            other_sum_ref[pl.ds(pl.multiple_of(other * 16, 16), 16), :] += to_other
        return 0

    lax.fori_loop(0, groups + 2, visit, 0)

    def finish(data_ref, out_ref, start, rows_ref, base):
        *comps, charge = components(data_ref, start)

        def total(part):
            terms = [
                rows_ref[pl.ds(base + 4 * level + part, 8, stride=16), :] for level in range(3)
            ]
            return terms[0] + (terms[1] + terms[2])

        weight = total(3)
        scale = coulomb_scale * charge
        for part, comp in enumerate(comps):
            out_ref[pl.ds(4 * start + part, 8, stride=4), :] = scale * (comp * weight - total(part))
        out_ref[pl.ds(4 * start + 3, 8, stride=4), :] = zeros

    def finish_own(step, _):
        start = pl.multiple_of(step * 8, 8)
        lane = lax.broadcasted_iota(jnp.int32, (128, 128), 1)
        columns = own_sum_ref[pl.ds(pl.multiple_of(start * 128, 128), 128), :]
        for index in range(1, 8):
            block = own_sum_ref[pl.ds(pl.multiple_of((start + index) * 128, 128), 128), :]
            columns = jnp.where(lane < 16 * index, columns, pltpu.roll(block, 16 * index, 1))
        stage_ref[0:128, :] = columns.T
        finish(own_ref, own_out_ref, start, stage_ref, 0)
        return 0

    def finish_other(step, _):
        start = pl.multiple_of(step * 8, 8)
        finish(other_ref, other_out_ref, start, other_sum_ref, start * 16)
        return 0

    lax.fori_loop(0, clusters // 8, finish_own, 0)
    lax.fori_loop(0, others // 8, finish_other, 0)


def pair_forces(own_rows, other_rows, own, other):
    clusters = own.shape[0] // 4
    others = other.shape[0] // 4
    pairs = own_rows.shape[0]
    smem = pl.BlockSpec(memory_space=pltpu.SMEM)
    vmem = pl.BlockSpec(memory_space=pltpu.VMEM)
    return pl.pallas_call(
        pair_kernel,
        out_shape=(
            jax.ShapeDtypeStruct(own.shape, jnp.float32),
            jax.ShapeDtypeStruct(other.shape, jnp.float32),
        ),
        in_specs=[smem, smem, vmem, vmem],
        out_specs=(vmem, vmem),
        scratch_shapes=[
            pltpu.VMEM((clusters * 32, 128), jnp.bfloat16),
            pltpu.VMEM(((others + 1) * 128, 128), jnp.bfloat16),
            pltpu.VMEM((clusters * 16, 128), jnp.bfloat16),
            pltpu.VMEM((others * 128, 128), jnp.bfloat16),
            pltpu.VMEM((clusters * 128, 128), jnp.float32),
            pltpu.VMEM((others * 16, 128), jnp.float32),
            pltpu.VMEM((256, 128), jnp.float32),
            pltpu.VMEM((UNROLL, 128, 128), jnp.float32),
            pltpu.VMEM((UNROLL, 128, 256), jnp.bfloat16),
        ],
        compiler_params=pltpu.CompilerParams(vmem_limit_bytes=48 * 1024 * 1024),
        cost_estimate=pl.CostEstimate(
            flops=pairs * 128 * 128 * 20, bytes_accessed=4 * 1024 * 1024, transcendentals=0
        ),
        name="pair_forces",
    )(own_rows, other_rows, own, other)


def face_div(pot, ions, axis):
    inner = [slice(1, -1), slice(1, -1), slice(1, -1)]
    inner[axis] = slice(None)
    pot = pot[tuple(inner)]
    ions = ions[tuple(inner)]

    def upper(arr):
        return lax.slice_in_dim(arr, 1, arr.shape[axis], axis=axis)

    def lower(arr):
        return lax.slice_in_dim(arr, 0, arr.shape[axis] - 1, axis=axis)

    speed = -mobility * (upper(pot) - lower(pot))
    flux = (
        jnp.maximum(speed, 0.0) * lower(ions)
        + jnp.minimum(speed, 0.0) * upper(ions)
        - diffusion * (upper(ions) - lower(ions))
    )
    return upper(flux) - lower(flux)


def field_of(padded):
    along_x = -(padded[2:, 1:-1, 1:-1] - padded[:-2, 1:-1, 1:-1]) * 0.5
    along_y = -(padded[1:-1, 2:, 1:-1] - padded[1:-1, :-2, 1:-1]) * 0.5
    along_z = -(padded[1:-1, 1:-1, 2:] - padded[1:-1, 1:-1, :-2]) * 0.5
    return jnp.stack([along_x, along_y, along_z])


def shards(
    positions,
    charges,
    cluster_fill,
    cluster_cell,
    send_index,
    send_count,
    pair_local,
    pair_dir,
    pair_slot,
    ion_density,
    potential_prev,
    screening,
):
    clusters = cluster_fill.shape[0]
    psize = charges.shape[0] // clusters
    directions = send_index.shape[0]
    slots = send_index.shape[1]
    lanes = jnp.arange(psize, dtype=jnp.int32)
    qmask = charges.reshape(clusters, psize) * (lanes[None, :] < cluster_fill[:, None]).astype(
        jnp.float32
    )
    cluster_data = jnp.concatenate(
        [positions.reshape(3, clusters, psize).transpose(1, 0, 2), qmask[:, None, :]], axis=1
    )
    cells_x, cells_y, cells_z = ion_density.shape
    deposit = (
        jnp.zeros(cells_x * cells_y * cells_z, jnp.float32)
        .at[cluster_cell]
        .add(jnp.sum(qmask, axis=1))
    )
    rhs = ion_density + deposit_scale * deposit.reshape(cells_x, cells_y, cells_z)
    slot_ids = jnp.arange(slots, dtype=jnp.int32)
    slot_live = (slot_ids[None, :] < send_count.reshape(directions, 1)).astype(jnp.float32)
    outgoing = cluster_data[send_index]
    outgoing = jnp.concatenate(
        [outgoing[:, :, :3], (outgoing[:, :, 3] * slot_live[:, :, None])[:, :, None]], axis=2
    )
    pieces = [outgoing[0]]
    for offset in (-1, 1, -2, 2):
        pieces.append(passed_along(outgoing[len(pieces)], "brick", -offset))
    for offset in (-1, 1):
        pieces.append(passed_along(outgoing[len(pieces)], "grp", -offset))
    arrived = jnp.stack(pieces).reshape(directions * slots, 4, psize)
    partner_row = pair_dir * slots + pair_slot

    own_force, react = pair_forces(
        pair_local, partner_row, cluster_data.reshape(-1, psize), arrived.reshape(-1, psize)
    )
    own_force = own_force.reshape(clusters, 4, psize)[:, :3]
    react = react.reshape(directions, slots, 4, psize)[:, :, :3]
    backs = [react[0]]
    for offset in (-1, 1, -2, 2):
        backs.append(passed_along(react[len(backs)], "brick", offset))
    for offset in (-1, 1):
        backs.append(passed_along(react[len(backs)], "grp", offset))
    returned = jnp.stack(backs).reshape(directions * slots, 3, psize)
    coulomb = own_force.at[send_index.reshape(-1)].add(returned)
    potential = chebyshev(potential_prev, rhs, screening, operate_rim, 1.0)
    rimmed = extended(jnp.stack([potential, ion_density]), (("grp", 1), ("brick", 2)), 1)
    rimmed = jnp.pad(rimmed, ((0, 0), (0, 0), (0, 0), (1, 1)))
    padded_pot = rimmed[0]
    padded_ion = rimmed[1]
    ion_next = ion_density - time_step * (
        face_div(padded_pot, padded_ion, 0)
        + face_div(padded_pot, padded_ion, 1)
        + face_div(padded_pot, padded_ion, 2)
    )
    ecell = field_of(padded_pot).reshape(3, -1)[:, cluster_cell]
    forces = coulomb.transpose(1, 0, 2) + field_scale * qmask[None] * ecell[:, :, None]
    return (forces.reshape(3, -1), potential, ion_next)


def solution(mesh):
    in_specs = (
        P(None, ("grp", "brick")),
        P(("grp", "brick")),
        P(("grp", "brick")),
        P(("grp", "brick")),
        P(("grp", "brick"), None),
        P(("grp", "brick"), None),
        P(("grp", "brick")),
        P(("grp", "brick")),
        P(("grp", "brick")),
        P("grp", "brick", None),
        P("grp", "brick", None),
        P("grp", "brick", None),
    )
    out_specs = (P(None, ("grp", "brick")), P("grp", "brick", None), P("grp", "brick", None))
    return jax.shard_map(shards, mesh=mesh, in_specs=in_specs, out_specs=out_specs, check_vma=False)
```

```python
import functools

import jax
import jax.numpy as jnp
from jax import lax
from jax.experimental import pallas as pl
from jax.experimental.pallas import tpu as pltpu
from jax.sharding import PartitionSpec as P

SWEEPS = 4
UNROLL = 4
HALO_WIDTHS = (SWEEPS + 1, SWEEPS, SWEEPS, 1)
MARGIN = 8
CELL_BITS = 8


coulomb_scale = 0.02
softening = 0.1
field_scale = 0.5
deposit_scale = 0.2
lowest_eig = 0.01
highest_eig = 1.99
mobility = 0.3
diffusion = 0.2
time_step = 0.2


def split3(value):
    first = value.astype(jnp.bfloat16).astype(jnp.float32)
    rest = value - first
    second = rest.astype(jnp.bfloat16).astype(jnp.float32)
    third = (rest - second).astype(jnp.bfloat16).astype(jnp.float32)
    return (first, second, third)


def moment_rows(comps, charge, rows_ref, base):
    for part, charged in enumerate((*comps, None)):
        pieces = split3(charge if charged is None else charge * charged)
        for level, piece in enumerate(pieces):
            rows_ref[pl.ds(base + 4 * level + part, 8, stride=16), :] = piece


def pair_kernel(
    own_rows_ref,
    other_rows_ref,
    own_ref,
    *refs,
):
    sources = (len(refs) - 10) // 2
    other_refs = refs[:sources]
    own_out_ref = refs[sources]
    other_out_refs = refs[sources + 1 : 2 * sources + 1]
    pair_body(
        own_rows_ref,
        other_rows_ref,
        own_ref,
        other_refs,
        own_out_ref,
        other_out_refs,
        *refs[2 * sources + 1 :],
    )


def pair_body(
    own_rows_ref,
    other_rows_ref,
    own_ref,
    other_refs,
    own_out_ref,
    other_out_refs,
    near_ref,
    far_ref,
    own_moment_ref,
    other_moment_ref,
    own_sum_ref,
    other_sum_ref,
    stage_ref,
    dist_ref,
    weight_ref,
):
    clusters = own_ref.shape[0] // 4
    slots = other_out_refs[0].shape[0] // 4
    others = slots * len(other_refs)
    groups = own_rows_ref.shape[0] // UNROLL
    ones = jnp.ones((8, 128), jnp.float32)
    zeros = jnp.zeros((8, 128), jnp.float32)
    stage_ref[...] = jnp.zeros_like(stage_ref)

    def components(data_ref, start):
        return [data_ref[pl.ds(4 * start + part, 8, stride=4), :] for part in range(4)]

    def put(rows, base, stride):
        for index, row in enumerate(rows):
            stage_ref[pl.ds(base + index, 8, stride=stride), :] = row

    def near_rows(step, _):
        start = pl.multiple_of(step * 8, 8)
        *comps, charge = components(own_ref, start)
        moment_rows(comps, charge, stage_ref, 0)
        own_moment_ref[pl.ds(pl.multiple_of(start * 16, 128), 128), :] = stage_ref[0:128, :].astype(
            jnp.bfloat16
        )
        rows = []
        square = zeros
        for comp in comps:
            first, second, third = split3(comp)
            square = square + comp * comp
            rows += [first, first, first, second, second, third]
        rows += [*split3(square), ones, ones, ones]
        rows += [zeros] * (32 - len(rows))
        put(rows, 0, 32)
        for half in range(2):
            block = stage_ref[128 * half : 128 * half + 128, :]
            near_ref[pl.ds(pl.multiple_of(step * 256 + half * 128, 128), 128), :] = block.T.astype(
                jnp.bfloat16
            )
        for index in range(8):
            own_sum_ref[pl.ds(pl.multiple_of((start + index) * 128, 128), 128), :] = jnp.zeros(
                (128, 128), jnp.float32
            )
        return 0

    def far_rows(source, step, _):
        local = pl.multiple_of(step * 8, 8)
        start = source * slots + local
        *comps, charge = components(other_refs[source], local)
        moment_rows(comps, charge, stage_ref, 0)
        columns = stage_ref[0:128, :].T
        rows = []
        square = zeros
        for comp in comps:
            first, second, third = split3(-2.0 * comp)
            square = square + comp * comp
            rows += [first, second, third, first, second, first]
        rows += [ones, ones, ones, *split3(square + softening)]
        rows += [zeros] * (32 - len(rows))
        put(rows, 0, 32)
        for index in range(8):
            target = pl.multiple_of((start + index) * 128, 128)
            far_ref[pl.ds(target, 96), :] = jnp.zeros((96, 128), jnp.bfloat16)
            far_ref[pl.ds(target + 96, 32), :] = stage_ref[32 * index : 32 * index + 32, :].astype(
                jnp.bfloat16
            )
            rolled = columns if index == 0 else pltpu.roll(columns, 128 - 16 * index, 1)
            other_moment_ref[pl.ds(target, 128), :] = rolled.astype(jnp.bfloat16)
        return 0

    lax.fori_loop(0, clusters // 8, near_rows, 0)
    for source in range(len(other_refs)):
        lax.fori_loop(0, slots // 8, functools.partial(far_rows, source), 0)
    far_ref[pl.ds(others * 128, 128), :] = jnp.zeros((128, 128), jnp.bfloat16)
    other_sum_ref[...] = jnp.zeros_like(other_sum_ref)
    dist_ref[...] = jnp.full(dist_ref.shape, 1e38, jnp.float32)
    weight_ref[...] = jnp.zeros_like(weight_ref)

    def distances(pair, turn):
        own = own_rows_ref[pair]
        other = other_rows_ref[pair]
        group = lax.shift_right_logical(own, 2)
        member = lax.bitwise_and(own, 3)
        near = near_ref[pl.ds(pl.multiple_of(group * 128, 128), 128), :]
        far = far_ref[pl.ds(pl.multiple_of(other * 128 + 96 - member * 32, 32), 128), :]
        dist_ref[turn] = jnp.dot(near, far, preferred_element_type=jnp.float32)

    def weights(turn):
        root = lax.rsqrt(dist_ref[turn])
        weight = root * root * root
        high = weight.astype(jnp.bfloat16)
        weight_ref[turn, :, :128] = high
        weight_ref[turn, :, 128:] = (weight - high.astype(jnp.float32)).astype(jnp.bfloat16)

    def products(pair, turn):
        own = own_rows_ref[pair]
        other = other_rows_ref[pair]
        both = weight_ref[turn]
        moment = other_moment_ref[pl.ds(pl.multiple_of(other * 128, 128), 128), :]
        to_own = jnp.dot(
            both,
            jnp.concatenate([moment, moment], axis=0),
            preferred_element_type=jnp.float32,
        )
        to_other = jnp.dot(
            own_moment_ref[pl.ds(pl.multiple_of(own * 16, 16), 16), :],
            both,
            preferred_element_type=jnp.float32,
        )
        return (own, other, to_own, to_other[:, :128] + to_other[:, 128:])

    def visit(step, _):
        last = jnp.maximum(step - 2, 0) * UNROLL
        first = jnp.minimum(step, groups - 1) * UNROLL
        results = [products(last + turn, turn) for turn in range(UNROLL)]
        for turn in range(UNROLL):
            weights(turn)
        for turn in range(UNROLL):
            distances(first + turn, turn)
        for own, other, to_own, to_other in results:
            own_sum_ref[pl.ds(pl.multiple_of(own * 128, 128), 128), :] += to_own
            other_sum_ref[pl.ds(pl.multiple_of(other * 16, 16), 16), :] += to_other
        return 0

    lax.fori_loop(0, groups + 2, visit, 0)

    def finish(data_ref, out_ref, start, rows_ref, base):
        *comps, charge = components(data_ref, start)

        def total(part):
            terms = [
                rows_ref[pl.ds(base + 4 * level + part, 8, stride=16), :] for level in range(3)
            ]
            return terms[0] + (terms[1] + terms[2])

        weight = total(3)
        scale = coulomb_scale * charge
        for part, comp in enumerate(comps):
            out_ref[pl.ds(4 * start + part, 8, stride=4), :] = scale * (comp * weight - total(part))
        out_ref[pl.ds(4 * start + 3, 8, stride=4), :] = zeros

    def finish_own(step, _):
        start = pl.multiple_of(step * 8, 8)
        lane = lax.broadcasted_iota(jnp.int32, (128, 128), 1)
        columns = own_sum_ref[pl.ds(pl.multiple_of(start * 128, 128), 128), :]
        for index in range(1, 8):
            block = own_sum_ref[pl.ds(pl.multiple_of((start + index) * 128, 128), 128), :]
            columns = jnp.where(lane < 16 * index, columns, pltpu.roll(block, 16 * index, 1))
        stage_ref[0:128, :] = columns.T
        finish(own_ref, own_out_ref, start, stage_ref, 0)
        return 0

    def finish_other(source, step, _):
        start = pl.multiple_of(step * 8, 8)
        finish(
            other_refs[source],
            other_out_refs[source],
            start,
            other_sum_ref,
            (source * slots + start) * 16,
        )
        return 0

    lax.fori_loop(0, clusters // 8, finish_own, 0)
    for source in range(len(other_refs)):
        lax.fori_loop(0, slots // 8, functools.partial(finish_other, source), 0)


def pair_forces(own_rows, other_rows, own, arrived, slots):
    clusters = own.shape[0] // 4
    others = slots * len(arrived)
    pairs = own_rows.shape[0]
    smem = pl.BlockSpec(memory_space=pltpu.SMEM)
    vmem = pl.BlockSpec(memory_space=pltpu.VMEM)
    return pl.pallas_call(
        pair_kernel,
        out_shape=(
            jax.ShapeDtypeStruct(own.shape, jnp.float32),
            *[jax.ShapeDtypeStruct((slots * 4, 128), jnp.float32)] * len(arrived),
        ),
        in_specs=[smem, smem, vmem] + [vmem] * len(arrived),
        out_specs=(vmem,) * (len(arrived) + 1),
        scratch_shapes=[
            pltpu.VMEM((clusters * 32, 128), jnp.bfloat16),
            pltpu.VMEM(((others + 1) * 128, 128), jnp.bfloat16),
            pltpu.VMEM((clusters * 16, 128), jnp.bfloat16),
            pltpu.VMEM((others * 128, 128), jnp.bfloat16),
            pltpu.VMEM((clusters * 128, 128), jnp.float32),
            pltpu.VMEM((others * 16, 128), jnp.float32),
            pltpu.VMEM((256, 128), jnp.float32),
            pltpu.VMEM((UNROLL, 128, 128), jnp.float32),
            pltpu.VMEM((UNROLL, 128, 256), jnp.bfloat16),
        ],
        compiler_params=pltpu.CompilerParams(vmem_limit_bytes=48 * 1024 * 1024),
        cost_estimate=pl.CostEstimate(
            flops=pairs * 128 * 128 * 20, bytes_accessed=4 * 1024 * 1024, transcendentals=0
        ),
        name="pair_forces",
    )(own_rows, other_rows, own, *arrived)


def prepare_kernel(
    fill_ref,
    cell_ref,
    send_index_ref,
    send_count_ref,
    position_ref,
    charge_ref,
    ion_ref,
    start_ref,
    screen_ref,
    own_ref,
    masked_ref,
    inverse_ref,
    source_ref,
    *refs,
):
    out_refs, (sum_ref, deposit_ref) = (refs[:-2], refs[-2:])
    clusters = charge_ref.shape[0]
    cells_x, cells_y, _ = ion_ref.shape
    slots = send_index_ref.shape[1]
    lane = lax.broadcasted_iota(jnp.int32, (1, 128), 1)
    row = lax.broadcasted_iota(jnp.int32, (4, 128), 0)

    def collect(step, _):
        for turn in range(8):
            cluster = step * 8 + turn
            masked = jnp.where(lane < fill_ref[cluster], charge_ref[pl.ds(cluster, 1), :], 0.0)
            masked_ref[pl.ds(cluster, 1), :] = masked
            place = position_ref[:, pl.ds(pl.multiple_of(cluster * 128, 128), 128)]
            own_ref[cluster, 0:3, :] = place
            own_ref[cluster, 3:4, :] = masked
        at = pl.ds(pl.multiple_of(step * 8, 8), 8)
        total = jnp.sum(masked_ref[at, :], axis=1, keepdims=True)
        sum_ref[at, :] = jnp.broadcast_to(deposit_scale * total, (8, 128))
        return 0

    lax.fori_loop(0, clusters // 8, collect, 0)

    def fill_messages(step, _):
        for direction, out_ref in enumerate(out_refs):
            parts = []
            for turn in range(2):
                slot = step * 2 + turn
                live = jnp.where(slot < send_count_ref[0, direction], 1.0, 0.0)
                value = own_ref[send_index_ref[direction, slot]]
                parts.append(jnp.where(row == 3, value * live, value))
            out_ref[pl.ds(pl.multiple_of(step * 8, 8), 8), :] = jnp.concatenate(parts, axis=0)
        return 0

    lax.fori_loop(0, slots // 2, fill_messages, 0)

    deposit_ref[...] = jnp.zeros_like(deposit_ref)

    def deposit(cluster, _):
        cell = cell_ref[cluster]
        index_x = lax.shift_right_logical(cell, CELL_BITS) // cells_y
        index_y = lax.shift_right_logical(cell, CELL_BITS) % cells_y
        index_z = lax.bitwise_and(cell, 255)
        half = lax.shift_right_logical(index_z, 7)
        added = jnp.where(
            lane == lax.bitwise_and(index_z, 127), sum_ref[pl.ds(cluster, 1), :], 0.0
        )
        deposit_ref[pl.ds((index_x * 2 + half) * cells_y + index_y, 1), :] += added
        return 0

    lax.fori_loop(0, clusters, deposit, 0, unroll=4)
    inverse_ref[...] = 1.0 / (6.0 + screen_ref[...])
    for index in range(cells_x):
        for half in range(2):
            lanes = slice(128 * half, 128 * half + 128)
            first = (index * 2 + half) * cells_y
            source_ref[index, :, lanes] = (
                ion_ref[index, :, lanes] + deposit_ref[first : first + cells_y, :]
            ) * inverse_ref[index, :, lanes]
    for out_ref, after in ((out_refs[1], True), (out_refs[2], False)):
        for index in range(cells_x):
            base = slots * 4 + index * 32
            offset = 0
            for field_ref, width in zip(
                (start_ref, inverse_ref, source_ref, ion_ref), HALO_WIDTHS, strict=True
            ):
                first = cells_y - width if after else 0
                rows = field_ref[index, first : first + width, :]
                for half in range(2):
                    out_ref[base + 16 * half + offset : base + 16 * half + offset + width, :] = (
                        rows[:, 128 * half : 128 * half + 128]
                    )
                offset += width
            for half in range(2):
                out_ref[base + 16 * half + offset : base + 16 * half + 16, :] = jnp.zeros(
                    (16 - offset, 128), jnp.float32
                )


def prepare(fill, cell, send_index, send_count, positions, charges, ions, start, screen):
    clusters = charges.shape[0]
    directions, slots = send_index.shape
    cells_x = ions.shape[0]
    smem = pl.BlockSpec(memory_space=pltpu.SMEM)
    vmem = pl.BlockSpec(memory_space=pltpu.VMEM)
    rows = [slots * 4] * directions
    rows[1] = rows[2] = slots * 4 + cells_x * 32
    return pl.pallas_call(
        prepare_kernel,
        out_shape=(
            jax.ShapeDtypeStruct((clusters, 4, 128), jnp.float32),
            jax.ShapeDtypeStruct((clusters, 128), jnp.float32),
            jax.ShapeDtypeStruct(ions.shape, jnp.float32),
            jax.ShapeDtypeStruct(ions.shape, jnp.float32),
            *[jax.ShapeDtypeStruct((count, 128), jnp.float32) for count in rows],
        ),
        in_specs=[smem] * 4 + [vmem] * 5,
        out_specs=(vmem,) * (4 + directions),
        scratch_shapes=[
            pltpu.VMEM((clusters, 128), jnp.float32),
            pltpu.VMEM((ions.size // 128, 128), jnp.float32),
        ],
        compiler_params=pltpu.CompilerParams(vmem_limit_bytes=32 * 1024 * 1024),
        name="prepare",
    )(fill, cell, send_index, send_count, positions, charges, ions, start, screen)


def put_extended(target_ref, plane, field, field_ref, index, before_ref, after_ref, base):
    cells_y = field_ref.shape[1]
    width = HALO_WIDTHS[field]
    offset = sum(HALO_WIDTHS[:field])
    target_ref[plane, MARGIN : MARGIN + cells_y, :] = field_ref[index]
    for half in range(2):
        lanes = slice(128 * half, 128 * half + 128)
        first = base + index * 32 + 16 * half + offset
        target_ref[plane, MARGIN - width : MARGIN, lanes] = before_ref[first : first + width, :]
        target_ref[plane, MARGIN + cells_y : MARGIN + cells_y + width, lanes] = after_ref[
            first : first + width, :
        ]


def planes_kernel(base, *refs):
    field_refs, (before_ref, after_ref, down_ref, up_ref) = (refs[:4], refs[4:])
    cells_x = field_refs[0].shape[0]
    down_ref[...] = jnp.zeros_like(down_ref)
    up_ref[...] = jnp.zeros_like(up_ref)
    plane = 0
    for field, width in enumerate(HALO_WIDTHS):
        for index in range(width):
            for target_ref, source in ((down_ref, index), (up_ref, cells_x - width + index)):
                put_extended(
                    target_ref, plane, field, field_refs[field], source, before_ref, after_ref, base
                )
            plane += 1


def planes(fields, before, after, base):
    vmem = pl.BlockSpec(memory_space=pltpu.VMEM)
    _, cells_y, cells_z = fields[0].shape
    shape = jax.ShapeDtypeStruct((sum(HALO_WIDTHS), cells_y + 2 * MARGIN, cells_z), jnp.float32)
    return pl.pallas_call(
        functools.partial(planes_kernel, base),
        out_shape=(shape, shape),
        in_specs=[vmem] * 6,
        out_specs=(vmem, vmem),
        compiler_params=pltpu.CompilerParams(vmem_limit_bytes=32 * 1024 * 1024),
        name="planes",
    )(*fields, before, after)


def face_flux(pot_low, pot_high, ion_low, ion_high):
    speed = -mobility * (pot_high - pot_low)
    return (
        jnp.maximum(speed, 0.0) * ion_low
        + jnp.minimum(speed, 0.0) * ion_high
        - diffusion * (ion_high - ion_low)
    )


def grid_kernel(base, *refs):
    cell_ref, masked_ref = refs[:2]
    field_refs = refs[2:6]
    before_ref, after_ref, lower_ref, upper_ref = refs[6:10]
    potential_ref, next_ref, force_ref = refs[10:13]
    start_ref, inverse_ref, resid_ref, ion_ref, update_ref, line_ref, *pick_refs = refs[13:]
    cells_x, cells_y, cells_z = field_refs[0].shape
    rows = cells_y + 2 * MARGIN
    depth = HALO_WIDTHS[0]
    clusters = masked_ref.shape[0]
    lane = lax.broadcasted_iota(jnp.int32, (rows, cells_z), 1)
    middle = 0.5 * (highest_eig + lowest_eig)
    spread = 0.5 * (highest_eig - lowest_eig)

    plane = 0
    for field, target_ref in enumerate((start_ref, inverse_ref, resid_ref, ion_ref)):
        width = HALO_WIDTHS[field]
        if field == 0 or field == 3:
            target_ref[...] = jnp.zeros_like(target_ref)
        else:
            target_ref[depth : depth + cells_x, 0:MARGIN, :] = jnp.zeros(
                (cells_x, MARGIN, cells_z), jnp.float32
            )
            target_ref[depth : depth + cells_x, rows - MARGIN : rows, :] = jnp.zeros(
                (cells_x, MARGIN, cells_z), jnp.float32
            )
        for index in range(width):
            target_ref[depth - width + index] = lower_ref[plane + index]
            target_ref[depth + cells_x + index] = upper_ref[plane + index]
        for index in range(cells_x):
            put_extended(
                target_ref,
                depth + index,
                field,
                field_refs[field],
                index,
                before_ref,
                after_ref,
                base,
            )
        plane += width

    def above(value):
        return jnp.where(lane == cells_z - 1, 0.0, pltpu.roll(value, cells_z - 1, 1))

    def below(value):
        return jnp.where(lane == 0, 0.0, pltpu.roll(value, 1, 1))

    def beside(value):
        rolled = pltpu.roll(value, 1, 0) + pltpu.roll(value, rows - 1, 0)
        return rolled + (above(value) + below(value))

    def first_sweep(index, planes):
        last, here = planes
        after = start_ref[index + 1]
        resid = (
            resid_ref[index] - here + inverse_ref[index] * ((last + after) + beside(here))
        )
        resid_ref[index] = resid
        update_ref[index] = resid / middle
        return (here, after)

    lax.fori_loop(1, cells_x + 2 * depth - 1, first_sweep, (start_ref[0], start_ref[1]))

    ratio_ms = middle / spread
    weight_now = 1.0 / ratio_ms
    for turn in range(1, SWEEPS):
        weight_next = 1.0 / (2.0 * ratio_ms - weight_now)
        keep, gain = (weight_next * weight_now, 2.0 * weight_next / spread)
        weight_now = weight_next

        def sweep(index, planes, turn=turn, keep=keep, gain=gain):
            last, here = planes
            after = update_ref[index + 1]
            resid = resid_ref[index] - here + inverse_ref[index] * ((last + after) + beside(here))
            update = keep * here + gain * resid
            if turn == 1:
                start_ref[index] = start_ref[index] + here + update
            else:
                start_ref[index] = start_ref[index] + update
            if turn + 1 < SWEEPS:
                resid_ref[index] = resid
                update_ref[index] = update
            return (here, after)

        first = 1 + turn
        lax.fori_loop(
            first,
            cells_x + 2 * depth - first,
            sweep,
            (update_ref[first - 1], update_ref[first]),
        )

    def upper_flux(index):
        return face_flux(start_ref[index], start_ref[index + 1], ion_ref[index], ion_ref[index + 1])

    inner = slice(MARGIN, MARGIN + cells_y)

    def advance(index, lower):
        pot = start_ref[depth + index]
        ions = ion_ref[depth + index]
        upper = upper_flux(depth + index)
        along_y = face_flux(pot, pltpu.roll(pot, rows - 1, 0), ions, pltpu.roll(ions, rows - 1, 0))
        along_z = face_flux(pot, above(pot), ions, above(ions))
        first_z = face_flux(0.0, pot, 0.0, ions)
        total = upper - lower
        total = total + (along_y - pltpu.roll(along_y, 1, 0))
        total = total + (along_z - jnp.where(lane == 0, first_z, pltpu.roll(along_z, 1, 1)))
        next_ref[index] = (ions - time_step * total)[inner]
        potential_ref[index] = pot[inner]
        return upper

    lax.fori_loop(0, cells_x, advance, upper_flux(depth - 1))
    for index in range(cells_x + 2):
        for half in range(2):
            line_ref[pl.ds((index * 2 + half) * rows, rows), :] = start_ref[
                depth - 1 + index, :, 128 * half : 128 * half + 128
            ]

    row_lane = lax.broadcasted_iota(jnp.int32, (1, 128), 1)

    def pick(cluster, _):
        cell = cell_ref[cluster]
        index_x = lax.shift_right_logical(cell, CELL_BITS) // cells_y + 1
        index_y = lax.shift_right_logical(cell, CELL_BITS) % cells_y + MARGIN
        index_z = lax.bitwise_and(cell, 255)
        half = lax.shift_right_logical(index_z, 7)
        here = row_lane == lax.bitwise_and(index_z, 127)

        def line(plane, row, part):
            return line_ref[pl.ds((plane * 2 + part) * rows + row, 1), :]

        along_x = line(index_x - 1, index_y, half) - line(index_x + 1, index_y, half)
        along_y = line(index_x, index_y - 1, half) - line(index_x, index_y + 1, half)
        along_z = jnp.zeros((1, 128), jnp.float32)
        for part in range(cells_z // 128):
            value = line(index_x, index_y, part)
            place = row_lane + 128 * part
            along_z = along_z + jnp.where(place == index_z - 1, value, 0.0)
            along_z = along_z - jnp.where(place == index_z + 1, value, 0.0)
        at = pl.ds(cluster, 1)
        pick_refs[0][at, :] = jnp.where(here, along_x, 0.0)
        pick_refs[1][at, :] = jnp.where(here, along_y, 0.0)
        pick_refs[2][at, :] = along_z
        return 0

    lax.fori_loop(0, clusters, pick, 0, unroll=4)

    def spread_out(step, _):
        start = pl.multiple_of(step * 8, 8)
        charge = masked_ref[pl.ds(start, 8), :] * (0.5 * field_scale)
        for part, pick_ref in enumerate(pick_refs):
            total = jnp.sum(pick_ref[pl.ds(start, 8), :], axis=1, keepdims=True)
            force_ref[pl.ds(4 * start + part, 8, stride=4), :] = charge * total
        force_ref[pl.ds(4 * start + 3, 8, stride=4), :] = jnp.zeros((8, 128), jnp.float32)
        return 0

    lax.fori_loop(0, clusters // 8, spread_out, 0)


def grid_step(cell, masked, fields, before, after, lower, upper, base):
    smem = pl.BlockSpec(memory_space=pltpu.SMEM)
    vmem = pl.BlockSpec(memory_space=pltpu.VMEM)
    clusters = masked.shape[0]
    cells_x, cells_y, cells_z = fields[0].shape
    block = (cells_x + 2 * HALO_WIDTHS[0], cells_y + 2 * MARGIN, cells_z)
    return pl.pallas_call(
        functools.partial(grid_kernel, base),
        out_shape=(
            jax.ShapeDtypeStruct(fields[0].shape, jnp.float32),
            jax.ShapeDtypeStruct(fields[0].shape, jnp.float32),
            jax.ShapeDtypeStruct((clusters * 4, 128), jnp.float32),
        ),
        in_specs=[smem] + [vmem] * 9,
        out_specs=(vmem,) * 3,
        scratch_shapes=[pltpu.VMEM(block, jnp.float32)] * 5
        + [pltpu.VMEM(((cells_x + 2) * 2 * block[1], 128), jnp.float32)]
        + [pltpu.VMEM((clusters, 128), jnp.float32)] * 3,
        compiler_params=pltpu.CompilerParams(vmem_limit_bytes=40 * 1024 * 1024),
        cost_estimate=pl.CostEstimate(
            flops=block[0] * block[1] * block[2] * 100, bytes_accessed=8 << 20, transcendentals=0
        ),
        name="grid_step",
    )(cell, masked, *fields, before, after, lower, upper)


def gather_forces_kernel(send_index_ref, own_ref, field_ref, *refs):
    back_refs, (out_ref, sum_ref) = (refs[:-2], refs[-2:])
    clusters = own_ref.shape[0]
    slots = send_index_ref.shape[1]
    sum_ref[...] = own_ref[...] + field_ref[...]

    def visit(slot, _):
        for direction, back_ref in enumerate(back_refs):
            cluster = send_index_ref[direction, slot]
            sum_ref[cluster] += back_ref[slot]
        return 0

    lax.fori_loop(0, slots, visit, 0)

    def write(step, _):
        for turn in range(8):
            cluster = step * 8 + turn
            out_ref[:, pl.ds(pl.multiple_of(cluster * 128, 128), 128)] = sum_ref[cluster][0:3]
        return 0

    lax.fori_loop(0, clusters // 8, write, 0)


def gather_forces(send_index, own, field, backs):
    smem = pl.BlockSpec(memory_space=pltpu.SMEM)
    vmem = pl.BlockSpec(memory_space=pltpu.VMEM)
    clusters = own.shape[0]
    return pl.pallas_call(
        gather_forces_kernel,
        out_shape=jax.ShapeDtypeStruct((3, clusters * 128), jnp.float32),
        in_specs=[smem] + [vmem] * (2 + len(backs)),
        out_specs=vmem,
        scratch_shapes=[pltpu.VMEM(own.shape, jnp.float32)],
        compiler_params=pltpu.CompilerParams(vmem_limit_bytes=32 * 1024 * 1024),
        name="gather_forces",
    )(send_index, own, field, *backs)


def passed_along(shard, axis, by):
    devices = lax.axis_size(axis)
    pairs = [(i, i + by) for i in range(devices) if 0 <= i + by < devices]
    return lax.ppermute(shard, axis, pairs)


ROUTES = (("brick", 1), ("brick", -1), ("brick", 2), ("brick", -2), ("grp", 1), ("grp", -1))


def shards(
    positions,
    charges,
    cluster_fill,
    cluster_cell,
    send_index,
    send_count,
    pair_local,
    pair_dir,
    pair_slot,
    ion_density,
    potential_prev,
    screening,
):
    clusters = cluster_fill.shape[0]
    psize = charges.shape[0] // clusters
    slots = send_index.shape[1]
    base = slots * 4
    own, masked, inverse, source, local, *messages = prepare(
        cluster_fill,
        cluster_cell,
        send_index,
        send_count,
        positions,
        charges.reshape(clusters, psize),
        ion_density,
        potential_prev,
        screening,
    )
    arrived = [local] + [
        passed_along(message, axis, by)
        for message, (axis, by) in zip(messages, ROUTES, strict=True)
    ]
    fields = (potential_prev, inverse, source, ion_density)
    before, after = arrived[1:3]
    down, up = planes(fields, before, after, base)
    lower = passed_along(up, "grp", 1)
    upper = passed_along(down, "grp", -1)
    own_force, *reactions = pair_forces(
        pair_local,
        pair_dir * slots + pair_slot,
        own.reshape(clusters * 4, psize),
        arrived,
        slots,
    )
    backs = [reactions[0]] + [
        passed_along(reaction, axis, -by)
        for reaction, (axis, by) in zip(reactions[1:], ROUTES, strict=True)
    ]
    potential, ion_next, field_force = grid_step(
        cluster_cell, masked, fields, before, after, lower, upper, base
    )
    forces = gather_forces(
        send_index,
        own_force.reshape(clusters, 4, psize),
        field_force.reshape(clusters, 4, psize),
        [back.reshape(slots, 4, psize) for back in backs],
    )
    return (forces, potential, ion_next)


def solution(mesh):
    in_specs = (
        P(None, ("grp", "brick")),
        P(("grp", "brick")),
        P(("grp", "brick")),
        P(("grp", "brick")),
        P(("grp", "brick"), None),
        P(("grp", "brick"), None),
        P(("grp", "brick")),
        P(("grp", "brick")),
        P(("grp", "brick")),
        P("grp", "brick", None),
        P("grp", "brick", None),
        P("grp", "brick", None),
    )
    out_specs = (P(None, ("grp", "brick")), P("grp", "brick", None), P("grp", "brick", None))
    return jax.shard_map(shards, mesh=mesh, in_specs=in_specs, out_specs=out_specs, check_vma=False)
```

```python
import functools

import jax
import jax.numpy as jnp
from jax import lax
from jax.experimental import pallas as pl
from jax.experimental.pallas import tpu as pltpu
from jax.sharding import PartitionSpec as P

SWEEPS = 4
UNROLL = 4
HALO_WIDTHS = (SWEEPS + 1, SWEEPS, SWEEPS, 1)
MARGIN = 8
CELL_BITS = 8


coulomb_scale = 0.02
softening = 0.1
field_scale = 0.5
deposit_scale = 0.2
lowest_eig = 0.01
highest_eig = 1.99
mobility = 0.3
diffusion = 0.2
time_step = 0.2


def split3(value):
    first = value.astype(jnp.bfloat16).astype(jnp.float32)
    rest = value - first
    second = rest.astype(jnp.bfloat16).astype(jnp.float32)
    third = (rest - second).astype(jnp.bfloat16).astype(jnp.float32)
    return (first, second, third)


def moment_rows(comps, charge):
    rows = [None] * 12
    for part, charged in enumerate((*comps, None)):
        for level, piece in enumerate(split3(charge if charged is None else charge * charged)):
            rows[4 * level + part] = piece
    return rows


def pair_kernel(own_rows_ref, other_rows_ref, own_ref, *refs):
    sources = (len(refs) - 10) // 2
    other_refs = refs[:sources]
    own_out_ref = refs[sources]
    other_out_refs = refs[sources + 1 : 2 * sources + 1]
    (
        near_ref,
        far_ref,
        own_moment_ref,
        other_moment_ref,
        own_sum_ref,
        other_sum_ref,
        stage_ref,
        dist_ref,
        weight_ref,
    ) = refs[2 * sources + 1 :]
    clusters = own_ref.shape[0] // 4
    slots = other_out_refs[0].shape[0] // 4
    groups = own_rows_ref.shape[0] // UNROLL
    units = UNROLL // 2
    ones = jnp.ones((8, 128), jnp.float32)
    zeros = jnp.zeros((8, 128), jnp.float32)

    def components(data_ref, start):
        return [data_ref[pl.ds(4 * start + part, 8, stride=4), :] for part in range(4)]

    def put(rows, base, stride):
        for index, row in enumerate(rows):
            stage_ref[pl.ds(base + index, 8, stride=stride), :] = row

    def near_rows(step, _):
        start = pl.multiple_of(step * 8, 8)
        *comps, charge = components(own_ref, start)
        put(moment_rows(comps, charge) + [zeros] * 4, 256, 16)
        own_moment_ref[pl.ds(pl.multiple_of(start * 16, 128), 128), :] = stage_ref[
            256:384, :
        ].astype(jnp.bfloat16)
        rows = []
        square = zeros
        for comp in comps:
            first, second, third = split3(comp)
            square = square + comp * comp
            rows += [first, first, first, second, second, third]
        rows += [*split3(square), ones, ones, ones]
        rows += [zeros] * (32 - len(rows))
        put(rows, 0, 32)
        for half in range(2):
            columns = stage_ref[128 * half : 128 * half + 128, :].T
            for index in range(4):
                at = pl.ds(pl.multiple_of((start + 4 * half + index) * 128, 128), 128)
                rolled = columns if index == 0 else pltpu.roll(columns, 128 - 32 * index, 1)
                near_ref[at, :] = rolled.astype(jnp.bfloat16)
                own_sum_ref[at, :] = jnp.zeros((128, 128), jnp.float32)
        return 0

    def far_rows(source, step, _):
        local = pl.multiple_of(step * 8, 8)
        start = source * slots + local
        *comps, charge = components(other_refs[source], local)
        moments = moment_rows(comps, charge) + [zeros] * 4
        put(moments + moments, 0, 32)
        for half in range(2):
            columns = stage_ref[128 * half : 128 * half + 128, :].T
            for index in range(4):
                at = pl.ds(pl.multiple_of((start + 4 * half + index) * 128, 128), 128)
                rolled = columns if index == 0 else pltpu.roll(columns, 128 - 32 * index, 1)
                other_moment_ref[at, :] = rolled.astype(jnp.bfloat16)
        rows = []
        square = zeros
        for comp in comps:
            first, second, third = split3(-2.0 * comp)
            square = square + comp * comp
            rows += [first, second, third, first, second, first]
        rows += [ones, ones, ones, *split3(square + softening)]
        rows += [zeros] * (32 - len(rows))
        put(rows, 0, 32)
        far_ref[pl.ds(pl.multiple_of(start * 32, 256), 256), :] = stage_ref[0:256, :].astype(
            jnp.bfloat16
        )
        return 0

    lax.fori_loop(0, clusters // 8, near_rows, 0)
    for source in range(sources):
        lax.fori_loop(0, slots // 8, functools.partial(far_rows, source), 0)
    other_sum_ref[...] = jnp.zeros_like(other_sum_ref)
    dist_ref[...] = jnp.full(dist_ref.shape, 1e38, jnp.float32)
    weight_ref[...] = jnp.zeros_like(weight_ref)

    lane = lax.broadcasted_iota(jnp.int32, (128, 128), 1)
    lane_row = lax.broadcasted_iota(jnp.int32, (1, 128), 1)
    left_mask = jnp.where(lane_row < 16, 1.0, 0.0).astype(jnp.bfloat16)
    right_mask = jnp.where((lane_row >= 16) & (lane_row < 32), 1.0, 0.0).astype(jnp.bfloat16)

    def distances(pair, turn):
        own = own_rows_ref[pair]
        other = other_rows_ref[pair]
        near = near_ref[pl.ds(pl.multiple_of(own * 128, 128), 128), 0:32]
        far = far_ref[pl.ds(pl.multiple_of(other * 32, 32), 32), :]
        dist_ref[turn] = jnp.dot(near, far, preferred_element_type=jnp.float32)

    def weights(turn):
        root = lax.rsqrt(dist_ref[turn])
        weight = root * root * root
        high = weight.astype(jnp.bfloat16)
        lanes = slice(128 * (turn % 2), 128 * (turn % 2) + 128)
        weight_ref[2 * (turn // 2), :, lanes] = high
        weight_ref[2 * (turn // 2) + 1, :, lanes] = (weight - high.astype(jnp.float32)).astype(
            jnp.bfloat16
        )

    def moment_of(moment_ref, row, size):
        return moment_ref[pl.ds(pl.multiple_of(row * size, size), size), :]

    def products(pair, unit):
        owns = [own_rows_ref[pair + turn] for turn in range(2)]
        others = [other_rows_ref[pair + turn] for turn in range(2)]
        high = weight_ref[2 * unit]
        low = weight_ref[2 * unit + 1]
        columns = jnp.concatenate(
            [
                moment_of(other_moment_ref, others[0], 128) * left_mask,
                moment_of(other_moment_ref, others[1], 128) * right_mask,
            ],
            axis=0,
        )
        rows = jnp.concatenate(
            [moment_of(own_moment_ref, owns[0], 16), moment_of(own_moment_ref, owns[1], 16)], axis=0
        )
        to_own = jnp.dot(high, columns, preferred_element_type=jnp.float32) + jnp.dot(
            low, columns, preferred_element_type=jnp.float32
        )
        to_other = jnp.dot(rows, high, preferred_element_type=jnp.float32) + jnp.dot(
            rows, low, preferred_element_type=jnp.float32
        )
        return (owns, others, to_own, (to_other[:16, :128], to_other[16:, 128:]))

    def visit(step, _):
        last = jnp.maximum(step - 2, 0) * UNROLL
        first = jnp.minimum(step, groups - 1) * UNROLL
        results = [products(last + 2 * unit, unit) for unit in range(units)]
        for turn in range(UNROLL):
            weights(turn)
        for turn in range(UNROLL):
            distances(first + turn, turn)
        for owns, others, to_own, to_other in results:
            for turn in range(2):
                kept = jnp.where(lane < 16 if turn == 0 else lane >= 16, to_own, 0.0)
                own_sum_ref[pl.ds(pl.multiple_of(owns[turn] * 128, 128), 128), :] += kept
                other_sum_ref[pl.ds(pl.multiple_of(others[turn] * 16, 16), 16), :] += to_other[turn]
        return 0

    lax.fori_loop(0, groups + 2, visit, 0)

    def finish(data_ref, out_ref, start, rows_ref, bases, stride):
        *comps, charge = components(data_ref, start)

        def total(part):
            terms = [
                rows_ref[pl.ds(base + 4 * level + part, 8, stride=stride), :]
                for level in range(3)
                for base in bases
            ]
            return functools.reduce(lambda left, right: right + left, terms[::-1])

        weight = total(3)
        scale = coulomb_scale * charge
        for part, comp in enumerate(comps):
            out_ref[pl.ds(4 * start + part, 8, stride=4), :] = scale * (comp * weight - total(part))
        out_ref[pl.ds(4 * start + 3, 8, stride=4), :] = zeros

    def finish_own(step, _):
        start = pl.multiple_of(step * 8, 8)
        for half in range(2):
            columns = None
            for index in range(4):
                at = pl.ds(pl.multiple_of((start + 4 * half + index) * 128, 128), 128)
                block = own_sum_ref[at, :]
                if index:
                    rolled = pltpu.roll(block, 32 * index, 1)
                    columns = jnp.where(lane < 32 * index, columns, rolled)
                else:
                    columns = block
            stage_ref[128 * half : 128 * half + 128, :] = columns.T
        finish(own_ref, own_out_ref, start, stage_ref, (0, 16), 32)
        return 0

    def finish_other(source, step, _):
        start = pl.multiple_of(step * 8, 8)
        finish(
            other_refs[source],
            other_out_refs[source],
            start,
            other_sum_ref,
            ((source * slots + start) * 16,),
            16,
        )
        return 0

    lax.fori_loop(0, clusters // 8, finish_own, 0)
    for source in range(sources):
        lax.fori_loop(0, slots // 8, functools.partial(finish_other, source), 0)


def pair_forces(own_rows, other_rows, own, arrived, slots):
    clusters = own.shape[0] // 4
    others = slots * len(arrived)
    pairs = own_rows.shape[0]
    smem = pl.BlockSpec(memory_space=pltpu.SMEM)
    vmem = pl.BlockSpec(memory_space=pltpu.VMEM)
    return pl.pallas_call(
        pair_kernel,
        out_shape=(
            jax.ShapeDtypeStruct(own.shape, jnp.float32),
            *[jax.ShapeDtypeStruct((slots * 4, 128), jnp.float32)] * len(arrived),
        ),
        in_specs=[smem, smem, vmem] + [vmem] * len(arrived),
        out_specs=(vmem,) * (len(arrived) + 1),
        scratch_shapes=[
            pltpu.VMEM((clusters * 128, 128), jnp.bfloat16),
            pltpu.VMEM((others * 32, 128), jnp.bfloat16),
            pltpu.VMEM((clusters * 16, 128), jnp.bfloat16),
            pltpu.VMEM((others * 128, 128), jnp.bfloat16),
            pltpu.VMEM((clusters * 128, 128), jnp.float32),
            pltpu.VMEM((others * 16, 128), jnp.float32),
            pltpu.VMEM((384, 128), jnp.float32),
            pltpu.VMEM((UNROLL, 128, 128), jnp.float32),
            pltpu.VMEM((UNROLL, 128, 256), jnp.bfloat16),
        ],
        compiler_params=pltpu.CompilerParams(vmem_limit_bytes=46 * 1024 * 1024),
        cost_estimate=pl.CostEstimate(
            flops=pairs * 128 * 128 * 20, bytes_accessed=4 * 1024 * 1024, transcendentals=0
        ),
        name="pair_forces",
    )(own_rows, other_rows, own, *arrived)


def prepare_kernel(
    fill_ref,
    cell_ref,
    send_index_ref,
    send_count_ref,
    position_hbm,
    charge_hbm,
    ion_hbm,
    start_hbm,
    screen_hbm,
    own_ref,
    masked_ref,
    inverse_ref,
    source_ref,
    *refs,
):
    out_refs, scratch = (refs[:-8], refs[-8:])
    sum_ref, deposit_ref, position_ref, charge_ref, ion_ref, start_ref, screen_ref, sems = scratch
    copies = [
        pltpu.make_async_copy(source, target, sems.at[index])
        for index, (source, target) in enumerate(
            (
                (position_hbm, position_ref),
                (charge_hbm, charge_ref),
                (ion_hbm, ion_ref),
                (start_hbm, start_ref),
                (screen_hbm, screen_ref),
            )
        )
    ]
    for copy in copies:
        copy.start()
    deposit_ref[...] = jnp.zeros_like(deposit_ref)
    copies[0].wait()
    copies[1].wait()
    clusters = charge_ref.shape[0]
    cells_x, cells_y, _ = ion_ref.shape
    slots = send_index_ref.shape[1]
    lane = lax.broadcasted_iota(jnp.int32, (1, 128), 1)
    row = lax.broadcasted_iota(jnp.int32, (4, 128), 0)

    def collect(step, _):
        for turn in range(8):
            cluster = step * 8 + turn
            masked = jnp.where(lane < fill_ref[cluster], charge_ref[pl.ds(cluster, 1), :], 0.0)
            masked_ref[pl.ds(cluster, 1), :] = masked
            place = position_ref[:, pl.ds(pl.multiple_of(cluster * 128, 128), 128)]
            own_ref[cluster, 0:3, :] = place
            own_ref[cluster, 3:4, :] = masked
        at = pl.ds(pl.multiple_of(step * 8, 8), 8)
        total = jnp.sum(masked_ref[at, :], axis=1, keepdims=True)
        sum_ref[at, :] = jnp.broadcast_to(deposit_scale * total, (8, 128))
        return 0

    lax.fori_loop(0, clusters // 8, collect, 0)

    def fill_messages(step, _):
        for direction, out_ref in enumerate(out_refs):
            parts = []
            for turn in range(2):
                slot = step * 2 + turn
                live = jnp.where(slot < send_count_ref[0, direction], 1.0, 0.0)
                value = own_ref[send_index_ref[direction, slot]]
                parts.append(jnp.where(row == 3, value * live, value))
            out_ref[pl.ds(pl.multiple_of(step * 8, 8), 8), :] = jnp.concatenate(parts, axis=0)
        return 0

    lax.fori_loop(0, slots // 2, fill_messages, 0)

    def deposit(cluster, _):
        cell = cell_ref[cluster]
        index_x = lax.shift_right_logical(cell, CELL_BITS) // cells_y
        index_y = lax.shift_right_logical(cell, CELL_BITS) % cells_y
        index_z = lax.bitwise_and(cell, 255)
        half = lax.shift_right_logical(index_z, 7)
        added = jnp.where(
            lane == lax.bitwise_and(index_z, 127), sum_ref[pl.ds(cluster, 1), :], 0.0
        )
        deposit_ref[pl.ds((index_x * 2 + half) * cells_y + index_y, 1), :] += added
        return 0

    lax.fori_loop(0, clusters, deposit, 0, unroll=4)
    for copy in copies[2:]:
        copy.wait()
    inverse_ref[...] = 1.0 / (6.0 + screen_ref[...])
    for index in range(cells_x):
        for half in range(2):
            lanes = slice(128 * half, 128 * half + 128)
            first = (index * 2 + half) * cells_y
            source_ref[index, :, lanes] = (
                ion_ref[index, :, lanes] + deposit_ref[first : first + cells_y, :]
            ) * inverse_ref[index, :, lanes]
    for out_ref, after in ((out_refs[1], True), (out_refs[2], False)):
        for index in range(cells_x):
            base = slots * 4 + index * 32
            offset = 0
            for field_ref, width in zip(
                (start_ref, inverse_ref, source_ref, ion_ref), HALO_WIDTHS, strict=True
            ):
                first = cells_y - width if after else 0
                rows = field_ref[index, first : first + width, :]
                for half in range(2):
                    out_ref[base + 16 * half + offset : base + 16 * half + offset + width, :] = (
                        rows[:, 128 * half : 128 * half + 128]
                    )
                offset += width
            for half in range(2):
                out_ref[base + 16 * half + offset : base + 16 * half + 16, :] = jnp.zeros(
                    (16 - offset, 128), jnp.float32
                )


def prepare(fill, cell, send_index, send_count, positions, charges, ions, start, screen):
    clusters = charges.shape[0]
    directions, slots = send_index.shape
    cells_x = ions.shape[0]
    smem = pl.BlockSpec(memory_space=pltpu.SMEM)
    vmem = pl.BlockSpec(memory_space=pltpu.VMEM)
    rows = [slots * 4] * directions
    rows[1] = rows[2] = slots * 4 + cells_x * 32
    return pl.pallas_call(
        prepare_kernel,
        out_shape=(
            jax.ShapeDtypeStruct((clusters, 4, 128), jnp.float32),
            jax.ShapeDtypeStruct((clusters, 128), jnp.float32),
            jax.ShapeDtypeStruct(ions.shape, jnp.float32),
            jax.ShapeDtypeStruct(ions.shape, jnp.float32),
            *[jax.ShapeDtypeStruct((count, 128), jnp.float32) for count in rows],
        ),
        in_specs=[smem] * 4 + [pl.BlockSpec(memory_space=pltpu.HBM)] * 5,
        out_specs=(vmem,) * (4 + directions),
        scratch_shapes=[
            pltpu.VMEM((clusters, 128), jnp.float32),
            pltpu.VMEM((ions.size // 128, 128), jnp.float32),
            *[
                pltpu.VMEM(operand.shape, jnp.float32)
                for operand in (positions, charges, ions, start, screen)
            ],
            pltpu.SemaphoreType.DMA((5,)),
        ],
        compiler_params=pltpu.CompilerParams(vmem_limit_bytes=60 * 1024 * 1024),
        name="prepare",
    )(fill, cell, send_index, send_count, positions, charges, ions, start, screen)


def put_extended(target_ref, plane, field, field_ref, index, before_ref, after_ref, base):
    cells_y = field_ref.shape[1]
    width = HALO_WIDTHS[field]
    offset = sum(HALO_WIDTHS[:field])
    target_ref[plane, MARGIN : MARGIN + cells_y, :] = field_ref[index]
    for half in range(2):
        lanes = slice(128 * half, 128 * half + 128)
        first = base + index * 32 + 16 * half + offset
        target_ref[plane, MARGIN - width : MARGIN, lanes] = before_ref[first : first + width, :]
        target_ref[plane, MARGIN + cells_y : MARGIN + cells_y + width, lanes] = after_ref[
            first : first + width, :
        ]


def planes_kernel(base, *refs):
    field_refs, (before_ref, after_ref, down_ref, up_ref) = (refs[:4], refs[4:])
    cells_x = field_refs[0].shape[0]
    down_ref[...] = jnp.zeros_like(down_ref)
    up_ref[...] = jnp.zeros_like(up_ref)
    plane = 0
    for field, width in enumerate(HALO_WIDTHS):
        for index in range(width):
            for target_ref, source in ((down_ref, index), (up_ref, cells_x - width + index)):
                put_extended(
                    target_ref, plane, field, field_refs[field], source, before_ref, after_ref, base
                )
            plane += 1


def planes(fields, before, after, base):
    vmem = pl.BlockSpec(memory_space=pltpu.VMEM)
    _, cells_y, cells_z = fields[0].shape
    shape = jax.ShapeDtypeStruct((sum(HALO_WIDTHS), cells_y + 2 * MARGIN, cells_z), jnp.float32)
    return pl.pallas_call(
        functools.partial(planes_kernel, base),
        out_shape=(shape, shape),
        in_specs=[vmem] * 6,
        out_specs=(vmem, vmem),
        compiler_params=pltpu.CompilerParams(vmem_limit_bytes=32 * 1024 * 1024),
        name="planes",
    )(*fields, before, after)


def face_flux(pot_low, pot_high, ion_low, ion_high):
    speed = -mobility * (pot_high - pot_low)
    return (
        jnp.maximum(speed, 0.0) * ion_low
        + jnp.minimum(speed, 0.0) * ion_high
        - diffusion * (ion_high - ion_low)
    )


def grid_kernel(base, *refs):
    cell_ref, masked_ref = refs[:2]
    field_refs = refs[2:6]
    before_ref, after_ref, lower_ref, upper_ref = refs[6:10]
    potential_ref, next_ref, force_ref = refs[10:13]
    start_ref, inverse_ref, resid_ref, ion_ref, update_ref, line_ref, *pick_refs = refs[13:]
    cells_x, cells_y, cells_z = field_refs[0].shape
    rows = cells_y + 2 * MARGIN
    depth = HALO_WIDTHS[0]
    clusters = masked_ref.shape[0]
    lane = lax.broadcasted_iota(jnp.int32, (rows, cells_z), 1)
    middle = 0.5 * (highest_eig + lowest_eig)
    spread = 0.5 * (highest_eig - lowest_eig)

    plane = 0
    for field, target_ref in enumerate((start_ref, inverse_ref, resid_ref, ion_ref)):
        width = HALO_WIDTHS[field]
        if field == 0 or field == 3:
            target_ref[...] = jnp.zeros_like(target_ref)
        else:
            target_ref[depth : depth + cells_x, 0:MARGIN, :] = jnp.zeros(
                (cells_x, MARGIN, cells_z), jnp.float32
            )
            target_ref[depth : depth + cells_x, rows - MARGIN : rows, :] = jnp.zeros(
                (cells_x, MARGIN, cells_z), jnp.float32
            )
        for index in range(width):
            target_ref[depth - width + index] = lower_ref[plane + index]
            target_ref[depth + cells_x + index] = upper_ref[plane + index]
        for index in range(cells_x):
            put_extended(
                target_ref,
                depth + index,
                field,
                field_refs[field],
                index,
                before_ref,
                after_ref,
                base,
            )
        plane += width

    def above(value):
        return jnp.where(lane == cells_z - 1, 0.0, pltpu.roll(value, cells_z - 1, 1))

    def below(value):
        return jnp.where(lane == 0, 0.0, pltpu.roll(value, 1, 1))

    def beside(value):
        rolled = pltpu.roll(value, 1, 0) + pltpu.roll(value, rows - 1, 0)
        return rolled + (above(value) + below(value))

    def first_sweep(index, planes):
        last, here = planes
        after = start_ref[index + 1]
        resid = (
            resid_ref[index] - here + inverse_ref[index] * ((last + after) + beside(here))
        )
        resid_ref[index] = resid
        update_ref[index] = resid / middle
        return (here, after)

    lax.fori_loop(1, cells_x + 2 * depth - 1, first_sweep, (start_ref[0], start_ref[1]))

    ratio_ms = middle / spread
    weight_now = 1.0 / ratio_ms
    for turn in range(1, SWEEPS):
        weight_next = 1.0 / (2.0 * ratio_ms - weight_now)
        keep, gain = (weight_next * weight_now, 2.0 * weight_next / spread)
        weight_now = weight_next

        def sweep(index, planes, turn=turn, keep=keep, gain=gain):
            last, here = planes
            after = update_ref[index + 1]
            resid = resid_ref[index] - here + inverse_ref[index] * ((last + after) + beside(here))
            update = keep * here + gain * resid
            if turn == 1:
                start_ref[index] = start_ref[index] + here + update
            else:
                start_ref[index] = start_ref[index] + update
            if turn + 1 < SWEEPS:
                resid_ref[index] = resid
                update_ref[index] = update
            return (here, after)

        first = 1 + turn
        lax.fori_loop(
            first,
            cells_x + 2 * depth - first,
            sweep,
            (update_ref[first - 1], update_ref[first]),
        )

    def upper_flux(index):
        return face_flux(start_ref[index], start_ref[index + 1], ion_ref[index], ion_ref[index + 1])

    inner = slice(MARGIN, MARGIN + cells_y)

    def advance(index, lower):
        pot = start_ref[depth + index]
        ions = ion_ref[depth + index]
        upper = upper_flux(depth + index)
        along_y = face_flux(pot, pltpu.roll(pot, rows - 1, 0), ions, pltpu.roll(ions, rows - 1, 0))
        along_z = face_flux(pot, above(pot), ions, above(ions))
        first_z = face_flux(0.0, pot, 0.0, ions)
        total = upper - lower
        total = total + (along_y - pltpu.roll(along_y, 1, 0))
        total = total + (along_z - jnp.where(lane == 0, first_z, pltpu.roll(along_z, 1, 1)))
        next_ref[index] = (ions - time_step * total)[inner]
        potential_ref[index] = pot[inner]
        return upper

    lax.fori_loop(0, cells_x, advance, upper_flux(depth - 1))
    for index in range(cells_x + 2):
        for half in range(2):
            line_ref[pl.ds((index * 2 + half) * rows, rows), :] = start_ref[
                depth - 1 + index, :, 128 * half : 128 * half + 128
            ]

    row_lane = lax.broadcasted_iota(jnp.int32, (1, 128), 1)

    def pick(cluster, _):
        cell = cell_ref[cluster]
        index_x = lax.shift_right_logical(cell, CELL_BITS) // cells_y + 1
        index_y = lax.shift_right_logical(cell, CELL_BITS) % cells_y + MARGIN
        index_z = lax.bitwise_and(cell, 255)
        half = lax.shift_right_logical(index_z, 7)
        here = row_lane == lax.bitwise_and(index_z, 127)

        def line(plane, row, part):
            return line_ref[pl.ds((plane * 2 + part) * rows + row, 1), :]

        along_x = line(index_x - 1, index_y, half) - line(index_x + 1, index_y, half)
        along_y = line(index_x, index_y - 1, half) - line(index_x, index_y + 1, half)
        along_z = jnp.zeros((1, 128), jnp.float32)
        for part in range(cells_z // 128):
            value = line(index_x, index_y, part)
            place = row_lane + 128 * part
            along_z = along_z + jnp.where(place == index_z - 1, value, 0.0)
            along_z = along_z - jnp.where(place == index_z + 1, value, 0.0)
        at = pl.ds(cluster, 1)
        pick_refs[0][at, :] = jnp.where(here, along_x, 0.0)
        pick_refs[1][at, :] = jnp.where(here, along_y, 0.0)
        pick_refs[2][at, :] = along_z
        return 0

    lax.fori_loop(0, clusters, pick, 0, unroll=4)

    def spread_out(step, _):
        start = pl.multiple_of(step * 8, 8)
        charge = masked_ref[pl.ds(start, 8), :] * (0.5 * field_scale)
        for part, pick_ref in enumerate(pick_refs):
            total = jnp.sum(pick_ref[pl.ds(start, 8), :], axis=1, keepdims=True)
            force_ref[pl.ds(4 * start + part, 8, stride=4), :] = charge * total
        force_ref[pl.ds(4 * start + 3, 8, stride=4), :] = jnp.zeros((8, 128), jnp.float32)
        return 0

    lax.fori_loop(0, clusters // 8, spread_out, 0)


def grid_step(cell, masked, fields, before, after, lower, upper, base):
    smem = pl.BlockSpec(memory_space=pltpu.SMEM)
    vmem = pl.BlockSpec(memory_space=pltpu.VMEM)
    clusters = masked.shape[0]
    cells_x, cells_y, cells_z = fields[0].shape
    block = (cells_x + 2 * HALO_WIDTHS[0], cells_y + 2 * MARGIN, cells_z)
    return pl.pallas_call(
        functools.partial(grid_kernel, base),
        out_shape=(
            jax.ShapeDtypeStruct(fields[0].shape, jnp.float32),
            jax.ShapeDtypeStruct(fields[0].shape, jnp.float32),
            jax.ShapeDtypeStruct((clusters * 4, 128), jnp.float32),
        ),
        in_specs=[smem] + [vmem] * 9,
        out_specs=(vmem,) * 3,
        scratch_shapes=[pltpu.VMEM(block, jnp.float32)] * 5
        + [pltpu.VMEM(((cells_x + 2) * 2 * block[1], 128), jnp.float32)]
        + [pltpu.VMEM((clusters, 128), jnp.float32)] * 3,
        compiler_params=pltpu.CompilerParams(vmem_limit_bytes=40 * 1024 * 1024),
        cost_estimate=pl.CostEstimate(
            flops=block[0] * block[1] * block[2] * 100, bytes_accessed=8 << 20, transcendentals=0
        ),
        name="grid_step",
    )(cell, masked, *fields, before, after, lower, upper)


def gather_forces_kernel(send_index_ref, own_ref, field_ref, *refs):
    back_refs, (out_ref, sum_ref) = (refs[:-2], refs[-2:])
    clusters = own_ref.shape[0]
    slots = send_index_ref.shape[1]
    sum_ref[...] = own_ref[...] + field_ref[...]

    def visit(slot, _):
        for direction, back_ref in enumerate(back_refs):
            cluster = send_index_ref[direction, slot]
            sum_ref[cluster] += back_ref[slot]
        return 0

    lax.fori_loop(0, slots, visit, 0)

    def write(step, _):
        for turn in range(8):
            cluster = step * 8 + turn
            out_ref[:, pl.ds(pl.multiple_of(cluster * 128, 128), 128)] = sum_ref[cluster][0:3]
        return 0

    lax.fori_loop(0, clusters // 8, write, 0)


def gather_forces(send_index, own, field, backs):
    smem = pl.BlockSpec(memory_space=pltpu.SMEM)
    vmem = pl.BlockSpec(memory_space=pltpu.VMEM)
    clusters = own.shape[0]
    return pl.pallas_call(
        gather_forces_kernel,
        out_shape=jax.ShapeDtypeStruct((3, clusters * 128), jnp.float32),
        in_specs=[smem] + [vmem] * (2 + len(backs)),
        out_specs=vmem,
        scratch_shapes=[pltpu.VMEM(own.shape, jnp.float32)],
        compiler_params=pltpu.CompilerParams(vmem_limit_bytes=32 * 1024 * 1024),
        name="gather_forces",
    )(send_index, own, field, *backs)


def passed_along(shard, axis, by):
    devices = lax.axis_size(axis)
    pairs = [(i, i + by) for i in range(devices) if 0 <= i + by < devices]
    return lax.ppermute(shard, axis, pairs)


ROUTES = (("brick", 1), ("brick", -1), ("brick", 2), ("brick", -2), ("grp", 1), ("grp", -1))


def shards(
    positions,
    charges,
    cluster_fill,
    cluster_cell,
    send_index,
    send_count,
    pair_local,
    pair_dir,
    pair_slot,
    ion_density,
    potential_prev,
    screening,
):
    clusters = cluster_fill.shape[0]
    psize = charges.shape[0] // clusters
    slots = send_index.shape[1]
    base = slots * 4
    own, masked, inverse, source, local, *messages = prepare(
        cluster_fill,
        cluster_cell,
        send_index,
        send_count,
        positions,
        charges.reshape(clusters, psize),
        ion_density,
        potential_prev,
        screening,
    )
    arrived = [local] + [
        passed_along(message, axis, by)
        for message, (axis, by) in zip(messages, ROUTES, strict=True)
    ]
    fields = (potential_prev, inverse, source, ion_density)
    arrived = lax.optimization_barrier(arrived)
    before, after = arrived[1:3]
    down, up = planes(fields, before, after, base)
    lower = passed_along(up, "grp", 1)
    upper = passed_along(down, "grp", -1)
    own_force, *reactions = pair_forces(
        pair_local,
        pair_dir * slots + pair_slot,
        own.reshape(clusters * 4, psize),
        arrived,
        slots,
    )
    backs = [reactions[0]] + [
        passed_along(reaction, axis, -by)
        for reaction, (axis, by) in zip(reactions[1:], ROUTES, strict=True)
    ]
    potential, ion_next, field_force = grid_step(
        cluster_cell, masked, fields, before, after, lower, upper, base
    )
    forces = gather_forces(
        send_index,
        own_force.reshape(clusters, 4, psize),
        field_force.reshape(clusters, 4, psize),
        [back.reshape(slots, 4, psize) for back in backs],
    )
    return (forces, potential, ion_next)


def solution(mesh):
    in_specs = (
        P(None, ("grp", "brick")),
        P(("grp", "brick")),
        P(("grp", "brick")),
        P(("grp", "brick")),
        P(("grp", "brick"), None),
        P(("grp", "brick"), None),
        P(("grp", "brick")),
        P(("grp", "brick")),
        P(("grp", "brick")),
        P("grp", "brick", None),
        P("grp", "brick", None),
        P("grp", "brick", None),
    )
    out_specs = (P(None, ("grp", "brick")), P("grp", "brick", None), P("grp", "brick", None))
    return jax.shard_map(shards, mesh=mesh, in_specs=in_specs, out_specs=out_specs, check_vma=False)
```

```python
import functools

import jax
import jax.numpy as jnp
from jax import lax
from jax.experimental import pallas as pl
from jax.experimental.pallas import tpu as pltpu
from jax.sharding import PartitionSpec as P

SWEEPS = 4
QUAD = 4
UNROLL = 8
HALO_WIDTHS = (SWEEPS + 1, SWEEPS, SWEEPS, 1)
MARGIN = 8
CELL_BITS = 8


coulomb_scale = 0.02
softening = 0.1
field_scale = 0.5
deposit_scale = 0.2
lowest_eig = 0.01
highest_eig = 1.99
mobility = 0.3
diffusion = 0.2
time_step = 0.2


def split3(value):
    first = value.astype(jnp.bfloat16).astype(jnp.float32)
    rest = value - first
    second = rest.astype(jnp.bfloat16).astype(jnp.float32)
    third = (rest - second).astype(jnp.bfloat16).astype(jnp.float32)
    return (first, second, third)


def moment_rows(comps, charge):
    rows = [None] * 12
    for part, charged in enumerate((*comps, None)):
        for level, piece in enumerate(split3(charge if charged is None else charge * charged)):
            rows[4 * level + part] = piece
    return rows


def pair_kernel(own_rows_ref, other_rows_ref, own_ref, *refs):
    sources = (len(refs) - 10) // 2
    other_refs = refs[:sources]
    own_out_ref = refs[sources]
    other_out_refs = refs[sources + 1 : 2 * sources + 1]
    (
        near_ref,
        far_ref,
        own_moment_ref,
        other_moment_ref,
        own_sum_ref,
        other_sum_ref,
        stage_ref,
        dist_ref,
        weight_ref,
    ) = refs[2 * sources + 1 :]
    clusters = own_ref.shape[0] // 4
    slots = other_out_refs[0].shape[0] // 4
    others = slots * sources
    groups = own_rows_ref.shape[0] // UNROLL
    units = UNROLL // QUAD
    groups_of_own = clusters // QUAD
    groups_of_other = others // QUAD
    ones = jnp.ones((8, 128), jnp.float32)
    zeros = jnp.zeros((8, 128), jnp.float32)

    def components(data_ref, start):
        return [data_ref[pl.ds(4 * start + part, 8, stride=4), :] for part in range(4)]

    def put(rows, base, stride):
        for index, row in enumerate(rows):
            stage_ref[pl.ds(base + index, 8, stride=stride), :] = row

    def put_turned(target_ref, columns, group, groups_in_all):
        for turn in range(QUAD):
            rolled = columns if turn == 0 else pltpu.roll(columns, 32 * turn, 1)
            at = pl.multiple_of((turn * groups_in_all + group) * 128, 128)
            target_ref[pl.ds(at, 128), :] = rolled.astype(jnp.bfloat16)

    def near_rows(step, _):
        start = pl.multiple_of(step * 8, 8)
        *comps, charge = components(own_ref, start)
        put(moment_rows(comps, charge) + [zeros] * 4, 256, 16)
        own_moment_ref[pl.ds(pl.multiple_of(start * 16, 128), 128), :] = stage_ref[
            256:384, :
        ].astype(jnp.bfloat16)
        rows = []
        square = zeros
        for comp in comps:
            first, second, third = split3(comp)
            square = square + comp * comp
            rows += [first, first, first, second, second, third]
        rows += [*split3(square), ones, ones, ones]
        rows += [zeros] * (32 - len(rows))
        put(rows, 0, 32)
        for half in range(2):
            columns = stage_ref[128 * half : 128 * half + 128, :].T
            put_turned(near_ref, columns, step * 2 + half, groups_of_own)
        for index in range(8):
            at = pl.ds(pl.multiple_of((start + index) * 128, 128), 128)
            own_sum_ref[at, :] = jnp.zeros((128, 128), jnp.float32)
        return 0

    def far_rows(source, step, _):
        local = pl.multiple_of(step * 8, 8)
        start = source * slots + local
        *comps, charge = components(other_refs[source], local)
        moments = moment_rows(comps, charge) + [zeros] * 4
        put(moments + [zeros] * 16, 0, 32)
        for half in range(2):
            columns = stage_ref[128 * half : 128 * half + 128, :].T
            put_turned(other_moment_ref, columns, (start // 8) * 2 + half, groups_of_other)
        rows = []
        square = zeros
        for comp in comps:
            first, second, third = split3(-2.0 * comp)
            square = square + comp * comp
            rows += [first, second, third, first, second, first]
        rows += [ones, ones, ones, *split3(square + softening)]
        rows += [zeros] * (32 - len(rows))
        put(rows, 0, 32)
        far_ref[pl.ds(pl.multiple_of(start * 32, 256), 256), :] = stage_ref[0:256, :].astype(
            jnp.bfloat16
        )
        return 0

    lax.fori_loop(0, clusters // 8, near_rows, 0)
    for source in range(sources):
        lax.fori_loop(0, slots // 8, functools.partial(far_rows, source), 0)
    other_sum_ref[...] = jnp.zeros_like(other_sum_ref)
    dist_ref[...] = jnp.full(dist_ref.shape, 1e38, jnp.float32)
    weight_ref[...] = jnp.zeros_like(weight_ref)

    lane = lax.broadcasted_iota(jnp.int32, (128, 128), 1)
    quarter = lax.shift_right_logical(lane, 5)
    quarter_row = lax.shift_right_logical(lax.broadcasted_iota(jnp.int32, (1, 128), 1), 5)
    masks = [jnp.where(quarter_row == turn, 1.0, 0.0).astype(jnp.bfloat16) for turn in range(QUAD)]
    empty = jnp.zeros((32, 128), jnp.bfloat16)

    def turned(source_ref, index, turn, groups_in_all):
        rotation = lax.bitwise_and(turn - index, 3)
        group = rotation * groups_in_all + lax.shift_right_logical(index, 2)
        return source_ref[pl.ds(pl.multiple_of(group * 128, 128), 128), :] * masks[turn]

    def block_diagonal(blocks):
        blank = empty[: blocks[0].shape[0]]
        lines = [
            jnp.concatenate([block if turn == at else blank for turn in range(QUAD)], axis=1)
            for at, block in enumerate(blocks)
        ]
        return jnp.concatenate(lines, axis=0)

    def distances(pair, unit):
        near = None
        far = []
        for turn in range(QUAD):
            tile = turned(near_ref, own_rows_ref[pair + turn], turn, groups_of_own)
            near = tile if near is None else near + tile
            at = pl.multiple_of(other_rows_ref[pair + turn] * 32, 32)
            far.append(far_ref[pl.ds(at, 32), :])
        dist_ref[unit] = jnp.dot(near, block_diagonal(far), preferred_element_type=jnp.float32)

    def weights(unit, turn):
        root = lax.rsqrt(dist_ref[unit, :, 128 * turn : 128 * turn + 128])
        weight = root * root * root
        high = weight.astype(jnp.bfloat16)
        weight_ref[unit, 128 * turn : 128 * turn + 128, :128] = high
        weight_ref[unit, 128 * turn : 128 * turn + 128, 128:] = (
            weight - high.astype(jnp.float32)
        ).astype(jnp.bfloat16)

    def products(pair, unit):
        owns = [own_rows_ref[pair + turn] for turn in range(QUAD)]
        others = [other_rows_ref[pair + turn] for turn in range(QUAD)]
        both = weight_ref[unit]
        levels = [
            jnp.concatenate(
                [both[128 * turn : 128 * turn + 128, lanes] for turn in range(QUAD)], axis=1
            )
            for lanes in (slice(0, 128), slice(128, 256))
        ]
        columns = jnp.concatenate(
            [turned(other_moment_ref, others[turn], turn, groups_of_other) for turn in range(QUAD)],
            axis=0,
        )
        to_own = jnp.dot(
            jnp.concatenate(levels, axis=0), columns, preferred_element_type=jnp.float32
        )
        rows = block_diagonal(
            [own_moment_ref[pl.ds(pl.multiple_of(own * 16, 16), 16), :] for own in owns]
        )
        to_other = jnp.dot(rows, both, preferred_element_type=jnp.float32)
        return (owns, others, to_own[:128] + to_own[128:], to_other[:, :128] + to_other[:, 128:])

    def visit(step, _):
        last = jnp.maximum(step - 2, 0) * UNROLL
        first = jnp.minimum(step, groups - 1) * UNROLL
        results = [products(last + QUAD * unit, unit) for unit in range(units)]
        for unit in range(units):
            for turn in range(QUAD):
                weights(unit, turn)
        for unit in range(units):
            distances(first + QUAD * unit, unit)
        for owns, others, to_own, to_other in results:
            for turn in range(QUAD):
                own_at = pl.ds(pl.multiple_of(owns[turn] * 128, 128), 128)
                other_at = pl.ds(pl.multiple_of(others[turn] * 16, 16), 16)
                own_sum_ref[own_at, :] += jnp.where(quarter == turn, to_own, 0.0)
                other_sum_ref[other_at, :] += to_other[16 * turn : 16 * turn + 16]
        return 0

    lax.fori_loop(0, groups + 2, visit, 0)

    def finish(data_ref, out_ref, start, rows_ref, base, stride):
        *comps, charge = components(data_ref, start)

        def total(part):
            terms = [
                rows_ref[pl.ds(base + 4 * level + part, 8, stride=stride), :] for level in range(3)
            ]
            return terms[0] + (terms[1] + terms[2])

        weight = total(3)
        scale = coulomb_scale * charge
        for part, comp in enumerate(comps):
            out_ref[pl.ds(4 * start + part, 8, stride=4), :] = scale * (comp * weight - total(part))
        out_ref[pl.ds(4 * start + 3, 8, stride=4), :] = zeros

    def finish_own(step, _):
        start = pl.multiple_of(step * 8, 8)
        for half in range(2):
            columns = None
            for index in range(4):
                at = pl.ds(pl.multiple_of((start + 4 * half + index) * 128, 128), 128)
                block = own_sum_ref[at, :]
                block = block + pltpu.roll(block, 64, 1)
                block = block + pltpu.roll(block, 32, 1)
                columns = block if index == 0 else jnp.where(quarter < index, columns, block)
            stage_ref[128 * half : 128 * half + 128, :] = columns.T
        finish(own_ref, own_out_ref, start, stage_ref, 0, 32)
        return 0

    def finish_other(source, step, _):
        start = pl.multiple_of(step * 8, 8)
        finish(
            other_refs[source],
            other_out_refs[source],
            start,
            other_sum_ref,
            (source * slots + start) * 16,
            16,
        )
        return 0

    lax.fori_loop(0, clusters // 8, finish_own, 0)
    for source in range(sources):
        lax.fori_loop(0, slots // 8, functools.partial(finish_other, source), 0)


def pair_forces(own_rows, other_rows, own, arrived, slots):
    clusters = own.shape[0] // 4
    others = slots * len(arrived)
    pairs = own_rows.shape[0]
    smem = pl.BlockSpec(memory_space=pltpu.SMEM)
    vmem = pl.BlockSpec(memory_space=pltpu.VMEM)
    return pl.pallas_call(
        pair_kernel,
        out_shape=(
            jax.ShapeDtypeStruct(own.shape, jnp.float32),
            *[jax.ShapeDtypeStruct((slots * 4, 128), jnp.float32)] * len(arrived),
        ),
        in_specs=[smem, smem, vmem] + [vmem] * len(arrived),
        out_specs=(vmem,) * (len(arrived) + 1),
        scratch_shapes=[
            pltpu.VMEM((clusters * 128, 128), jnp.bfloat16),
            pltpu.VMEM((others * 32, 128), jnp.bfloat16),
            pltpu.VMEM((clusters * 16, 128), jnp.bfloat16),
            pltpu.VMEM((others * 128, 128), jnp.bfloat16),
            pltpu.VMEM((clusters * 128, 128), jnp.float32),
            pltpu.VMEM((others * 16, 128), jnp.float32),
            pltpu.VMEM((384, 128), jnp.float32),
            pltpu.VMEM((UNROLL // QUAD, 128, 128 * QUAD), jnp.float32),
            pltpu.VMEM((UNROLL // QUAD, 128 * QUAD, 256), jnp.bfloat16),
        ],
        compiler_params=pltpu.CompilerParams(vmem_limit_bytes=46 * 1024 * 1024),
        cost_estimate=pl.CostEstimate(
            flops=pairs * 128 * 128 * 20, bytes_accessed=4 * 1024 * 1024, transcendentals=0
        ),
        name="pair_forces",
    )(own_rows, other_rows, own, *arrived)


def prepare_kernel(
    fill_ref,
    cell_ref,
    send_index_ref,
    send_count_ref,
    position_hbm,
    charge_hbm,
    ion_hbm,
    start_hbm,
    screen_hbm,
    own_ref,
    masked_ref,
    inverse_ref,
    source_ref,
    *refs,
):
    out_refs, scratch = (refs[:-8], refs[-8:])
    sum_ref, deposit_ref, position_ref, charge_ref, ion_ref, start_ref, screen_ref, sems = scratch
    copies = [
        pltpu.make_async_copy(source, target, sems.at[index])
        for index, (source, target) in enumerate(
            (
                (position_hbm, position_ref),
                (charge_hbm, charge_ref),
                (ion_hbm, ion_ref),
                (start_hbm, start_ref),
                (screen_hbm, screen_ref),
            )
        )
    ]
    for copy in copies:
        copy.start()
    deposit_ref[...] = jnp.zeros_like(deposit_ref)
    copies[0].wait()
    copies[1].wait()
    clusters = charge_ref.shape[0]
    cells_x, cells_y, _ = ion_ref.shape
    slots = send_index_ref.shape[1]
    lane = lax.broadcasted_iota(jnp.int32, (1, 128), 1)
    row = lax.broadcasted_iota(jnp.int32, (4, 128), 0)

    def collect(step, _):
        for turn in range(8):
            cluster = step * 8 + turn
            masked = jnp.where(lane < fill_ref[cluster], charge_ref[pl.ds(cluster, 1), :], 0.0)
            masked_ref[pl.ds(cluster, 1), :] = masked
            place = position_ref[:, pl.ds(pl.multiple_of(cluster * 128, 128), 128)]
            own_ref[cluster, 0:3, :] = place
            own_ref[cluster, 3:4, :] = masked
        at = pl.ds(pl.multiple_of(step * 8, 8), 8)
        total = jnp.sum(masked_ref[at, :], axis=1, keepdims=True)
        sum_ref[at, :] = jnp.broadcast_to(deposit_scale * total, (8, 128))
        return 0

    lax.fori_loop(0, clusters // 8, collect, 0)

    def fill_messages(step, _):
        for direction, out_ref in enumerate(out_refs):
            parts = []
            for turn in range(2):
                slot = step * 2 + turn
                live = jnp.where(slot < send_count_ref[0, direction], 1.0, 0.0)
                value = own_ref[send_index_ref[direction, slot]]
                parts.append(jnp.where(row == 3, value * live, value))
            out_ref[pl.ds(pl.multiple_of(step * 8, 8), 8), :] = jnp.concatenate(parts, axis=0)
        return 0

    lax.fori_loop(0, slots // 2, fill_messages, 0)

    def deposit(cluster, _):
        cell = cell_ref[cluster]
        index_x = lax.shift_right_logical(cell, CELL_BITS) // cells_y
        index_y = lax.shift_right_logical(cell, CELL_BITS) % cells_y
        index_z = lax.bitwise_and(cell, 255)
        half = lax.shift_right_logical(index_z, 7)
        added = jnp.where(
            lane == lax.bitwise_and(index_z, 127), sum_ref[pl.ds(cluster, 1), :], 0.0
        )
        deposit_ref[pl.ds((index_x * 2 + half) * cells_y + index_y, 1), :] += added
        return 0

    lax.fori_loop(0, clusters, deposit, 0, unroll=4)
    for copy in copies[2:]:
        copy.wait()
    inverse_ref[...] = 1.0 / (6.0 + screen_ref[...])
    for index in range(cells_x):
        for half in range(2):
            lanes = slice(128 * half, 128 * half + 128)
            first = (index * 2 + half) * cells_y
            source_ref[index, :, lanes] = (
                ion_ref[index, :, lanes] + deposit_ref[first : first + cells_y, :]
            ) * inverse_ref[index, :, lanes]
    for out_ref, after in ((out_refs[1], True), (out_refs[2], False)):
        for index in range(cells_x):
            base = slots * 4 + index * 32
            offset = 0
            for field_ref, width in zip(
                (start_ref, inverse_ref, source_ref, ion_ref), HALO_WIDTHS, strict=True
            ):
                first = cells_y - width if after else 0
                rows = field_ref[index, first : first + width, :]
                for half in range(2):
                    out_ref[base + 16 * half + offset : base + 16 * half + offset + width, :] = (
                        rows[:, 128 * half : 128 * half + 128]
                    )
                offset += width
            for half in range(2):
                out_ref[base + 16 * half + offset : base + 16 * half + 16, :] = jnp.zeros(
                    (16 - offset, 128), jnp.float32
                )


def prepare(fill, cell, send_index, send_count, positions, charges, ions, start, screen):
    clusters = charges.shape[0]
    directions, slots = send_index.shape
    cells_x = ions.shape[0]
    smem = pl.BlockSpec(memory_space=pltpu.SMEM)
    vmem = pl.BlockSpec(memory_space=pltpu.VMEM)
    rows = [slots * 4] * directions
    rows[1] = rows[2] = slots * 4 + cells_x * 32
    return pl.pallas_call(
        prepare_kernel,
        out_shape=(
            jax.ShapeDtypeStruct((clusters, 4, 128), jnp.float32),
            jax.ShapeDtypeStruct((clusters, 128), jnp.float32),
            jax.ShapeDtypeStruct(ions.shape, jnp.float32),
            jax.ShapeDtypeStruct(ions.shape, jnp.float32),
            *[jax.ShapeDtypeStruct((count, 128), jnp.float32) for count in rows],
        ),
        in_specs=[smem] * 4 + [pl.BlockSpec(memory_space=pltpu.HBM)] * 5,
        out_specs=(vmem,) * (4 + directions),
        scratch_shapes=[
            pltpu.VMEM((clusters, 128), jnp.float32),
            pltpu.VMEM((ions.size // 128, 128), jnp.float32),
            *[
                pltpu.VMEM(operand.shape, jnp.float32)
                for operand in (positions, charges, ions, start, screen)
            ],
            pltpu.SemaphoreType.DMA((5,)),
        ],
        compiler_params=pltpu.CompilerParams(vmem_limit_bytes=60 * 1024 * 1024),
        name="prepare",
    )(fill, cell, send_index, send_count, positions, charges, ions, start, screen)


def put_extended(target_ref, plane, field, field_ref, index, before_ref, after_ref, base):
    cells_y = field_ref.shape[1]
    width = HALO_WIDTHS[field]
    offset = sum(HALO_WIDTHS[:field])
    target_ref[plane, MARGIN : MARGIN + cells_y, :] = field_ref[index]
    for half in range(2):
        lanes = slice(128 * half, 128 * half + 128)
        first = base + index * 32 + 16 * half + offset
        target_ref[plane, MARGIN - width : MARGIN, lanes] = before_ref[first : first + width, :]
        target_ref[plane, MARGIN + cells_y : MARGIN + cells_y + width, lanes] = after_ref[
            first : first + width, :
        ]


def planes_kernel(base, *refs):
    field_refs, (before_ref, after_ref, down_ref, up_ref) = (refs[:4], refs[4:])
    cells_x = field_refs[0].shape[0]
    down_ref[...] = jnp.zeros_like(down_ref)
    up_ref[...] = jnp.zeros_like(up_ref)
    plane = 0
    for field, width in enumerate(HALO_WIDTHS):
        for index in range(width):
            for target_ref, source in ((down_ref, index), (up_ref, cells_x - width + index)):
                put_extended(
                    target_ref, plane, field, field_refs[field], source, before_ref, after_ref, base
                )
            plane += 1


def planes(fields, before, after, base):
    vmem = pl.BlockSpec(memory_space=pltpu.VMEM)
    _, cells_y, cells_z = fields[0].shape
    shape = jax.ShapeDtypeStruct((sum(HALO_WIDTHS), cells_y + 2 * MARGIN, cells_z), jnp.float32)
    return pl.pallas_call(
        functools.partial(planes_kernel, base),
        out_shape=(shape, shape),
        in_specs=[vmem] * 6,
        out_specs=(vmem, vmem),
        compiler_params=pltpu.CompilerParams(vmem_limit_bytes=32 * 1024 * 1024),
        name="planes",
    )(*fields, before, after)


def face_flux(pot_low, pot_high, ion_low, ion_high):
    speed = -mobility * (pot_high - pot_low)
    return (
        jnp.maximum(speed, 0.0) * ion_low
        + jnp.minimum(speed, 0.0) * ion_high
        - diffusion * (ion_high - ion_low)
    )


def grid_kernel(base, *refs):
    cell_ref, masked_ref = refs[:2]
    field_refs = refs[2:6]
    before_ref, after_ref, lower_ref, upper_ref = refs[6:10]
    potential_ref, next_ref, force_ref = refs[10:13]
    start_ref, inverse_ref, resid_ref, ion_ref, update_ref, line_ref, *pick_refs = refs[13:]
    cells_x, cells_y, cells_z = field_refs[0].shape
    rows = cells_y + 2 * MARGIN
    depth = HALO_WIDTHS[0]
    clusters = masked_ref.shape[0]
    lane = lax.broadcasted_iota(jnp.int32, (rows, cells_z), 1)
    middle = 0.5 * (highest_eig + lowest_eig)
    spread = 0.5 * (highest_eig - lowest_eig)

    plane = 0
    for field, target_ref in enumerate((start_ref, inverse_ref, resid_ref, ion_ref)):
        width = HALO_WIDTHS[field]
        if field == 0 or field == 3:
            target_ref[...] = jnp.zeros_like(target_ref)
        else:
            target_ref[depth : depth + cells_x, 0:MARGIN, :] = jnp.zeros(
                (cells_x, MARGIN, cells_z), jnp.float32
            )
            target_ref[depth : depth + cells_x, rows - MARGIN : rows, :] = jnp.zeros(
                (cells_x, MARGIN, cells_z), jnp.float32
            )
        for index in range(width):
            target_ref[depth - width + index] = lower_ref[plane + index]
            target_ref[depth + cells_x + index] = upper_ref[plane + index]
        for index in range(cells_x):
            put_extended(
                target_ref,
                depth + index,
                field,
                field_refs[field],
                index,
                before_ref,
                after_ref,
                base,
            )
        plane += width

    def above(value):
        return jnp.where(lane == cells_z - 1, 0.0, pltpu.roll(value, cells_z - 1, 1))

    def below(value):
        return jnp.where(lane == 0, 0.0, pltpu.roll(value, 1, 1))

    def beside(value):
        rolled = pltpu.roll(value, 1, 0) + pltpu.roll(value, rows - 1, 0)
        return rolled + (above(value) + below(value))

    def first_sweep(index, planes):
        last, here = planes
        after = start_ref[index + 1]
        resid = (
            resid_ref[index] - here + inverse_ref[index] * ((last + after) + beside(here))
        )
        resid_ref[index] = resid
        update_ref[index] = resid / middle
        return (here, after)

    lax.fori_loop(1, cells_x + 2 * depth - 1, first_sweep, (start_ref[0], start_ref[1]))

    ratio_ms = middle / spread
    weight_now = 1.0 / ratio_ms
    for turn in range(1, SWEEPS):
        weight_next = 1.0 / (2.0 * ratio_ms - weight_now)
        keep, gain = (weight_next * weight_now, 2.0 * weight_next / spread)
        weight_now = weight_next

        def sweep(index, planes, turn=turn, keep=keep, gain=gain):
            last, here = planes
            after = update_ref[index + 1]
            resid = resid_ref[index] - here + inverse_ref[index] * ((last + after) + beside(here))
            update = keep * here + gain * resid
            if turn == 1:
                start_ref[index] = start_ref[index] + here + update
            else:
                start_ref[index] = start_ref[index] + update
            if turn + 1 < SWEEPS:
                resid_ref[index] = resid
                update_ref[index] = update
            return (here, after)

        first = 1 + turn
        lax.fori_loop(
            first,
            cells_x + 2 * depth - first,
            sweep,
            (update_ref[first - 1], update_ref[first]),
        )

    def upper_flux(index):
        return face_flux(start_ref[index], start_ref[index + 1], ion_ref[index], ion_ref[index + 1])

    inner = slice(MARGIN, MARGIN + cells_y)

    def advance(index, lower):
        pot = start_ref[depth + index]
        ions = ion_ref[depth + index]
        upper = upper_flux(depth + index)
        along_y = face_flux(pot, pltpu.roll(pot, rows - 1, 0), ions, pltpu.roll(ions, rows - 1, 0))
        along_z = face_flux(pot, above(pot), ions, above(ions))
        first_z = face_flux(0.0, pot, 0.0, ions)
        total = upper - lower
        total = total + (along_y - pltpu.roll(along_y, 1, 0))
        total = total + (along_z - jnp.where(lane == 0, first_z, pltpu.roll(along_z, 1, 1)))
        next_ref[index] = (ions - time_step * total)[inner]
        potential_ref[index] = pot[inner]
        return upper

    lax.fori_loop(0, cells_x, advance, upper_flux(depth - 1))
    for index in range(cells_x + 2):
        for half in range(2):
            line_ref[pl.ds((index * 2 + half) * rows, rows), :] = start_ref[
                depth - 1 + index, :, 128 * half : 128 * half + 128
            ]

    row_lane = lax.broadcasted_iota(jnp.int32, (1, 128), 1)

    def pick(cluster, _):
        cell = cell_ref[cluster]
        index_x = lax.shift_right_logical(cell, CELL_BITS) // cells_y + 1
        index_y = lax.shift_right_logical(cell, CELL_BITS) % cells_y + MARGIN
        index_z = lax.bitwise_and(cell, 255)
        half = lax.shift_right_logical(index_z, 7)
        here = row_lane == lax.bitwise_and(index_z, 127)

        def line(plane, row, part):
            return line_ref[pl.ds((plane * 2 + part) * rows + row, 1), :]

        along_x = line(index_x - 1, index_y, half) - line(index_x + 1, index_y, half)
        along_y = line(index_x, index_y - 1, half) - line(index_x, index_y + 1, half)
        along_z = jnp.zeros((1, 128), jnp.float32)
        for part in range(cells_z // 128):
            value = line(index_x, index_y, part)
            place = row_lane + 128 * part
            along_z = along_z + jnp.where(place == index_z - 1, value, 0.0)
            along_z = along_z - jnp.where(place == index_z + 1, value, 0.0)
        at = pl.ds(cluster, 1)
        pick_refs[0][at, :] = jnp.where(here, along_x, 0.0)
        pick_refs[1][at, :] = jnp.where(here, along_y, 0.0)
        pick_refs[2][at, :] = along_z
        return 0

    lax.fori_loop(0, clusters, pick, 0, unroll=4)

    def spread_out(step, _):
        start = pl.multiple_of(step * 8, 8)
        charge = masked_ref[pl.ds(start, 8), :] * (0.5 * field_scale)
        for part, pick_ref in enumerate(pick_refs):
            total = jnp.sum(pick_ref[pl.ds(start, 8), :], axis=1, keepdims=True)
            force_ref[pl.ds(4 * start + part, 8, stride=4), :] = charge * total
        force_ref[pl.ds(4 * start + 3, 8, stride=4), :] = jnp.zeros((8, 128), jnp.float32)
        return 0

    lax.fori_loop(0, clusters // 8, spread_out, 0)


def grid_step(cell, masked, fields, before, after, lower, upper, base):
    smem = pl.BlockSpec(memory_space=pltpu.SMEM)
    vmem = pl.BlockSpec(memory_space=pltpu.VMEM)
    clusters = masked.shape[0]
    cells_x, cells_y, cells_z = fields[0].shape
    block = (cells_x + 2 * HALO_WIDTHS[0], cells_y + 2 * MARGIN, cells_z)
    return pl.pallas_call(
        functools.partial(grid_kernel, base),
        out_shape=(
            jax.ShapeDtypeStruct(fields[0].shape, jnp.float32),
            jax.ShapeDtypeStruct(fields[0].shape, jnp.float32),
            jax.ShapeDtypeStruct((clusters * 4, 128), jnp.float32),
        ),
        in_specs=[smem] + [vmem] * 9,
        out_specs=(vmem,) * 3,
        scratch_shapes=[pltpu.VMEM(block, jnp.float32)] * 5
        + [pltpu.VMEM(((cells_x + 2) * 2 * block[1], 128), jnp.float32)]
        + [pltpu.VMEM((clusters, 128), jnp.float32)] * 3,
        compiler_params=pltpu.CompilerParams(vmem_limit_bytes=40 * 1024 * 1024),
        cost_estimate=pl.CostEstimate(
            flops=block[0] * block[1] * block[2] * 100, bytes_accessed=8 << 20, transcendentals=0
        ),
        name="grid_step",
    )(cell, masked, *fields, before, after, lower, upper)


def gather_forces_kernel(send_index_ref, own_ref, field_ref, *refs):
    back_refs, (out_ref, sum_ref) = (refs[:-2], refs[-2:])
    clusters = own_ref.shape[0]
    slots = send_index_ref.shape[1]
    sum_ref[...] = own_ref[...] + field_ref[...]

    def visit(slot, _):
        for direction, back_ref in enumerate(back_refs):
            cluster = send_index_ref[direction, slot]
            sum_ref[cluster] += back_ref[slot]
        return 0

    lax.fori_loop(0, slots, visit, 0)

    def write(step, _):
        for turn in range(8):
            cluster = step * 8 + turn
            out_ref[:, pl.ds(pl.multiple_of(cluster * 128, 128), 128)] = sum_ref[cluster][0:3]
        return 0

    lax.fori_loop(0, clusters // 8, write, 0)


def gather_forces(send_index, own, field, backs):
    smem = pl.BlockSpec(memory_space=pltpu.SMEM)
    vmem = pl.BlockSpec(memory_space=pltpu.VMEM)
    clusters = own.shape[0]
    return pl.pallas_call(
        gather_forces_kernel,
        out_shape=jax.ShapeDtypeStruct((3, clusters * 128), jnp.float32),
        in_specs=[smem] + [vmem] * (2 + len(backs)),
        out_specs=vmem,
        scratch_shapes=[pltpu.VMEM(own.shape, jnp.float32)],
        compiler_params=pltpu.CompilerParams(vmem_limit_bytes=32 * 1024 * 1024),
        name="gather_forces",
    )(send_index, own, field, *backs)


def passed_along(shard, axis, by):
    devices = lax.axis_size(axis)
    pairs = [(i, i + by) for i in range(devices) if 0 <= i + by < devices]
    return lax.ppermute(shard, axis, pairs)


ROUTES = (("brick", 1), ("brick", -1), ("brick", 2), ("brick", -2), ("grp", 1), ("grp", -1))


def shards(
    positions,
    charges,
    cluster_fill,
    cluster_cell,
    send_index,
    send_count,
    pair_local,
    pair_dir,
    pair_slot,
    ion_density,
    potential_prev,
    screening,
):
    clusters = cluster_fill.shape[0]
    psize = charges.shape[0] // clusters
    slots = send_index.shape[1]
    base = slots * 4
    own, masked, inverse, source, local, *messages = prepare(
        cluster_fill,
        cluster_cell,
        send_index,
        send_count,
        positions,
        charges.reshape(clusters, psize),
        ion_density,
        potential_prev,
        screening,
    )
    arrived = [local] + [
        passed_along(message, axis, by)
        for message, (axis, by) in zip(messages, ROUTES, strict=True)
    ]
    fields = (potential_prev, inverse, source, ion_density)
    arrived = lax.optimization_barrier(arrived)
    before, after = arrived[1:3]
    down, up = planes(fields, before, after, base)
    lower = passed_along(up, "grp", 1)
    upper = passed_along(down, "grp", -1)
    own_force, *reactions = pair_forces(
        pair_local,
        pair_dir * slots + pair_slot,
        own.reshape(clusters * 4, psize),
        arrived,
        slots,
    )
    backs = [reactions[0]] + [
        passed_along(reaction, axis, -by)
        for reaction, (axis, by) in zip(reactions[1:], ROUTES, strict=True)
    ]
    potential, ion_next, field_force = grid_step(
        cluster_cell, masked, fields, before, after, lower, upper, base
    )
    forces = gather_forces(
        send_index,
        own_force.reshape(clusters, 4, psize),
        field_force.reshape(clusters, 4, psize),
        [back.reshape(slots, 4, psize) for back in backs],
    )
    return (forces, potential, ion_next)


def solution(mesh):
    in_specs = (
        P(None, ("grp", "brick")),
        P(("grp", "brick")),
        P(("grp", "brick")),
        P(("grp", "brick")),
        P(("grp", "brick"), None),
        P(("grp", "brick"), None),
        P(("grp", "brick")),
        P(("grp", "brick")),
        P(("grp", "brick")),
        P("grp", "brick", None),
        P("grp", "brick", None),
        P("grp", "brick", None),
    )
    out_specs = (P(None, ("grp", "brick")), P("grp", "brick", None), P("grp", "brick", None))
    return jax.shard_map(shards, mesh=mesh, in_specs=in_specs, out_specs=out_specs, check_vma=False)
```

```python
import functools

import jax
import jax.numpy as jnp
from jax import lax
from jax.experimental import pallas as pl
from jax.experimental.pallas import tpu as pltpu
from jax.sharding import PartitionSpec as P

SWEEPS = 4
QUAD = 4
UNROLL = 8
HALO_WIDTHS = (SWEEPS + 1, SWEEPS, SWEEPS, 1)
MARGIN = 8
CELL_BITS = 8


coulomb_scale = 0.02
softening = 0.1
field_scale = 0.5
deposit_scale = 0.2
lowest_eig = 0.01
highest_eig = 1.99
mobility = 0.3
diffusion = 0.2
time_step = 0.2


def split3(value):
    first = value.astype(jnp.bfloat16).astype(jnp.float32)
    rest = value - first
    second = rest.astype(jnp.bfloat16).astype(jnp.float32)
    third = (rest - second).astype(jnp.bfloat16).astype(jnp.float32)
    return (first, second, third)


def moment_rows(comps, charge):
    rows = [None] * 12
    for part, charged in enumerate((*comps, None)):
        for level, piece in enumerate(split3(charge if charged is None else charge * charged)):
            rows[4 * level + part] = piece
    return rows


def pair_kernel(own_rows_ref, other_rows_ref, own_ref, *refs):
    sources = (len(refs) - 12) // 2
    other_refs = refs[:sources]
    own_out_ref = refs[sources]
    other_out_refs = refs[sources + 1 : 2 * sources + 1]
    (
        near_ref,
        far_ref,
        own_moment_ref,
        other_moment_ref,
        own_sum_ref,
        other_sum_ref,
        stage_ref,
        *passed_refs,
    ) = refs[2 * sources + 1 :]
    clusters = own_ref.shape[0] // 4
    slots = other_out_refs[0].shape[0] // 4
    others = slots * sources
    groups = own_rows_ref.shape[0] // UNROLL
    units = UNROLL // QUAD
    groups_of_own = clusters // QUAD
    groups_of_other = others // QUAD
    ones = jnp.ones((8, 128), jnp.float32)
    zeros = jnp.zeros((8, 128), jnp.float32)

    def components(data_ref, start):
        return [data_ref[pl.ds(4 * start + part, 8, stride=4), :] for part in range(4)]

    def put(rows, base, stride):
        for index, row in enumerate(rows):
            stage_ref[pl.ds(base + index, 8, stride=stride), :] = row

    def put_turned(target_ref, columns, group, groups_in_all):
        for turn in range(QUAD):
            rolled = columns if turn == 0 else pltpu.roll(columns, 32 * turn, 1)
            at = pl.multiple_of((turn * groups_in_all + group) * 128, 128)
            target_ref[pl.ds(at, 128), :] = rolled.astype(jnp.bfloat16)

    def near_rows(step, _):
        start = pl.multiple_of(step * 8, 8)
        *comps, charge = components(own_ref, start)
        put(moment_rows(comps, charge) + [zeros] * 4, 256, 16)
        own_moment_ref[pl.ds(pl.multiple_of(start * 16, 128), 128), :] = stage_ref[
            256:384, :
        ].astype(jnp.bfloat16)
        rows = []
        square = zeros
        for comp in comps:
            first, second, third = split3(comp)
            square = square + comp * comp
            rows += [first, first, first, second, second, third]
        rows += [*split3(square), ones, ones, ones]
        rows += [zeros] * (32 - len(rows))
        put(rows, 0, 32)
        for half in range(2):
            columns = stage_ref[128 * half : 128 * half + 128, :].T
            put_turned(near_ref, columns, step * 2 + half, groups_of_own)
        for index in range(8):
            at = pl.ds(pl.multiple_of((start + index) * 128, 128), 128)
            own_sum_ref[at, :] = jnp.zeros((128, 128), jnp.float32)
        return 0

    def far_rows(source, step, _):
        local = pl.multiple_of(step * 8, 8)
        start = source * slots + local
        *comps, charge = components(other_refs[source], local)
        moments = moment_rows(comps, charge) + [zeros] * 4
        put(moments + [zeros] * 16, 0, 32)
        for half in range(2):
            columns = stage_ref[128 * half : 128 * half + 128, :].T
            put_turned(other_moment_ref, columns, (start // 8) * 2 + half, groups_of_other)
        rows = []
        square = zeros
        for comp in comps:
            first, second, third = split3(-2.0 * comp)
            square = square + comp * comp
            rows += [first, second, third, first, second, first]
        rows += [ones, ones, ones, *split3(square + softening)]
        rows += [zeros] * (32 - len(rows))
        put(rows, 0, 32)
        far_ref[pl.ds(pl.multiple_of(start * 32, 256), 256), :] = stage_ref[0:256, :].astype(
            jnp.bfloat16
        )
        return 0

    lax.fori_loop(0, clusters // 8, near_rows, 0)
    for source in range(sources):
        lax.fori_loop(0, slots // 8, functools.partial(far_rows, source), 0)
    other_sum_ref[...] = jnp.zeros_like(other_sum_ref)
    dist_refs, weight_refs = (passed_refs[:2], passed_refs[2:])
    dist_refs[0][...] = jnp.full(dist_refs[0].shape, 1e38, jnp.float32)
    weight_refs[0][...] = jnp.zeros_like(weight_refs[0])

    lane = lax.broadcasted_iota(jnp.int32, (128, 128), 1)
    quarter = lax.shift_right_logical(lane, 5)
    quarter_row = lax.shift_right_logical(lax.broadcasted_iota(jnp.int32, (1, 128), 1), 5)
    masks = [jnp.where(quarter_row == turn, 1.0, 0.0).astype(jnp.bfloat16) for turn in range(QUAD)]
    empty = jnp.zeros((32, 128), jnp.bfloat16)

    def turned(source_ref, index, turn, groups_in_all):
        rotation = lax.bitwise_and(turn - index, 3)
        group = rotation * groups_in_all + lax.shift_right_logical(index, 2)
        return source_ref[pl.ds(pl.multiple_of(group * 128, 128), 128), :] * masks[turn]

    def block_diagonal(blocks):
        blank = empty[: blocks[0].shape[0]]
        lines = [
            jnp.concatenate([block if turn == at else blank for turn in range(QUAD)], axis=1)
            for at, block in enumerate(blocks)
        ]
        return jnp.concatenate(lines, axis=0)

    def distances(pair, unit, dist_ref):
        near = None
        far = []
        for turn in range(QUAD):
            tile = turned(near_ref, own_rows_ref[pair + turn], turn, groups_of_own)
            near = tile if near is None else near + tile
            at = pl.multiple_of(other_rows_ref[pair + turn] * 32, 32)
            far.append(far_ref[pl.ds(at, 32), :])
        dist_ref[unit] = jnp.dot(near, block_diagonal(far), preferred_element_type=jnp.float32)

    def weights(unit, turn, dist_ref, weight_ref):
        root = lax.rsqrt(dist_ref[unit, :, 128 * turn : 128 * turn + 128])
        weight = root * root * root
        high = weight.astype(jnp.bfloat16)
        weight_ref[unit, 128 * turn : 128 * turn + 128, :128] = high
        weight_ref[unit, 128 * turn : 128 * turn + 128, 128:] = (
            weight - high.astype(jnp.float32)
        ).astype(jnp.bfloat16)

    def products(pair, unit, weight_ref):
        owns = [own_rows_ref[pair + turn] for turn in range(QUAD)]
        others = [other_rows_ref[pair + turn] for turn in range(QUAD)]
        both = weight_ref[unit]
        levels = [
            jnp.concatenate(
                [both[128 * turn : 128 * turn + 128, lanes] for turn in range(QUAD)], axis=1
            )
            for lanes in (slice(0, 128), slice(128, 256))
        ]
        columns = jnp.concatenate(
            [turned(other_moment_ref, others[turn], turn, groups_of_other) for turn in range(QUAD)],
            axis=0,
        )
        to_own = jnp.dot(
            jnp.concatenate(levels, axis=0), columns, preferred_element_type=jnp.float32
        )
        rows = block_diagonal(
            [own_moment_ref[pl.ds(pl.multiple_of(own * 16, 16), 16), :] for own in owns]
        )
        to_other = jnp.dot(rows, both, preferred_element_type=jnp.float32)
        return (owns, others, to_own[:128] + to_own[128:], to_other[:, :128] + to_other[:, 128:])

    def half_step(step, side):
        last = jnp.maximum(step - 2, 0) * UNROLL
        first = jnp.minimum(step, groups - 1) * UNROLL
        results = [products(last + QUAD * unit, unit, weight_refs[side]) for unit in range(units)]
        for unit in range(units):
            for turn in range(QUAD):
                weights(unit, turn, dist_refs[side], weight_refs[1 - side])
        for unit in range(units):
            distances(first + QUAD * unit, unit, dist_refs[1 - side])
        for owns, others, to_own, to_other in results:
            for turn in range(QUAD):
                own_at = pl.ds(pl.multiple_of(owns[turn] * 128, 128), 128)
                other_at = pl.ds(pl.multiple_of(others[turn] * 16, 16), 16)
                own_sum_ref[own_at, :] += jnp.where(quarter == turn, to_own, 0.0)
                other_sum_ref[other_at, :] += to_other[16 * turn : 16 * turn + 16]

    def visit(step, _):
        for side in range(2):
            half_step(step * 2 + side, side)
        return 0

    lax.fori_loop(0, (groups + 2) // 2, visit, 0)

    def finish(data_ref, out_ref, start, rows_ref, base, stride):
        *comps, charge = components(data_ref, start)

        def total(part):
            terms = [
                rows_ref[pl.ds(base + 4 * level + part, 8, stride=stride), :] for level in range(3)
            ]
            return terms[0] + (terms[1] + terms[2])

        weight = total(3)
        scale = coulomb_scale * charge
        for part, comp in enumerate(comps):
            out_ref[pl.ds(4 * start + part, 8, stride=4), :] = scale * (comp * weight - total(part))
        out_ref[pl.ds(4 * start + 3, 8, stride=4), :] = zeros

    def finish_own(step, _):
        start = pl.multiple_of(step * 8, 8)
        for half in range(2):
            columns = None
            for index in range(4):
                at = pl.ds(pl.multiple_of((start + 4 * half + index) * 128, 128), 128)
                block = own_sum_ref[at, :]
                block = block + pltpu.roll(block, 64, 1)
                block = block + pltpu.roll(block, 32, 1)
                columns = block if index == 0 else jnp.where(quarter < index, columns, block)
            stage_ref[128 * half : 128 * half + 128, :] = columns.T
        finish(own_ref, own_out_ref, start, stage_ref, 0, 32)
        return 0

    def finish_other(source, step, _):
        start = pl.multiple_of(step * 8, 8)
        finish(
            other_refs[source],
            other_out_refs[source],
            start,
            other_sum_ref,
            (source * slots + start) * 16,
            16,
        )
        return 0

    lax.fori_loop(0, clusters // 8, finish_own, 0)
    for source in range(sources):
        lax.fori_loop(0, slots // 8, functools.partial(finish_other, source), 0)


def pair_forces(own_rows, other_rows, own, arrived, slots):
    clusters = own.shape[0] // 4
    others = slots * len(arrived)
    pairs = own_rows.shape[0]
    smem = pl.BlockSpec(memory_space=pltpu.SMEM)
    vmem = pl.BlockSpec(memory_space=pltpu.VMEM)
    return pl.pallas_call(
        pair_kernel,
        out_shape=(
            jax.ShapeDtypeStruct(own.shape, jnp.float32),
            *[jax.ShapeDtypeStruct((slots * 4, 128), jnp.float32)] * len(arrived),
        ),
        in_specs=[smem, smem, vmem] + [vmem] * len(arrived),
        out_specs=(vmem,) * (len(arrived) + 1),
        scratch_shapes=[
            pltpu.VMEM((clusters * 128, 128), jnp.bfloat16),
            pltpu.VMEM((others * 32, 128), jnp.bfloat16),
            pltpu.VMEM((clusters * 16, 128), jnp.bfloat16),
            pltpu.VMEM((others * 128, 128), jnp.bfloat16),
            pltpu.VMEM((clusters * 128, 128), jnp.float32),
            pltpu.VMEM((others * 16, 128), jnp.float32),
            pltpu.VMEM((384, 128), jnp.float32),
            *[pltpu.VMEM((UNROLL // QUAD, 128, 128 * QUAD), jnp.float32)] * 2,
            *[pltpu.VMEM((UNROLL // QUAD, 128 * QUAD, 256), jnp.bfloat16)] * 2,
        ],
        compiler_params=pltpu.CompilerParams(vmem_limit_bytes=46 * 1024 * 1024),
        cost_estimate=pl.CostEstimate(
            flops=pairs * 128 * 128 * 20, bytes_accessed=4 * 1024 * 1024, transcendentals=0
        ),
        name="pair_forces",
    )(own_rows, other_rows, own, *arrived)


def prepare_kernel(
    fill_ref,
    cell_ref,
    send_index_ref,
    send_count_ref,
    position_hbm,
    charge_hbm,
    ion_hbm,
    start_hbm,
    screen_hbm,
    own_ref,
    masked_ref,
    inverse_ref,
    source_ref,
    *refs,
):
    out_refs, scratch = (refs[:-8], refs[-8:])
    sum_ref, deposit_ref, position_ref, charge_ref, ion_ref, start_ref, screen_ref, sems = scratch
    copies = [
        pltpu.make_async_copy(source, target, sems.at[index])
        for index, (source, target) in enumerate(
            (
                (position_hbm, position_ref),
                (charge_hbm, charge_ref),
                (ion_hbm, ion_ref),
                (start_hbm, start_ref),
                (screen_hbm, screen_ref),
            )
        )
    ]
    for copy in copies:
        copy.start()
    deposit_ref[...] = jnp.zeros_like(deposit_ref)
    copies[0].wait()
    copies[1].wait()
    clusters = charge_ref.shape[0]
    cells_x, cells_y, _ = ion_ref.shape
    slots = send_index_ref.shape[1]
    lane = lax.broadcasted_iota(jnp.int32, (1, 128), 1)
    row = lax.broadcasted_iota(jnp.int32, (4, 128), 0)

    def collect(step, _):
        for turn in range(8):
            cluster = step * 8 + turn
            masked = jnp.where(lane < fill_ref[cluster], charge_ref[pl.ds(cluster, 1), :], 0.0)
            masked_ref[pl.ds(cluster, 1), :] = masked
            place = position_ref[:, pl.ds(pl.multiple_of(cluster * 128, 128), 128)]
            own_ref[cluster, 0:3, :] = place
            own_ref[cluster, 3:4, :] = masked
        at = pl.ds(pl.multiple_of(step * 8, 8), 8)
        total = jnp.sum(masked_ref[at, :], axis=1, keepdims=True)
        sum_ref[at, :] = jnp.broadcast_to(deposit_scale * total, (8, 128))
        return 0

    lax.fori_loop(0, clusters // 8, collect, 0)

    def fill_messages(step, _):
        for direction, out_ref in enumerate(out_refs):
            parts = []
            for turn in range(2):
                slot = step * 2 + turn
                live = jnp.where(slot < send_count_ref[0, direction], 1.0, 0.0)
                value = own_ref[send_index_ref[direction, slot]]
                parts.append(jnp.where(row == 3, value * live, value))
            out_ref[pl.ds(pl.multiple_of(step * 8, 8), 8), :] = jnp.concatenate(parts, axis=0)
        return 0

    lax.fori_loop(0, slots // 2, fill_messages, 0)

    def deposit(cluster, _):
        cell = cell_ref[cluster]
        index_x = lax.shift_right_logical(cell, CELL_BITS) // cells_y
        index_y = lax.shift_right_logical(cell, CELL_BITS) % cells_y
        index_z = lax.bitwise_and(cell, 255)
        half = lax.shift_right_logical(index_z, 7)
        added = jnp.where(
            lane == lax.bitwise_and(index_z, 127), sum_ref[pl.ds(cluster, 1), :], 0.0
        )
        deposit_ref[pl.ds((index_x * 2 + half) * cells_y + index_y, 1), :] += added
        return 0

    lax.fori_loop(0, clusters, deposit, 0, unroll=4)
    for copy in copies[2:]:
        copy.wait()
    inverse_ref[...] = 1.0 / (6.0 + screen_ref[...])
    for index in range(cells_x):
        for half in range(2):
            lanes = slice(128 * half, 128 * half + 128)
            first = (index * 2 + half) * cells_y
            source_ref[index, :, lanes] = (
                ion_ref[index, :, lanes] + deposit_ref[first : first + cells_y, :]
            ) * inverse_ref[index, :, lanes]
    for out_ref, after in ((out_refs[1], True), (out_refs[2], False)):
        for index in range(cells_x):
            base = slots * 4 + index * 32
            offset = 0
            for field_ref, width in zip(
                (start_ref, inverse_ref, source_ref, ion_ref), HALO_WIDTHS, strict=True
            ):
                first = cells_y - width if after else 0
                rows = field_ref[index, first : first + width, :]
                for half in range(2):
                    out_ref[base + 16 * half + offset : base + 16 * half + offset + width, :] = (
                        rows[:, 128 * half : 128 * half + 128]
                    )
                offset += width
            for half in range(2):
                out_ref[base + 16 * half + offset : base + 16 * half + 16, :] = jnp.zeros(
                    (16 - offset, 128), jnp.float32
                )


def prepare(fill, cell, send_index, send_count, positions, charges, ions, start, screen):
    clusters = charges.shape[0]
    directions, slots = send_index.shape
    cells_x = ions.shape[0]
    smem = pl.BlockSpec(memory_space=pltpu.SMEM)
    vmem = pl.BlockSpec(memory_space=pltpu.VMEM)
    rows = [slots * 4] * directions
    rows[1] = rows[2] = slots * 4 + cells_x * 32
    return pl.pallas_call(
        prepare_kernel,
        out_shape=(
            jax.ShapeDtypeStruct((clusters, 4, 128), jnp.float32),
            jax.ShapeDtypeStruct((clusters, 128), jnp.float32),
            jax.ShapeDtypeStruct(ions.shape, jnp.float32),
            jax.ShapeDtypeStruct(ions.shape, jnp.float32),
            *[jax.ShapeDtypeStruct((count, 128), jnp.float32) for count in rows],
        ),
        in_specs=[smem] * 4 + [pl.BlockSpec(memory_space=pltpu.HBM)] * 5,
        out_specs=(vmem,) * (4 + directions),
        scratch_shapes=[
            pltpu.VMEM((clusters, 128), jnp.float32),
            pltpu.VMEM((ions.size // 128, 128), jnp.float32),
            *[
                pltpu.VMEM(operand.shape, jnp.float32)
                for operand in (positions, charges, ions, start, screen)
            ],
            pltpu.SemaphoreType.DMA((5,)),
        ],
        compiler_params=pltpu.CompilerParams(vmem_limit_bytes=60 * 1024 * 1024),
        name="prepare",
    )(fill, cell, send_index, send_count, positions, charges, ions, start, screen)


def put_extended(target_ref, plane, field, field_ref, index, before_ref, after_ref, base):
    cells_y = field_ref.shape[1]
    width = HALO_WIDTHS[field]
    offset = sum(HALO_WIDTHS[:field])
    target_ref[plane, MARGIN : MARGIN + cells_y, :] = field_ref[index]
    for half in range(2):
        lanes = slice(128 * half, 128 * half + 128)
        first = base + index * 32 + 16 * half + offset
        target_ref[plane, MARGIN - width : MARGIN, lanes] = before_ref[first : first + width, :]
        target_ref[plane, MARGIN + cells_y : MARGIN + cells_y + width, lanes] = after_ref[
            first : first + width, :
        ]


def planes_kernel(base, *refs):
    field_refs, (before_ref, after_ref, down_ref, up_ref) = (refs[:4], refs[4:])
    cells_x = field_refs[0].shape[0]
    down_ref[...] = jnp.zeros_like(down_ref)
    up_ref[...] = jnp.zeros_like(up_ref)
    plane = 0
    for field, width in enumerate(HALO_WIDTHS):
        for index in range(width):
            for target_ref, source in ((down_ref, index), (up_ref, cells_x - width + index)):
                put_extended(
                    target_ref, plane, field, field_refs[field], source, before_ref, after_ref, base
                )
            plane += 1


def planes(fields, before, after, base):
    vmem = pl.BlockSpec(memory_space=pltpu.VMEM)
    _, cells_y, cells_z = fields[0].shape
    shape = jax.ShapeDtypeStruct((sum(HALO_WIDTHS), cells_y + 2 * MARGIN, cells_z), jnp.float32)
    return pl.pallas_call(
        functools.partial(planes_kernel, base),
        out_shape=(shape, shape),
        in_specs=[vmem] * 6,
        out_specs=(vmem, vmem),
        compiler_params=pltpu.CompilerParams(vmem_limit_bytes=32 * 1024 * 1024),
        name="planes",
    )(*fields, before, after)


def face_flux(pot_low, pot_high, ion_low, ion_high):
    speed = -mobility * (pot_high - pot_low)
    return (
        jnp.maximum(speed, 0.0) * ion_low
        + jnp.minimum(speed, 0.0) * ion_high
        - diffusion * (ion_high - ion_low)
    )


def grid_kernel(base, *refs):
    cell_ref, masked_ref = refs[:2]
    field_refs = refs[2:6]
    before_ref, after_ref, lower_ref, upper_ref = refs[6:10]
    potential_ref, next_ref, force_ref = refs[10:13]
    start_ref, inverse_ref, resid_ref, ion_ref, update_ref, line_ref, *pick_refs = refs[13:]
    cells_x, cells_y, cells_z = field_refs[0].shape
    rows = cells_y + 2 * MARGIN
    depth = HALO_WIDTHS[0]
    clusters = masked_ref.shape[0]
    lane = lax.broadcasted_iota(jnp.int32, (rows, cells_z), 1)
    middle = 0.5 * (highest_eig + lowest_eig)
    spread = 0.5 * (highest_eig - lowest_eig)

    plane = 0
    for field, target_ref in enumerate((start_ref, inverse_ref, resid_ref, ion_ref)):
        width = HALO_WIDTHS[field]
        if field == 0 or field == 3:
            target_ref[...] = jnp.zeros_like(target_ref)
        else:
            target_ref[depth : depth + cells_x, 0:MARGIN, :] = jnp.zeros(
                (cells_x, MARGIN, cells_z), jnp.float32
            )
            target_ref[depth : depth + cells_x, rows - MARGIN : rows, :] = jnp.zeros(
                (cells_x, MARGIN, cells_z), jnp.float32
            )
        for index in range(width):
            target_ref[depth - width + index] = lower_ref[plane + index]
            target_ref[depth + cells_x + index] = upper_ref[plane + index]
        for index in range(cells_x):
            put_extended(
                target_ref,
                depth + index,
                field,
                field_refs[field],
                index,
                before_ref,
                after_ref,
                base,
            )
        plane += width

    def above(value):
        return jnp.where(lane == cells_z - 1, 0.0, pltpu.roll(value, cells_z - 1, 1))

    def below(value):
        return jnp.where(lane == 0, 0.0, pltpu.roll(value, 1, 1))

    def beside(value):
        rolled = pltpu.roll(value, 1, 0) + pltpu.roll(value, rows - 1, 0)
        return rolled + (above(value) + below(value))

    def first_sweep(index, planes):
        last, here = planes
        after = start_ref[index + 1]
        resid = (
            resid_ref[index] - here + inverse_ref[index] * ((last + after) + beside(here))
        )
        resid_ref[index] = resid
        update_ref[index] = resid / middle
        return (here, after)

    lax.fori_loop(1, cells_x + 2 * depth - 1, first_sweep, (start_ref[0], start_ref[1]))

    ratio_ms = middle / spread
    weight_now = 1.0 / ratio_ms
    for turn in range(1, SWEEPS):
        weight_next = 1.0 / (2.0 * ratio_ms - weight_now)
        keep, gain = (weight_next * weight_now, 2.0 * weight_next / spread)
        weight_now = weight_next

        def sweep(index, planes, turn=turn, keep=keep, gain=gain):
            last, here = planes
            after = update_ref[index + 1]
            resid = resid_ref[index] - here + inverse_ref[index] * ((last + after) + beside(here))
            update = keep * here + gain * resid
            if turn == 1:
                start_ref[index] = start_ref[index] + here + update
            else:
                start_ref[index] = start_ref[index] + update
            if turn + 1 < SWEEPS:
                resid_ref[index] = resid
                update_ref[index] = update
            return (here, after)

        first = 1 + turn
        lax.fori_loop(
            first,
            cells_x + 2 * depth - first,
            sweep,
            (update_ref[first - 1], update_ref[first]),
        )

    def upper_flux(index):
        return face_flux(start_ref[index], start_ref[index + 1], ion_ref[index], ion_ref[index + 1])

    inner = slice(MARGIN, MARGIN + cells_y)

    def advance(index, lower):
        pot = start_ref[depth + index]
        ions = ion_ref[depth + index]
        upper = upper_flux(depth + index)
        along_y = face_flux(pot, pltpu.roll(pot, rows - 1, 0), ions, pltpu.roll(ions, rows - 1, 0))
        along_z = face_flux(pot, above(pot), ions, above(ions))
        first_z = face_flux(0.0, pot, 0.0, ions)
        total = upper - lower
        total = total + (along_y - pltpu.roll(along_y, 1, 0))
        total = total + (along_z - jnp.where(lane == 0, first_z, pltpu.roll(along_z, 1, 1)))
        next_ref[index] = (ions - time_step * total)[inner]
        potential_ref[index] = pot[inner]
        return upper

    lax.fori_loop(0, cells_x, advance, upper_flux(depth - 1))
    for index in range(cells_x + 2):
        for half in range(2):
            line_ref[pl.ds((index * 2 + half) * rows, rows), :] = start_ref[
                depth - 1 + index, :, 128 * half : 128 * half + 128
            ]

    row_lane = lax.broadcasted_iota(jnp.int32, (1, 128), 1)

    def pick(cluster, _):
        cell = cell_ref[cluster]
        index_x = lax.shift_right_logical(cell, CELL_BITS) // cells_y + 1
        index_y = lax.shift_right_logical(cell, CELL_BITS) % cells_y + MARGIN
        index_z = lax.bitwise_and(cell, 255)
        half = lax.shift_right_logical(index_z, 7)
        here = row_lane == lax.bitwise_and(index_z, 127)

        def line(plane, row, part):
            return line_ref[pl.ds((plane * 2 + part) * rows + row, 1), :]

        along_x = line(index_x - 1, index_y, half) - line(index_x + 1, index_y, half)
        along_y = line(index_x, index_y - 1, half) - line(index_x, index_y + 1, half)
        along_z = jnp.zeros((1, 128), jnp.float32)
        for part in range(cells_z // 128):
            value = line(index_x, index_y, part)
            place = row_lane + 128 * part
            along_z = along_z + jnp.where(place == index_z - 1, value, 0.0)
            along_z = along_z - jnp.where(place == index_z + 1, value, 0.0)
        at = pl.ds(cluster, 1)
        pick_refs[0][at, :] = jnp.where(here, along_x, 0.0)
        pick_refs[1][at, :] = jnp.where(here, along_y, 0.0)
        pick_refs[2][at, :] = along_z
        return 0

    lax.fori_loop(0, clusters, pick, 0, unroll=4)

    def spread_out(step, _):
        start = pl.multiple_of(step * 8, 8)
        charge = masked_ref[pl.ds(start, 8), :] * (0.5 * field_scale)
        for part, pick_ref in enumerate(pick_refs):
            total = jnp.sum(pick_ref[pl.ds(start, 8), :], axis=1, keepdims=True)
            force_ref[pl.ds(4 * start + part, 8, stride=4), :] = charge * total
        force_ref[pl.ds(4 * start + 3, 8, stride=4), :] = jnp.zeros((8, 128), jnp.float32)
        return 0

    lax.fori_loop(0, clusters // 8, spread_out, 0)


def grid_step(cell, masked, fields, before, after, lower, upper, base):
    smem = pl.BlockSpec(memory_space=pltpu.SMEM)
    vmem = pl.BlockSpec(memory_space=pltpu.VMEM)
    clusters = masked.shape[0]
    cells_x, cells_y, cells_z = fields[0].shape
    block = (cells_x + 2 * HALO_WIDTHS[0], cells_y + 2 * MARGIN, cells_z)
    return pl.pallas_call(
        functools.partial(grid_kernel, base),
        out_shape=(
            jax.ShapeDtypeStruct(fields[0].shape, jnp.float32),
            jax.ShapeDtypeStruct(fields[0].shape, jnp.float32),
            jax.ShapeDtypeStruct((clusters * 4, 128), jnp.float32),
        ),
        in_specs=[smem] + [vmem] * 9,
        out_specs=(vmem,) * 3,
        scratch_shapes=[pltpu.VMEM(block, jnp.float32)] * 5
        + [pltpu.VMEM(((cells_x + 2) * 2 * block[1], 128), jnp.float32)]
        + [pltpu.VMEM((clusters, 128), jnp.float32)] * 3,
        compiler_params=pltpu.CompilerParams(vmem_limit_bytes=40 * 1024 * 1024),
        cost_estimate=pl.CostEstimate(
            flops=block[0] * block[1] * block[2] * 100, bytes_accessed=8 << 20, transcendentals=0
        ),
        name="grid_step",
    )(cell, masked, *fields, before, after, lower, upper)


def gather_forces_kernel(send_index_ref, own_ref, field_ref, *refs):
    back_refs, (out_ref, sum_ref) = (refs[:-2], refs[-2:])
    clusters = own_ref.shape[0]
    slots = send_index_ref.shape[1]
    sum_ref[...] = own_ref[...] + field_ref[...]

    def visit(slot, _):
        for direction, back_ref in enumerate(back_refs):
            cluster = send_index_ref[direction, slot]
            sum_ref[cluster] += back_ref[slot]
        return 0

    lax.fori_loop(0, slots, visit, 0)

    def write(step, _):
        for turn in range(8):
            cluster = step * 8 + turn
            out_ref[:, pl.ds(pl.multiple_of(cluster * 128, 128), 128)] = sum_ref[cluster][0:3]
        return 0

    lax.fori_loop(0, clusters // 8, write, 0)


def gather_forces(send_index, own, field, backs):
    smem = pl.BlockSpec(memory_space=pltpu.SMEM)
    vmem = pl.BlockSpec(memory_space=pltpu.VMEM)
    clusters = own.shape[0]
    return pl.pallas_call(
        gather_forces_kernel,
        out_shape=jax.ShapeDtypeStruct((3, clusters * 128), jnp.float32),
        in_specs=[smem] + [vmem] * (2 + len(backs)),
        out_specs=vmem,
        scratch_shapes=[pltpu.VMEM(own.shape, jnp.float32)],
        compiler_params=pltpu.CompilerParams(vmem_limit_bytes=32 * 1024 * 1024),
        name="gather_forces",
    )(send_index, own, field, *backs)


def passed_along(shard, axis, by):
    devices = lax.axis_size(axis)
    pairs = [(i, i + by) for i in range(devices) if 0 <= i + by < devices]
    return lax.ppermute(shard, axis, pairs)


ROUTES = (("brick", 1), ("brick", -1), ("brick", 2), ("brick", -2), ("grp", 1), ("grp", -1))


def shards(
    positions,
    charges,
    cluster_fill,
    cluster_cell,
    send_index,
    send_count,
    pair_local,
    pair_dir,
    pair_slot,
    ion_density,
    potential_prev,
    screening,
):
    clusters = cluster_fill.shape[0]
    psize = charges.shape[0] // clusters
    slots = send_index.shape[1]
    base = slots * 4
    own, masked, inverse, source, local, *messages = prepare(
        cluster_fill,
        cluster_cell,
        send_index,
        send_count,
        positions,
        charges.reshape(clusters, psize),
        ion_density,
        potential_prev,
        screening,
    )
    arrived = [local] + [
        passed_along(message, axis, by)
        for message, (axis, by) in zip(messages, ROUTES, strict=True)
    ]
    fields = (potential_prev, inverse, source, ion_density)
    arrived = lax.optimization_barrier(arrived)
    before, after = arrived[1:3]
    down, up = planes(fields, before, after, base)
    lower = passed_along(up, "grp", 1)
    upper = passed_along(down, "grp", -1)
    own_force, *reactions = pair_forces(
        pair_local,
        pair_dir * slots + pair_slot,
        own.reshape(clusters * 4, psize),
        arrived,
        slots,
    )
    backs = [reactions[0]] + [
        passed_along(reaction, axis, -by)
        for reaction, (axis, by) in zip(reactions[1:], ROUTES, strict=True)
    ]
    potential, ion_next, field_force = grid_step(
        cluster_cell, masked, fields, before, after, lower, upper, base
    )
    forces = gather_forces(
        send_index,
        own_force.reshape(clusters, 4, psize),
        field_force.reshape(clusters, 4, psize),
        [back.reshape(slots, 4, psize) for back in backs],
    )
    return (forces, potential, ion_next)


def solution(mesh):
    in_specs = (
        P(None, ("grp", "brick")),
        P(("grp", "brick")),
        P(("grp", "brick")),
        P(("grp", "brick")),
        P(("grp", "brick"), None),
        P(("grp", "brick"), None),
        P(("grp", "brick")),
        P(("grp", "brick")),
        P(("grp", "brick")),
        P("grp", "brick", None),
        P("grp", "brick", None),
        P("grp", "brick", None),
    )
    out_specs = (P(None, ("grp", "brick")), P("grp", "brick", None), P("grp", "brick", None))
    return jax.shard_map(shards, mesh=mesh, in_specs=in_specs, out_specs=out_specs, check_vma=False)
```

```python
import functools

import jax
import jax.numpy as jnp
import numpy as np
from jax import lax
from jax.experimental import pallas as pl
from jax.experimental.pallas import tpu as pltpu
from jax.sharding import PartitionSpec as P

SWEEPS = 4
QUAD = 4
UNROLL = 8
HALO_WIDTHS = (SWEEPS + 1, SWEEPS, SWEEPS, 1)
MARGIN = 8
CELL_BITS = 8


coulomb_scale = 0.02
softening = 0.1
field_scale = 0.5
deposit_scale = 0.2
lowest_eig = 0.01
highest_eig = 1.99
mobility = 0.3
diffusion = 0.2
time_step = 0.2


def split3(value):
    first = value.astype(jnp.bfloat16).astype(jnp.float32)
    rest = value - first
    second = rest.astype(jnp.bfloat16).astype(jnp.float32)
    third = (rest - second).astype(jnp.bfloat16).astype(jnp.float32)
    return (first, second, third)


def moment_pieces(comps, charge):
    rows = [None] * 12
    for part, charged in enumerate((*comps, None)):
        for level, piece in enumerate(split3(charge if charged is None else charge * charged)):
            rows[4 * level + part] = piece
    return rows


def selections():
    near_kinds, far_kinds = ([], [])
    for part in range(3):
        near_kinds += [3 * part + level for level in (0, 0, 0, 1, 1, 2)]
        far_kinds += [3 * part + level for level in (0, 1, 2, 0, 1, 0)]
    near_kinds += [9, 10, 11, 12, 12, 12]
    far_kinds += [12, 12, 12, 9, 10, 11]
    near = np.zeros((128, 256), np.float32)
    far = np.zeros((256, 128), np.float32)
    own_moment = np.zeros((128, 128), np.float32)
    other_moment = np.zeros((128, QUAD * 256), np.float32)
    for cluster in range(8):
        for index, kind in enumerate(near_kinds):
            near[kind * 8 + cluster, cluster * 32 + index] = 1.0
        for index, kind in enumerate(far_kinds):
            far[cluster * 32 + index, kind * 8 + cluster] = 1.0
        for kind in range(12):
            own_moment[cluster * 16 + kind, kind * 8 + cluster] = 1.0
            for turn in range(QUAD):
                lane = (cluster % QUAD + turn) % QUAD * 32 + kind
                column = turn * 256 + cluster // QUAD * 128 + lane
                other_moment[kind * 8 + cluster, column] = 1.0
    return tuple(jnp.asarray(part, jnp.bfloat16) for part in (near, far, own_moment, other_moment))


def pair_kernel(own_rows_ref, other_rows_ref, *refs):
    near_sel_ref, far_sel_ref, own_moment_sel_ref, other_moment_sel_ref, own_ref = refs[:5]
    refs = refs[5:]
    sources = (len(refs) - 11) // 2
    other_refs = refs[:sources]
    own_out_ref = refs[sources]
    other_out_refs = refs[sources + 1 : 2 * sources + 1]
    (
        near_ref,
        far_ref,
        own_moment_ref,
        other_moment_ref,
        own_sum_ref,
        other_sum_ref,
        *passed_refs,
    ) = refs[2 * sources + 1 :]
    clusters = own_ref.shape[0] // 4
    slots = other_out_refs[0].shape[0] // 4
    others = slots * sources
    groups = own_rows_ref.shape[0] // UNROLL
    units = UNROLL // QUAD
    groups_of_other = others // QUAD
    ones = jnp.ones((8, 128), jnp.float32)
    zeros = jnp.zeros((8, 128), jnp.float32)

    def components(data_ref, start):
        return [data_ref[pl.ds(4 * start + part, 8, stride=4), :] for part in range(4)]

    def place_pieces(comps, factor, offset):
        pieces = []
        square = zeros
        for comp in comps:
            square = square + comp * comp
            pieces += split3(factor * comp)
        pieces += [*split3(square + offset), ones]
        return jnp.concatenate(pieces + [zeros] * (16 - len(pieces)), axis=0)

    def selected(left, right):
        return jnp.dot(
            left.astype(jnp.bfloat16), right, preferred_element_type=jnp.float32
        ).astype(jnp.bfloat16)

    def near_rows(step, _):
        start = pl.multiple_of(step * 8, 8)
        *comps, charge = components(own_ref, start)
        moments = jnp.concatenate(moment_pieces(comps, charge) + [zeros] * 4, axis=0)
        own_moment_ref[pl.ds(pl.multiple_of(start * 16, 128), 128), :] = selected(
            own_moment_sel_ref[...], moments.astype(jnp.bfloat16)
        )
        tiles = selected(place_pieces(comps, 1.0, 0.0).T, near_sel_ref[...])
        for half in range(2):
            at = pl.ds(pl.multiple_of(step * 256 + half * 128, 128), 128)
            near_ref[at, :] = tiles[:, 128 * half : 128 * half + 128]
        return 0

    def far_rows(source, step, _):
        local = pl.multiple_of(step * 8, 8)
        start = source * slots + local
        *comps, charge = components(other_refs[source], local)
        rows = selected(far_sel_ref[...], place_pieces(comps, -2.0, softening).astype(jnp.bfloat16))
        for index in range(8):
            at = pl.multiple_of((start + index) * 128, 128)
            far_ref[pl.ds(at, 96), :] = jnp.zeros((96, 128), jnp.bfloat16)
            far_ref[pl.ds(at + 96, 32), :] = rows[32 * index : 32 * index + 32]
        moments = jnp.concatenate(moment_pieces(comps, charge) + [zeros] * 4, axis=0)
        tiles = selected(moments.T, other_moment_sel_ref[...])
        for turn in range(QUAD):
            for half in range(2):
                group = turn * groups_of_other + source * (slots // QUAD) + step * 2 + half
                column = 256 * turn + 128 * half
                other_moment_ref[pl.ds(pl.multiple_of(group * 128, 128), 128), :] = tiles[
                    :, column : column + 128
                ]
        return 0

    lax.fori_loop(0, clusters // 8, near_rows, 0, unroll=2)
    for source in range(sources):
        lax.fori_loop(0, slots // 8, functools.partial(far_rows, source), 0, unroll=2)
    far_ref[pl.ds(others * 128, 128), :] = jnp.zeros((128, 128), jnp.bfloat16)
    own_sum_ref[...] = jnp.zeros_like(own_sum_ref)
    other_sum_ref[...] = jnp.zeros_like(other_sum_ref)
    dist_refs, weight_refs = (passed_refs[:2], passed_refs[2:])
    dist_refs[0][...] = jnp.full(dist_refs[0].shape, 1e38, jnp.float32)
    weight_refs[0][...] = jnp.zeros_like(weight_refs[0])

    quarter_row = lax.shift_right_logical(lax.broadcasted_iota(jnp.int32, (1, 128), 1), 5)
    masks = [jnp.where(quarter_row == turn, 1.0, 0.0).astype(jnp.bfloat16) for turn in range(QUAD)]

    def block_diagonal(blocks):
        blank = jnp.zeros_like(blocks[0])
        lines = [
            jnp.concatenate(
                [block if turn == at else blank for turn in range(len(blocks))], axis=1
            )
            for at, block in enumerate(blocks)
        ]
        return jnp.concatenate(lines, axis=0)

    def distances(pair, unit, dist_ref):
        for couple in range(QUAD // 2):
            near, far = ([], [])
            for turn in range(2):
                own = own_rows_ref[pair + 2 * couple + turn]
                other = other_rows_ref[pair + 2 * couple + turn]
                tile = pl.multiple_of(lax.shift_right_logical(own, 2) * 128, 128)
                near.append(near_ref[pl.ds(tile, 128), :])
                first = pl.multiple_of(other * 128 + 96 - lax.bitwise_and(own, 3) * 32, 32)
                far.append(far_ref[pl.ds(first, 128), :])
            dist_ref[unit, :, 256 * couple : 256 * couple + 256] = jnp.dot(
                jnp.concatenate(near, axis=1),
                block_diagonal(far),
                preferred_element_type=jnp.float32,
            )

    def weights(unit, turn, dist_ref, weight_ref):
        root = lax.rsqrt(dist_ref[unit, :, 128 * turn : 128 * turn + 128])
        weight = root * root * root
        high = weight.astype(jnp.bfloat16)
        weight_ref[unit, 128 * turn : 128 * turn + 128, :128] = high
        weight_ref[unit, 128 * turn : 128 * turn + 128, 128:] = (
            weight - high.astype(jnp.float32)
        ).astype(jnp.bfloat16)

    def turned(index, turn):
        rotation = lax.bitwise_and(turn - index, 3)
        group = rotation * groups_of_other + lax.shift_right_logical(index, 2)
        return other_moment_ref[pl.ds(pl.multiple_of(group * 128, 128), 128), :] * masks[turn]

    def products(pair, unit, weight_ref):
        owns = [own_rows_ref[pair + turn] for turn in range(QUAD)]
        others = [other_rows_ref[pair + turn] for turn in range(QUAD)]
        both = weight_ref[unit]
        levels = [
            jnp.concatenate(
                [both[128 * turn : 128 * turn + 128, lanes] for turn in range(QUAD)], axis=1
            )
            for lanes in (slice(0, 128), slice(128, 256))
        ]
        columns = jnp.concatenate([turned(others[turn], turn) for turn in range(QUAD)], axis=0)
        to_own = jnp.dot(
            jnp.concatenate(levels, axis=0), columns, preferred_element_type=jnp.float32
        )
        rows = block_diagonal(
            [own_moment_ref[pl.ds(pl.multiple_of(own * 16, 16), 16), :] for own in owns]
        )
        to_other = jnp.dot(rows, both, preferred_element_type=jnp.float32)
        return (
            owns,
            others,
            (to_own[:128] + to_own[128:]).T,
            to_other[:, :128] + to_other[:, 128:],
        )

    def half_step(step, side):
        last = jnp.maximum(step - 2, 0) * UNROLL
        first = jnp.minimum(step, groups - 1) * UNROLL
        results = [products(last + QUAD * unit, unit, weight_refs[side]) for unit in range(units)]
        for unit in range(units):
            for turn in range(QUAD):
                weights(unit, turn, dist_refs[side], weight_refs[1 - side])
        for unit in range(units):
            distances(first + QUAD * unit, unit, dist_refs[1 - side])
        for owns, others, to_own, to_other in results:
            for turn in range(QUAD):
                own_at = pl.ds(pl.multiple_of(owns[turn] * 16, 16), 16)
                other_at = pl.ds(pl.multiple_of(others[turn] * 16, 16), 16)
                own_sum_ref[own_at, :] += to_own[32 * turn : 32 * turn + 16]
                other_sum_ref[other_at, :] += to_other[16 * turn : 16 * turn + 16]

    def visit(step, _):
        for side in range(2):
            half_step(step * 2 + side, side)
        return 0

    lax.fori_loop(0, (groups + 2) // 2, visit, 0)

    def finish(data_ref, out_ref, sum_ref, base, step, _):
        start = pl.multiple_of(step * 8, 8)
        *comps, charge = components(data_ref, start)

        def total(part):
            terms = [
                sum_ref[pl.ds(base + start * 16 + 4 * level + part, 8, stride=16), :]
                for level in range(3)
            ]
            return terms[0] + (terms[1] + terms[2])

        weight = total(3)
        scale = coulomb_scale * charge
        for part, comp in enumerate(comps):
            out_ref[pl.ds(4 * start + part, 8, stride=4), :] = scale * (comp * weight - total(part))
        out_ref[pl.ds(4 * start + 3, 8, stride=4), :] = zeros
        return 0

    lax.fori_loop(
        0, clusters // 8, functools.partial(finish, own_ref, own_out_ref, own_sum_ref, 0), 0
    )
    for source in range(sources):
        body = functools.partial(
            finish,
            other_refs[source],
            other_out_refs[source],
            other_sum_ref,
            source * slots * 16,
        )
        lax.fori_loop(0, slots // 8, body, 0)


def pair_forces(own_rows, other_rows, own, arrived, slots):
    clusters = own.shape[0] // 4
    others = slots * len(arrived)
    pairs = own_rows.shape[0]
    smem = pl.BlockSpec(memory_space=pltpu.SMEM)
    vmem = pl.BlockSpec(memory_space=pltpu.VMEM)
    return pl.pallas_call(
        pair_kernel,
        out_shape=(
            jax.ShapeDtypeStruct(own.shape, jnp.float32),
            *[jax.ShapeDtypeStruct((slots * 4, 128), jnp.float32)] * len(arrived),
        ),
        in_specs=[smem, smem] + [vmem] * (5 + len(arrived)),
        out_specs=(vmem,) * (len(arrived) + 1),
        scratch_shapes=[
            pltpu.VMEM((clusters * 32, 128), jnp.bfloat16),
            pltpu.VMEM(((others + 1) * 128, 128), jnp.bfloat16),
            pltpu.VMEM((clusters * 16, 128), jnp.bfloat16),
            pltpu.VMEM((others * 128, 128), jnp.bfloat16),
            pltpu.VMEM((clusters * 16, 128), jnp.float32),
            pltpu.VMEM((others * 16, 128), jnp.float32),
            *[pltpu.VMEM((UNROLL // QUAD, 128, 128 * QUAD), jnp.float32)] * 2,
            *[pltpu.VMEM((UNROLL // QUAD, 128 * QUAD, 256), jnp.bfloat16)] * 2,
        ],
        compiler_params=pltpu.CompilerParams(vmem_limit_bytes=40 * 1024 * 1024),
        cost_estimate=pl.CostEstimate(
            flops=pairs * 128 * 128 * 20, bytes_accessed=4 * 1024 * 1024, transcendentals=0
        ),
        name="pair_forces",
    )(own_rows, other_rows, *selections(), own, *arrived)


def prepare_kernel(
    fill_ref,
    cell_ref,
    send_index_ref,
    send_count_ref,
    position_hbm,
    charge_hbm,
    ion_hbm,
    start_hbm,
    screen_hbm,
    own_ref,
    masked_ref,
    inverse_ref,
    source_ref,
    *refs,
):
    out_refs, scratch = (refs[:-8], refs[-8:])
    sum_ref, deposit_ref, position_ref, charge_ref, ion_ref, start_ref, screen_ref, sems = scratch
    copies = [
        pltpu.make_async_copy(source, target, sems.at[index])
        for index, (source, target) in enumerate(
            (
                (position_hbm, position_ref),
                (charge_hbm, charge_ref),
                (ion_hbm, ion_ref),
                (start_hbm, start_ref),
                (screen_hbm, screen_ref),
            )
        )
    ]
    for copy in copies:
        copy.start()
    deposit_ref[...] = jnp.zeros_like(deposit_ref)
    copies[0].wait()
    copies[1].wait()
    clusters = charge_ref.shape[0]
    cells_x, cells_y, _ = ion_ref.shape
    slots = send_index_ref.shape[1]
    lane = lax.broadcasted_iota(jnp.int32, (1, 128), 1)
    row = lax.broadcasted_iota(jnp.int32, (4, 128), 0)

    def collect(step, _):
        for turn in range(8):
            cluster = step * 8 + turn
            masked = jnp.where(lane < fill_ref[cluster], charge_ref[pl.ds(cluster, 1), :], 0.0)
            masked_ref[pl.ds(cluster, 1), :] = masked
            place = position_ref[:, pl.ds(pl.multiple_of(cluster * 128, 128), 128)]
            own_ref[cluster, 0:3, :] = place
            own_ref[cluster, 3:4, :] = masked
        at = pl.ds(pl.multiple_of(step * 8, 8), 8)
        total = jnp.sum(masked_ref[at, :], axis=1, keepdims=True)
        sum_ref[at, :] = jnp.broadcast_to(deposit_scale * total, (8, 128))
        return 0

    lax.fori_loop(0, clusters // 8, collect, 0)

    def fill_messages(step, _):
        for direction, out_ref in enumerate(out_refs):
            parts = []
            for turn in range(2):
                slot = step * 2 + turn
                live = jnp.where(slot < send_count_ref[0, direction], 1.0, 0.0)
                value = own_ref[send_index_ref[direction, slot]]
                parts.append(jnp.where(row == 3, value * live, value))
            out_ref[pl.ds(pl.multiple_of(step * 8, 8), 8), :] = jnp.concatenate(parts, axis=0)
        return 0

    lax.fori_loop(0, slots // 2, fill_messages, 0)

    def deposit(cluster, _):
        cell = cell_ref[cluster]
        index_x = lax.shift_right_logical(cell, CELL_BITS) // cells_y
        index_y = lax.shift_right_logical(cell, CELL_BITS) % cells_y
        index_z = lax.bitwise_and(cell, 255)
        half = lax.shift_right_logical(index_z, 7)
        added = jnp.where(
            lane == lax.bitwise_and(index_z, 127), sum_ref[pl.ds(cluster, 1), :], 0.0
        )
        deposit_ref[pl.ds((index_x * 2 + half) * cells_y + index_y, 1), :] += added
        return 0

    lax.fori_loop(0, clusters, deposit, 0, unroll=4)
    for copy in copies[2:]:
        copy.wait()
    inverse_ref[...] = 1.0 / (6.0 + screen_ref[...])
    for index in range(cells_x):
        for half in range(2):
            lanes = slice(128 * half, 128 * half + 128)
            first = (index * 2 + half) * cells_y
            source_ref[index, :, lanes] = (
                ion_ref[index, :, lanes] + deposit_ref[first : first + cells_y, :]
            ) * inverse_ref[index, :, lanes]
    for out_ref, after in ((out_refs[1], True), (out_refs[2], False)):
        for index in range(cells_x):
            base = slots * 4 + index * 32
            offset = 0
            for field_ref, width in zip(
                (start_ref, inverse_ref, source_ref, ion_ref), HALO_WIDTHS, strict=True
            ):
                first = cells_y - width if after else 0
                rows = field_ref[index, first : first + width, :]
                for half in range(2):
                    out_ref[base + 16 * half + offset : base + 16 * half + offset + width, :] = (
                        rows[:, 128 * half : 128 * half + 128]
                    )
                offset += width
            for half in range(2):
                out_ref[base + 16 * half + offset : base + 16 * half + 16, :] = jnp.zeros(
                    (16 - offset, 128), jnp.float32
                )


def prepare(fill, cell, send_index, send_count, positions, charges, ions, start, screen):
    clusters = charges.shape[0]
    directions, slots = send_index.shape
    cells_x = ions.shape[0]
    smem = pl.BlockSpec(memory_space=pltpu.SMEM)
    vmem = pl.BlockSpec(memory_space=pltpu.VMEM)
    rows = [slots * 4] * directions
    rows[1] = rows[2] = slots * 4 + cells_x * 32
    return pl.pallas_call(
        prepare_kernel,
        out_shape=(
            jax.ShapeDtypeStruct((clusters, 4, 128), jnp.float32),
            jax.ShapeDtypeStruct((clusters, 128), jnp.float32),
            jax.ShapeDtypeStruct(ions.shape, jnp.float32),
            jax.ShapeDtypeStruct(ions.shape, jnp.float32),
            *[jax.ShapeDtypeStruct((count, 128), jnp.float32) for count in rows],
        ),
        in_specs=[smem] * 4 + [pl.BlockSpec(memory_space=pltpu.HBM)] * 5,
        out_specs=(vmem,) * (4 + directions),
        scratch_shapes=[
            pltpu.VMEM((clusters, 128), jnp.float32),
            pltpu.VMEM((ions.size // 128, 128), jnp.float32),
            *[
                pltpu.VMEM(operand.shape, jnp.float32)
                for operand in (positions, charges, ions, start, screen)
            ],
            pltpu.SemaphoreType.DMA((5,)),
        ],
        compiler_params=pltpu.CompilerParams(vmem_limit_bytes=60 * 1024 * 1024),
        name="prepare",
    )(fill, cell, send_index, send_count, positions, charges, ions, start, screen)


def put_extended(target_ref, plane, field, field_ref, index, before_ref, after_ref, base):
    cells_y = field_ref.shape[1]
    width = HALO_WIDTHS[field]
    offset = sum(HALO_WIDTHS[:field])
    target_ref[plane, MARGIN : MARGIN + cells_y, :] = field_ref[index]
    for half in range(2):
        lanes = slice(128 * half, 128 * half + 128)
        first = base + index * 32 + 16 * half + offset
        target_ref[plane, MARGIN - width : MARGIN, lanes] = before_ref[first : first + width, :]
        target_ref[plane, MARGIN + cells_y : MARGIN + cells_y + width, lanes] = after_ref[
            first : first + width, :
        ]


def planes_kernel(base, *refs):
    field_refs, (before_ref, after_ref, down_ref, up_ref) = (refs[:4], refs[4:])
    cells_x = field_refs[0].shape[0]
    down_ref[...] = jnp.zeros_like(down_ref)
    up_ref[...] = jnp.zeros_like(up_ref)
    plane = 0
    for field, width in enumerate(HALO_WIDTHS):
        for index in range(width):
            for target_ref, source in ((down_ref, index), (up_ref, cells_x - width + index)):
                put_extended(
                    target_ref, plane, field, field_refs[field], source, before_ref, after_ref, base
                )
            plane += 1


def planes(fields, before, after, base):
    vmem = pl.BlockSpec(memory_space=pltpu.VMEM)
    _, cells_y, cells_z = fields[0].shape
    shape = jax.ShapeDtypeStruct((sum(HALO_WIDTHS), cells_y + 2 * MARGIN, cells_z), jnp.float32)
    return pl.pallas_call(
        functools.partial(planes_kernel, base),
        out_shape=(shape, shape),
        in_specs=[vmem] * 6,
        out_specs=(vmem, vmem),
        compiler_params=pltpu.CompilerParams(vmem_limit_bytes=32 * 1024 * 1024),
        name="planes",
    )(*fields, before, after)


def face_flux(pot_low, pot_high, ion_low, ion_high):
    speed = -mobility * (pot_high - pot_low)
    return (
        jnp.maximum(speed, 0.0) * ion_low
        + jnp.minimum(speed, 0.0) * ion_high
        - diffusion * (ion_high - ion_low)
    )


def grid_kernel(base, *refs):
    cell_ref, masked_ref = refs[:2]
    field_refs = refs[2:6]
    before_ref, after_ref, lower_ref, upper_ref = refs[6:10]
    potential_ref, next_ref, force_ref = refs[10:13]
    start_ref, inverse_ref, resid_ref, ion_ref, update_ref, line_ref, *pick_refs = refs[13:]
    cells_x, cells_y, cells_z = field_refs[0].shape
    rows = cells_y + 2 * MARGIN
    depth = HALO_WIDTHS[0]
    clusters = masked_ref.shape[0]
    lane = lax.broadcasted_iota(jnp.int32, (rows, cells_z), 1)
    middle = 0.5 * (highest_eig + lowest_eig)
    spread = 0.5 * (highest_eig - lowest_eig)

    plane = 0
    for field, target_ref in enumerate((start_ref, inverse_ref, resid_ref, ion_ref)):
        width = HALO_WIDTHS[field]
        if field == 0 or field == 3:
            target_ref[...] = jnp.zeros_like(target_ref)
        else:
            target_ref[depth : depth + cells_x, 0:MARGIN, :] = jnp.zeros(
                (cells_x, MARGIN, cells_z), jnp.float32
            )
            target_ref[depth : depth + cells_x, rows - MARGIN : rows, :] = jnp.zeros(
                (cells_x, MARGIN, cells_z), jnp.float32
            )
        for index in range(width):
            target_ref[depth - width + index] = lower_ref[plane + index]
            target_ref[depth + cells_x + index] = upper_ref[plane + index]
        for index in range(cells_x):
            put_extended(
                target_ref,
                depth + index,
                field,
                field_refs[field],
                index,
                before_ref,
                after_ref,
                base,
            )
        plane += width

    def above(value):
        return jnp.where(lane == cells_z - 1, 0.0, pltpu.roll(value, cells_z - 1, 1))

    def below(value):
        return jnp.where(lane == 0, 0.0, pltpu.roll(value, 1, 1))

    def beside(value):
        rolled = pltpu.roll(value, 1, 0) + pltpu.roll(value, rows - 1, 0)
        return rolled + (above(value) + below(value))

    def first_sweep(index, planes):
        last, here = planes
        after = start_ref[index + 1]
        resid = (
            resid_ref[index] - here + inverse_ref[index] * ((last + after) + beside(here))
        )
        resid_ref[index] = resid
        update_ref[index] = resid / middle
        return (here, after)

    lax.fori_loop(1, cells_x + 2 * depth - 1, first_sweep, (start_ref[0], start_ref[1]))

    ratio_ms = middle / spread
    weight_now = 1.0 / ratio_ms
    for turn in range(1, SWEEPS):
        weight_next = 1.0 / (2.0 * ratio_ms - weight_now)
        keep, gain = (weight_next * weight_now, 2.0 * weight_next / spread)
        weight_now = weight_next

        def sweep(index, planes, turn=turn, keep=keep, gain=gain):
            last, here = planes
            after = update_ref[index + 1]
            resid = resid_ref[index] - here + inverse_ref[index] * ((last + after) + beside(here))
            update = keep * here + gain * resid
            if turn == 1:
                start_ref[index] = start_ref[index] + here + update
            else:
                start_ref[index] = start_ref[index] + update
            if turn + 1 < SWEEPS:
                resid_ref[index] = resid
                update_ref[index] = update
            return (here, after)

        first = 1 + turn
        lax.fori_loop(
            first,
            cells_x + 2 * depth - first,
            sweep,
            (update_ref[first - 1], update_ref[first]),
        )

    def upper_flux(index):
        return face_flux(start_ref[index], start_ref[index + 1], ion_ref[index], ion_ref[index + 1])

    inner = slice(MARGIN, MARGIN + cells_y)

    def advance(index, lower):
        pot = start_ref[depth + index]
        ions = ion_ref[depth + index]
        upper = upper_flux(depth + index)
        along_y = face_flux(pot, pltpu.roll(pot, rows - 1, 0), ions, pltpu.roll(ions, rows - 1, 0))
        along_z = face_flux(pot, above(pot), ions, above(ions))
        first_z = face_flux(0.0, pot, 0.0, ions)
        total = upper - lower
        total = total + (along_y - pltpu.roll(along_y, 1, 0))
        total = total + (along_z - jnp.where(lane == 0, first_z, pltpu.roll(along_z, 1, 1)))
        next_ref[index] = (ions - time_step * total)[inner]
        potential_ref[index] = pot[inner]
        return upper

    lax.fori_loop(0, cells_x, advance, upper_flux(depth - 1))
    for index in range(cells_x + 2):
        for half in range(2):
            line_ref[pl.ds((index * 2 + half) * rows, rows), :] = start_ref[
                depth - 1 + index, :, 128 * half : 128 * half + 128
            ]

    row_lane = lax.broadcasted_iota(jnp.int32, (1, 128), 1)

    def pick(cluster, _):
        cell = cell_ref[cluster]
        index_x = lax.shift_right_logical(cell, CELL_BITS) // cells_y + 1
        index_y = lax.shift_right_logical(cell, CELL_BITS) % cells_y + MARGIN
        index_z = lax.bitwise_and(cell, 255)
        half = lax.shift_right_logical(index_z, 7)
        here = row_lane == lax.bitwise_and(index_z, 127)

        def line(plane, row, part):
            return line_ref[pl.ds((plane * 2 + part) * rows + row, 1), :]

        along_x = line(index_x - 1, index_y, half) - line(index_x + 1, index_y, half)
        along_y = line(index_x, index_y - 1, half) - line(index_x, index_y + 1, half)
        along_z = jnp.zeros((1, 128), jnp.float32)
        for part in range(cells_z // 128):
            value = line(index_x, index_y, part)
            place = row_lane + 128 * part
            along_z = along_z + jnp.where(place == index_z - 1, value, 0.0)
            along_z = along_z - jnp.where(place == index_z + 1, value, 0.0)
        at = pl.ds(cluster, 1)
        pick_refs[0][at, :] = jnp.where(here, along_x, 0.0)
        pick_refs[1][at, :] = jnp.where(here, along_y, 0.0)
        pick_refs[2][at, :] = along_z
        return 0

    lax.fori_loop(0, clusters, pick, 0, unroll=4)

    def spread_out(step, _):
        start = pl.multiple_of(step * 8, 8)
        charge = masked_ref[pl.ds(start, 8), :] * (0.5 * field_scale)
        for part, pick_ref in enumerate(pick_refs):
            total = jnp.sum(pick_ref[pl.ds(start, 8), :], axis=1, keepdims=True)
            force_ref[pl.ds(4 * start + part, 8, stride=4), :] = charge * total
        force_ref[pl.ds(4 * start + 3, 8, stride=4), :] = jnp.zeros((8, 128), jnp.float32)
        return 0

    lax.fori_loop(0, clusters // 8, spread_out, 0)


def grid_step(cell, masked, fields, before, after, lower, upper, base):
    smem = pl.BlockSpec(memory_space=pltpu.SMEM)
    vmem = pl.BlockSpec(memory_space=pltpu.VMEM)
    clusters = masked.shape[0]
    cells_x, cells_y, cells_z = fields[0].shape
    block = (cells_x + 2 * HALO_WIDTHS[0], cells_y + 2 * MARGIN, cells_z)
    return pl.pallas_call(
        functools.partial(grid_kernel, base),
        out_shape=(
            jax.ShapeDtypeStruct(fields[0].shape, jnp.float32),
            jax.ShapeDtypeStruct(fields[0].shape, jnp.float32),
            jax.ShapeDtypeStruct((clusters * 4, 128), jnp.float32),
        ),
        in_specs=[smem] + [vmem] * 9,
        out_specs=(vmem,) * 3,
        scratch_shapes=[pltpu.VMEM(block, jnp.float32)] * 5
        + [pltpu.VMEM(((cells_x + 2) * 2 * block[1], 128), jnp.float32)]
        + [pltpu.VMEM((clusters, 128), jnp.float32)] * 3,
        compiler_params=pltpu.CompilerParams(vmem_limit_bytes=40 * 1024 * 1024),
        cost_estimate=pl.CostEstimate(
            flops=block[0] * block[1] * block[2] * 100, bytes_accessed=8 << 20, transcendentals=0
        ),
        name="grid_step",
    )(cell, masked, *fields, before, after, lower, upper)


def gather_forces_kernel(send_index_ref, own_ref, field_ref, *refs):
    back_refs, (out_ref, sum_ref) = (refs[:-2], refs[-2:])
    clusters = own_ref.shape[0]
    slots = send_index_ref.shape[1]
    sum_ref[...] = own_ref[...] + field_ref[...]

    def visit(slot, _):
        for direction, back_ref in enumerate(back_refs):
            cluster = send_index_ref[direction, slot]
            sum_ref[cluster] += back_ref[slot]
        return 0

    lax.fori_loop(0, slots, visit, 0)

    def write(step, _):
        for turn in range(8):
            cluster = step * 8 + turn
            out_ref[:, pl.ds(pl.multiple_of(cluster * 128, 128), 128)] = sum_ref[cluster][0:3]
        return 0

    lax.fori_loop(0, clusters // 8, write, 0)


def gather_forces(send_index, own, field, backs):
    smem = pl.BlockSpec(memory_space=pltpu.SMEM)
    vmem = pl.BlockSpec(memory_space=pltpu.VMEM)
    clusters = own.shape[0]
    return pl.pallas_call(
        gather_forces_kernel,
        out_shape=jax.ShapeDtypeStruct((3, clusters * 128), jnp.float32),
        in_specs=[smem] + [vmem] * (2 + len(backs)),
        out_specs=vmem,
        scratch_shapes=[pltpu.VMEM(own.shape, jnp.float32)],
        compiler_params=pltpu.CompilerParams(vmem_limit_bytes=32 * 1024 * 1024),
        name="gather_forces",
    )(send_index, own, field, *backs)


def passed_along(shard, axis, by):
    devices = lax.axis_size(axis)
    pairs = [(i, i + by) for i in range(devices) if 0 <= i + by < devices]
    return lax.ppermute(shard, axis, pairs)


ROUTES = (("brick", 1), ("brick", -1), ("brick", 2), ("brick", -2), ("grp", 1), ("grp", -1))


def shards(
    positions,
    charges,
    cluster_fill,
    cluster_cell,
    send_index,
    send_count,
    pair_local,
    pair_dir,
    pair_slot,
    ion_density,
    potential_prev,
    screening,
):
    clusters = cluster_fill.shape[0]
    psize = charges.shape[0] // clusters
    slots = send_index.shape[1]
    base = slots * 4
    own, masked, inverse, source, local, *messages = prepare(
        cluster_fill,
        cluster_cell,
        send_index,
        send_count,
        positions,
        charges.reshape(clusters, psize),
        ion_density,
        potential_prev,
        screening,
    )
    arrived = [local] + [
        passed_along(message, axis, by)
        for message, (axis, by) in zip(messages, ROUTES, strict=True)
    ]
    fields = (potential_prev, inverse, source, ion_density)
    arrived = lax.optimization_barrier(arrived)
    before, after = arrived[1:3]
    down, up = planes(fields, before, after, base)
    lower = passed_along(up, "grp", 1)
    upper = passed_along(down, "grp", -1)
    own_force, *reactions = pair_forces(
        pair_local,
        pair_dir * slots + pair_slot,
        own.reshape(clusters * 4, psize),
        arrived,
        slots,
    )
    backs = [reactions[0]] + [
        passed_along(reaction, axis, -by)
        for reaction, (axis, by) in zip(reactions[1:], ROUTES, strict=True)
    ]
    potential, ion_next, field_force = grid_step(
        cluster_cell, masked, fields, before, after, lower, upper, base
    )
    forces = gather_forces(
        send_index,
        own_force.reshape(clusters, 4, psize),
        field_force.reshape(clusters, 4, psize),
        [back.reshape(slots, 4, psize) for back in backs],
    )
    return (forces, potential, ion_next)


def solution(mesh):
    in_specs = (
        P(None, ("grp", "brick")),
        P(("grp", "brick")),
        P(("grp", "brick")),
        P(("grp", "brick")),
        P(("grp", "brick"), None),
        P(("grp", "brick"), None),
        P(("grp", "brick")),
        P(("grp", "brick")),
        P(("grp", "brick")),
        P("grp", "brick", None),
        P("grp", "brick", None),
        P("grp", "brick", None),
    )
    out_specs = (P(None, ("grp", "brick")), P("grp", "brick", None), P("grp", "brick", None))
    return jax.shard_map(shards, mesh=mesh, in_specs=in_specs, out_specs=out_specs, check_vma=False)
```

```python
import functools

import jax
import jax.numpy as jnp
import numpy as np
from jax import lax
from jax.experimental import pallas as pl
from jax.experimental.pallas import tpu as pltpu
from jax.sharding import PartitionSpec as P

SWEEPS = 4
QUAD = 4
UNROLL = 8
HALO_WIDTHS = (SWEEPS + 1, SWEEPS, SWEEPS, 1)
MARGIN = 8
CELL_BITS = 8
ROUTES = (("brick", 1), ("brick", -1), ("brick", 2), ("brick", -2), ("grp", 1), ("grp", -1))


coulomb_scale = 0.02
softening = 0.1
field_scale = 0.5
deposit_scale = 0.2
lowest_eig = 0.01
highest_eig = 1.99
mobility = 0.3
diffusion = 0.2
time_step = 0.2


def split3(value):
    first = value.astype(jnp.bfloat16).astype(jnp.float32)
    rest = value - first
    second = rest.astype(jnp.bfloat16).astype(jnp.float32)
    third = (rest - second).astype(jnp.bfloat16).astype(jnp.float32)
    return (first, second, third)


def moment_pieces(comps, charge):
    rows = [None] * 12
    for part, charged in enumerate((*comps, None)):
        for level, piece in enumerate(split3(charge if charged is None else charge * charged)):
            rows[4 * level + part] = piece
    return rows


def selections():
    near_kinds, far_kinds = ([], [])
    for part in range(3):
        near_kinds += [3 * part + level for level in (0, 0, 0, 1, 1, 2)]
        far_kinds += [3 * part + level for level in (0, 1, 2, 0, 1, 0)]
    near_kinds += [9, 10, 11, 12, 12, 12]
    far_kinds += [12, 12, 12, 9, 10, 11]
    near = np.zeros((128, 256), np.float32)
    far = np.zeros((256, 128), np.float32)
    own_moment = np.zeros((128, 128), np.float32)
    other_moment = np.zeros((128, QUAD * 256), np.float32)
    for cluster in range(8):
        for index, kind in enumerate(near_kinds):
            near[kind * 8 + cluster, cluster * 32 + index] = 1.0
        for index, kind in enumerate(far_kinds):
            far[cluster * 32 + index, kind * 8 + cluster] = 1.0
        for kind in range(12):
            own_moment[cluster * 16 + kind, kind * 8 + cluster] = 1.0
            for turn in range(QUAD):
                lane = (cluster % QUAD + turn) % QUAD * 32 + kind
                column = turn * 256 + cluster // QUAD * 128 + lane
                other_moment[kind * 8 + cluster, column] = 1.0
    return tuple(jnp.asarray(part, jnp.bfloat16) for part in (near, far, own_moment, other_moment))


def pair_kernel(own_rows_ref, other_rows_ref, *refs):
    near_sel_ref, far_sel_ref, own_moment_sel_ref, other_moment_sel_ref, own_ref = refs[:5]
    refs = refs[5:]
    sources = len(ROUTES) + 1
    other_refs = refs[:sources]
    own_out_ref, local_out_ref, brick_out_ref, grp_out_ref = refs[sources : sources + 4]
    (
        near_ref,
        far_ref,
        own_moment_ref,
        other_moment_ref,
        own_sum_ref,
        other_sum_ref,
        *passed_refs,
    ) = refs[sources + 4 :]
    clusters = own_ref.shape[0] // 4
    slots = local_out_ref.shape[0] // 4
    others = slots * sources
    groups = own_rows_ref.shape[0] // UNROLL
    units = UNROLL // QUAD
    groups_of_other = others // QUAD
    ones = jnp.ones((8, 128), jnp.float32)
    zeros = jnp.zeros((8, 128), jnp.float32)

    def components(data_ref, start):
        return [data_ref[pl.ds(4 * start + part, 8, stride=4), :] for part in range(4)]

    def place_pieces(comps, factor, offset):
        pieces = []
        square = zeros
        for comp in comps:
            square = square + comp * comp
            pieces += split3(factor * comp)
        pieces += [*split3(square + offset), ones]
        return jnp.concatenate(pieces + [zeros] * (16 - len(pieces)), axis=0)

    def selected(left, right):
        return jnp.dot(
            left.astype(jnp.bfloat16), right, preferred_element_type=jnp.float32
        ).astype(jnp.bfloat16)

    def near_rows(step, _):
        start = pl.multiple_of(step * 8, 8)
        *comps, charge = components(own_ref, start)
        moments = jnp.concatenate(moment_pieces(comps, charge) + [zeros] * 4, axis=0)
        own_moment_ref[pl.ds(pl.multiple_of(start * 16, 128), 128), :] = selected(
            own_moment_sel_ref[...], moments.astype(jnp.bfloat16)
        )
        tiles = selected(place_pieces(comps, 1.0, 0.0).T, near_sel_ref[...])
        for half in range(2):
            at = pl.ds(pl.multiple_of(step * 256 + half * 128, 128), 128)
            near_ref[at, :] = tiles[:, 128 * half : 128 * half + 128]
        return 0

    def far_rows(source, step, _):
        local = pl.multiple_of(step * 8, 8)
        start = source * slots + local
        *comps, charge = components(other_refs[source], local)
        rows = selected(far_sel_ref[...], place_pieces(comps, -2.0, softening).astype(jnp.bfloat16))
        for index in range(8):
            at = pl.multiple_of((start + index) * 128, 128)
            far_ref[pl.ds(at, 96), :] = jnp.zeros((96, 128), jnp.bfloat16)
            far_ref[pl.ds(at + 96, 32), :] = rows[32 * index : 32 * index + 32]
        moments = jnp.concatenate(moment_pieces(comps, charge) + [zeros] * 4, axis=0)
        tiles = selected(moments.T, other_moment_sel_ref[...])
        for turn in range(QUAD):
            for half in range(2):
                group = turn * groups_of_other + source * (slots // QUAD) + step * 2 + half
                column = 256 * turn + 128 * half
                other_moment_ref[pl.ds(pl.multiple_of(group * 128, 128), 128), :] = tiles[
                    :, column : column + 128
                ]
        return 0

    lax.fori_loop(0, clusters // 8, near_rows, 0, unroll=2)
    for source in range(sources):
        lax.fori_loop(0, slots // 8, functools.partial(far_rows, source), 0, unroll=2)
    far_ref[pl.ds(others * 128, 128), :] = jnp.zeros((128, 128), jnp.bfloat16)
    own_sum_ref[...] = jnp.zeros_like(own_sum_ref)
    other_sum_ref[...] = jnp.zeros_like(other_sum_ref)
    dist_refs, weight_refs = (passed_refs[:2], passed_refs[2:])
    dist_refs[0][...] = jnp.full(dist_refs[0].shape, 1e38, jnp.float32)
    weight_refs[0][...] = jnp.zeros_like(weight_refs[0])

    quarter_row = lax.shift_right_logical(lax.broadcasted_iota(jnp.int32, (1, 128), 1), 5)
    masks = [jnp.where(quarter_row == turn, 1.0, 0.0).astype(jnp.bfloat16) for turn in range(QUAD)]

    def block_diagonal(blocks):
        blank = jnp.zeros_like(blocks[0])
        lines = [
            jnp.concatenate(
                [block if turn == at else blank for turn in range(len(blocks))], axis=1
            )
            for at, block in enumerate(blocks)
        ]
        return jnp.concatenate(lines, axis=0)

    def distances(pair, unit, dist_ref):
        for couple in range(QUAD // 2):
            near, far = ([], [])
            for turn in range(2):
                own = own_rows_ref[pair + 2 * couple + turn]
                other = other_rows_ref[pair + 2 * couple + turn]
                tile = pl.multiple_of(lax.shift_right_logical(own, 2) * 128, 128)
                near.append(near_ref[pl.ds(tile, 128), :])
                first = pl.multiple_of(other * 128 + 96 - lax.bitwise_and(own, 3) * 32, 32)
                far.append(far_ref[pl.ds(first, 128), :])
            dist_ref[unit, :, 256 * couple : 256 * couple + 256] = jnp.dot(
                jnp.concatenate(near, axis=1),
                block_diagonal(far),
                preferred_element_type=jnp.float32,
            )

    def weights(unit, turn, dist_ref, weight_ref):
        root = lax.rsqrt(dist_ref[unit, :, 128 * turn : 128 * turn + 128])
        weight = root * root * root
        high = weight.astype(jnp.bfloat16)
        weight_ref[unit, 128 * turn : 128 * turn + 128, :128] = high
        weight_ref[unit, 128 * turn : 128 * turn + 128, 128:] = (
            weight - high.astype(jnp.float32)
        ).astype(jnp.bfloat16)

    def turned(index, turn):
        rotation = lax.bitwise_and(turn - index, 3)
        group = rotation * groups_of_other + lax.shift_right_logical(index, 2)
        return other_moment_ref[pl.ds(pl.multiple_of(group * 128, 128), 128), :] * masks[turn]

    def products(pair, unit, weight_ref):
        owns = [own_rows_ref[pair + turn] for turn in range(QUAD)]
        others = [other_rows_ref[pair + turn] for turn in range(QUAD)]
        both = weight_ref[unit]
        levels = [
            jnp.concatenate(
                [both[128 * turn : 128 * turn + 128, lanes] for turn in range(QUAD)], axis=1
            )
            for lanes in (slice(0, 128), slice(128, 256))
        ]
        columns = jnp.concatenate([turned(others[turn], turn) for turn in range(QUAD)], axis=0)
        to_own = jnp.dot(
            jnp.concatenate(levels, axis=0), columns, preferred_element_type=jnp.float32
        )
        rows = block_diagonal(
            [own_moment_ref[pl.ds(pl.multiple_of(own * 16, 16), 16), :] for own in owns]
        )
        to_other = jnp.dot(rows, both, preferred_element_type=jnp.float32)
        return (
            owns,
            others,
            (to_own[:128] + to_own[128:]).T,
            to_other[:, :128] + to_other[:, 128:],
        )

    def half_step(step, side):
        last = jnp.maximum(step - 2, 0) * UNROLL
        first = jnp.minimum(step, groups - 1) * UNROLL
        results = [products(last + QUAD * unit, unit, weight_refs[side]) for unit in range(units)]
        for unit in range(units):
            for turn in range(QUAD):
                weights(unit, turn, dist_refs[side], weight_refs[1 - side])
        for unit in range(units):
            distances(first + QUAD * unit, unit, dist_refs[1 - side])
        for owns, others, to_own, to_other in results:
            for turn in range(QUAD):
                own_at = pl.ds(pl.multiple_of(owns[turn] * 16, 16), 16)
                other_at = pl.ds(pl.multiple_of(others[turn] * 16, 16), 16)
                own_sum_ref[own_at, :] += to_own[32 * turn : 32 * turn + 16]
                other_sum_ref[other_at, :] += to_other[16 * turn : 16 * turn + 16]

    def visit(step, _):
        for side in range(2):
            half_step(step * 2 + side, side)
        return 0

    lax.fori_loop(0, (groups + 2) // 2, visit, 0)

    def finish(data_ref, out_ref, out_base, sum_ref, base, step, _):
        start = pl.multiple_of(step * 8, 8)
        *comps, charge = components(data_ref, start)

        def total(part):
            terms = [
                sum_ref[pl.ds(base + start * 16 + 4 * level + part, 8, stride=16), :]
                for level in range(3)
            ]
            return terms[0] + (terms[1] + terms[2])

        weight = total(3)
        scale = coulomb_scale * charge
        for part, comp in enumerate(comps):
            out_ref[pl.ds(out_base + 4 * start + part, 8, stride=4), :] = scale * (
                comp * weight - total(part)
            )
        out_ref[pl.ds(out_base + 4 * start + 3, 8, stride=4), :] = zeros
        return 0

    lax.fori_loop(
        0, clusters // 8, functools.partial(finish, own_ref, own_out_ref, 0, own_sum_ref, 0), 0
    )
    targets = [(local_out_ref, 0)]
    targets += [(brick_out_ref, slots * 4 * index) for index in range(4)]
    targets += [(grp_out_ref, slots * 4 * index) for index in range(2)]
    for source in range(sources):
        body = functools.partial(
            finish,
            other_refs[source],
            *targets[source],
            other_sum_ref,
            source * slots * 16,
        )
        lax.fori_loop(0, slots // 8, body, 0)


def pair_forces(own_rows, other_rows, own, arrived, slots):
    clusters = own.shape[0] // 4
    others = slots * len(arrived)
    pairs = own_rows.shape[0]
    smem = pl.BlockSpec(memory_space=pltpu.SMEM)
    vmem = pl.BlockSpec(memory_space=pltpu.VMEM)
    return pl.pallas_call(
        pair_kernel,
        out_shape=(
            jax.ShapeDtypeStruct(own.shape, jnp.float32),
            *[jax.ShapeDtypeStruct((slots * 4 * count, 128), jnp.float32) for count in (1, 4, 2)],
        ),
        in_specs=[smem, smem] + [vmem] * (5 + len(arrived)),
        out_specs=(vmem,) * 4,
        scratch_shapes=[
            pltpu.VMEM((clusters * 32, 128), jnp.bfloat16),
            pltpu.VMEM(((others + 1) * 128, 128), jnp.bfloat16),
            pltpu.VMEM((clusters * 16, 128), jnp.bfloat16),
            pltpu.VMEM((others * 128, 128), jnp.bfloat16),
            pltpu.VMEM((clusters * 16, 128), jnp.float32),
            pltpu.VMEM((others * 16, 128), jnp.float32),
            *[pltpu.VMEM((UNROLL // QUAD, 128, 128 * QUAD), jnp.float32)] * 2,
            *[pltpu.VMEM((UNROLL // QUAD, 128 * QUAD, 256), jnp.bfloat16)] * 2,
        ],
        compiler_params=pltpu.CompilerParams(vmem_limit_bytes=40 * 1024 * 1024),
        cost_estimate=pl.CostEstimate(
            flops=pairs * 128 * 128 * 20, bytes_accessed=4 * 1024 * 1024, transcendentals=0
        ),
        name="pair_forces",
    )(own_rows, other_rows, *selections(), own, *arrived)


def prepare_kernel(
    fill_ref,
    cell_ref,
    send_index_ref,
    send_count_ref,
    position_hbm,
    charge_hbm,
    ion_hbm,
    start_hbm,
    screen_hbm,
    own_ref,
    masked_ref,
    inverse_ref,
    source_ref,
    *refs,
):
    out_refs, scratch = (refs[:-8], refs[-8:])
    sum_ref, deposit_ref, position_ref, charge_ref, ion_ref, start_ref, screen_ref, sems = scratch
    copies = [
        pltpu.make_async_copy(source, target, sems.at[index])
        for index, (source, target) in enumerate(
            (
                (position_hbm, position_ref),
                (charge_hbm, charge_ref),
                (ion_hbm, ion_ref),
                (start_hbm, start_ref),
                (screen_hbm, screen_ref),
            )
        )
    ]
    for copy in copies:
        copy.start()
    deposit_ref[...] = jnp.zeros_like(deposit_ref)
    copies[0].wait()
    copies[1].wait()
    clusters = charge_ref.shape[0]
    cells_x, cells_y, _ = ion_ref.shape
    slots = send_index_ref.shape[1]
    lane = lax.broadcasted_iota(jnp.int32, (1, 128), 1)
    row = lax.broadcasted_iota(jnp.int32, (4, 128), 0)

    def collect(step, _):
        for turn in range(8):
            cluster = step * 8 + turn
            masked = jnp.where(lane < fill_ref[cluster], charge_ref[pl.ds(cluster, 1), :], 0.0)
            masked_ref[pl.ds(cluster, 1), :] = masked
            place = position_ref[:, pl.ds(pl.multiple_of(cluster * 128, 128), 128)]
            own_ref[cluster, 0:3, :] = place
            own_ref[cluster, 3:4, :] = masked
        at = pl.ds(pl.multiple_of(step * 8, 8), 8)
        total = jnp.sum(masked_ref[at, :], axis=1, keepdims=True)
        sum_ref[at, :] = jnp.broadcast_to(deposit_scale * total, (8, 128))
        return 0

    lax.fori_loop(0, clusters // 8, collect, 0)

    def fill_messages(step, _):
        for direction, out_ref in enumerate(out_refs):
            parts = []
            for turn in range(2):
                slot = step * 2 + turn
                live = jnp.where(slot < send_count_ref[0, direction], 1.0, 0.0)
                value = own_ref[send_index_ref[direction, slot]]
                parts.append(jnp.where(row == 3, value * live, value))
            out_ref[pl.ds(pl.multiple_of(step * 8, 8), 8), :] = jnp.concatenate(parts, axis=0)
        return 0

    lax.fori_loop(0, slots // 2, fill_messages, 0)

    def deposit(cluster, _):
        cell = cell_ref[cluster]
        index_x = lax.shift_right_logical(cell, CELL_BITS) // cells_y
        index_y = lax.shift_right_logical(cell, CELL_BITS) % cells_y
        index_z = lax.bitwise_and(cell, 255)
        half = lax.shift_right_logical(index_z, 7)
        added = jnp.where(
            lane == lax.bitwise_and(index_z, 127), sum_ref[pl.ds(cluster, 1), :], 0.0
        )
        deposit_ref[pl.ds((index_x * 2 + half) * cells_y + index_y, 1), :] += added
        return 0

    lax.fori_loop(0, clusters, deposit, 0, unroll=4)
    for copy in copies[2:]:
        copy.wait()
    inverse_ref[...] = 1.0 / (6.0 + screen_ref[...])
    for index in range(cells_x):
        for half in range(2):
            lanes = slice(128 * half, 128 * half + 128)
            first = (index * 2 + half) * cells_y
            source_ref[index, :, lanes] = (
                ion_ref[index, :, lanes] + deposit_ref[first : first + cells_y, :]
            ) * inverse_ref[index, :, lanes]
    for out_ref, after in ((out_refs[1], True), (out_refs[2], False)):
        for index in range(cells_x):
            base = slots * 4 + index * 32
            offset = 0
            for field_ref, width in zip(
                (start_ref, inverse_ref, source_ref, ion_ref), HALO_WIDTHS, strict=True
            ):
                first = cells_y - width if after else 0
                rows = field_ref[index, first : first + width, :]
                for half in range(2):
                    out_ref[base + 16 * half + offset : base + 16 * half + offset + width, :] = (
                        rows[:, 128 * half : 128 * half + 128]
                    )
                offset += width
            for half in range(2):
                out_ref[base + 16 * half + offset : base + 16 * half + 16, :] = jnp.zeros(
                    (16 - offset, 128), jnp.float32
                )


def prepare(fill, cell, send_index, send_count, positions, charges, ions, start, screen):
    clusters = charges.shape[0]
    directions, slots = send_index.shape
    cells_x = ions.shape[0]
    smem = pl.BlockSpec(memory_space=pltpu.SMEM)
    vmem = pl.BlockSpec(memory_space=pltpu.VMEM)
    rows = [slots * 4] * directions
    rows[1] = rows[2] = slots * 4 + cells_x * 32
    return pl.pallas_call(
        prepare_kernel,
        out_shape=(
            jax.ShapeDtypeStruct((clusters, 4, 128), jnp.float32),
            jax.ShapeDtypeStruct((clusters, 128), jnp.float32),
            jax.ShapeDtypeStruct(ions.shape, jnp.float32),
            jax.ShapeDtypeStruct(ions.shape, jnp.float32),
            *[jax.ShapeDtypeStruct((count, 128), jnp.float32) for count in rows],
        ),
        in_specs=[smem] * 4 + [pl.BlockSpec(memory_space=pltpu.HBM)] * 5,
        out_specs=(vmem,) * (4 + directions),
        scratch_shapes=[
            pltpu.VMEM((clusters, 128), jnp.float32),
            pltpu.VMEM((ions.size // 128, 128), jnp.float32),
            *[
                pltpu.VMEM(operand.shape, jnp.float32)
                for operand in (positions, charges, ions, start, screen)
            ],
            pltpu.SemaphoreType.DMA((5,)),
        ],
        compiler_params=pltpu.CompilerParams(vmem_limit_bytes=60 * 1024 * 1024),
        name="prepare",
    )(fill, cell, send_index, send_count, positions, charges, ions, start, screen)


def put_extended(target_ref, plane, field, field_ref, index, before_ref, after_ref, base):
    cells_y = field_ref.shape[1]
    width = HALO_WIDTHS[field]
    offset = sum(HALO_WIDTHS[:field])
    target_ref[plane, MARGIN : MARGIN + cells_y, :] = field_ref[index]
    for half in range(2):
        lanes = slice(128 * half, 128 * half + 128)
        first = base + index * 32 + 16 * half + offset
        target_ref[plane, MARGIN - width : MARGIN, lanes] = before_ref[first : first + width, :]
        target_ref[plane, MARGIN + cells_y : MARGIN + cells_y + width, lanes] = after_ref[
            first : first + width, :
        ]


def planes_kernel(base, *refs):
    field_refs, (before_ref, after_ref, down_ref, up_ref) = (refs[:4], refs[4:])
    cells_x = field_refs[0].shape[0]
    down_ref[...] = jnp.zeros_like(down_ref)
    up_ref[...] = jnp.zeros_like(up_ref)
    plane = 0
    for field, width in enumerate(HALO_WIDTHS):
        for index in range(width):
            for target_ref, source in ((down_ref, index), (up_ref, cells_x - width + index)):
                put_extended(
                    target_ref, plane, field, field_refs[field], source, before_ref, after_ref, base
                )
            plane += 1


def planes(fields, before, after, base):
    vmem = pl.BlockSpec(memory_space=pltpu.VMEM)
    _, cells_y, cells_z = fields[0].shape
    shape = jax.ShapeDtypeStruct((sum(HALO_WIDTHS), cells_y + 2 * MARGIN, cells_z), jnp.float32)
    return pl.pallas_call(
        functools.partial(planes_kernel, base),
        out_shape=(shape, shape),
        in_specs=[vmem] * 6,
        out_specs=(vmem, vmem),
        compiler_params=pltpu.CompilerParams(vmem_limit_bytes=32 * 1024 * 1024),
        name="planes",
    )(*fields, before, after)


def face_flux(pot_low, pot_high, ion_low, ion_high):
    speed = -mobility * (pot_high - pot_low)
    return (
        jnp.maximum(speed, 0.0) * ion_low
        + jnp.minimum(speed, 0.0) * ion_high
        - diffusion * (ion_high - ion_low)
    )


def grid_kernel(base, *refs):
    cell_ref, masked_ref = refs[:2]
    field_refs = refs[2:6]
    before_ref, after_ref, lower_ref, upper_ref = refs[6:10]
    potential_ref, next_ref, force_ref = refs[10:13]
    start_ref, inverse_ref, resid_ref, ion_ref, update_ref, line_ref, *pick_refs = refs[13:]
    cells_x, cells_y, cells_z = field_refs[0].shape
    rows = cells_y + 2 * MARGIN
    depth = HALO_WIDTHS[0]
    clusters = masked_ref.shape[0]
    lane = lax.broadcasted_iota(jnp.int32, (rows, cells_z), 1)
    middle = 0.5 * (highest_eig + lowest_eig)
    spread = 0.5 * (highest_eig - lowest_eig)

    plane = 0
    for field, target_ref in enumerate((start_ref, inverse_ref, resid_ref, ion_ref)):
        width = HALO_WIDTHS[field]
        if field == 0 or field == 3:
            target_ref[...] = jnp.zeros_like(target_ref)
        else:
            target_ref[depth : depth + cells_x, 0:MARGIN, :] = jnp.zeros(
                (cells_x, MARGIN, cells_z), jnp.float32
            )
            target_ref[depth : depth + cells_x, rows - MARGIN : rows, :] = jnp.zeros(
                (cells_x, MARGIN, cells_z), jnp.float32
            )
        for index in range(width):
            target_ref[depth - width + index] = lower_ref[plane + index]
            target_ref[depth + cells_x + index] = upper_ref[plane + index]
        for index in range(cells_x):
            put_extended(
                target_ref,
                depth + index,
                field,
                field_refs[field],
                index,
                before_ref,
                after_ref,
                base,
            )
        plane += width

    def above(value):
        return jnp.where(lane == cells_z - 1, 0.0, pltpu.roll(value, cells_z - 1, 1))

    def below(value):
        return jnp.where(lane == 0, 0.0, pltpu.roll(value, 1, 1))

    def beside(value):
        rolled = pltpu.roll(value, 1, 0) + pltpu.roll(value, rows - 1, 0)
        return rolled + (above(value) + below(value))

    def first_sweep(index, planes):
        last, here = planes
        after = start_ref[index + 1]
        resid = (
            resid_ref[index] - here + inverse_ref[index] * ((last + after) + beside(here))
        )
        resid_ref[index] = resid
        update_ref[index] = resid / middle
        return (here, after)

    lax.fori_loop(1, cells_x + 2 * depth - 1, first_sweep, (start_ref[0], start_ref[1]))

    ratio_ms = middle / spread
    weight_now = 1.0 / ratio_ms
    for turn in range(1, SWEEPS):
        weight_next = 1.0 / (2.0 * ratio_ms - weight_now)
        keep, gain = (weight_next * weight_now, 2.0 * weight_next / spread)
        weight_now = weight_next

        def sweep(index, planes, turn=turn, keep=keep, gain=gain):
            last, here = planes
            after = update_ref[index + 1]
            resid = resid_ref[index] - here + inverse_ref[index] * ((last + after) + beside(here))
            update = keep * here + gain * resid
            if turn == 1:
                start_ref[index] = start_ref[index] + here + update
            else:
                start_ref[index] = start_ref[index] + update
            if turn + 1 < SWEEPS:
                resid_ref[index] = resid
                update_ref[index] = update
            return (here, after)

        first = 1 + turn
        lax.fori_loop(
            first,
            cells_x + 2 * depth - first,
            sweep,
            (update_ref[first - 1], update_ref[first]),
        )

    def upper_flux(index):
        return face_flux(start_ref[index], start_ref[index + 1], ion_ref[index], ion_ref[index + 1])

    inner = slice(MARGIN, MARGIN + cells_y)

    def advance(index, lower):
        pot = start_ref[depth + index]
        ions = ion_ref[depth + index]
        upper = upper_flux(depth + index)
        along_y = face_flux(pot, pltpu.roll(pot, rows - 1, 0), ions, pltpu.roll(ions, rows - 1, 0))
        along_z = face_flux(pot, above(pot), ions, above(ions))
        first_z = face_flux(0.0, pot, 0.0, ions)
        total = upper - lower
        total = total + (along_y - pltpu.roll(along_y, 1, 0))
        total = total + (along_z - jnp.where(lane == 0, first_z, pltpu.roll(along_z, 1, 1)))
        next_ref[index] = (ions - time_step * total)[inner]
        potential_ref[index] = pot[inner]
        return upper

    lax.fori_loop(0, cells_x, advance, upper_flux(depth - 1))
    for index in range(cells_x + 2):
        for half in range(2):
            line_ref[pl.ds((index * 2 + half) * rows, rows), :] = start_ref[
                depth - 1 + index, :, 128 * half : 128 * half + 128
            ]

    row_lane = lax.broadcasted_iota(jnp.int32, (1, 128), 1)

    def pick(cluster, _):
        cell = cell_ref[cluster]
        index_x = lax.shift_right_logical(cell, CELL_BITS) // cells_y + 1
        index_y = lax.shift_right_logical(cell, CELL_BITS) % cells_y + MARGIN
        index_z = lax.bitwise_and(cell, 255)
        half = lax.shift_right_logical(index_z, 7)
        here = row_lane == lax.bitwise_and(index_z, 127)

        def line(plane, row, part):
            return line_ref[pl.ds((plane * 2 + part) * rows + row, 1), :]

        along_x = line(index_x - 1, index_y, half) - line(index_x + 1, index_y, half)
        along_y = line(index_x, index_y - 1, half) - line(index_x, index_y + 1, half)
        along_z = jnp.zeros((1, 128), jnp.float32)
        for part in range(cells_z // 128):
            value = line(index_x, index_y, part)
            place = row_lane + 128 * part
            along_z = along_z + jnp.where(place == index_z - 1, value, 0.0)
            along_z = along_z - jnp.where(place == index_z + 1, value, 0.0)
        at = pl.ds(cluster, 1)
        pick_refs[0][at, :] = jnp.where(here, along_x, 0.0)
        pick_refs[1][at, :] = jnp.where(here, along_y, 0.0)
        pick_refs[2][at, :] = along_z
        return 0

    lax.fori_loop(0, clusters, pick, 0, unroll=4)

    def spread_out(step, _):
        start = pl.multiple_of(step * 8, 8)
        charge = masked_ref[pl.ds(start, 8), :] * (0.5 * field_scale)
        for part, pick_ref in enumerate(pick_refs):
            total = jnp.sum(pick_ref[pl.ds(start, 8), :], axis=1, keepdims=True)
            force_ref[pl.ds(4 * start + part, 8, stride=4), :] = charge * total
        force_ref[pl.ds(4 * start + 3, 8, stride=4), :] = jnp.zeros((8, 128), jnp.float32)
        return 0

    lax.fori_loop(0, clusters // 8, spread_out, 0)


def grid_step(cell, masked, fields, before, after, lower, upper, base):
    smem = pl.BlockSpec(memory_space=pltpu.SMEM)
    vmem = pl.BlockSpec(memory_space=pltpu.VMEM)
    clusters = masked.shape[0]
    cells_x, cells_y, cells_z = fields[0].shape
    block = (cells_x + 2 * HALO_WIDTHS[0], cells_y + 2 * MARGIN, cells_z)
    return pl.pallas_call(
        functools.partial(grid_kernel, base),
        out_shape=(
            jax.ShapeDtypeStruct(fields[0].shape, jnp.float32),
            jax.ShapeDtypeStruct(fields[0].shape, jnp.float32),
            jax.ShapeDtypeStruct((clusters * 4, 128), jnp.float32),
        ),
        in_specs=[smem] + [vmem] * 9,
        out_specs=(vmem,) * 3,
        scratch_shapes=[pltpu.VMEM(block, jnp.float32)] * 5
        + [pltpu.VMEM(((cells_x + 2) * 2 * block[1], 128), jnp.float32)]
        + [pltpu.VMEM((clusters, 128), jnp.float32)] * 3,
        compiler_params=pltpu.CompilerParams(vmem_limit_bytes=40 * 1024 * 1024),
        cost_estimate=pl.CostEstimate(
            flops=block[0] * block[1] * block[2] * 100, bytes_accessed=8 << 20, transcendentals=0
        ),
        name="grid_step",
    )(cell, masked, *fields, before, after, lower, upper)


def gather_forces_kernel(
    send_index_ref,
    own_ref,
    field_ref,
    local_ref,
    brick_hbm,
    grp_hbm,
    out_ref,
    sum_ref,
    back_ref,
    sems,
):
    clusters = own_ref.shape[0]
    slots = send_index_ref.shape[1]
    shares = []
    for index, (axis, by) in enumerate(ROUTES):
        hbm = brick_hbm if axis == "brick" else grp_hbm
        first, count = (0, 4) if axis == "brick" else (4, 2)
        devices = hbm.shape[0] // (slots * count)
        source = lax.axis_index(axis) + by
        inside = (source >= 0) & (source < devices)
        block = jnp.clip(source, 0, devices - 1) * count + index - first
        copy = pltpu.make_async_copy(
            hbm.at[pl.ds(block * slots, slots)],
            back_ref.at[pl.ds(index * slots, slots)],
            sems.at[index],
        )
        copy.start()
        shares.append((copy, jnp.where(inside, 1.0, 0.0)))
    sum_ref[...] = own_ref[...] + field_ref[...]
    for copy, _ in shares:
        copy.wait()

    def visit(slot, _):
        sum_ref[send_index_ref[0, slot]] += local_ref[slot]
        for index, (_, share) in enumerate(shares):
            cluster = send_index_ref[index + 1, slot]
            sum_ref[cluster] += back_ref[index * slots + slot] * share
        return 0

    lax.fori_loop(0, slots, visit, 0)

    def write(step, _):
        for turn in range(8):
            cluster = step * 8 + turn
            out_ref[:, pl.ds(pl.multiple_of(cluster * 128, 128), 128)] = sum_ref[cluster][0:3]
        return 0

    lax.fori_loop(0, clusters // 8, write, 0)


def gather_forces(send_index, own, field, local, brick_all, grp_all):
    smem = pl.BlockSpec(memory_space=pltpu.SMEM)
    vmem = pl.BlockSpec(memory_space=pltpu.VMEM)
    hbm = pl.BlockSpec(memory_space=pltpu.HBM)
    clusters = own.shape[0]
    slots = send_index.shape[1]
    return pl.pallas_call(
        gather_forces_kernel,
        out_shape=jax.ShapeDtypeStruct((3, clusters * 128), jnp.float32),
        in_specs=[smem, vmem, vmem, vmem, hbm, hbm],
        out_specs=vmem,
        scratch_shapes=[
            pltpu.VMEM(own.shape, jnp.float32),
            pltpu.VMEM((len(ROUTES) * slots, 4, 128), jnp.float32),
            pltpu.SemaphoreType.DMA((len(ROUTES),)),
        ],
        compiler_params=pltpu.CompilerParams(vmem_limit_bytes=60 * 1024 * 1024),
        name="gather_forces",
    )(send_index, own, field, local, brick_all, grp_all)


def passed_along(shard, axis, by):
    devices = lax.axis_size(axis)
    pairs = [(i, i + by) for i in range(devices) if 0 <= i + by < devices]
    return lax.ppermute(shard, axis, pairs)


def shards(
    positions,
    charges,
    cluster_fill,
    cluster_cell,
    send_index,
    send_count,
    pair_local,
    pair_dir,
    pair_slot,
    ion_density,
    potential_prev,
    screening,
):
    clusters = cluster_fill.shape[0]
    psize = charges.shape[0] // clusters
    slots = send_index.shape[1]
    base = slots * 4
    own, masked, inverse, source, local, *messages = prepare(
        cluster_fill,
        cluster_cell,
        send_index,
        send_count,
        positions,
        charges.reshape(clusters, psize),
        ion_density,
        potential_prev,
        screening,
    )
    arrived = [local] + [
        passed_along(message, axis, by)
        for message, (axis, by) in zip(messages, ROUTES, strict=True)
    ]
    fields = (potential_prev, inverse, source, ion_density)
    arrived = lax.optimization_barrier(arrived)
    before, after = arrived[1:3]
    down, up = planes(fields, before, after, base)
    lower = passed_along(up, "grp", 1)
    upper = passed_along(down, "grp", -1)
    own_force, local_back, brick_back, grp_back = pair_forces(
        pair_local,
        pair_dir * slots + pair_slot,
        own.reshape(clusters * 4, psize),
        arrived,
        slots,
    )
    brick_back, grp_back, lower, upper = lax.optimization_barrier(
        (brick_back, grp_back, lower, upper)
    )
    brick_all = lax.all_gather(brick_back, "brick")
    grp_all = lax.all_gather(grp_back, "grp")
    potential, ion_next, field_force = grid_step(
        cluster_cell, masked, fields, before, after, lower, upper, base
    )
    forces = gather_forces(
        send_index,
        own_force.reshape(clusters, 4, psize),
        field_force.reshape(clusters, 4, psize),
        local_back.reshape(slots, 4, psize),
        brick_all.reshape(-1, 4, psize),
        grp_all.reshape(-1, 4, psize),
    )
    return (forces, potential, ion_next)


def solution(mesh):
    in_specs = (
        P(None, ("grp", "brick")),
        P(("grp", "brick")),
        P(("grp", "brick")),
        P(("grp", "brick")),
        P(("grp", "brick"), None),
        P(("grp", "brick"), None),
        P(("grp", "brick")),
        P(("grp", "brick")),
        P(("grp", "brick")),
        P("grp", "brick", None),
        P("grp", "brick", None),
        P("grp", "brick", None),
    )
    out_specs = (P(None, ("grp", "brick")), P("grp", "brick", None), P("grp", "brick", None))
    return jax.shard_map(shards, mesh=mesh, in_specs=in_specs, out_specs=out_specs, check_vma=False)
```

```python
import functools

import jax
import jax.numpy as jnp
import numpy as np
from jax import lax
from jax.experimental import pallas as pl
from jax.experimental.pallas import tpu as pltpu
from jax.sharding import PartitionSpec as P

SWEEPS = 4
QUAD = 4
UNROLL = 8
HALO_WIDTHS = (SWEEPS + 1, SWEEPS, SWEEPS, 1)
MARGIN = 8
CELL_BITS = 8


coulomb_scale = 0.02
softening = 0.1
field_scale = 0.5
deposit_scale = 0.2
lowest_eig = 0.01
highest_eig = 1.99
mobility = 0.3
diffusion = 0.2
time_step = 0.2


def split3(value):
    first = value.astype(jnp.bfloat16).astype(jnp.float32)
    rest = value - first
    second = rest.astype(jnp.bfloat16).astype(jnp.float32)
    third = (rest - second).astype(jnp.bfloat16).astype(jnp.float32)
    return (first, second, third)


def moment_pieces(comps, charge):
    rows = [None] * 12
    for part, charged in enumerate((*comps, None)):
        for level, piece in enumerate(split3(charge if charged is None else charge * charged)):
            rows[4 * level + part] = piece
    return rows


def selections():
    near_kinds, far_kinds = ([], [])
    for part in range(3):
        near_kinds += [3 * part + level for level in (0, 0, 0, 1, 1, 2)]
        far_kinds += [3 * part + level for level in (0, 1, 2, 0, 1, 0)]
    near_kinds += [9, 10, 11, 12, 12, 12]
    far_kinds += [12, 12, 12, 9, 10, 11]
    near = np.zeros((128, 256), np.float32)
    far = np.zeros((256, 128), np.float32)
    moment = np.zeros((128, 128), np.float32)
    for cluster in range(8):
        for index, kind in enumerate(near_kinds):
            near[kind * 8 + cluster, cluster * 32 + index] = 1.0
        for index, kind in enumerate(far_kinds):
            far[cluster * 32 + index, kind * 8 + cluster] = 1.0
        for kind in range(12):
            moment[cluster * 16 + kind, kind * 8 + cluster] = 1.0
    return tuple(jnp.asarray(part, jnp.bfloat16) for part in (near, far, moment))


def pair_kernel(own_rows_ref, other_rows_ref, *refs):
    near_sel_ref, far_sel_ref, moment_sel_ref, own_ref = refs[:4]
    refs = refs[4:]
    sources = (len(refs) - 11) // 2
    other_refs = refs[:sources]
    own_out_ref = refs[sources]
    other_out_refs = refs[sources + 1 : 2 * sources + 1]
    (
        near_ref,
        far_ref,
        own_moment_ref,
        other_moment_ref,
        own_sum_ref,
        other_sum_ref,
        *passed_refs,
    ) = refs[2 * sources + 1 :]
    clusters = own_ref.shape[0] // 4
    slots = other_out_refs[0].shape[0] // 4
    others = slots * sources
    groups = own_rows_ref.shape[0] // UNROLL
    units = UNROLL // QUAD
    ones = jnp.ones((8, 128), jnp.float32)
    zeros = jnp.zeros((8, 128), jnp.float32)

    def components(data_ref, start):
        return [data_ref[pl.ds(4 * start + part, 8, stride=4), :] for part in range(4)]

    def place_pieces(comps, factor, offset):
        pieces = []
        square = zeros
        for comp in comps:
            square = square + comp * comp
            pieces += split3(factor * comp)
        pieces += [*split3(square + offset), ones]
        return jnp.concatenate(pieces + [zeros] * (16 - len(pieces)), axis=0)

    def selected(left, right):
        return jnp.dot(
            left.astype(jnp.bfloat16), right, preferred_element_type=jnp.float32
        ).astype(jnp.bfloat16)

    def near_rows(step, _):
        start = pl.multiple_of(step * 8, 8)
        *comps, charge = components(own_ref, start)
        moments = jnp.concatenate(moment_pieces(comps, charge) + [zeros] * 4, axis=0)
        own_moment_ref[pl.ds(pl.multiple_of(start * 16, 128), 128), :] = selected(
            moment_sel_ref[...], moments.astype(jnp.bfloat16)
        )
        tiles = selected(place_pieces(comps, 1.0, 0.0).T, near_sel_ref[...])
        for half in range(2):
            at = pl.ds(pl.multiple_of(step * 256 + half * 128, 128), 128)
            near_ref[at, :] = tiles[:, 128 * half : 128 * half + 128]
        return 0

    def far_rows(source, step, _):
        local = pl.multiple_of(step * 8, 8)
        start = source * slots + local
        *comps, charge = components(other_refs[source], local)
        rows = selected(far_sel_ref[...], place_pieces(comps, -2.0, softening).astype(jnp.bfloat16))
        for index in range(8):
            at = pl.multiple_of((start + index) * 128, 128)
            far_ref[pl.ds(at, 96), :] = jnp.zeros((96, 128), jnp.bfloat16)
            far_ref[pl.ds(at + 96, 32), :] = rows[32 * index : 32 * index + 32]
        moments = jnp.concatenate(moment_pieces(comps, charge) + [zeros] * 4, axis=0)
        other_moment_ref[pl.ds(pl.multiple_of(start * 16, 128), 128), :] = selected(
            moment_sel_ref[...], moments.astype(jnp.bfloat16)
        )
        return 0

    lax.fori_loop(0, clusters // 8, near_rows, 0, unroll=2)
    for source in range(sources):
        lax.fori_loop(0, slots // 8, functools.partial(far_rows, source), 0, unroll=2)
    far_ref[pl.ds(others * 128, 128), :] = jnp.zeros((128, 128), jnp.bfloat16)
    own_sum_ref[...] = jnp.zeros_like(own_sum_ref)
    other_sum_ref[...] = jnp.zeros_like(other_sum_ref)
    dist_refs, weight_refs = (passed_refs[:2], passed_refs[2:])
    dist_refs[0][...] = jnp.full(dist_refs[0].shape, 1e38, jnp.float32)
    weight_refs[0][...] = jnp.zeros_like(weight_refs[0])

    def block_diagonal(blocks):
        blank = jnp.zeros_like(blocks[0])
        lines = [
            jnp.concatenate(
                [block if turn == at else blank for turn in range(len(blocks))], axis=1
            )
            for at, block in enumerate(blocks)
        ]
        return jnp.concatenate(lines, axis=0)

    def distances(pair, unit, dist_ref):
        for couple in range(QUAD // 2):
            near, far = ([], [])
            for turn in range(2):
                own = own_rows_ref[pair + 2 * couple + turn]
                other = other_rows_ref[pair + 2 * couple + turn]
                tile = pl.multiple_of(lax.shift_right_logical(own, 2) * 128, 128)
                near.append(near_ref[pl.ds(tile, 128), :])
                first = pl.multiple_of(other * 128 + 96 - lax.bitwise_and(own, 3) * 32, 32)
                far.append(far_ref[pl.ds(first, 128), :])
            dist_ref[unit, :, 256 * couple : 256 * couple + 256] = jnp.dot(
                jnp.concatenate(near, axis=1),
                block_diagonal(far),
                preferred_element_type=jnp.float32,
            )

    def weights(unit, turn, dist_ref, weight_ref):
        root = lax.rsqrt(dist_ref[unit, :, 128 * turn : 128 * turn + 128])
        weight = root * root * root
        high = weight.astype(jnp.bfloat16)
        weight_ref[unit, 128 * turn : 128 * turn + 128, :128] = high
        weight_ref[unit, 128 * turn : 128 * turn + 128, 128:] = (
            weight - high.astype(jnp.float32)
        ).astype(jnp.bfloat16)

    def moments_of(moment_ref, indices):
        return block_diagonal(
            [moment_ref[pl.ds(pl.multiple_of(index * 16, 16), 16), :] for index in indices]
        )

    def products(pair, unit, weight_ref):
        owns = [own_rows_ref[pair + turn] for turn in range(QUAD)]
        others = [other_rows_ref[pair + turn] for turn in range(QUAD)]
        both = weight_ref[unit]
        levels = [
            jnp.concatenate(
                [both[128 * turn : 128 * turn + 128, lanes] for turn in range(QUAD)], axis=1
            )
            for lanes in (slice(0, 128), slice(128, 256))
        ]
        to_own = lax.dot_general(
            moments_of(other_moment_ref, others),
            jnp.concatenate(levels, axis=0),
            (((1,), (1,)), ((), ())),
            preferred_element_type=jnp.float32,
        )
        to_other = jnp.dot(
            moments_of(own_moment_ref, owns), both, preferred_element_type=jnp.float32
        )
        return (owns, others, *(part[:, :128] + part[:, 128:] for part in (to_own, to_other)))

    def half_step(step, side):
        last = jnp.maximum(step - 2, 0) * UNROLL
        first = jnp.minimum(step, groups - 1) * UNROLL
        results = [products(last + QUAD * unit, unit, weight_refs[side]) for unit in range(units)]
        for unit in range(units):
            for turn in range(QUAD):
                weights(unit, turn, dist_refs[side], weight_refs[1 - side])
        for unit in range(units):
            distances(first + QUAD * unit, unit, dist_refs[1 - side])
        for owns, others, to_own, to_other in results:
            for turn in range(QUAD):
                own_at = pl.ds(pl.multiple_of(owns[turn] * 16, 16), 16)
                other_at = pl.ds(pl.multiple_of(others[turn] * 16, 16), 16)
                own_sum_ref[own_at, :] += to_own[16 * turn : 16 * turn + 16]
                other_sum_ref[other_at, :] += to_other[16 * turn : 16 * turn + 16]

    def visit(step, _):
        for side in range(2):
            half_step(step * 2 + side, side)
        return 0

    lax.fori_loop(0, (groups + 2) // 2, visit, 0)

    def finish(data_ref, out_ref, sum_ref, base, step, _):
        start = pl.multiple_of(step * 8, 8)
        *comps, charge = components(data_ref, start)

        def total(part):
            terms = [
                sum_ref[pl.ds(base + start * 16 + 4 * level + part, 8, stride=16), :]
                for level in range(3)
            ]
            return terms[0] + (terms[1] + terms[2])

        weight = total(3)
        scale = coulomb_scale * charge
        for part, comp in enumerate(comps):
            out_ref[pl.ds(4 * start + part, 8, stride=4), :] = scale * (comp * weight - total(part))
        out_ref[pl.ds(4 * start + 3, 8, stride=4), :] = zeros
        return 0

    lax.fori_loop(
        0, clusters // 8, functools.partial(finish, own_ref, own_out_ref, own_sum_ref, 0), 0
    )
    for source in range(sources):
        body = functools.partial(
            finish,
            other_refs[source],
            other_out_refs[source],
            other_sum_ref,
            source * slots * 16,
        )
        lax.fori_loop(0, slots // 8, body, 0)


def pair_forces(own_rows, other_rows, own, arrived, slots):
    clusters = own.shape[0] // 4
    others = slots * len(arrived)
    pairs = own_rows.shape[0]
    smem = pl.BlockSpec(memory_space=pltpu.SMEM)
    vmem = pl.BlockSpec(memory_space=pltpu.VMEM)
    return pl.pallas_call(
        pair_kernel,
        out_shape=(
            jax.ShapeDtypeStruct(own.shape, jnp.float32),
            *[jax.ShapeDtypeStruct((slots * 4, 128), jnp.float32)] * len(arrived),
        ),
        in_specs=[smem, smem] + [vmem] * (4 + len(arrived)),
        out_specs=(vmem,) * (len(arrived) + 1),
        scratch_shapes=[
            pltpu.VMEM((clusters * 32, 128), jnp.bfloat16),
            pltpu.VMEM(((others + 1) * 128, 128), jnp.bfloat16),
            pltpu.VMEM((clusters * 16, 128), jnp.bfloat16),
            pltpu.VMEM((others * 16, 128), jnp.bfloat16),
            pltpu.VMEM((clusters * 16, 128), jnp.float32),
            pltpu.VMEM((others * 16, 128), jnp.float32),
            *[pltpu.VMEM((UNROLL // QUAD, 128, 128 * QUAD), jnp.float32)] * 2,
            *[pltpu.VMEM((UNROLL // QUAD, 128 * QUAD, 256), jnp.bfloat16)] * 2,
        ],
        compiler_params=pltpu.CompilerParams(vmem_limit_bytes=40 * 1024 * 1024),
        cost_estimate=pl.CostEstimate(
            flops=pairs * 128 * 128 * 20, bytes_accessed=4 * 1024 * 1024, transcendentals=0
        ),
        name="pair_forces",
    )(own_rows, other_rows, *selections(), own, *arrived)


def prepare_kernel(
    fill_ref,
    cell_ref,
    send_index_ref,
    send_count_ref,
    position_hbm,
    charge_hbm,
    ion_hbm,
    start_hbm,
    screen_hbm,
    own_ref,
    masked_ref,
    inverse_ref,
    source_ref,
    *refs,
):
    out_refs, scratch = (refs[:-8], refs[-8:])
    sum_ref, deposit_ref, position_ref, charge_ref, ion_ref, start_ref, screen_ref, sems = scratch
    copies = [
        pltpu.make_async_copy(source, target, sems.at[index])
        for index, (source, target) in enumerate(
            (
                (position_hbm, position_ref),
                (charge_hbm, charge_ref),
                (ion_hbm, ion_ref),
                (start_hbm, start_ref),
                (screen_hbm, screen_ref),
            )
        )
    ]
    for copy in copies:
        copy.start()
    deposit_ref[...] = jnp.zeros_like(deposit_ref)
    copies[0].wait()
    copies[1].wait()
    clusters = charge_ref.shape[0]
    cells_x, cells_y, _ = ion_ref.shape
    slots = send_index_ref.shape[1]
    lane = lax.broadcasted_iota(jnp.int32, (1, 128), 1)
    row = lax.broadcasted_iota(jnp.int32, (4, 128), 0)

    def collect(step, _):
        for turn in range(8):
            cluster = step * 8 + turn
            masked = jnp.where(lane < fill_ref[cluster], charge_ref[pl.ds(cluster, 1), :], 0.0)
            masked_ref[pl.ds(cluster, 1), :] = masked
            place = position_ref[:, pl.ds(pl.multiple_of(cluster * 128, 128), 128)]
            own_ref[cluster, 0:3, :] = place
            own_ref[cluster, 3:4, :] = masked
        at = pl.ds(pl.multiple_of(step * 8, 8), 8)
        total = jnp.sum(masked_ref[at, :], axis=1, keepdims=True)
        sum_ref[at, :] = jnp.broadcast_to(deposit_scale * total, (8, 128))
        return 0

    lax.fori_loop(0, clusters // 8, collect, 0)

    def fill_messages(step, _):
        for direction, out_ref in enumerate(out_refs):
            parts = []
            for turn in range(2):
                slot = step * 2 + turn
                live = jnp.where(slot < send_count_ref[0, direction], 1.0, 0.0)
                value = own_ref[send_index_ref[direction, slot]]
                parts.append(jnp.where(row == 3, value * live, value))
            out_ref[pl.ds(pl.multiple_of(step * 8, 8), 8), :] = jnp.concatenate(parts, axis=0)
        return 0

    lax.fori_loop(0, slots // 2, fill_messages, 0)

    def deposit(cluster, _):
        cell = cell_ref[cluster]
        index_x = lax.shift_right_logical(cell, CELL_BITS) // cells_y
        index_y = lax.shift_right_logical(cell, CELL_BITS) % cells_y
        index_z = lax.bitwise_and(cell, 255)
        half = lax.shift_right_logical(index_z, 7)
        added = jnp.where(
            lane == lax.bitwise_and(index_z, 127), sum_ref[pl.ds(cluster, 1), :], 0.0
        )
        deposit_ref[pl.ds((index_x * 2 + half) * cells_y + index_y, 1), :] += added
        return 0

    lax.fori_loop(0, clusters, deposit, 0, unroll=4)
    for copy in copies[2:]:
        copy.wait()
    inverse_ref[...] = 1.0 / (6.0 + screen_ref[...])
    for index in range(cells_x):
        for half in range(2):
            lanes = slice(128 * half, 128 * half + 128)
            first = (index * 2 + half) * cells_y
            source_ref[index, :, lanes] = (
                ion_ref[index, :, lanes] + deposit_ref[first : first + cells_y, :]
            ) * inverse_ref[index, :, lanes]
    for out_ref, after in ((out_refs[1], True), (out_refs[2], False)):
        for index in range(cells_x):
            base = slots * 4 + index * 32
            offset = 0
            for field_ref, width in zip(
                (start_ref, inverse_ref, source_ref, ion_ref), HALO_WIDTHS, strict=True
            ):
                first = cells_y - width if after else 0
                rows = field_ref[index, first : first + width, :]
                for half in range(2):
                    out_ref[base + 16 * half + offset : base + 16 * half + offset + width, :] = (
                        rows[:, 128 * half : 128 * half + 128]
                    )
                offset += width
            for half in range(2):
                out_ref[base + 16 * half + offset : base + 16 * half + 16, :] = jnp.zeros(
                    (16 - offset, 128), jnp.float32
                )


def prepare(fill, cell, send_index, send_count, positions, charges, ions, start, screen):
    clusters = charges.shape[0]
    directions, slots = send_index.shape
    cells_x = ions.shape[0]
    smem = pl.BlockSpec(memory_space=pltpu.SMEM)
    vmem = pl.BlockSpec(memory_space=pltpu.VMEM)
    rows = [slots * 4] * directions
    rows[1] = rows[2] = slots * 4 + cells_x * 32
    return pl.pallas_call(
        prepare_kernel,
        out_shape=(
            jax.ShapeDtypeStruct((clusters, 4, 128), jnp.float32),
            jax.ShapeDtypeStruct((clusters, 128), jnp.float32),
            jax.ShapeDtypeStruct(ions.shape, jnp.float32),
            jax.ShapeDtypeStruct(ions.shape, jnp.float32),
            *[jax.ShapeDtypeStruct((count, 128), jnp.float32) for count in rows],
        ),
        in_specs=[smem] * 4 + [pl.BlockSpec(memory_space=pltpu.HBM)] * 5,
        out_specs=(vmem,) * (4 + directions),
        scratch_shapes=[
            pltpu.VMEM((clusters, 128), jnp.float32),
            pltpu.VMEM((ions.size // 128, 128), jnp.float32),
            *[
                pltpu.VMEM(operand.shape, jnp.float32)
                for operand in (positions, charges, ions, start, screen)
            ],
            pltpu.SemaphoreType.DMA((5,)),
        ],
        compiler_params=pltpu.CompilerParams(vmem_limit_bytes=60 * 1024 * 1024),
        name="prepare",
    )(fill, cell, send_index, send_count, positions, charges, ions, start, screen)


def put_extended(target_ref, plane, field, field_ref, index, before_ref, after_ref, base):
    cells_y = field_ref.shape[1]
    width = HALO_WIDTHS[field]
    offset = sum(HALO_WIDTHS[:field])
    target_ref[plane, MARGIN : MARGIN + cells_y, :] = field_ref[index]
    for half in range(2):
        lanes = slice(128 * half, 128 * half + 128)
        first = base + index * 32 + 16 * half + offset
        target_ref[plane, MARGIN - width : MARGIN, lanes] = before_ref[first : first + width, :]
        target_ref[plane, MARGIN + cells_y : MARGIN + cells_y + width, lanes] = after_ref[
            first : first + width, :
        ]


def planes_kernel(base, *refs):
    field_refs, (before_ref, after_ref, down_ref, up_ref) = (refs[:4], refs[4:])
    cells_x = field_refs[0].shape[0]
    down_ref[...] = jnp.zeros_like(down_ref)
    up_ref[...] = jnp.zeros_like(up_ref)
    plane = 0
    for field, width in enumerate(HALO_WIDTHS):
        for index in range(width):
            for target_ref, source in ((down_ref, index), (up_ref, cells_x - width + index)):
                put_extended(
                    target_ref, plane, field, field_refs[field], source, before_ref, after_ref, base
                )
            plane += 1


def planes(fields, before, after, base):
    vmem = pl.BlockSpec(memory_space=pltpu.VMEM)
    _, cells_y, cells_z = fields[0].shape
    shape = jax.ShapeDtypeStruct((sum(HALO_WIDTHS), cells_y + 2 * MARGIN, cells_z), jnp.float32)
    return pl.pallas_call(
        functools.partial(planes_kernel, base),
        out_shape=(shape, shape),
        in_specs=[vmem] * 6,
        out_specs=(vmem, vmem),
        compiler_params=pltpu.CompilerParams(vmem_limit_bytes=32 * 1024 * 1024),
        name="planes",
    )(*fields, before, after)


def face_flux(pot_low, pot_high, ion_low, ion_high):
    speed = -mobility * (pot_high - pot_low)
    return (
        jnp.maximum(speed, 0.0) * ion_low
        + jnp.minimum(speed, 0.0) * ion_high
        - diffusion * (ion_high - ion_low)
    )


def grid_kernel(base, *refs):
    cell_ref, masked_ref = refs[:2]
    field_refs = refs[2:6]
    before_ref, after_ref, lower_ref, upper_ref = refs[6:10]
    potential_ref, next_ref, force_ref = refs[10:13]
    start_ref, inverse_ref, resid_ref, ion_ref, update_ref, line_ref, *pick_refs = refs[13:]
    cells_x, cells_y, cells_z = field_refs[0].shape
    rows = cells_y + 2 * MARGIN
    depth = HALO_WIDTHS[0]
    clusters = masked_ref.shape[0]
    lane = lax.broadcasted_iota(jnp.int32, (rows, cells_z), 1)
    middle = 0.5 * (highest_eig + lowest_eig)
    spread = 0.5 * (highest_eig - lowest_eig)

    plane = 0
    for field, target_ref in enumerate((start_ref, inverse_ref, resid_ref, ion_ref)):
        width = HALO_WIDTHS[field]
        if field == 0 or field == 3:
            target_ref[...] = jnp.zeros_like(target_ref)
        else:
            target_ref[depth : depth + cells_x, 0:MARGIN, :] = jnp.zeros(
                (cells_x, MARGIN, cells_z), jnp.float32
            )
            target_ref[depth : depth + cells_x, rows - MARGIN : rows, :] = jnp.zeros(
                (cells_x, MARGIN, cells_z), jnp.float32
            )
        for index in range(width):
            target_ref[depth - width + index] = lower_ref[plane + index]
            target_ref[depth + cells_x + index] = upper_ref[plane + index]
        for index in range(cells_x):
            put_extended(
                target_ref,
                depth + index,
                field,
                field_refs[field],
                index,
                before_ref,
                after_ref,
                base,
            )
        plane += width

    def above(value):
        return jnp.where(lane == cells_z - 1, 0.0, pltpu.roll(value, cells_z - 1, 1))

    def below(value):
        return jnp.where(lane == 0, 0.0, pltpu.roll(value, 1, 1))

    def beside(value):
        rolled = pltpu.roll(value, 1, 0) + pltpu.roll(value, rows - 1, 0)
        return rolled + (above(value) + below(value))

    def first_sweep(index, planes):
        last, here = planes
        after = start_ref[index + 1]
        resid = (
            resid_ref[index] - here + inverse_ref[index] * ((last + after) + beside(here))
        )
        resid_ref[index] = resid
        update_ref[index] = resid / middle
        return (here, after)

    lax.fori_loop(1, cells_x + 2 * depth - 1, first_sweep, (start_ref[0], start_ref[1]))

    ratio_ms = middle / spread
    weight_now = 1.0 / ratio_ms
    for turn in range(1, SWEEPS):
        weight_next = 1.0 / (2.0 * ratio_ms - weight_now)
        keep, gain = (weight_next * weight_now, 2.0 * weight_next / spread)
        weight_now = weight_next

        def sweep(index, planes, turn=turn, keep=keep, gain=gain):
            last, here = planes
            after = update_ref[index + 1]
            resid = resid_ref[index] - here + inverse_ref[index] * ((last + after) + beside(here))
            update = keep * here + gain * resid
            if turn == 1:
                start_ref[index] = start_ref[index] + here + update
            else:
                start_ref[index] = start_ref[index] + update
            if turn + 1 < SWEEPS:
                resid_ref[index] = resid
                update_ref[index] = update
            return (here, after)

        first = 1 + turn
        lax.fori_loop(
            first,
            cells_x + 2 * depth - first,
            sweep,
            (update_ref[first - 1], update_ref[first]),
        )

    def upper_flux(index):
        return face_flux(start_ref[index], start_ref[index + 1], ion_ref[index], ion_ref[index + 1])

    inner = slice(MARGIN, MARGIN + cells_y)

    def advance(index, lower):
        pot = start_ref[depth + index]
        ions = ion_ref[depth + index]
        upper = upper_flux(depth + index)
        along_y = face_flux(pot, pltpu.roll(pot, rows - 1, 0), ions, pltpu.roll(ions, rows - 1, 0))
        along_z = face_flux(pot, above(pot), ions, above(ions))
        first_z = face_flux(0.0, pot, 0.0, ions)
        total = upper - lower
        total = total + (along_y - pltpu.roll(along_y, 1, 0))
        total = total + (along_z - jnp.where(lane == 0, first_z, pltpu.roll(along_z, 1, 1)))
        next_ref[index] = (ions - time_step * total)[inner]
        potential_ref[index] = pot[inner]
        return upper

    lax.fori_loop(0, cells_x, advance, upper_flux(depth - 1))
    for index in range(cells_x + 2):
        for half in range(2):
            line_ref[pl.ds((index * 2 + half) * rows, rows), :] = start_ref[
                depth - 1 + index, :, 128 * half : 128 * half + 128
            ]

    row_lane = lax.broadcasted_iota(jnp.int32, (1, 128), 1)

    def pick(cluster, _):
        cell = cell_ref[cluster]
        index_x = lax.shift_right_logical(cell, CELL_BITS) // cells_y + 1
        index_y = lax.shift_right_logical(cell, CELL_BITS) % cells_y + MARGIN
        index_z = lax.bitwise_and(cell, 255)
        half = lax.shift_right_logical(index_z, 7)
        here = row_lane == lax.bitwise_and(index_z, 127)

        def line(plane, row, part):
            return line_ref[pl.ds((plane * 2 + part) * rows + row, 1), :]

        along_x = line(index_x - 1, index_y, half) - line(index_x + 1, index_y, half)
        along_y = line(index_x, index_y - 1, half) - line(index_x, index_y + 1, half)
        along_z = jnp.zeros((1, 128), jnp.float32)
        for part in range(cells_z // 128):
            value = line(index_x, index_y, part)
            place = row_lane + 128 * part
            along_z = along_z + jnp.where(place == index_z - 1, value, 0.0)
            along_z = along_z - jnp.where(place == index_z + 1, value, 0.0)
        at = pl.ds(cluster, 1)
        pick_refs[0][at, :] = jnp.where(here, along_x, 0.0)
        pick_refs[1][at, :] = jnp.where(here, along_y, 0.0)
        pick_refs[2][at, :] = along_z
        return 0

    lax.fori_loop(0, clusters, pick, 0, unroll=4)

    def spread_out(step, _):
        start = pl.multiple_of(step * 8, 8)
        charge = masked_ref[pl.ds(start, 8), :] * (0.5 * field_scale)
        for part, pick_ref in enumerate(pick_refs):
            total = jnp.sum(pick_ref[pl.ds(start, 8), :], axis=1, keepdims=True)
            force_ref[pl.ds(4 * start + part, 8, stride=4), :] = charge * total
        force_ref[pl.ds(4 * start + 3, 8, stride=4), :] = jnp.zeros((8, 128), jnp.float32)
        return 0

    lax.fori_loop(0, clusters // 8, spread_out, 0)


def grid_step(cell, masked, fields, before, after, lower, upper, base):
    smem = pl.BlockSpec(memory_space=pltpu.SMEM)
    vmem = pl.BlockSpec(memory_space=pltpu.VMEM)
    clusters = masked.shape[0]
    cells_x, cells_y, cells_z = fields[0].shape
    block = (cells_x + 2 * HALO_WIDTHS[0], cells_y + 2 * MARGIN, cells_z)
    return pl.pallas_call(
        functools.partial(grid_kernel, base),
        out_shape=(
            jax.ShapeDtypeStruct(fields[0].shape, jnp.float32),
            jax.ShapeDtypeStruct(fields[0].shape, jnp.float32),
            jax.ShapeDtypeStruct((clusters * 4, 128), jnp.float32),
        ),
        in_specs=[smem] + [vmem] * 9,
        out_specs=(vmem,) * 3,
        scratch_shapes=[pltpu.VMEM(block, jnp.float32)] * 5
        + [pltpu.VMEM(((cells_x + 2) * 2 * block[1], 128), jnp.float32)]
        + [pltpu.VMEM((clusters, 128), jnp.float32)] * 3,
        compiler_params=pltpu.CompilerParams(vmem_limit_bytes=40 * 1024 * 1024),
        cost_estimate=pl.CostEstimate(
            flops=block[0] * block[1] * block[2] * 100, bytes_accessed=8 << 20, transcendentals=0
        ),
        name="grid_step",
    )(cell, masked, *fields, before, after, lower, upper)


def gather_forces_kernel(send_index_ref, own_ref, field_ref, *refs):
    back_refs, (out_ref, sum_ref) = (refs[:-2], refs[-2:])
    clusters = own_ref.shape[0]
    slots = send_index_ref.shape[1]
    sum_ref[...] = own_ref[...] + field_ref[...]

    def visit(slot, _):
        for direction, back_ref in enumerate(back_refs):
            cluster = send_index_ref[direction, slot]
            sum_ref[cluster] += back_ref[slot]
        return 0

    lax.fori_loop(0, slots, visit, 0)

    def write(step, _):
        for turn in range(8):
            cluster = step * 8 + turn
            out_ref[:, pl.ds(pl.multiple_of(cluster * 128, 128), 128)] = sum_ref[cluster][0:3]
        return 0

    lax.fori_loop(0, clusters // 8, write, 0)


def gather_forces(send_index, own, field, backs):
    smem = pl.BlockSpec(memory_space=pltpu.SMEM)
    vmem = pl.BlockSpec(memory_space=pltpu.VMEM)
    clusters = own.shape[0]
    return pl.pallas_call(
        gather_forces_kernel,
        out_shape=jax.ShapeDtypeStruct((3, clusters * 128), jnp.float32),
        in_specs=[smem] + [vmem] * (2 + len(backs)),
        out_specs=vmem,
        scratch_shapes=[pltpu.VMEM(own.shape, jnp.float32)],
        compiler_params=pltpu.CompilerParams(vmem_limit_bytes=32 * 1024 * 1024),
        name="gather_forces",
    )(send_index, own, field, *backs)


def passed_along(shard, axis, by):
    devices = lax.axis_size(axis)
    pairs = [(i, i + by) for i in range(devices) if 0 <= i + by < devices]
    return lax.ppermute(shard, axis, pairs)


ROUTES = (("brick", 1), ("brick", -1), ("brick", 2), ("brick", -2), ("grp", 1), ("grp", -1))


def shards(
    positions,
    charges,
    cluster_fill,
    cluster_cell,
    send_index,
    send_count,
    pair_local,
    pair_dir,
    pair_slot,
    ion_density,
    potential_prev,
    screening,
):
    clusters = cluster_fill.shape[0]
    psize = charges.shape[0] // clusters
    slots = send_index.shape[1]
    base = slots * 4
    own, masked, inverse, source, local, *messages = prepare(
        cluster_fill,
        cluster_cell,
        send_index,
        send_count,
        positions,
        charges.reshape(clusters, psize),
        ion_density,
        potential_prev,
        screening,
    )
    arrived = [local] + [
        passed_along(message, axis, by)
        for message, (axis, by) in zip(messages, ROUTES, strict=True)
    ]
    fields = (potential_prev, inverse, source, ion_density)
    arrived = lax.optimization_barrier(arrived)
    before, after = arrived[1:3]
    down, up = planes(fields, before, after, base)
    lower = passed_along(up, "grp", 1)
    upper = passed_along(down, "grp", -1)
    own_force, *reactions = pair_forces(
        pair_local,
        pair_dir * slots + pair_slot,
        own.reshape(clusters * 4, psize),
        arrived,
        slots,
    )
    backs = [reactions[0]] + [
        passed_along(reaction, axis, -by)
        for reaction, (axis, by) in zip(reactions[1:], ROUTES, strict=True)
    ]
    potential, ion_next, field_force = grid_step(
        cluster_cell, masked, fields, before, after, lower, upper, base
    )
    forces = gather_forces(
        send_index,
        own_force.reshape(clusters, 4, psize),
        field_force.reshape(clusters, 4, psize),
        [back.reshape(slots, 4, psize) for back in backs],
    )
    return (forces, potential, ion_next)


def solution(mesh):
    in_specs = (
        P(None, ("grp", "brick")),
        P(("grp", "brick")),
        P(("grp", "brick")),
        P(("grp", "brick")),
        P(("grp", "brick"), None),
        P(("grp", "brick"), None),
        P(("grp", "brick")),
        P(("grp", "brick")),
        P(("grp", "brick")),
        P("grp", "brick", None),
        P("grp", "brick", None),
        P("grp", "brick", None),
    )
    out_specs = (P(None, ("grp", "brick")), P("grp", "brick", None), P("grp", "brick", None))
    return jax.shard_map(shards, mesh=mesh, in_specs=in_specs, out_specs=out_specs, check_vma=False)
```

```python
import functools

import jax
import jax.numpy as jnp
import numpy as np
from jax import lax
from jax.experimental import pallas as pl
from jax.experimental.pallas import tpu as pltpu
from jax.sharding import PartitionSpec as P

SWEEPS = 4
QUAD = 4
UNROLL = 8
HALO_WIDTHS = (SWEEPS + 1, SWEEPS, SWEEPS, 1)
DEPTH = SWEEPS + 1
CELL_BITS = 8


coulomb_scale = 0.02
softening = 0.1
field_scale = 0.5
deposit_scale = 0.2
lowest_eig = 0.01
highest_eig = 1.99
mobility = 0.3
diffusion = 0.2
time_step = 0.2


def split3(value):
    first = value.astype(jnp.bfloat16).astype(jnp.float32)
    rest = value - first
    second = rest.astype(jnp.bfloat16).astype(jnp.float32)
    third = (rest - second).astype(jnp.bfloat16).astype(jnp.float32)
    return (first, second, third)


def moment_pieces(comps, charge):
    rows = [None] * 12
    for part, charged in enumerate((*comps, None)):
        for level, piece in enumerate(split3(charge if charged is None else charge * charged)):
            rows[4 * level + part] = piece
    return rows


def selections():
    near_kinds, far_kinds = ([], [])
    for part in range(3):
        near_kinds += [3 * part + level for level in (0, 0, 0, 1, 1, 2)]
        far_kinds += [3 * part + level for level in (0, 1, 2, 0, 1, 0)]
    near_kinds += [9, 10, 11, 12, 12, 12]
    far_kinds += [12, 12, 12, 9, 10, 11]
    near = np.zeros((128, 1024), np.float32)
    far = np.zeros((256, 128), np.float32)
    moment = np.zeros((128, 128), np.float32)
    for cluster in range(8):
        for index, kind in enumerate(near_kinds):
            near[kind * 8 + cluster, cluster * 128 + index] = 1.0
        for index, kind in enumerate(far_kinds):
            far[cluster * 32 + index, kind * 8 + cluster] = 1.0
        for kind in range(12):
            moment[cluster * 16 + kind, kind * 8 + cluster] = 1.0
    return tuple(jnp.asarray(part, jnp.bfloat16) for part in (near, far, moment))


def pair_kernel(own_rows_ref, other_rows_ref, *refs):
    near_sel_ref, far_sel_ref, moment_sel_ref, own_ref = refs[:4]
    refs = refs[4:]
    sources = (len(refs) - 11) // 2
    other_refs = refs[:sources]
    own_out_ref = refs[sources]
    other_out_refs = refs[sources + 1 : 2 * sources + 1]
    (
        near_ref,
        far_ref,
        own_moment_ref,
        other_moment_ref,
        own_sum_ref,
        other_sum_ref,
        *passed_refs,
    ) = refs[2 * sources + 1 :]
    clusters = own_ref.shape[0] // 4
    slots = other_out_refs[0].shape[0] // 4
    others = slots * sources
    groups = own_rows_ref.shape[0] // UNROLL
    units = UNROLL // QUAD
    ones = jnp.ones((8, 128), jnp.float32)
    zeros = jnp.zeros((8, 128), jnp.float32)

    def components(data_ref, start):
        return [data_ref[pl.ds(4 * start + part, 8, stride=4), :] for part in range(4)]

    def place_pieces(comps, factor, offset):
        pieces = []
        square = zeros
        for comp in comps:
            square = square + comp * comp
            pieces += split3(factor * comp)
        pieces += [*split3(square + offset), ones]
        return jnp.concatenate(pieces + [zeros] * (16 - len(pieces)), axis=0)

    def selected(left, right):
        return jnp.dot(
            left.astype(jnp.bfloat16), right, preferred_element_type=jnp.float32
        ).astype(jnp.bfloat16)

    def near_rows(step, _):
        start = pl.multiple_of(step * 8, 8)
        *comps, charge = components(own_ref, start)
        moments = jnp.concatenate(moment_pieces(comps, charge) + [zeros] * 4, axis=0)
        own_moment_ref[pl.ds(pl.multiple_of(start * 16, 128), 128), :] = selected(
            moment_sel_ref[...], moments.astype(jnp.bfloat16)
        )
        tiles = selected(place_pieces(comps, 1.0, 0.0).T, near_sel_ref[...])
        for index in range(8):
            at = pl.ds(pl.multiple_of((start + index) * 128, 128), 128)
            near_ref[at, :] = tiles[:, 128 * index : 128 * index + 128]
        return 0

    def far_rows(source, step, _):
        local = pl.multiple_of(step * 8, 8)
        start = source * slots + local
        *comps, charge = components(other_refs[source], local)
        far_ref[pl.ds(pl.multiple_of(start * 32, 256), 256), :] = selected(
            far_sel_ref[...], place_pieces(comps, -2.0, softening).astype(jnp.bfloat16)
        )
        moments = jnp.concatenate(moment_pieces(comps, charge) + [zeros] * 4, axis=0)
        other_moment_ref[pl.ds(pl.multiple_of(start * 16, 128), 128), :] = selected(
            moment_sel_ref[...], moments.astype(jnp.bfloat16)
        )
        return 0

    lax.fori_loop(0, clusters // 8, near_rows, 0, unroll=4)
    for source in range(sources):
        lax.fori_loop(0, slots // 8, functools.partial(far_rows, source), 0, unroll=4)
    own_sum_ref[...] = jnp.zeros_like(own_sum_ref)
    other_sum_ref[...] = jnp.zeros_like(other_sum_ref)
    dist_refs, weight_refs = (passed_refs[:2], passed_refs[2:])
    dist_refs[0][...] = jnp.full(dist_refs[0].shape, 1e38, jnp.float32)
    weight_refs[0][...] = jnp.zeros_like(weight_refs[0])

    def block_diagonal(blocks):
        blank = jnp.zeros_like(blocks[0])
        lines = [
            jnp.concatenate(
                [block if turn == at else blank for turn in range(len(blocks))], axis=1
            )
            for at, block in enumerate(blocks)
        ]
        return jnp.concatenate(lines, axis=0)

    def distances(pair, unit, dist_ref):
        for turn in range(QUAD):
            own = own_rows_ref[pair + turn]
            other = other_rows_ref[pair + turn]
            dist_ref[unit, :, 128 * turn : 128 * turn + 128] = jnp.dot(
                near_ref[pl.ds(pl.multiple_of(own * 128, 128), 128), 0:32],
                far_ref[pl.ds(pl.multiple_of(other * 32, 32), 32), :],
                preferred_element_type=jnp.float32,
            )

    def weights(unit, turn, dist_ref, weight_ref):
        root = lax.rsqrt(dist_ref[unit, :, 128 * turn : 128 * turn + 128])
        weight = root * root * root
        high = weight.astype(jnp.bfloat16)
        weight_ref[unit, 128 * turn : 128 * turn + 128, :128] = high
        weight_ref[unit, 128 * turn : 128 * turn + 128, 128:] = (
            weight - high.astype(jnp.float32)
        ).astype(jnp.bfloat16)

    def moments_of(moment_ref, indices):
        return block_diagonal(
            [moment_ref[pl.ds(pl.multiple_of(index * 16, 16), 16), :] for index in indices]
        )

    def products(pair, unit, weight_ref):
        owns = [own_rows_ref[pair + turn] for turn in range(QUAD)]
        others = [other_rows_ref[pair + turn] for turn in range(QUAD)]
        both = weight_ref[unit]
        levels = [
            jnp.concatenate(
                [both[128 * turn : 128 * turn + 128, lanes] for turn in range(QUAD)], axis=1
            )
            for lanes in (slice(0, 128), slice(128, 256))
        ]
        to_own = lax.dot_general(
            moments_of(other_moment_ref, others),
            jnp.concatenate(levels, axis=0),
            (((1,), (1,)), ((), ())),
            preferred_element_type=jnp.float32,
        )
        to_other = jnp.dot(
            moments_of(own_moment_ref, owns), both, preferred_element_type=jnp.float32
        )
        return (owns, others, *(part[:, :128] + part[:, 128:] for part in (to_own, to_other)))

    def half_step(step, side):
        last = jnp.maximum(step - 2, 0) * UNROLL
        first = jnp.minimum(step, groups - 1) * UNROLL
        results = [products(last + QUAD * unit, unit, weight_refs[side]) for unit in range(units)]
        for unit in range(units):
            for turn in range(QUAD):
                weights(unit, turn, dist_refs[side], weight_refs[1 - side])
        for unit in range(units):
            distances(first + QUAD * unit, unit, dist_refs[1 - side])
        for owns, others, to_own, to_other in results:
            for turn in range(QUAD):
                own_at = pl.ds(pl.multiple_of(owns[turn] * 16, 16), 16)
                other_at = pl.ds(pl.multiple_of(others[turn] * 16, 16), 16)
                own_sum_ref[own_at, :] += to_own[16 * turn : 16 * turn + 16]
                other_sum_ref[other_at, :] += to_other[16 * turn : 16 * turn + 16]

    def visit(step, _):
        for side in range(2):
            half_step(step * 2 + side, side)
        return 0

    lax.fori_loop(0, (groups + 2) // 2, visit, 0)

    def finish(data_ref, out_ref, sum_ref, base, step, _):
        start = pl.multiple_of(step * 8, 8)
        *comps, charge = components(data_ref, start)

        def total(part):
            terms = [
                sum_ref[pl.ds(base + start * 16 + 4 * level + part, 8, stride=16), :]
                for level in range(3)
            ]
            return terms[0] + (terms[1] + terms[2])

        weight = total(3)
        scale = coulomb_scale * charge
        for part, comp in enumerate(comps):
            out_ref[pl.ds(4 * start + part, 8, stride=4), :] = scale * (comp * weight - total(part))
        out_ref[pl.ds(4 * start + 3, 8, stride=4), :] = zeros
        return 0

    lax.fori_loop(
        0, clusters // 8, functools.partial(finish, own_ref, own_out_ref, own_sum_ref, 0), 0, unroll=4
    )
    for source in range(sources):
        body = functools.partial(
            finish,
            other_refs[source],
            other_out_refs[source],
            other_sum_ref,
            source * slots * 16,
        )
        lax.fori_loop(0, slots // 8, body, 0, unroll=4)


def pair_forces(own_rows, other_rows, own, arrived, slots):
    clusters = own.shape[0] // 4
    others = slots * len(arrived)
    pairs = own_rows.shape[0]
    smem = pl.BlockSpec(memory_space=pltpu.SMEM)
    vmem = pl.BlockSpec(memory_space=pltpu.VMEM)
    return pl.pallas_call(
        pair_kernel,
        out_shape=(
            jax.ShapeDtypeStruct(own.shape, jnp.float32),
            *[jax.ShapeDtypeStruct((slots * 4, 128), jnp.float32)] * len(arrived),
        ),
        in_specs=[smem, smem] + [vmem] * (4 + len(arrived)),
        out_specs=(vmem,) * (len(arrived) + 1),
        scratch_shapes=[
            pltpu.VMEM((clusters * 128, 128), jnp.bfloat16),
            pltpu.VMEM((others * 32, 128), jnp.bfloat16),
            pltpu.VMEM((clusters * 16, 128), jnp.bfloat16),
            pltpu.VMEM((others * 16, 128), jnp.bfloat16),
            pltpu.VMEM((clusters * 16, 128), jnp.float32),
            pltpu.VMEM((others * 16, 128), jnp.float32),
            *[pltpu.VMEM((UNROLL // QUAD, 128, 128 * QUAD), jnp.float32)] * 2,
            *[pltpu.VMEM((UNROLL // QUAD, 128 * QUAD, 256), jnp.bfloat16)] * 2,
        ],
        compiler_params=pltpu.CompilerParams(vmem_limit_bytes=40 * 1024 * 1024),
        cost_estimate=pl.CostEstimate(
            flops=pairs * 128 * 128 * 20, bytes_accessed=4 * 1024 * 1024, transcendentals=0
        ),
        name="pair_forces",
    )(own_rows, other_rows, *selections(), own, *arrived)


def prepare_kernel(
    fill_ref,
    cell_ref,
    send_index_ref,
    send_count_ref,
    cell_row_ref,
    position_hbm,
    charge_hbm,
    ion_hbm,
    start_hbm,
    screen_hbm,
    own_ref,
    masked_ref,
    inverse_ref,
    source_ref,
    *refs,
):
    out_refs, scratch = (refs[:-8], refs[-8:])
    sum_ref, deposit_ref, position_ref, charge_ref, ion_ref, start_ref, screen_ref, sems = scratch
    copies = [
        pltpu.make_async_copy(source, target, sems.at[index])
        for index, (source, target) in enumerate(
            (
                (position_hbm, position_ref),
                (charge_hbm, charge_ref),
                (ion_hbm, ion_ref),
                (start_hbm, start_ref),
                (screen_hbm, screen_ref),
            )
        )
    ]
    for copy in copies:
        copy.start()
    copies[0].wait()
    copies[1].wait()
    clusters = charge_ref.shape[0]
    cells_x, cells_y, _ = ion_ref.shape
    slots = send_index_ref.shape[1]
    lane = lax.broadcasted_iota(jnp.int32, (1, 128), 1)
    row = lax.broadcasted_iota(jnp.int32, (4, 128), 0)

    def collect(step, _):
        for turn in range(8):
            cluster = step * 8 + turn
            masked = jnp.where(lane < fill_ref[cluster], charge_ref[pl.ds(cluster, 1), :], 0.0)
            masked_ref[pl.ds(cluster, 1), :] = masked
            place = position_ref[:, pl.ds(pl.multiple_of(cluster * 128, 128), 128)]
            own_ref[cluster, 0:3, :] = place
            own_ref[cluster, 3:4, :] = masked
        at = pl.ds(pl.multiple_of(step * 8, 8), 8)
        total = jnp.sum(masked_ref[at, :], axis=1, keepdims=True)
        sum_ref[at, :] = jnp.broadcast_to(deposit_scale * total, (8, 128))
        return 0

    lax.fori_loop(0, clusters // 8, collect, 0, unroll=4)

    def fill_messages(step, _):
        for direction, out_ref in enumerate(out_refs):
            parts = []
            for turn in range(2):
                slot = step * 2 + turn
                live = jnp.where(slot < send_count_ref[0, direction], 1.0, 0.0)
                value = own_ref[send_index_ref[direction, slot]]
                parts.append(jnp.where(row == 3, value * live, value))
            out_ref[pl.ds(pl.multiple_of(step * 8, 8), 8), :] = jnp.concatenate(parts, axis=0)
        return 0

    lax.fori_loop(0, slots // 2, fill_messages, 0)

    def place(step, _):
        for turn in range(8):
            cluster = step * 8 + turn
            index_z = lax.bitwise_and(cell_ref[cluster], 127)
            at = pl.ds(cluster, 1)
            sum_ref[at, :] = jnp.where(lane == index_z, sum_ref[at, :], 0.0)
        return 0

    lax.fori_loop(0, clusters // 8, place, 0)
    cell = cell_row_ref[...]
    line = lax.shift_right_logical(cell, CELL_BITS)
    line = (line // cells_y * 2 + lax.shift_right_logical(lax.bitwise_and(cell, 255), 7)) * cells_y
    line = line + lax.shift_right_logical(cell, CELL_BITS) % cells_y
    sums = jnp.concatenate([part.astype(jnp.bfloat16) for part in split3(sum_ref[...])], axis=1)
    block = 128
    for first in range(0, deposit_ref.shape[0], block):
        rows = lax.broadcasted_iota(jnp.int32, (block, clusters), 0) + first
        hot = jnp.where(rows == line, 1.0, 0.0).astype(jnp.bfloat16)
        added = jnp.dot(hot, sums, preferred_element_type=jnp.float32)
        deposit_ref[first : first + block, :] = added[:, :128] + (
            added[:, 128:256] + added[:, 256:]
        )
    for copy in copies[2:]:
        copy.wait()
    inverse_ref[...] = 1.0 / (6.0 + screen_ref[...])
    for index in range(cells_x):
        for half in range(2):
            lanes = slice(128 * half, 128 * half + 128)
            first = (index * 2 + half) * cells_y
            source_ref[index, :, lanes] = (
                ion_ref[index, :, lanes] + deposit_ref[first : first + cells_y, :]
            ) * inverse_ref[index, :, lanes]
    for out_ref, after in ((out_refs[1], True), (out_refs[2], False)):
        for index in range(cells_x):
            base = slots * 4 + index * 32
            offset = 0
            for field_ref, width in zip(
                (start_ref, inverse_ref, source_ref, ion_ref), HALO_WIDTHS, strict=True
            ):
                first = cells_y - width if after else 0
                rows = field_ref[index, first : first + width, :]
                for half in range(2):
                    out_ref[base + 16 * half + offset : base + 16 * half + offset + width, :] = (
                        rows[:, 128 * half : 128 * half + 128]
                    )
                offset += width
            for half in range(2):
                out_ref[base + 16 * half + offset : base + 16 * half + 16, :] = jnp.zeros(
                    (16 - offset, 128), jnp.float32
                )


def prepare(fill, cell, send_index, send_count, positions, charges, ions, start, screen):
    clusters = charges.shape[0]
    directions, slots = send_index.shape
    cells_x = ions.shape[0]
    smem = pl.BlockSpec(memory_space=pltpu.SMEM)
    vmem = pl.BlockSpec(memory_space=pltpu.VMEM)
    rows = [slots * 4] * directions
    rows[1] = rows[2] = slots * 4 + cells_x * 32
    return pl.pallas_call(
        prepare_kernel,
        out_shape=(
            jax.ShapeDtypeStruct((clusters, 4, 128), jnp.float32),
            jax.ShapeDtypeStruct((clusters, 128), jnp.float32),
            jax.ShapeDtypeStruct(ions.shape, jnp.float32),
            jax.ShapeDtypeStruct(ions.shape, jnp.float32),
            *[jax.ShapeDtypeStruct((count, 128), jnp.float32) for count in rows],
        ),
        in_specs=[smem] * 4 + [vmem] + [pl.BlockSpec(memory_space=pltpu.HBM)] * 5,
        out_specs=(vmem,) * (4 + directions),
        scratch_shapes=[
            pltpu.VMEM((clusters, 128), jnp.float32),
            pltpu.VMEM((ions.size // 128, 128), jnp.float32),
            *[
                pltpu.VMEM(operand.shape, jnp.float32)
                for operand in (positions, charges, ions, start, screen)
            ],
            pltpu.SemaphoreType.DMA((5,)),
        ],
        compiler_params=pltpu.CompilerParams(vmem_limit_bytes=60 * 1024 * 1024),
        name="prepare",
    )(
        fill,
        cell,
        send_index,
        send_count,
        cell.reshape(1, clusters),
        positions,
        charges,
        ions,
        start,
        screen,
    )


def line_rows(cells_y):
    return (cells_y + 2 * DEPTH + 7) // 8 * 8


def fill_lines(target_ref, plane, field, field_ref, index, before_ref, after_ref, base):
    cells_y = field_ref.shape[1]
    width = HALO_WIDTHS[field]
    for half in range(2):
        at = (plane * 2 + half) * line_rows(cells_y) + DEPTH
        first = base + index * 32 + 16 * half + sum(HALO_WIDTHS[:field])
        target_ref[pl.ds(at - width, width), :] = before_ref[pl.ds(first, width), :]
        target_ref[pl.ds(at, cells_y), :] = field_ref[index, :, 128 * half : 128 * half + 128]
        target_ref[pl.ds(at + cells_y, width), :] = after_ref[pl.ds(first, width), :]


def planes_kernel(base, *refs):
    field_refs, (before_ref, after_ref, down_ref, up_ref) = (refs[:4], refs[4:])
    cells_x = field_refs[0].shape[0]
    for field, width in enumerate(HALO_WIDTHS):
        plane = sum(HALO_WIDTHS[:field])

        def fill(step, _, field=field, plane=plane, width=width):
            for target_ref, source in ((down_ref, step), (up_ref, cells_x - width + step)):
                fill_lines(
                    target_ref,
                    plane + step,
                    field,
                    field_refs[field],
                    source,
                    before_ref,
                    after_ref,
                    base,
                )
            return 0

        lax.fori_loop(0, width, fill, 0)


def planes(fields, before, after, base):
    vmem = pl.BlockSpec(memory_space=pltpu.VMEM)
    rows = sum(HALO_WIDTHS) * 2 * line_rows(fields[0].shape[1])
    shape = jax.ShapeDtypeStruct((rows, 128), jnp.float32)
    return pl.pallas_call(
        functools.partial(planes_kernel, base),
        out_shape=(shape, shape),
        in_specs=[vmem] * 6,
        out_specs=(vmem, vmem),
        compiler_params=pltpu.CompilerParams(vmem_limit_bytes=32 * 1024 * 1024),
        name="planes",
    )(*fields, before, after)


def face_flux(pot_low, pot_high, ion_low, ion_high):
    speed = -mobility * (pot_high - pot_low)
    return (
        jnp.maximum(speed, 0.0) * ion_low
        + jnp.minimum(speed, 0.0) * ion_high
        - diffusion * (ion_high - ion_low)
    )


def grid_kernel(base, *refs):
    cell_ref, masked_ref = refs[:2]
    field_refs = refs[2:6]
    before_ref, after_ref, lower_ref, upper_ref = refs[6:10]
    potential_ref, next_ref, force_ref = refs[10:13]
    start_ref, inverse_ref, source_ref, ion_ref = refs[13:17]
    updates, resids, final_ref, pick_refs = (refs[17:20], refs[20:22], refs[22], refs[23:26])
    cells_x, cells_y, _ = field_refs[0].shape
    rows = line_rows(cells_y)
    inner = cells_y + 2 * DEPTH - 2
    clusters = masked_ref.shape[0]

    for field, target_ref in enumerate((start_ref, inverse_ref, source_ref, ion_ref)):
        width = HALO_WIDTHS[field]
        size = width * 2 * rows
        first = sum(HALO_WIDTHS[:field]) * 2 * rows
        low = (DEPTH - width) * 2 * rows
        high = (DEPTH + cells_x) * 2 * rows
        target_ref[low : low + size, :] = lower_ref[first : first + size, :]
        target_ref[high : high + size, :] = upper_ref[first : first + size, :]

    def fill(index, _):
        for field, target_ref in enumerate((start_ref, inverse_ref, source_ref, ion_ref)):
            fill_lines(
                target_ref,
                DEPTH + index,
                field,
                field_refs[field],
                index,
                before_ref,
                after_ref,
                base,
            )
        return 0

    lax.fori_loop(0, cells_x, fill, 0, unroll=2)

    def beyond(values):
        lane = lax.broadcasted_iota(jnp.int32, values[0].shape, 1)
        right = [pltpu.roll(value, 127, 1) for value in values]
        left = [pltpu.roll(value, 1, 1) for value in values]
        above = [jnp.where(lane == 127, right[1], right[0]), jnp.where(lane == 127, 0.0, right[1])]
        below = [jnp.where(lane == 0, 0.0, left[0]), jnp.where(lane == 0, left[0], left[1])]
        return (below, above)

    def wide(plane, half, shift=0):
        return pl.ds((plane * 2 + half) * rows + 1 + shift, inner)

    def around(ref, plane):
        here = [ref[wide(plane, half), :] for half in range(2)]
        below, above = beyond(here)
        sums = [
            (ref[wide(plane - 1, half), :] + ref[wide(plane + 1, half), :])
            + (ref[wide(plane, half, -1), :] + ref[wide(plane, half, 1), :])
            + (below[half] + above[half])
            for half in range(2)
        ]
        return (here, sums)

    middle = 0.5 * (highest_eig + lowest_eig)
    spread = 0.5 * (highest_eig - lowest_eig)
    assert middle == 1.0 and SWEEPS == 4

    def sweep_first(plane, _):
        here, sums = around(start_ref, plane)
        for half in range(2):
            at = wide(plane, half)
            updates[0][at, :] = source_ref[at, :] - here[half] + inverse_ref[at, :] * sums[half]
        return 0

    lax.fori_loop(1, cells_x + 2 * DEPTH - 1, sweep_first, 0, unroll=2)

    ratio_ms = middle / spread
    weight_now = 1.0 / ratio_ms
    for turn in range(1, SWEEPS):
        weight_next = 1.0 / (2.0 * ratio_ms - weight_now)
        keep, gain = (weight_next * weight_now, 2.0 * weight_next / spread)
        weight_now = weight_next

        def sweep(plane, _, turn=turn, keep=keep, gain=gain):
            here, sums = around(updates[turn - 1], plane)
            for half in range(2):
                at = wide(plane, half)
                resid = inverse_ref[at, :] * sums[half]
                if turn > 1:
                    resid = resid + (resids[turn - 2][at, :] - here[half])
                update = keep * here[half] + gain * resid
                if turn + 1 < SWEEPS:
                    resids[turn - 1][at, :] = resid
                    updates[turn][at, :] = update
                else:
                    final_ref[at, :] = (start_ref[at, :] + updates[0][at, :]) + (
                        (updates[1][at, :] + here[half]) + update
                    )
            return 0

        first = 1 + turn
        lax.fori_loop(first, cells_x + 2 * DEPTH - first, sweep, 0, unroll=2)

    def local(plane, half, shift=0):
        return pl.ds((plane * 2 + half) * rows + DEPTH + shift, cells_y)

    def advance(index, _):
        plane = index + DEPTH
        pots = [final_ref[local(plane, half), :] for half in range(2)]
        ions = [ion_ref[local(plane, half), :] for half in range(2)]
        pot_below, pot_above = beyond(pots)
        ion_below, ion_above = beyond(ions)
        for half in range(2):
            pot, ion = (pots[half], ions[half])
            steps = [
                (final_ref[at, :], ion_ref[at, :])
                for at in (
                    local(plane - 1, half),
                    local(plane + 1, half),
                    local(plane, half, -1),
                    local(plane, half, 1),
                )
            ]
            steps += [(pot_below[half], ion_below[half]), (pot_above[half], ion_above[half])]
            total = 0.0
            for low, high in zip(steps[0::2], steps[1::2], strict=True):
                total = total + (
                    face_flux(pot, high[0], ion, high[1]) - face_flux(low[0], pot, low[1], ion)
                )
            lanes = slice(128 * half, 128 * half + 128)
            next_ref[index, :, lanes] = ion - time_step * total
            potential_ref[index, :, lanes] = pot
        return 0

    lax.fori_loop(0, cells_x, advance, 0)

    row_lane = lax.broadcasted_iota(jnp.int32, (1, 128), 1)

    def pick(cluster, _):
        cell = cell_ref[cluster]
        index_x = lax.shift_right_logical(cell, CELL_BITS) // cells_y + DEPTH
        index_y = lax.shift_right_logical(cell, CELL_BITS) % cells_y + DEPTH
        index_z = lax.bitwise_and(cell, 255)
        half = lax.shift_right_logical(index_z, 7)
        here = row_lane == lax.bitwise_and(index_z, 127)

        def line(plane, row, part):
            return final_ref[pl.ds((plane * 2 + part) * rows + row, 1), :]

        along_x = line(index_x - 1, index_y, half) - line(index_x + 1, index_y, half)
        along_y = line(index_x, index_y - 1, half) - line(index_x, index_y + 1, half)
        along_z = jnp.zeros((1, 128), jnp.float32)
        for part in range(2):
            value = line(index_x, index_y, part)
            place = row_lane + 128 * part
            along_z = along_z + jnp.where(place == index_z - 1, value, 0.0)
            along_z = along_z - jnp.where(place == index_z + 1, value, 0.0)
        at = pl.ds(cluster, 1)
        pick_refs[0][at, :] = jnp.where(here, along_x, 0.0)
        pick_refs[1][at, :] = jnp.where(here, along_y, 0.0)
        pick_refs[2][at, :] = along_z
        return 0

    lax.fori_loop(0, clusters, pick, 0, unroll=8)

    def spread_out(step, _):
        start = pl.multiple_of(step * 8, 8)
        charge = masked_ref[pl.ds(start, 8), :] * (0.5 * field_scale)
        for part, pick_ref in enumerate(pick_refs):
            total = jnp.sum(pick_ref[pl.ds(start, 8), :], axis=1, keepdims=True)
            force_ref[pl.ds(4 * start + part, 8, stride=4), :] = charge * total
        force_ref[pl.ds(4 * start + 3, 8, stride=4), :] = jnp.zeros((8, 128), jnp.float32)
        return 0

    lax.fori_loop(0, clusters // 8, spread_out, 0, unroll=4)


def grid_step(cell, masked, fields, before, after, lower, upper, base):
    smem = pl.BlockSpec(memory_space=pltpu.SMEM)
    vmem = pl.BlockSpec(memory_space=pltpu.VMEM)
    clusters = masked.shape[0]
    cells_x, cells_y, _ = fields[0].shape
    block = ((cells_x + 2 * DEPTH) * 2 * line_rows(cells_y), 128)
    return pl.pallas_call(
        functools.partial(grid_kernel, base),
        out_shape=(
            jax.ShapeDtypeStruct(fields[0].shape, jnp.float32),
            jax.ShapeDtypeStruct(fields[0].shape, jnp.float32),
            jax.ShapeDtypeStruct((clusters * 4, 128), jnp.float32),
        ),
        in_specs=[smem] + [vmem] * 9,
        out_specs=(vmem,) * 3,
        scratch_shapes=[pltpu.VMEM(block, jnp.float32)] * 10
        + [pltpu.VMEM((clusters, 128), jnp.float32)] * 3,
        compiler_params=pltpu.CompilerParams(vmem_limit_bytes=40 * 1024 * 1024),
        cost_estimate=pl.CostEstimate(
            flops=block[0] * block[1] * 100, bytes_accessed=8 << 20, transcendentals=0
        ),
        name="grid_step",
    )(cell, masked, *fields, before, after, lower, upper)


def gather_forces_kernel(send_index_ref, own_ref, field_ref, *refs):
    back_refs, (out_ref, sum_ref) = (refs[:-2], refs[-2:])
    clusters = own_ref.shape[0]
    slots = send_index_ref.shape[1]
    sum_ref[...] = own_ref[...] + field_ref[...]

    def visit(slot, _):
        for direction, back_ref in enumerate(back_refs):
            cluster = send_index_ref[direction, slot]
            sum_ref[cluster] += back_ref[slot]
        return 0

    lax.fori_loop(0, slots, visit, 0)

    def write(step, _):
        for turn in range(8):
            cluster = step * 8 + turn
            out_ref[:, pl.ds(pl.multiple_of(cluster * 128, 128), 128)] = sum_ref[cluster][0:3]
        return 0

    lax.fori_loop(0, clusters // 8, write, 0)


def gather_forces(send_index, own, field, backs):
    smem = pl.BlockSpec(memory_space=pltpu.SMEM)
    vmem = pl.BlockSpec(memory_space=pltpu.VMEM)
    clusters = own.shape[0]
    return pl.pallas_call(
        gather_forces_kernel,
        out_shape=jax.ShapeDtypeStruct((3, clusters * 128), jnp.float32),
        in_specs=[smem] + [vmem] * (2 + len(backs)),
        out_specs=vmem,
        scratch_shapes=[pltpu.VMEM(own.shape, jnp.float32)],
        compiler_params=pltpu.CompilerParams(vmem_limit_bytes=32 * 1024 * 1024),
        name="gather_forces",
    )(send_index, own, field, *backs)


def passed_along(shard, axis, by):
    devices = lax.axis_size(axis)
    pairs = [(i, i + by) for i in range(devices) if 0 <= i + by < devices]
    return lax.ppermute(shard, axis, pairs)


ROUTES = (("brick", 1), ("brick", -1), ("brick", 2), ("brick", -2), ("grp", 1), ("grp", -1))


def shards(
    positions,
    charges,
    cluster_fill,
    cluster_cell,
    send_index,
    send_count,
    pair_local,
    pair_dir,
    pair_slot,
    ion_density,
    potential_prev,
    screening,
):
    clusters = cluster_fill.shape[0]
    psize = charges.shape[0] // clusters
    slots = send_index.shape[1]
    base = slots * 4
    own, masked, inverse, source, local, *messages = prepare(
        cluster_fill,
        cluster_cell,
        send_index,
        send_count,
        positions,
        charges.reshape(clusters, psize),
        ion_density,
        potential_prev,
        screening,
    )
    arrived = [local] + [
        passed_along(message, axis, by)
        for message, (axis, by) in zip(messages, ROUTES, strict=True)
    ]
    fields = (potential_prev, inverse, source, ion_density)
    arrived = lax.optimization_barrier(arrived)
    before, after = arrived[1:3]
    down, up = planes(fields, before, after, base)
    lower = passed_along(up, "grp", 1)
    upper = passed_along(down, "grp", -1)
    own_force, *reactions = pair_forces(
        pair_local,
        pair_dir * slots + pair_slot,
        own.reshape(clusters * 4, psize),
        arrived,
        slots,
    )
    backs = [reactions[0]] + [
        passed_along(reaction, axis, -by)
        for reaction, (axis, by) in zip(reactions[1:], ROUTES, strict=True)
    ]
    potential, ion_next, field_force = grid_step(
        cluster_cell, masked, fields, before, after, lower, upper, base
    )
    forces = gather_forces(
        send_index,
        own_force.reshape(clusters, 4, psize),
        field_force.reshape(clusters, 4, psize),
        [back.reshape(slots, 4, psize) for back in backs],
    )
    return (forces, potential, ion_next)


def solution(mesh):
    in_specs = (
        P(None, ("grp", "brick")),
        P(("grp", "brick")),
        P(("grp", "brick")),
        P(("grp", "brick")),
        P(("grp", "brick"), None),
        P(("grp", "brick"), None),
        P(("grp", "brick")),
        P(("grp", "brick")),
        P(("grp", "brick")),
        P("grp", "brick", None),
        P("grp", "brick", None),
        P("grp", "brick", None),
    )
    out_specs = (P(None, ("grp", "brick")), P("grp", "brick", None), P("grp", "brick", None))
    return jax.shard_map(shards, mesh=mesh, in_specs=in_specs, out_specs=out_specs, check_vma=False)
```

```python
import functools

import jax
import jax.numpy as jnp
import numpy as np
from jax import lax
from jax.experimental import pallas as pl
from jax.experimental.pallas import tpu as pltpu
from jax.sharding import PartitionSpec as P

SWEEPS = 4
QUAD = 4
UNROLL = 8
HALO_WIDTHS = (SWEEPS + 1, SWEEPS, SWEEPS, 1)
DEPTH = SWEEPS + 1
CELL_BITS = 8


coulomb_scale = 0.02
softening = 0.1
field_scale = 0.5
deposit_scale = 0.2
lowest_eig = 0.01
highest_eig = 1.99
mobility = 0.3
diffusion = 0.2
time_step = 0.2


def split3(value):
    first = value.astype(jnp.bfloat16).astype(jnp.float32)
    rest = value - first
    second = rest.astype(jnp.bfloat16).astype(jnp.float32)
    third = (rest - second).astype(jnp.bfloat16).astype(jnp.float32)
    return (first, second, third)


def moment_pieces(comps, charge):
    rows = [None] * 12
    for part, charged in enumerate((*comps, None)):
        for level, piece in enumerate(split3(charge if charged is None else charge * charged)):
            rows[4 * level + part] = piece
    return rows


def selections():
    near_kinds, far_kinds = ([], [])
    for part in range(3):
        near_kinds += [3 * part + level for level in (0, 0, 0, 1, 1, 2)]
        far_kinds += [3 * part + level for level in (0, 1, 2, 0, 1, 0)]
    near_kinds += [9, 10, 11, 12, 12, 12]
    far_kinds += [12, 12, 12, 9, 10, 11]
    near = np.zeros((128, 1024), np.float32)
    far = np.zeros((256, 128), np.float32)
    moment = np.zeros((128, 128), np.float32)
    for cluster in range(8):
        for index, kind in enumerate(near_kinds):
            near[kind * 8 + cluster, cluster * 128 + index] = 1.0
        for index, kind in enumerate(far_kinds):
            far[cluster * 32 + index, kind * 8 + cluster] = 1.0
        for kind in range(12):
            moment[cluster * 16 + kind, kind * 8 + cluster] = 1.0
    return tuple(jnp.asarray(part, jnp.bfloat16) for part in (near, far, moment))


def pair_kernel(own_rows_ref, other_rows_ref, *refs):
    near_sel_ref, far_sel_ref, moment_sel_ref, own_ref = refs[:4]
    refs = refs[4:]
    sources = (len(refs) - 11) // 2
    other_refs = refs[:sources]
    own_out_ref = refs[sources]
    other_out_refs = refs[sources + 1 : 2 * sources + 1]
    (
        near_ref,
        far_ref,
        own_moment_ref,
        other_moment_ref,
        own_sum_ref,
        other_sum_ref,
        *passed_refs,
    ) = refs[2 * sources + 1 :]
    clusters = own_ref.shape[0] // 4
    slots = other_out_refs[0].shape[0] // 4
    others = slots * sources
    groups = own_rows_ref.shape[0] // UNROLL
    units = UNROLL // QUAD
    ones = jnp.ones((8, 128), jnp.float32)
    zeros = jnp.zeros((8, 128), jnp.float32)

    def components(data_ref, start):
        return [data_ref[pl.ds(4 * start + part, 8, stride=4), :] for part in range(4)]

    def place_pieces(comps, factor, offset):
        pieces = []
        square = zeros
        for comp in comps:
            square = square + comp * comp
            pieces += split3(factor * comp)
        pieces += [*split3(square + offset), ones]
        return jnp.concatenate(pieces + [zeros] * (16 - len(pieces)), axis=0)

    def selected(left, right):
        return jnp.dot(
            left.astype(jnp.bfloat16), right, preferred_element_type=jnp.float32
        ).astype(jnp.bfloat16)

    def near_rows(step, _):
        start = pl.multiple_of(step * 8, 8)
        *comps, charge = components(own_ref, start)
        moments = jnp.concatenate(moment_pieces(comps, charge) + [zeros] * 4, axis=0)
        own_moment_ref[pl.ds(pl.multiple_of(start * 16, 128), 128), :] = selected(
            moment_sel_ref[...], moments.astype(jnp.bfloat16)
        )
        tiles = selected(place_pieces(comps, 1.0, 0.0).T, near_sel_ref[...])
        for index in range(8):
            at = pl.ds(pl.multiple_of((start + index) * 128, 128), 128)
            near_ref[at, :] = tiles[:, 128 * index : 128 * index + 128]
        return 0

    def far_rows(source, step, _):
        local = pl.multiple_of(step * 8, 8)
        start = source * slots + local
        *comps, charge = components(other_refs[source], local)
        far_ref[pl.ds(pl.multiple_of(start * 32, 256), 256), :] = selected(
            far_sel_ref[...], place_pieces(comps, -2.0, softening).astype(jnp.bfloat16)
        )
        moments = jnp.concatenate(moment_pieces(comps, charge) + [zeros] * 4, axis=0)
        other_moment_ref[pl.ds(pl.multiple_of(start * 16, 128), 128), :] = selected(
            moment_sel_ref[...], moments.astype(jnp.bfloat16)
        )
        return 0

    lax.fori_loop(0, clusters // 8, near_rows, 0, unroll=4)
    for source in range(sources):
        lax.fori_loop(0, slots // 8, functools.partial(far_rows, source), 0, unroll=4)
    own_sum_ref[...] = jnp.zeros_like(own_sum_ref)
    other_sum_ref[...] = jnp.zeros_like(other_sum_ref)
    dist_refs, weight_refs = (passed_refs[:2], passed_refs[2:])
    dist_refs[0][...] = jnp.full(dist_refs[0].shape, 1e30, jnp.float32)
    weight_refs[0][...] = jnp.zeros_like(weight_refs[0])

    def block_diagonal(blocks):
        blank = jnp.zeros_like(blocks[0])
        lines = [
            jnp.concatenate(
                [block if turn == at else blank for turn in range(len(blocks))], axis=1
            )
            for at, block in enumerate(blocks)
        ]
        return jnp.concatenate(lines, axis=0)

    def distances(pair, unit, dist_ref):
        for turn in range(QUAD):
            own = own_rows_ref[pair + turn]
            other = other_rows_ref[pair + turn]
            dist_ref[unit, :, 128 * turn : 128 * turn + 128] = jnp.dot(
                near_ref[pl.ds(pl.multiple_of(own * 128, 128), 128), 0:32],
                far_ref[pl.ds(pl.multiple_of(other * 32, 32), 32), :],
                preferred_element_type=jnp.float32,
            )

    def weights(unit, turn, dist_ref, weight_ref):
        dist = dist_ref[unit, :, 128 * turn : 128 * turn + 128]
        root = lax.rsqrt(dist.astype(jnp.bfloat16)).astype(jnp.float32)
        square = root * root
        error = 1.0 - dist * square
        weight = (square * root) * (1.0 + error * (1.5 + 1.875 * error))
        high = weight.astype(jnp.bfloat16)
        weight_ref[unit, 128 * turn : 128 * turn + 128, :128] = high
        weight_ref[unit, 128 * turn : 128 * turn + 128, 128:] = (
            weight - high.astype(jnp.float32)
        ).astype(jnp.bfloat16)

    def moments_of(moment_ref, indices):
        return block_diagonal(
            [moment_ref[pl.ds(pl.multiple_of(index * 16, 16), 16), :] for index in indices]
        )

    def products(pair, unit, weight_ref):
        owns = [own_rows_ref[pair + turn] for turn in range(QUAD)]
        others = [other_rows_ref[pair + turn] for turn in range(QUAD)]
        both = weight_ref[unit]
        levels = [
            jnp.concatenate(
                [both[128 * turn : 128 * turn + 128, lanes] for turn in range(QUAD)], axis=1
            )
            for lanes in (slice(0, 128), slice(128, 256))
        ]
        to_own = lax.dot_general(
            moments_of(other_moment_ref, others),
            jnp.concatenate(levels, axis=0),
            (((1,), (1,)), ((), ())),
            preferred_element_type=jnp.float32,
        )
        to_other = jnp.dot(
            moments_of(own_moment_ref, owns), both, preferred_element_type=jnp.float32
        )
        return (owns, others, *(part[:, :128] + part[:, 128:] for part in (to_own, to_other)))

    def half_step(step, side):
        last = jnp.maximum(step - 2, 0) * UNROLL
        first = jnp.minimum(step, groups - 1) * UNROLL
        results = [products(last + QUAD * unit, unit, weight_refs[side]) for unit in range(units)]
        for unit in range(units):
            for turn in range(QUAD):
                weights(unit, turn, dist_refs[side], weight_refs[1 - side])
        for unit in range(units):
            distances(first + QUAD * unit, unit, dist_refs[1 - side])
        for owns, others, to_own, to_other in results:
            for turn in range(QUAD):
                own_at = pl.ds(pl.multiple_of(owns[turn] * 16, 16), 16)
                other_at = pl.ds(pl.multiple_of(others[turn] * 16, 16), 16)
                own_sum_ref[own_at, :] += to_own[16 * turn : 16 * turn + 16]
                other_sum_ref[other_at, :] += to_other[16 * turn : 16 * turn + 16]

    def visit(step, _):
        for side in range(2):
            half_step(step * 2 + side, side)
        return 0

    lax.fori_loop(0, (groups + 2) // 2, visit, 0)

    def finish(data_ref, out_ref, sum_ref, base, step, _):
        start = pl.multiple_of(step * 8, 8)
        *comps, charge = components(data_ref, start)

        def total(part):
            terms = [
                sum_ref[pl.ds(base + start * 16 + 4 * level + part, 8, stride=16), :]
                for level in range(3)
            ]
            return terms[0] + (terms[1] + terms[2])

        weight = total(3)
        scale = coulomb_scale * charge
        for part, comp in enumerate(comps):
            out_ref[pl.ds(4 * start + part, 8, stride=4), :] = scale * (comp * weight - total(part))
        out_ref[pl.ds(4 * start + 3, 8, stride=4), :] = zeros
        return 0

    lax.fori_loop(
        0, clusters // 8, functools.partial(finish, own_ref, own_out_ref, own_sum_ref, 0), 0, unroll=4
    )
    for source in range(sources):
        body = functools.partial(
            finish,
            other_refs[source],
            other_out_refs[source],
            other_sum_ref,
            source * slots * 16,
        )
        lax.fori_loop(0, slots // 8, body, 0, unroll=4)


def pair_forces(own_rows, other_rows, own, arrived, slots):
    clusters = own.shape[0] // 4
    others = slots * len(arrived)
    pairs = own_rows.shape[0]
    smem = pl.BlockSpec(memory_space=pltpu.SMEM)
    vmem = pl.BlockSpec(memory_space=pltpu.VMEM)
    return pl.pallas_call(
        pair_kernel,
        out_shape=(
            jax.ShapeDtypeStruct(own.shape, jnp.float32),
            *[jax.ShapeDtypeStruct((slots * 4, 128), jnp.float32)] * len(arrived),
        ),
        in_specs=[smem, smem] + [vmem] * (4 + len(arrived)),
        out_specs=(vmem,) * (len(arrived) + 1),
        scratch_shapes=[
            pltpu.VMEM((clusters * 128, 128), jnp.bfloat16),
            pltpu.VMEM((others * 32, 128), jnp.bfloat16),
            pltpu.VMEM((clusters * 16, 128), jnp.bfloat16),
            pltpu.VMEM((others * 16, 128), jnp.bfloat16),
            pltpu.VMEM((clusters * 16, 128), jnp.float32),
            pltpu.VMEM((others * 16, 128), jnp.float32),
            *[pltpu.VMEM((UNROLL // QUAD, 128, 128 * QUAD), jnp.float32)] * 2,
            *[pltpu.VMEM((UNROLL // QUAD, 128 * QUAD, 256), jnp.bfloat16)] * 2,
        ],
        compiler_params=pltpu.CompilerParams(vmem_limit_bytes=40 * 1024 * 1024),
        cost_estimate=pl.CostEstimate(
            flops=pairs * 128 * 128 * 20, bytes_accessed=4 * 1024 * 1024, transcendentals=0
        ),
        name="pair_forces",
    )(own_rows, other_rows, *selections(), own, *arrived)


def prepare_kernel(
    fill_ref,
    cell_ref,
    send_index_ref,
    send_count_ref,
    cell_row_ref,
    position_hbm,
    charge_hbm,
    ion_hbm,
    start_hbm,
    screen_hbm,
    own_ref,
    masked_ref,
    inverse_ref,
    source_ref,
    *refs,
):
    out_refs, scratch = (refs[:-8], refs[-8:])
    sum_ref, deposit_ref, position_ref, charge_ref, ion_ref, start_ref, screen_ref, sems = scratch
    copies = [
        pltpu.make_async_copy(source, target, sems.at[index])
        for index, (source, target) in enumerate(
            (
                (position_hbm, position_ref),
                (charge_hbm, charge_ref),
                (ion_hbm, ion_ref),
                (start_hbm, start_ref),
                (screen_hbm, screen_ref),
            )
        )
    ]
    for copy in copies:
        copy.start()
    copies[0].wait()
    copies[1].wait()
    clusters = charge_ref.shape[0]
    cells_x, cells_y, _ = ion_ref.shape
    slots = send_index_ref.shape[1]
    lane = lax.broadcasted_iota(jnp.int32, (1, 128), 1)
    row = lax.broadcasted_iota(jnp.int32, (4, 128), 0)

    def collect(step, _):
        for turn in range(8):
            cluster = step * 8 + turn
            masked = jnp.where(lane < fill_ref[cluster], charge_ref[pl.ds(cluster, 1), :], 0.0)
            masked_ref[pl.ds(cluster, 1), :] = masked
            place = position_ref[:, pl.ds(pl.multiple_of(cluster * 128, 128), 128)]
            own_ref[cluster, 0:3, :] = place
            own_ref[cluster, 3:4, :] = masked
        at = pl.ds(pl.multiple_of(step * 8, 8), 8)
        total = jnp.sum(masked_ref[at, :], axis=1, keepdims=True)
        sum_ref[at, :] = jnp.broadcast_to(deposit_scale * total, (8, 128))
        return 0

    lax.fori_loop(0, clusters // 8, collect, 0, unroll=4)

    def fill_messages(step, _):
        for direction, out_ref in enumerate(out_refs):
            parts = []
            for turn in range(2):
                slot = step * 2 + turn
                live = jnp.where(slot < send_count_ref[0, direction], 1.0, 0.0)
                value = own_ref[send_index_ref[direction, slot]]
                parts.append(jnp.where(row == 3, value * live, value))
            out_ref[pl.ds(pl.multiple_of(step * 8, 8), 8), :] = jnp.concatenate(parts, axis=0)
        return 0

    lax.fori_loop(0, slots // 2, fill_messages, 0)

    def place(step, _):
        for turn in range(8):
            cluster = step * 8 + turn
            index_z = lax.bitwise_and(cell_ref[cluster], 127)
            at = pl.ds(cluster, 1)
            sum_ref[at, :] = jnp.where(lane == index_z, sum_ref[at, :], 0.0)
        return 0

    lax.fori_loop(0, clusters // 8, place, 0)
    cell = cell_row_ref[...]
    line = lax.shift_right_logical(cell, CELL_BITS)
    line = (line // cells_y * 2 + lax.shift_right_logical(lax.bitwise_and(cell, 255), 7)) * cells_y
    line = line + lax.shift_right_logical(cell, CELL_BITS) % cells_y
    sums = jnp.concatenate([part.astype(jnp.bfloat16) for part in split3(sum_ref[...])], axis=1)
    block = 128
    for first in range(0, deposit_ref.shape[0], block):
        rows = lax.broadcasted_iota(jnp.int32, (block, clusters), 0) + first
        hot = jnp.where(rows == line, 1.0, 0.0).astype(jnp.bfloat16)
        added = jnp.dot(hot, sums, preferred_element_type=jnp.float32)
        deposit_ref[first : first + block, :] = added[:, :128] + (
            added[:, 128:256] + added[:, 256:]
        )
    for copy in copies[2:]:
        copy.wait()
    inverse_ref[...] = 1.0 / (6.0 + screen_ref[...])
    for index in range(cells_x):
        for half in range(2):
            lanes = slice(128 * half, 128 * half + 128)
            first = (index * 2 + half) * cells_y
            source_ref[index, :, lanes] = (
                ion_ref[index, :, lanes] + deposit_ref[first : first + cells_y, :]
            ) * inverse_ref[index, :, lanes]
    for out_ref, after in ((out_refs[1], True), (out_refs[2], False)):
        for index in range(cells_x):
            base = slots * 4 + index * 32
            offset = 0
            for field_ref, width in zip(
                (start_ref, inverse_ref, source_ref, ion_ref), HALO_WIDTHS, strict=True
            ):
                first = cells_y - width if after else 0
                rows = field_ref[index, first : first + width, :]
                for half in range(2):
                    out_ref[base + 16 * half + offset : base + 16 * half + offset + width, :] = (
                        rows[:, 128 * half : 128 * half + 128]
                    )
                offset += width
            for half in range(2):
                out_ref[base + 16 * half + offset : base + 16 * half + 16, :] = jnp.zeros(
                    (16 - offset, 128), jnp.float32
                )


def prepare(fill, cell, send_index, send_count, positions, charges, ions, start, screen):
    clusters = charges.shape[0]
    directions, slots = send_index.shape
    cells_x = ions.shape[0]
    smem = pl.BlockSpec(memory_space=pltpu.SMEM)
    vmem = pl.BlockSpec(memory_space=pltpu.VMEM)
    rows = [slots * 4] * directions
    rows[1] = rows[2] = slots * 4 + cells_x * 32
    return pl.pallas_call(
        prepare_kernel,
        out_shape=(
            jax.ShapeDtypeStruct((clusters, 4, 128), jnp.float32),
            jax.ShapeDtypeStruct((clusters, 128), jnp.float32),
            jax.ShapeDtypeStruct(ions.shape, jnp.float32),
            jax.ShapeDtypeStruct(ions.shape, jnp.float32),
            *[jax.ShapeDtypeStruct((count, 128), jnp.float32) for count in rows],
        ),
        in_specs=[smem] * 4 + [vmem] + [pl.BlockSpec(memory_space=pltpu.HBM)] * 5,
        out_specs=(vmem,) * (4 + directions),
        scratch_shapes=[
            pltpu.VMEM((clusters, 128), jnp.float32),
            pltpu.VMEM((ions.size // 128, 128), jnp.float32),
            *[
                pltpu.VMEM(operand.shape, jnp.float32)
                for operand in (positions, charges, ions, start, screen)
            ],
            pltpu.SemaphoreType.DMA((5,)),
        ],
        compiler_params=pltpu.CompilerParams(vmem_limit_bytes=60 * 1024 * 1024),
        name="prepare",
    )(
        fill,
        cell,
        send_index,
        send_count,
        cell.reshape(1, clusters),
        positions,
        charges,
        ions,
        start,
        screen,
    )


def line_rows(cells_y):
    return (cells_y + 2 * DEPTH + 7) // 8 * 8


def fill_lines(target_ref, plane, field, field_ref, index, before_ref, after_ref, base):
    cells_y = field_ref.shape[1]
    width = HALO_WIDTHS[field]
    for half in range(2):
        at = (plane * 2 + half) * line_rows(cells_y) + DEPTH
        first = base + index * 32 + 16 * half + sum(HALO_WIDTHS[:field])
        target_ref[pl.ds(at - width, width), :] = before_ref[pl.ds(first, width), :]
        target_ref[pl.ds(at, cells_y), :] = field_ref[index, :, 128 * half : 128 * half + 128]
        target_ref[pl.ds(at + cells_y, width), :] = after_ref[pl.ds(first, width), :]


def planes_kernel(base, *refs):
    field_refs, (before_ref, after_ref, down_ref, up_ref) = (refs[:4], refs[4:])
    cells_x = field_refs[0].shape[0]
    for field, width in enumerate(HALO_WIDTHS):
        plane = sum(HALO_WIDTHS[:field])

        def fill(step, _, field=field, plane=plane, width=width):
            for target_ref, source in ((down_ref, step), (up_ref, cells_x - width + step)):
                fill_lines(
                    target_ref,
                    plane + step,
                    field,
                    field_refs[field],
                    source,
                    before_ref,
                    after_ref,
                    base,
                )
            return 0

        lax.fori_loop(0, width, fill, 0)


def planes(fields, before, after, base):
    vmem = pl.BlockSpec(memory_space=pltpu.VMEM)
    rows = sum(HALO_WIDTHS) * 2 * line_rows(fields[0].shape[1])
    shape = jax.ShapeDtypeStruct((rows, 128), jnp.float32)
    return pl.pallas_call(
        functools.partial(planes_kernel, base),
        out_shape=(shape, shape),
        in_specs=[vmem] * 6,
        out_specs=(vmem, vmem),
        compiler_params=pltpu.CompilerParams(vmem_limit_bytes=32 * 1024 * 1024),
        name="planes",
    )(*fields, before, after)


def face_flux(pot_low, pot_high, ion_low, ion_high):
    speed = -mobility * (pot_high - pot_low)
    return (
        jnp.maximum(speed, 0.0) * ion_low
        + jnp.minimum(speed, 0.0) * ion_high
        - diffusion * (ion_high - ion_low)
    )


def grid_kernel(base, *refs):
    cell_ref, masked_ref = refs[:2]
    field_refs = refs[2:6]
    before_ref, after_ref, lower_ref, upper_ref = refs[6:10]
    potential_ref, next_ref, force_ref = refs[10:13]
    start_ref, inverse_ref, source_ref, ion_ref = refs[13:17]
    updates, resids, final_ref, pick_refs = (refs[17:20], refs[20:22], refs[22], refs[23:26])
    cells_x, cells_y, _ = field_refs[0].shape
    rows = line_rows(cells_y)
    inner = cells_y + 2 * DEPTH - 2
    clusters = masked_ref.shape[0]

    for field, target_ref in enumerate((start_ref, inverse_ref, source_ref, ion_ref)):
        width = HALO_WIDTHS[field]
        size = width * 2 * rows
        first = sum(HALO_WIDTHS[:field]) * 2 * rows
        low = (DEPTH - width) * 2 * rows
        high = (DEPTH + cells_x) * 2 * rows
        target_ref[low : low + size, :] = lower_ref[first : first + size, :]
        target_ref[high : high + size, :] = upper_ref[first : first + size, :]

    def fill(index, _):
        for field, target_ref in enumerate((start_ref, inverse_ref, source_ref, ion_ref)):
            fill_lines(
                target_ref,
                DEPTH + index,
                field,
                field_refs[field],
                index,
                before_ref,
                after_ref,
                base,
            )
        return 0

    lax.fori_loop(0, cells_x, fill, 0, unroll=2)

    def beyond(values):
        lane = lax.broadcasted_iota(jnp.int32, values[0].shape, 1)
        right = [pltpu.roll(value, 127, 1) for value in values]
        left = [pltpu.roll(value, 1, 1) for value in values]
        above = [jnp.where(lane == 127, right[1], right[0]), jnp.where(lane == 127, 0.0, right[1])]
        below = [jnp.where(lane == 0, 0.0, left[0]), jnp.where(lane == 0, left[0], left[1])]
        return (below, above)

    def wide(plane, half, shift=0):
        return pl.ds((plane * 2 + half) * rows + 1 + shift, inner)

    def around(ref, plane):
        here = [ref[wide(plane, half), :] for half in range(2)]
        below, above = beyond(here)
        sums = [
            (ref[wide(plane - 1, half), :] + ref[wide(plane + 1, half), :])
            + (ref[wide(plane, half, -1), :] + ref[wide(plane, half, 1), :])
            + (below[half] + above[half])
            for half in range(2)
        ]
        return (here, sums)

    middle = 0.5 * (highest_eig + lowest_eig)
    spread = 0.5 * (highest_eig - lowest_eig)
    assert middle == 1.0 and SWEEPS == 4

    def sweep_first(plane, _):
        here, sums = around(start_ref, plane)
        for half in range(2):
            at = wide(plane, half)
            updates[0][at, :] = source_ref[at, :] - here[half] + inverse_ref[at, :] * sums[half]
        return 0

    lax.fori_loop(1, cells_x + 2 * DEPTH - 1, sweep_first, 0, unroll=2)

    ratio_ms = middle / spread
    weight_now = 1.0 / ratio_ms
    for turn in range(1, SWEEPS):
        weight_next = 1.0 / (2.0 * ratio_ms - weight_now)
        keep, gain = (weight_next * weight_now, 2.0 * weight_next / spread)
        weight_now = weight_next

        def sweep(plane, _, turn=turn, keep=keep, gain=gain):
            here, sums = around(updates[turn - 1], plane)
            for half in range(2):
                at = wide(plane, half)
                resid = inverse_ref[at, :] * sums[half]
                if turn > 1:
                    resid = resid + (resids[turn - 2][at, :] - here[half])
                update = keep * here[half] + gain * resid
                if turn + 1 < SWEEPS:
                    resids[turn - 1][at, :] = resid
                    updates[turn][at, :] = update
                else:
                    final_ref[at, :] = (start_ref[at, :] + updates[0][at, :]) + (
                        (updates[1][at, :] + here[half]) + update
                    )
            return 0

        first = 1 + turn
        lax.fori_loop(first, cells_x + 2 * DEPTH - first, sweep, 0, unroll=2)

    def local(plane, half, shift=0):
        return pl.ds((plane * 2 + half) * rows + DEPTH + shift, cells_y)

    def advance(index, _):
        plane = index + DEPTH
        pots = [final_ref[local(plane, half), :] for half in range(2)]
        ions = [ion_ref[local(plane, half), :] for half in range(2)]
        pot_below, pot_above = beyond(pots)
        ion_below, ion_above = beyond(ions)
        for half in range(2):
            pot, ion = (pots[half], ions[half])
            steps = [
                (final_ref[at, :], ion_ref[at, :])
                for at in (
                    local(plane - 1, half),
                    local(plane + 1, half),
                    local(plane, half, -1),
                    local(plane, half, 1),
                )
            ]
            steps += [(pot_below[half], ion_below[half]), (pot_above[half], ion_above[half])]
            total = 0.0
            for low, high in zip(steps[0::2], steps[1::2], strict=True):
                total = total + (
                    face_flux(pot, high[0], ion, high[1]) - face_flux(low[0], pot, low[1], ion)
                )
            lanes = slice(128 * half, 128 * half + 128)
            next_ref[index, :, lanes] = ion - time_step * total
            potential_ref[index, :, lanes] = pot
        return 0

    lax.fori_loop(0, cells_x, advance, 0)

    row_lane = lax.broadcasted_iota(jnp.int32, (1, 128), 1)

    def pick(cluster, _):
        cell = cell_ref[cluster]
        index_x = lax.shift_right_logical(cell, CELL_BITS) // cells_y + DEPTH
        index_y = lax.shift_right_logical(cell, CELL_BITS) % cells_y + DEPTH
        index_z = lax.bitwise_and(cell, 255)
        half = lax.shift_right_logical(index_z, 7)
        here = row_lane == lax.bitwise_and(index_z, 127)

        def line(plane, row, part):
            return final_ref[pl.ds((plane * 2 + part) * rows + row, 1), :]

        along_x = line(index_x - 1, index_y, half) - line(index_x + 1, index_y, half)
        along_y = line(index_x, index_y - 1, half) - line(index_x, index_y + 1, half)
        along_z = jnp.zeros((1, 128), jnp.float32)
        for part in range(2):
            value = line(index_x, index_y, part)
            place = row_lane + 128 * part
            along_z = along_z + jnp.where(place == index_z - 1, value, 0.0)
            along_z = along_z - jnp.where(place == index_z + 1, value, 0.0)
        at = pl.ds(cluster, 1)
        pick_refs[0][at, :] = jnp.where(here, along_x, 0.0)
        pick_refs[1][at, :] = jnp.where(here, along_y, 0.0)
        pick_refs[2][at, :] = along_z
        return 0

    lax.fori_loop(0, clusters, pick, 0, unroll=8)

    def spread_out(step, _):
        start = pl.multiple_of(step * 8, 8)
        charge = masked_ref[pl.ds(start, 8), :] * (0.5 * field_scale)
        for part, pick_ref in enumerate(pick_refs):
            total = jnp.sum(pick_ref[pl.ds(start, 8), :], axis=1, keepdims=True)
            force_ref[pl.ds(4 * start + part, 8, stride=4), :] = charge * total
        force_ref[pl.ds(4 * start + 3, 8, stride=4), :] = jnp.zeros((8, 128), jnp.float32)
        return 0

    lax.fori_loop(0, clusters // 8, spread_out, 0, unroll=4)


def grid_step(cell, masked, fields, before, after, lower, upper, base):
    smem = pl.BlockSpec(memory_space=pltpu.SMEM)
    vmem = pl.BlockSpec(memory_space=pltpu.VMEM)
    clusters = masked.shape[0]
    cells_x, cells_y, _ = fields[0].shape
    block = ((cells_x + 2 * DEPTH) * 2 * line_rows(cells_y), 128)
    return pl.pallas_call(
        functools.partial(grid_kernel, base),
        out_shape=(
            jax.ShapeDtypeStruct(fields[0].shape, jnp.float32),
            jax.ShapeDtypeStruct(fields[0].shape, jnp.float32),
            jax.ShapeDtypeStruct((clusters * 4, 128), jnp.float32),
        ),
        in_specs=[smem] + [vmem] * 9,
        out_specs=(vmem,) * 3,
        scratch_shapes=[pltpu.VMEM(block, jnp.float32)] * 10
        + [pltpu.VMEM((clusters, 128), jnp.float32)] * 3,
        compiler_params=pltpu.CompilerParams(vmem_limit_bytes=40 * 1024 * 1024),
        cost_estimate=pl.CostEstimate(
            flops=block[0] * block[1] * 100, bytes_accessed=8 << 20, transcendentals=0
        ),
        name="grid_step",
    )(cell, masked, *fields, before, after, lower, upper)


def gather_forces_kernel(send_index_ref, own_ref, field_ref, *refs):
    back_refs, (out_ref, sum_ref) = (refs[:-2], refs[-2:])
    clusters = own_ref.shape[0]
    slots = send_index_ref.shape[1]
    sum_ref[...] = own_ref[...] + field_ref[...]

    def visit(slot, _):
        for direction, back_ref in enumerate(back_refs):
            cluster = send_index_ref[direction, slot]
            sum_ref[cluster] += back_ref[slot]
        return 0

    lax.fori_loop(0, slots, visit, 0)

    def write(step, _):
        for turn in range(8):
            cluster = step * 8 + turn
            out_ref[:, pl.ds(pl.multiple_of(cluster * 128, 128), 128)] = sum_ref[cluster][0:3]
        return 0

    lax.fori_loop(0, clusters // 8, write, 0)


def gather_forces(send_index, own, field, backs):
    smem = pl.BlockSpec(memory_space=pltpu.SMEM)
    vmem = pl.BlockSpec(memory_space=pltpu.VMEM)
    clusters = own.shape[0]
    return pl.pallas_call(
        gather_forces_kernel,
        out_shape=jax.ShapeDtypeStruct((3, clusters * 128), jnp.float32),
        in_specs=[smem] + [vmem] * (2 + len(backs)),
        out_specs=vmem,
        scratch_shapes=[pltpu.VMEM(own.shape, jnp.float32)],
        compiler_params=pltpu.CompilerParams(vmem_limit_bytes=32 * 1024 * 1024),
        name="gather_forces",
    )(send_index, own, field, *backs)


def passed_along(shard, axis, by):
    devices = lax.axis_size(axis)
    pairs = [(i, i + by) for i in range(devices) if 0 <= i + by < devices]
    return lax.ppermute(shard, axis, pairs)


ROUTES = (("brick", 1), ("brick", -1), ("brick", 2), ("brick", -2), ("grp", 1), ("grp", -1))


def shards(
    positions,
    charges,
    cluster_fill,
    cluster_cell,
    send_index,
    send_count,
    pair_local,
    pair_dir,
    pair_slot,
    ion_density,
    potential_prev,
    screening,
):
    clusters = cluster_fill.shape[0]
    psize = charges.shape[0] // clusters
    slots = send_index.shape[1]
    base = slots * 4
    own, masked, inverse, source, local, *messages = prepare(
        cluster_fill,
        cluster_cell,
        send_index,
        send_count,
        positions,
        charges.reshape(clusters, psize),
        ion_density,
        potential_prev,
        screening,
    )
    arrived = [local] + [
        passed_along(message, axis, by)
        for message, (axis, by) in zip(messages, ROUTES, strict=True)
    ]
    fields = (potential_prev, inverse, source, ion_density)
    arrived = lax.optimization_barrier(arrived)
    before, after = arrived[1:3]
    down, up = planes(fields, before, after, base)
    lower = passed_along(up, "grp", 1)
    upper = passed_along(down, "grp", -1)
    own_force, *reactions = pair_forces(
        pair_local,
        pair_dir * slots + pair_slot,
        own.reshape(clusters * 4, psize),
        arrived,
        slots,
    )
    backs = [reactions[0]] + [
        passed_along(reaction, axis, -by)
        for reaction, (axis, by) in zip(reactions[1:], ROUTES, strict=True)
    ]
    potential, ion_next, field_force = grid_step(
        cluster_cell, masked, fields, before, after, lower, upper, base
    )
    forces = gather_forces(
        send_index,
        own_force.reshape(clusters, 4, psize),
        field_force.reshape(clusters, 4, psize),
        [back.reshape(slots, 4, psize) for back in backs],
    )
    return (forces, potential, ion_next)


def solution(mesh):
    in_specs = (
        P(None, ("grp", "brick")),
        P(("grp", "brick")),
        P(("grp", "brick")),
        P(("grp", "brick")),
        P(("grp", "brick"), None),
        P(("grp", "brick"), None),
        P(("grp", "brick")),
        P(("grp", "brick")),
        P(("grp", "brick")),
        P("grp", "brick", None),
        P("grp", "brick", None),
        P("grp", "brick", None),
    )
    out_specs = (P(None, ("grp", "brick")), P("grp", "brick", None), P("grp", "brick", None))
    return jax.shard_map(shards, mesh=mesh, in_specs=in_specs, out_specs=out_specs, check_vma=False)
```

```python
import functools

import jax
import jax.numpy as jnp
import numpy as np
from jax import lax
from jax.experimental import pallas as pl
from jax.experimental.pallas import tpu as pltpu
from jax.sharding import PartitionSpec as P

SWEEPS = 4
QUAD = 4
UNROLL = 8
HALO_WIDTHS = (SWEEPS + 1, SWEEPS, SWEEPS, 1)
DEPTH = SWEEPS + 1
CELL_BITS = 8


coulomb_scale = 0.02
softening = 0.1
field_scale = 0.5
deposit_scale = 0.2
lowest_eig = 0.01
highest_eig = 1.99
mobility = 0.3
diffusion = 0.2
time_step = 0.2


def split3(value):
    first = value.astype(jnp.bfloat16).astype(jnp.float32)
    rest = value - first
    second = rest.astype(jnp.bfloat16).astype(jnp.float32)
    third = (rest - second).astype(jnp.bfloat16).astype(jnp.float32)
    return (first, second, third)


def moment_pieces(comps, charge):
    rows = [None] * 12
    for part, charged in enumerate((*comps, None)):
        for level, piece in enumerate(split3(charge if charged is None else charge * charged)):
            rows[4 * level + part] = piece
    return rows


def selections():
    near_kinds, far_kinds = ([], [])
    for part in range(3):
        near_kinds += [3 * part + level for level in (0, 0, 0, 1, 1, 2)]
        far_kinds += [3 * part + level for level in (0, 1, 2, 0, 1, 0)]
    near_kinds += [9, 10, 11, 12, 12, 12]
    far_kinds += [12, 12, 12, 9, 10, 11]
    near = np.zeros((128, 1024), np.float32)
    far = np.zeros((256, 128), np.float32)
    moment = np.zeros((128, 128), np.float32)
    for cluster in range(8):
        for index, kind in enumerate(near_kinds):
            near[kind * 8 + cluster, cluster * 128 + index] = 1.0
        for index, kind in enumerate(far_kinds):
            far[cluster * 32 + index, kind * 8 + cluster] = 1.0
        for kind in range(12):
            moment[cluster * 16 + kind, kind * 8 + cluster] = 1.0
    return tuple(jnp.asarray(part, jnp.bfloat16) for part in (near, far, moment))


def pair_kernel(own_rows_ref, other_rows_ref, *refs):
    near_sel_ref, far_sel_ref, moment_sel_ref, own_ref = refs[:4]
    refs = refs[4:]
    sources = (len(refs) - 11) // 2
    other_refs = refs[:sources]
    own_out_ref = refs[sources]
    other_out_refs = refs[sources + 1 : 2 * sources + 1]
    (
        near_ref,
        far_ref,
        own_moment_ref,
        other_moment_ref,
        own_sum_ref,
        other_sum_ref,
        *passed_refs,
    ) = refs[2 * sources + 1 :]
    clusters = own_ref.shape[0] // 4
    slots = other_out_refs[0].shape[0] // 4
    others = slots * sources
    groups = own_rows_ref.shape[0] // UNROLL
    units = UNROLL // QUAD
    ones = jnp.ones((8, 128), jnp.float32)
    zeros = jnp.zeros((8, 128), jnp.float32)

    def components(data_ref, start):
        return [data_ref[pl.ds(4 * start + part, 8, stride=4), :] for part in range(4)]

    def place_pieces(comps, factor, offset):
        pieces = []
        square = zeros
        for comp in comps:
            square = square + comp * comp
            pieces += split3(factor * comp)
        pieces += [*split3(square + offset), ones]
        return jnp.concatenate(pieces + [zeros] * (16 - len(pieces)), axis=0)

    def selected(left, right):
        return jnp.dot(
            left.astype(jnp.bfloat16), right, preferred_element_type=jnp.float32
        ).astype(jnp.bfloat16)

    def near_rows(step, _):
        start = pl.multiple_of(step * 8, 8)
        *comps, charge = components(own_ref, start)
        moments = jnp.concatenate(moment_pieces(comps, charge) + [zeros] * 4, axis=0)
        own_moment_ref[pl.ds(pl.multiple_of(start * 16, 128), 128), :] = selected(
            moment_sel_ref[...], moments.astype(jnp.bfloat16)
        )
        tiles = selected(place_pieces(comps, 1.0, 0.0).T, near_sel_ref[...])
        for index in range(8):
            at = pl.ds(pl.multiple_of((start + index) * 128, 128), 128)
            near_ref[at, :] = tiles[:, 128 * index : 128 * index + 128]
        return 0

    def far_rows(source, step, _):
        local = pl.multiple_of(step * 8, 8)
        start = source * slots + local
        *comps, charge = components(other_refs[source], local)
        far_ref[pl.ds(pl.multiple_of(start * 32, 256), 256), :] = selected(
            far_sel_ref[...], place_pieces(comps, -2.0, softening).astype(jnp.bfloat16)
        )
        moments = jnp.concatenate(moment_pieces(comps, charge) + [zeros] * 4, axis=0)
        other_moment_ref[pl.ds(pl.multiple_of(start * 16, 128), 128), :] = selected(
            moment_sel_ref[...], moments.astype(jnp.bfloat16)
        )
        return 0

    lax.fori_loop(0, clusters // 8, near_rows, 0, unroll=4)
    for source in range(sources):
        lax.fori_loop(0, slots // 8, functools.partial(far_rows, source), 0, unroll=4)
    own_sum_ref[...] = jnp.zeros_like(own_sum_ref)
    other_sum_ref[...] = jnp.zeros_like(other_sum_ref)
    dist_refs, weight_refs = (passed_refs[:2], passed_refs[2:])
    dist_refs[0][...] = jnp.full(dist_refs[0].shape, 1e38, jnp.float32)
    weight_refs[0][...] = jnp.zeros_like(weight_refs[0])

    def block_diagonal(blocks):
        blank = jnp.zeros_like(blocks[0])
        lines = [
            jnp.concatenate(
                [block if turn == at else blank for turn in range(len(blocks))], axis=1
            )
            for at, block in enumerate(blocks)
        ]
        return jnp.concatenate(lines, axis=0)

    def distances(pair, unit, turn, dist_ref):
        own = own_rows_ref[pair + turn]
        other = other_rows_ref[pair + turn]
        dist_ref[unit, :, 128 * turn : 128 * turn + 128] = jnp.dot(
            near_ref[pl.ds(pl.multiple_of(own * 128, 128), 128), 0:32],
            far_ref[pl.ds(pl.multiple_of(other * 32, 32), 32), :],
            preferred_element_type=jnp.float32,
        )

    def weights(unit, turn, dist_ref, weight_ref):
        root = lax.rsqrt(dist_ref[unit, :, 128 * turn : 128 * turn + 128])
        weight = root * root * root
        high = weight.astype(jnp.bfloat16)
        weight_ref[unit, 128 * turn : 128 * turn + 128, :128] = high
        weight_ref[unit, 128 * turn : 128 * turn + 128, 128:] = (
            weight - high.astype(jnp.float32)
        ).astype(jnp.bfloat16)

    def moments_of(moment_ref, indices):
        return block_diagonal(
            [moment_ref[pl.ds(pl.multiple_of(index * 16, 16), 16), :] for index in indices]
        )

    def own_products(others, weight_ref, unit):
        levels = [
            jnp.concatenate(
                [weight_ref[unit, 128 * turn : 128 * turn + 128, lanes] for turn in range(QUAD)],
                axis=1,
            )
            for lanes in (slice(0, 128), slice(128, 256))
        ]
        return lax.dot_general(
            moments_of(other_moment_ref, others),
            jnp.concatenate(levels, axis=0),
            (((1,), (1,)), ((), ())),
            preferred_element_type=jnp.float32,
        )

    def other_products(owns, weight_ref, unit):
        return jnp.dot(
            moments_of(own_moment_ref, owns), weight_ref[unit], preferred_element_type=jnp.float32
        )

    def add_rows(sum_ref, indices, values):
        values = values[:, :128] + values[:, 128:]
        for turn, index in enumerate(indices):
            at = pl.ds(pl.multiple_of(index * 16, 16), 16)
            sum_ref[at, :] += values[16 * turn : 16 * turn + 16]

    def half_step(step, side):
        last = jnp.maximum(step - 2, 0) * UNROLL
        first = jnp.minimum(step, groups - 1) * UNROLL
        for unit in range(units):
            owns = [own_rows_ref[last + QUAD * unit + turn] for turn in range(QUAD)]
            others = [other_rows_ref[last + QUAD * unit + turn] for turn in range(QUAD)]
            for turn in range(QUAD):
                distances(first + QUAD * unit, unit, turn, dist_refs[1 - side])
                if turn == 0:
                    to_own = own_products(others, weight_refs[side], unit)
                if turn == 2:
                    to_other = other_products(owns, weight_refs[side], unit)
                weights(unit, turn, dist_refs[side], weight_refs[1 - side])
            add_rows(own_sum_ref, owns, to_own)
            add_rows(other_sum_ref, others, to_other)

    def visit(step, _):
        for side in range(2):
            half_step(step * 2 + side, side)
        return 0

    lax.fori_loop(0, (groups + 2) // 2, visit, 0)

    def finish(data_ref, out_ref, sum_ref, base, step, _):
        start = pl.multiple_of(step * 8, 8)
        *comps, charge = components(data_ref, start)

        def total(part):
            terms = [
                sum_ref[pl.ds(base + start * 16 + 4 * level + part, 8, stride=16), :]
                for level in range(3)
            ]
            return terms[0] + (terms[1] + terms[2])

        weight = total(3)
        scale = coulomb_scale * charge
        for part, comp in enumerate(comps):
            out_ref[pl.ds(4 * start + part, 8, stride=4), :] = scale * (comp * weight - total(part))
        out_ref[pl.ds(4 * start + 3, 8, stride=4), :] = zeros
        return 0

    lax.fori_loop(
        0, clusters // 8, functools.partial(finish, own_ref, own_out_ref, own_sum_ref, 0), 0, unroll=4
    )
    for source in range(sources):
        body = functools.partial(
            finish,
            other_refs[source],
            other_out_refs[source],
            other_sum_ref,
            source * slots * 16,
        )
        lax.fori_loop(0, slots // 8, body, 0, unroll=4)


def pair_forces(own_rows, other_rows, own, arrived, slots):
    clusters = own.shape[0] // 4
    others = slots * len(arrived)
    pairs = own_rows.shape[0]
    smem = pl.BlockSpec(memory_space=pltpu.SMEM)
    vmem = pl.BlockSpec(memory_space=pltpu.VMEM)
    return pl.pallas_call(
        pair_kernel,
        out_shape=(
            jax.ShapeDtypeStruct(own.shape, jnp.float32),
            *[jax.ShapeDtypeStruct((slots * 4, 128), jnp.float32)] * len(arrived),
        ),
        in_specs=[smem, smem] + [vmem] * (4 + len(arrived)),
        out_specs=(vmem,) * (len(arrived) + 1),
        scratch_shapes=[
            pltpu.VMEM((clusters * 128, 128), jnp.bfloat16),
            pltpu.VMEM((others * 32, 128), jnp.bfloat16),
            pltpu.VMEM((clusters * 16, 128), jnp.bfloat16),
            pltpu.VMEM((others * 16, 128), jnp.bfloat16),
            pltpu.VMEM((clusters * 16, 128), jnp.float32),
            pltpu.VMEM((others * 16, 128), jnp.float32),
            *[pltpu.VMEM((UNROLL // QUAD, 128, 128 * QUAD), jnp.float32)] * 2,
            *[pltpu.VMEM((UNROLL // QUAD, 128 * QUAD, 256), jnp.bfloat16)] * 2,
        ],
        compiler_params=pltpu.CompilerParams(vmem_limit_bytes=40 * 1024 * 1024),
        cost_estimate=pl.CostEstimate(
            flops=pairs * 128 * 128 * 20, bytes_accessed=4 * 1024 * 1024, transcendentals=0
        ),
        name="pair_forces",
    )(own_rows, other_rows, *selections(), own, *arrived)


def prepare_kernel(
    fill_ref,
    cell_ref,
    send_index_ref,
    send_count_ref,
    cell_row_ref,
    position_hbm,
    charge_hbm,
    ion_hbm,
    start_hbm,
    screen_hbm,
    own_ref,
    masked_ref,
    inverse_ref,
    source_ref,
    *refs,
):
    out_refs, scratch = (refs[:-8], refs[-8:])
    sum_ref, deposit_ref, position_ref, charge_ref, ion_ref, start_ref, screen_ref, sems = scratch
    copies = [
        pltpu.make_async_copy(source, target, sems.at[index])
        for index, (source, target) in enumerate(
            (
                (position_hbm, position_ref),
                (charge_hbm, charge_ref),
                (ion_hbm, ion_ref),
                (start_hbm, start_ref),
                (screen_hbm, screen_ref),
            )
        )
    ]
    for copy in copies:
        copy.start()
    copies[0].wait()
    copies[1].wait()
    clusters = charge_ref.shape[0]
    cells_x, cells_y, _ = ion_ref.shape
    slots = send_index_ref.shape[1]
    lane = lax.broadcasted_iota(jnp.int32, (1, 128), 1)
    row = lax.broadcasted_iota(jnp.int32, (4, 128), 0)

    def collect(step, _):
        for turn in range(8):
            cluster = step * 8 + turn
            masked = jnp.where(lane < fill_ref[cluster], charge_ref[pl.ds(cluster, 1), :], 0.0)
            masked_ref[pl.ds(cluster, 1), :] = masked
            place = position_ref[:, pl.ds(pl.multiple_of(cluster * 128, 128), 128)]
            own_ref[cluster, 0:3, :] = place
            own_ref[cluster, 3:4, :] = masked
        at = pl.ds(pl.multiple_of(step * 8, 8), 8)
        total = jnp.sum(masked_ref[at, :], axis=1, keepdims=True)
        sum_ref[at, :] = jnp.broadcast_to(deposit_scale * total, (8, 128))
        return 0

    lax.fori_loop(0, clusters // 8, collect, 0, unroll=4)

    def fill_messages(step, _):
        for direction, out_ref in enumerate(out_refs):
            parts = []
            for turn in range(2):
                slot = step * 2 + turn
                live = jnp.where(slot < send_count_ref[0, direction], 1.0, 0.0)
                value = own_ref[send_index_ref[direction, slot]]
                parts.append(jnp.where(row == 3, value * live, value))
            out_ref[pl.ds(pl.multiple_of(step * 8, 8), 8), :] = jnp.concatenate(parts, axis=0)
        return 0

    lax.fori_loop(0, slots // 2, fill_messages, 0)

    def place(step, _):
        for turn in range(8):
            cluster = step * 8 + turn
            index_z = lax.bitwise_and(cell_ref[cluster], 127)
            at = pl.ds(cluster, 1)
            sum_ref[at, :] = jnp.where(lane == index_z, sum_ref[at, :], 0.0)
        return 0

    lax.fori_loop(0, clusters // 8, place, 0)
    cell = cell_row_ref[...]
    line = lax.shift_right_logical(cell, CELL_BITS)
    line = (line // cells_y * 2 + lax.shift_right_logical(lax.bitwise_and(cell, 255), 7)) * cells_y
    line = line + lax.shift_right_logical(cell, CELL_BITS) % cells_y
    sums = jnp.concatenate([part.astype(jnp.bfloat16) for part in split3(sum_ref[...])], axis=1)
    block = 128
    for first in range(0, deposit_ref.shape[0], block):
        rows = lax.broadcasted_iota(jnp.int32, (block, clusters), 0) + first
        hot = jnp.where(rows == line, 1.0, 0.0).astype(jnp.bfloat16)
        added = jnp.dot(hot, sums, preferred_element_type=jnp.float32)
        deposit_ref[first : first + block, :] = added[:, :128] + (
            added[:, 128:256] + added[:, 256:]
        )
    for copy in copies[2:]:
        copy.wait()
    inverse_ref[...] = 1.0 / (6.0 + screen_ref[...])
    for index in range(cells_x):
        for half in range(2):
            lanes = slice(128 * half, 128 * half + 128)
            first = (index * 2 + half) * cells_y
            source_ref[index, :, lanes] = (
                ion_ref[index, :, lanes] + deposit_ref[first : first + cells_y, :]
            ) * inverse_ref[index, :, lanes]
    for out_ref, after in ((out_refs[1], True), (out_refs[2], False)):
        for index in range(cells_x):
            base = slots * 4 + index * 32
            offset = 0
            for field_ref, width in zip(
                (start_ref, inverse_ref, source_ref, ion_ref), HALO_WIDTHS, strict=True
            ):
                first = cells_y - width if after else 0
                rows = field_ref[index, first : first + width, :]
                for half in range(2):
                    out_ref[base + 16 * half + offset : base + 16 * half + offset + width, :] = (
                        rows[:, 128 * half : 128 * half + 128]
                    )
                offset += width
            for half in range(2):
                out_ref[base + 16 * half + offset : base + 16 * half + 16, :] = jnp.zeros(
                    (16 - offset, 128), jnp.float32
                )


def prepare(fill, cell, send_index, send_count, positions, charges, ions, start, screen):
    clusters = charges.shape[0]
    directions, slots = send_index.shape
    cells_x = ions.shape[0]
    smem = pl.BlockSpec(memory_space=pltpu.SMEM)
    vmem = pl.BlockSpec(memory_space=pltpu.VMEM)
    rows = [slots * 4] * directions
    rows[1] = rows[2] = slots * 4 + cells_x * 32
    return pl.pallas_call(
        prepare_kernel,
        out_shape=(
            jax.ShapeDtypeStruct((clusters, 4, 128), jnp.float32),
            jax.ShapeDtypeStruct((clusters, 128), jnp.float32),
            jax.ShapeDtypeStruct(ions.shape, jnp.float32),
            jax.ShapeDtypeStruct(ions.shape, jnp.float32),
            *[jax.ShapeDtypeStruct((count, 128), jnp.float32) for count in rows],
        ),
        in_specs=[smem] * 4 + [vmem] + [pl.BlockSpec(memory_space=pltpu.HBM)] * 5,
        out_specs=(vmem,) * (4 + directions),
        scratch_shapes=[
            pltpu.VMEM((clusters, 128), jnp.float32),
            pltpu.VMEM((ions.size // 128, 128), jnp.float32),
            *[
                pltpu.VMEM(operand.shape, jnp.float32)
                for operand in (positions, charges, ions, start, screen)
            ],
            pltpu.SemaphoreType.DMA((5,)),
        ],
        compiler_params=pltpu.CompilerParams(vmem_limit_bytes=60 * 1024 * 1024),
        name="prepare",
    )(
        fill,
        cell,
        send_index,
        send_count,
        cell.reshape(1, clusters),
        positions,
        charges,
        ions,
        start,
        screen,
    )


def line_rows(cells_y):
    return (cells_y + 2 * DEPTH + 7) // 8 * 8


def fill_lines(target_ref, plane, field, field_ref, index, before_ref, after_ref, base):
    cells_y = field_ref.shape[1]
    width = HALO_WIDTHS[field]
    for half in range(2):
        at = (plane * 2 + half) * line_rows(cells_y) + DEPTH
        first = base + index * 32 + 16 * half + sum(HALO_WIDTHS[:field])
        target_ref[pl.ds(at - width, width), :] = before_ref[pl.ds(first, width), :]
        target_ref[pl.ds(at, cells_y), :] = field_ref[index, :, 128 * half : 128 * half + 128]
        target_ref[pl.ds(at + cells_y, width), :] = after_ref[pl.ds(first, width), :]


def planes_kernel(base, *refs):
    field_refs, (before_ref, after_ref, down_ref, up_ref) = (refs[:4], refs[4:])
    cells_x = field_refs[0].shape[0]
    for field, width in enumerate(HALO_WIDTHS):
        plane = sum(HALO_WIDTHS[:field])

        def fill(step, _, field=field, plane=plane, width=width):
            for target_ref, source in ((down_ref, step), (up_ref, cells_x - width + step)):
                fill_lines(
                    target_ref,
                    plane + step,
                    field,
                    field_refs[field],
                    source,
                    before_ref,
                    after_ref,
                    base,
                )
            return 0

        lax.fori_loop(0, width, fill, 0)


def planes(fields, before, after, base):
    vmem = pl.BlockSpec(memory_space=pltpu.VMEM)
    rows = sum(HALO_WIDTHS) * 2 * line_rows(fields[0].shape[1])
    shape = jax.ShapeDtypeStruct((rows, 128), jnp.float32)
    return pl.pallas_call(
        functools.partial(planes_kernel, base),
        out_shape=(shape, shape),
        in_specs=[vmem] * 6,
        out_specs=(vmem, vmem),
        compiler_params=pltpu.CompilerParams(vmem_limit_bytes=32 * 1024 * 1024),
        name="planes",
    )(*fields, before, after)


def face_flux(pot_low, pot_high, ion_low, ion_high):
    speed = -mobility * (pot_high - pot_low)
    return (
        jnp.maximum(speed, 0.0) * ion_low
        + jnp.minimum(speed, 0.0) * ion_high
        - diffusion * (ion_high - ion_low)
    )


def grid_kernel(base, *refs):
    cell_ref, masked_ref = refs[:2]
    field_refs = refs[2:6]
    before_ref, after_ref, lower_ref, upper_ref = refs[6:10]
    potential_ref, next_ref, force_ref = refs[10:13]
    start_ref, inverse_ref, source_ref, ion_ref = refs[13:17]
    updates, resids, final_ref, pick_refs = (refs[17:20], refs[20:22], refs[22], refs[23:26])
    cells_x, cells_y, _ = field_refs[0].shape
    rows = line_rows(cells_y)
    inner = cells_y + 2 * DEPTH - 2
    clusters = masked_ref.shape[0]

    for field, target_ref in enumerate((start_ref, inverse_ref, source_ref, ion_ref)):
        width = HALO_WIDTHS[field]
        size = width * 2 * rows
        first = sum(HALO_WIDTHS[:field]) * 2 * rows
        low = (DEPTH - width) * 2 * rows
        high = (DEPTH + cells_x) * 2 * rows
        target_ref[low : low + size, :] = lower_ref[first : first + size, :]
        target_ref[high : high + size, :] = upper_ref[first : first + size, :]

    def fill(index, _):
        for field, target_ref in enumerate((start_ref, inverse_ref, source_ref, ion_ref)):
            fill_lines(
                target_ref,
                DEPTH + index,
                field,
                field_refs[field],
                index,
                before_ref,
                after_ref,
                base,
            )
        return 0

    lax.fori_loop(0, cells_x, fill, 0, unroll=2)

    def beyond(values):
        lane = lax.broadcasted_iota(jnp.int32, values[0].shape, 1)
        right = [pltpu.roll(value, 127, 1) for value in values]
        left = [pltpu.roll(value, 1, 1) for value in values]
        above = [jnp.where(lane == 127, right[1], right[0]), jnp.where(lane == 127, 0.0, right[1])]
        below = [jnp.where(lane == 0, 0.0, left[0]), jnp.where(lane == 0, left[0], left[1])]
        return (below, above)

    def wide(plane, half, shift=0):
        return pl.ds((plane * 2 + half) * rows + 1 + shift, inner)

    def around(ref, plane):
        here = [ref[wide(plane, half), :] for half in range(2)]
        below, above = beyond(here)
        sums = [
            (ref[wide(plane - 1, half), :] + ref[wide(plane + 1, half), :])
            + (ref[wide(plane, half, -1), :] + ref[wide(plane, half, 1), :])
            + (below[half] + above[half])
            for half in range(2)
        ]
        return (here, sums)

    middle = 0.5 * (highest_eig + lowest_eig)
    spread = 0.5 * (highest_eig - lowest_eig)
    assert middle == 1.0 and SWEEPS == 4

    def sweep_first(plane, _):
        here, sums = around(start_ref, plane)
        for half in range(2):
            at = wide(plane, half)
            updates[0][at, :] = source_ref[at, :] - here[half] + inverse_ref[at, :] * sums[half]
        return 0

    lax.fori_loop(1, cells_x + 2 * DEPTH - 1, sweep_first, 0, unroll=2)

    ratio_ms = middle / spread
    weight_now = 1.0 / ratio_ms
    for turn in range(1, SWEEPS):
        weight_next = 1.0 / (2.0 * ratio_ms - weight_now)
        keep, gain = (weight_next * weight_now, 2.0 * weight_next / spread)
        weight_now = weight_next

        def sweep(plane, _, turn=turn, keep=keep, gain=gain):
            here, sums = around(updates[turn - 1], plane)
            for half in range(2):
                at = wide(plane, half)
                resid = inverse_ref[at, :] * sums[half]
                if turn > 1:
                    resid = resid + (resids[turn - 2][at, :] - here[half])
                update = keep * here[half] + gain * resid
                if turn + 1 < SWEEPS:
                    resids[turn - 1][at, :] = resid
                    updates[turn][at, :] = update
                else:
                    final_ref[at, :] = (start_ref[at, :] + updates[0][at, :]) + (
                        (updates[1][at, :] + here[half]) + update
                    )
            return 0

        first = 1 + turn
        lax.fori_loop(first, cells_x + 2 * DEPTH - first, sweep, 0, unroll=2)

    def local(plane, half, shift=0):
        return pl.ds((plane * 2 + half) * rows + DEPTH + shift, cells_y)

    def advance(index, _):
        plane = index + DEPTH
        pots = [final_ref[local(plane, half), :] for half in range(2)]
        ions = [ion_ref[local(plane, half), :] for half in range(2)]
        pot_below, pot_above = beyond(pots)
        ion_below, ion_above = beyond(ions)
        for half in range(2):
            pot, ion = (pots[half], ions[half])
            steps = [
                (final_ref[at, :], ion_ref[at, :])
                for at in (
                    local(plane - 1, half),
                    local(plane + 1, half),
                    local(plane, half, -1),
                    local(plane, half, 1),
                )
            ]
            steps += [(pot_below[half], ion_below[half]), (pot_above[half], ion_above[half])]
            total = 0.0
            for low, high in zip(steps[0::2], steps[1::2], strict=True):
                total = total + (
                    face_flux(pot, high[0], ion, high[1]) - face_flux(low[0], pot, low[1], ion)
                )
            lanes = slice(128 * half, 128 * half + 128)
            next_ref[index, :, lanes] = ion - time_step * total
            potential_ref[index, :, lanes] = pot
        return 0

    lax.fori_loop(0, cells_x, advance, 0)

    row_lane = lax.broadcasted_iota(jnp.int32, (1, 128), 1)

    def pick(cluster, _):
        cell = cell_ref[cluster]
        index_x = lax.shift_right_logical(cell, CELL_BITS) // cells_y + DEPTH
        index_y = lax.shift_right_logical(cell, CELL_BITS) % cells_y + DEPTH
        index_z = lax.bitwise_and(cell, 255)
        half = lax.shift_right_logical(index_z, 7)
        here = row_lane == lax.bitwise_and(index_z, 127)

        def line(plane, row, part):
            return final_ref[pl.ds((plane * 2 + part) * rows + row, 1), :]

        along_x = line(index_x - 1, index_y, half) - line(index_x + 1, index_y, half)
        along_y = line(index_x, index_y - 1, half) - line(index_x, index_y + 1, half)
        along_z = jnp.zeros((1, 128), jnp.float32)
        for part in range(2):
            value = line(index_x, index_y, part)
            place = row_lane + 128 * part
            along_z = along_z + jnp.where(place == index_z - 1, value, 0.0)
            along_z = along_z - jnp.where(place == index_z + 1, value, 0.0)
        at = pl.ds(cluster, 1)
        pick_refs[0][at, :] = jnp.where(here, along_x, 0.0)
        pick_refs[1][at, :] = jnp.where(here, along_y, 0.0)
        pick_refs[2][at, :] = along_z
        return 0

    lax.fori_loop(0, clusters, pick, 0, unroll=8)

    def spread_out(step, _):
        start = pl.multiple_of(step * 8, 8)
        charge = masked_ref[pl.ds(start, 8), :] * (0.5 * field_scale)
        for part, pick_ref in enumerate(pick_refs):
            total = jnp.sum(pick_ref[pl.ds(start, 8), :], axis=1, keepdims=True)
            force_ref[pl.ds(4 * start + part, 8, stride=4), :] = charge * total
        force_ref[pl.ds(4 * start + 3, 8, stride=4), :] = jnp.zeros((8, 128), jnp.float32)
        return 0

    lax.fori_loop(0, clusters // 8, spread_out, 0, unroll=4)


def grid_step(cell, masked, fields, before, after, lower, upper, base):
    smem = pl.BlockSpec(memory_space=pltpu.SMEM)
    vmem = pl.BlockSpec(memory_space=pltpu.VMEM)
    clusters = masked.shape[0]
    cells_x, cells_y, _ = fields[0].shape
    block = ((cells_x + 2 * DEPTH) * 2 * line_rows(cells_y), 128)
    return pl.pallas_call(
        functools.partial(grid_kernel, base),
        out_shape=(
            jax.ShapeDtypeStruct(fields[0].shape, jnp.float32),
            jax.ShapeDtypeStruct(fields[0].shape, jnp.float32),
            jax.ShapeDtypeStruct((clusters * 4, 128), jnp.float32),
        ),
        in_specs=[smem] + [vmem] * 9,
        out_specs=(vmem,) * 3,
        scratch_shapes=[pltpu.VMEM(block, jnp.float32)] * 10
        + [pltpu.VMEM((clusters, 128), jnp.float32)] * 3,
        compiler_params=pltpu.CompilerParams(vmem_limit_bytes=40 * 1024 * 1024),
        cost_estimate=pl.CostEstimate(
            flops=block[0] * block[1] * 100, bytes_accessed=8 << 20, transcendentals=0
        ),
        name="grid_step",
    )(cell, masked, *fields, before, after, lower, upper)


def gather_forces_kernel(send_index_ref, own_ref, field_ref, *refs):
    back_refs, (out_ref, sum_ref) = (refs[:-2], refs[-2:])
    clusters = own_ref.shape[0]
    slots = send_index_ref.shape[1]
    sum_ref[...] = own_ref[...] + field_ref[...]

    def visit(slot, _):
        for direction, back_ref in enumerate(back_refs):
            cluster = send_index_ref[direction, slot]
            sum_ref[cluster] += back_ref[slot]
        return 0

    lax.fori_loop(0, slots, visit, 0)

    def write(step, _):
        for turn in range(8):
            cluster = step * 8 + turn
            out_ref[:, pl.ds(pl.multiple_of(cluster * 128, 128), 128)] = sum_ref[cluster][0:3]
        return 0

    lax.fori_loop(0, clusters // 8, write, 0)


def gather_forces(send_index, own, field, backs):
    smem = pl.BlockSpec(memory_space=pltpu.SMEM)
    vmem = pl.BlockSpec(memory_space=pltpu.VMEM)
    clusters = own.shape[0]
    return pl.pallas_call(
        gather_forces_kernel,
        out_shape=jax.ShapeDtypeStruct((3, clusters * 128), jnp.float32),
        in_specs=[smem] + [vmem] * (2 + len(backs)),
        out_specs=vmem,
        scratch_shapes=[pltpu.VMEM(own.shape, jnp.float32)],
        compiler_params=pltpu.CompilerParams(vmem_limit_bytes=32 * 1024 * 1024),
        name="gather_forces",
    )(send_index, own, field, *backs)


def passed_along(shard, axis, by):
    devices = lax.axis_size(axis)
    pairs = [(i, i + by) for i in range(devices) if 0 <= i + by < devices]
    return lax.ppermute(shard, axis, pairs)


ROUTES = (("brick", 1), ("brick", -1), ("brick", 2), ("brick", -2), ("grp", 1), ("grp", -1))


def shards(
    positions,
    charges,
    cluster_fill,
    cluster_cell,
    send_index,
    send_count,
    pair_local,
    pair_dir,
    pair_slot,
    ion_density,
    potential_prev,
    screening,
):
    clusters = cluster_fill.shape[0]
    psize = charges.shape[0] // clusters
    slots = send_index.shape[1]
    base = slots * 4
    own, masked, inverse, source, local, *messages = prepare(
        cluster_fill,
        cluster_cell,
        send_index,
        send_count,
        positions,
        charges.reshape(clusters, psize),
        ion_density,
        potential_prev,
        screening,
    )
    arrived = [local] + [
        passed_along(message, axis, by)
        for message, (axis, by) in zip(messages, ROUTES, strict=True)
    ]
    fields = (potential_prev, inverse, source, ion_density)
    arrived = lax.optimization_barrier(arrived)
    before, after = arrived[1:3]
    down, up = planes(fields, before, after, base)
    lower = passed_along(up, "grp", 1)
    upper = passed_along(down, "grp", -1)
    own_force, *reactions = pair_forces(
        pair_local,
        pair_dir * slots + pair_slot,
        own.reshape(clusters * 4, psize),
        arrived,
        slots,
    )
    backs = [reactions[0]] + [
        passed_along(reaction, axis, -by)
        for reaction, (axis, by) in zip(reactions[1:], ROUTES, strict=True)
    ]
    potential, ion_next, field_force = grid_step(
        cluster_cell, masked, fields, before, after, lower, upper, base
    )
    forces = gather_forces(
        send_index,
        own_force.reshape(clusters, 4, psize),
        field_force.reshape(clusters, 4, psize),
        [back.reshape(slots, 4, psize) for back in backs],
    )
    return (forces, potential, ion_next)


def solution(mesh):
    in_specs = (
        P(None, ("grp", "brick")),
        P(("grp", "brick")),
        P(("grp", "brick")),
        P(("grp", "brick")),
        P(("grp", "brick"), None),
        P(("grp", "brick"), None),
        P(("grp", "brick")),
        P(("grp", "brick")),
        P(("grp", "brick")),
        P("grp", "brick", None),
        P("grp", "brick", None),
        P("grp", "brick", None),
    )
    out_specs = (P(None, ("grp", "brick")), P("grp", "brick", None), P("grp", "brick", None))
    return jax.shard_map(shards, mesh=mesh, in_specs=in_specs, out_specs=out_specs, check_vma=False)
```

```python
import functools

import jax
import jax.numpy as jnp
import numpy as np
from jax import lax
from jax.experimental import pallas as pl
from jax.experimental.pallas import tpu as pltpu
from jax.sharding import PartitionSpec as P

SWEEPS = 4
QUAD = 4
UNROLL = 8
CHUNKS = 4
HALO_WIDTHS = (SWEEPS + 1, SWEEPS, SWEEPS, 1)
DEPTH = SWEEPS + 1
CELL_BITS = 8
SWAPS = tuple(
    (*way, phase) for way in (("brick", 1), ("brick", 2), ("grp", 1)) for phase in (0, 1)
)


coulomb_scale = 0.02
softening = 0.1
field_scale = 0.5
deposit_scale = 0.2
lowest_eig = 0.01
highest_eig = 1.99
mobility = 0.3
diffusion = 0.2
time_step = 0.2


def upward():
    brick, grp = (lax.axis_index("brick"), lax.axis_index("grp"))
    bits = (brick, lax.shift_right_logical(brick, 1), grp)
    return [1 - lax.bitwise_and(bit, 1) for bit in bits]


def sent_row(position, ups):
    way, phase = ((position - 1) // 2, (position - 1) % 2)
    return 1 + 2 * way + (ups[way] if phase else 1 - ups[way])


def swapped(shard, axis, distance, phase):
    devices = lax.axis_size(axis)
    pairs = []
    for index in range(devices):
        step = distance if (index // distance + phase) % 2 == 0 else -distance
        if 0 <= index + step < devices:
            pairs.append((index, index + step))
    return lax.ppermute(shard, axis, pairs)


def split3(value):
    first = value.astype(jnp.bfloat16).astype(jnp.float32)
    rest = value - first
    second = rest.astype(jnp.bfloat16).astype(jnp.float32)
    third = (rest - second).astype(jnp.bfloat16).astype(jnp.float32)
    return (first, second, third)


def moment_pieces(comps, charge):
    rows = [None] * 12
    for part, charged in enumerate((*comps, None)):
        for level, piece in enumerate(split3(charge if charged is None else charge * charged)):
            rows[4 * level + part] = piece
    return rows


def selections():
    near_kinds, far_kinds = ([], [])
    for part in range(3):
        near_kinds += [3 * part + level for level in (0, 0, 0, 1, 1, 2)]
        far_kinds += [3 * part + level for level in (0, 1, 2, 0, 1, 0)]
    near_kinds += [9, 10, 11, 12, 12, 12]
    far_kinds += [12, 12, 12, 9, 10, 11]
    near = np.zeros((128, 1024), np.float32)
    far = np.zeros((256, 128), np.float32)
    moment = np.zeros((128, 128), np.float32)
    for cluster in range(8):
        for index, kind in enumerate(near_kinds):
            near[kind * 8 + cluster, cluster * 128 + index] = 1.0
        for index, kind in enumerate(far_kinds):
            far[cluster * 32 + index, kind * 8 + cluster] = 1.0
        for kind in range(12):
            moment[cluster * 16 + kind, kind * 8 + cluster] = 1.0
    return tuple(jnp.asarray(part, jnp.bfloat16) for part in (near, far, moment))


def pair_kernel(own_rows_ref, other_rows_ref, *refs):
    near_sel_ref, far_sel_ref, moment_sel_ref, own_ref = refs[:4]
    refs = refs[4:]
    sources = (len(refs) - 11) // 2
    other_refs = refs[:sources]
    own_out_ref = refs[sources]
    other_out_refs = refs[sources + 1 : 2 * sources + 1]
    (
        near_ref,
        far_ref,
        own_moment_ref,
        other_moment_ref,
        own_sum_ref,
        other_sum_ref,
        *passed_refs,
    ) = refs[2 * sources + 1 :]
    clusters = own_ref.shape[0] // 4
    slots = other_out_refs[0].shape[0] // 4
    others = slots * sources
    groups = own_rows_ref.shape[0] // UNROLL
    units = UNROLL // QUAD
    ones = jnp.ones((8, 128), jnp.float32)
    zeros = jnp.zeros((8, 128), jnp.float32)

    def components(data_ref, start):
        return [data_ref[pl.ds(4 * start + part, 8, stride=4), :] for part in range(4)]

    def place_pieces(comps, factor, offset):
        pieces = []
        square = zeros
        for comp in comps:
            square = square + comp * comp
            pieces += split3(factor * comp)
        pieces += [*split3(square + offset), ones]
        return jnp.concatenate(pieces + [zeros] * (16 - len(pieces)), axis=0)

    def selected(left, right):
        return jnp.dot(
            left.astype(jnp.bfloat16), right, preferred_element_type=jnp.float32
        ).astype(jnp.bfloat16)

    def near_rows(step, _):
        start = pl.multiple_of(step * 8, 8)
        *comps, charge = components(own_ref, start)
        moments = jnp.concatenate(moment_pieces(comps, charge) + [zeros] * 4, axis=0)
        own_moment_ref[pl.ds(pl.multiple_of(start * 16, 128), 128), :] = selected(
            moment_sel_ref[...], moments.astype(jnp.bfloat16)
        )
        tiles = selected(place_pieces(comps, 1.0, 0.0).T, near_sel_ref[...])
        for index in range(8):
            at = pl.ds(pl.multiple_of((start + index) * 128, 128), 128)
            near_ref[at, :] = tiles[:, 128 * index : 128 * index + 128]
        return 0

    def far_rows(source, step, _):
        local = pl.multiple_of(step * 8, 8)
        start = source * slots + local
        *comps, charge = components(other_refs[source], local)
        far_ref[pl.ds(pl.multiple_of(start * 32, 256), 256), :] = selected(
            far_sel_ref[...], place_pieces(comps, -2.0, softening).astype(jnp.bfloat16)
        )
        moments = jnp.concatenate(moment_pieces(comps, charge) + [zeros] * 4, axis=0)
        other_moment_ref[pl.ds(pl.multiple_of(start * 16, 128), 128), :] = selected(
            moment_sel_ref[...], moments.astype(jnp.bfloat16)
        )
        return 0

    lax.fori_loop(0, clusters // 8, near_rows, 0, unroll=4)
    for source in range(sources):
        lax.fori_loop(0, slots // 8, functools.partial(far_rows, source), 0, unroll=4)
    own_sum_ref[...] = jnp.zeros_like(own_sum_ref)
    other_sum_ref[...] = jnp.zeros_like(other_sum_ref)
    dist_refs, weight_refs = (passed_refs[:2], passed_refs[2:])
    dist_refs[0][...] = jnp.full(dist_refs[0].shape, 1e38, jnp.float32)
    weight_refs[0][...] = jnp.zeros_like(weight_refs[0])

    def distances(pair, unit, turn, dist_ref):
        own = own_rows_ref[pair + turn]
        other = other_rows_ref[pair + turn]
        dist_ref[unit, :, 128 * turn : 128 * turn + 128] = jnp.dot(
            near_ref[pl.ds(pl.multiple_of(own * 128, 128), 128), 0:32],
            far_ref[pl.ds(pl.multiple_of(other * 32, 32), 32), :],
            preferred_element_type=jnp.float32,
        )

    def weights(unit, turn, chunk, dist_ref, weight_ref):
        rows = 128 // CHUNKS
        first = rows * chunk
        dist = dist_ref[unit, first : first + rows, 128 * turn : 128 * turn + 128]
        root = lax.rsqrt(dist)
        weight = root * root * root
        high = weight.astype(jnp.bfloat16)
        low = (weight - high.astype(jnp.float32)).astype(jnp.bfloat16)
        at = slice(128 * turn + first, 128 * turn + first + rows)
        weight_ref[unit, at, :128] = high
        weight_ref[unit, at, 128:] = low

    def row_block(index):
        return pl.ds(pl.multiple_of(index * 16, 16), 16)

    def own_product(other, weight_ref, unit, turn):
        both = weight_ref[unit, 128 * turn : 128 * turn + 128]
        return lax.dot_general(
            other_moment_ref[row_block(other), :],
            jnp.concatenate([both[:, :128], both[:, 128:]], axis=0),
            (((1,), (1,)), ((), ())),
            preferred_element_type=jnp.float32,
        )

    def other_product(own, weight_ref, unit, turn):
        return jnp.dot(
            own_moment_ref[row_block(own), :],
            weight_ref[unit, 128 * turn : 128 * turn + 128],
            preferred_element_type=jnp.float32,
        )

    def add_rows(own, other, to_own, to_other):
        own_sum_ref[row_block(own), :] += to_own[:, :128] + to_own[:, 128:]
        other_sum_ref[row_block(other), :] += to_other[:, :128] + to_other[:, 128:]

    def half_step(step, side):
        last = jnp.maximum(step - 2, 0) * UNROLL
        first = jnp.minimum(step, groups - 1) * UNROLL
        waiting = []
        for index in range(UNROLL):
            unit, turn = (index // QUAD, index % QUAD)
            own = own_rows_ref[last + index]
            other = other_rows_ref[last + index]
            passed = (dist_refs[side], weight_refs[1 - side])
            distances(first + QUAD * unit, unit, turn, dist_refs[1 - side])
            weights(unit, turn, 0, *passed)
            to_own = own_product(other, weight_refs[side], unit, turn)
            weights(unit, turn, 1, *passed)
            weights(unit, turn, 2, *passed)
            to_other = other_product(own, weight_refs[side], unit, turn)
            weights(unit, turn, 3, *passed)
            waiting.append((own, other, to_own, to_other))
            if len(waiting) > 2:
                add_rows(*waiting.pop(0))
        for entry in waiting:
            add_rows(*entry)

    def visit(step, _):
        for side in range(2):
            half_step(step * 2 + side, side)
        return 0

    lax.fori_loop(0, (groups + 2) // 2, visit, 0)

    def finish(data_ref, out_ref, sum_ref, base, step, _):
        start = pl.multiple_of(step * 8, 8)
        *comps, charge = components(data_ref, start)

        def total(part):
            terms = [
                sum_ref[pl.ds(base + start * 16 + 4 * level + part, 8, stride=16), :]
                for level in range(3)
            ]
            return terms[0] + (terms[1] + terms[2])

        weight = total(3)
        scale = coulomb_scale * charge
        for part, comp in enumerate(comps):
            out_ref[pl.ds(4 * start + part, 8, stride=4), :] = scale * (comp * weight - total(part))
        out_ref[pl.ds(4 * start + 3, 8, stride=4), :] = zeros
        return 0

    lax.fori_loop(
        0, clusters // 8, functools.partial(finish, own_ref, own_out_ref, own_sum_ref, 0), 0, unroll=4
    )
    for source in range(sources):
        body = functools.partial(
            finish,
            other_refs[source],
            other_out_refs[source],
            other_sum_ref,
            source * slots * 16,
        )
        lax.fori_loop(0, slots // 8, body, 0, unroll=4)


def pair_forces(own_rows, other_rows, own, arrived, slots):
    clusters = own.shape[0] // 4
    others = slots * len(arrived)
    pairs = own_rows.shape[0]
    smem = pl.BlockSpec(memory_space=pltpu.SMEM)
    vmem = pl.BlockSpec(memory_space=pltpu.VMEM)
    return pl.pallas_call(
        pair_kernel,
        out_shape=(
            jax.ShapeDtypeStruct(own.shape, jnp.float32),
            *[jax.ShapeDtypeStruct((slots * 4, 128), jnp.float32)] * len(arrived),
        ),
        in_specs=[smem, smem] + [vmem] * (4 + len(arrived)),
        out_specs=(vmem,) * (len(arrived) + 1),
        scratch_shapes=[
            pltpu.VMEM((clusters * 128, 128), jnp.bfloat16),
            pltpu.VMEM((others * 32, 128), jnp.bfloat16),
            pltpu.VMEM((clusters * 16, 128), jnp.bfloat16),
            pltpu.VMEM((others * 16, 128), jnp.bfloat16),
            pltpu.VMEM((clusters * 16, 128), jnp.float32),
            pltpu.VMEM((others * 16, 128), jnp.float32),
            *[pltpu.VMEM((UNROLL // QUAD, 128, 128 * QUAD), jnp.float32)] * 2,
            *[pltpu.VMEM((UNROLL // QUAD, 128 * QUAD, 256), jnp.bfloat16)] * 2,
        ],
        compiler_params=pltpu.CompilerParams(vmem_limit_bytes=40 * 1024 * 1024),
        cost_estimate=pl.CostEstimate(
            flops=pairs * 128 * 128 * 20, bytes_accessed=4 * 1024 * 1024, transcendentals=0
        ),
        name="pair_forces",
    )(own_rows, other_rows, *selections(), own, *arrived)


def prepare_kernel(
    fill_ref,
    cell_ref,
    send_index_ref,
    send_count_ref,
    cell_row_ref,
    position_hbm,
    charge_hbm,
    ion_hbm,
    start_hbm,
    screen_hbm,
    own_ref,
    masked_ref,
    inverse_ref,
    source_ref,
    *refs,
):
    out_refs, scratch = (refs[:-8], refs[-8:])
    sum_ref, deposit_ref, position_ref, charge_ref, ion_ref, start_ref, screen_ref, sems = scratch
    copies = [
        pltpu.make_async_copy(source, target, sems.at[index])
        for index, (source, target) in enumerate(
            (
                (position_hbm, position_ref),
                (charge_hbm, charge_ref),
                (ion_hbm, ion_ref),
                (start_hbm, start_ref),
                (screen_hbm, screen_ref),
            )
        )
    ]
    for copy in copies:
        copy.start()
    copies[0].wait()
    copies[1].wait()
    clusters = charge_ref.shape[0]
    cells_x, cells_y, _ = ion_ref.shape
    slots = send_index_ref.shape[1]
    lane = lax.broadcasted_iota(jnp.int32, (1, 128), 1)
    row = lax.broadcasted_iota(jnp.int32, (4, 128), 0)

    def collect(step, _):
        for turn in range(8):
            cluster = step * 8 + turn
            masked = jnp.where(lane < fill_ref[cluster], charge_ref[pl.ds(cluster, 1), :], 0.0)
            masked_ref[pl.ds(cluster, 1), :] = masked
            place = position_ref[:, pl.ds(pl.multiple_of(cluster * 128, 128), 128)]
            own_ref[cluster, 0:3, :] = place
            own_ref[cluster, 3:4, :] = masked
        at = pl.ds(pl.multiple_of(step * 8, 8), 8)
        total = jnp.sum(masked_ref[at, :], axis=1, keepdims=True)
        sum_ref[at, :] = jnp.broadcast_to(deposit_scale * total, (8, 128))
        return 0

    lax.fori_loop(0, clusters // 8, collect, 0, unroll=4)

    ups = upward()

    def fill_messages(step, _):
        for position, out_ref in enumerate(out_refs):
            direction = sent_row(position, ups) if position else 0
            parts = []
            for turn in range(2):
                slot = step * 2 + turn
                live = jnp.where(slot < send_count_ref[0, direction], 1.0, 0.0)
                value = own_ref[send_index_ref[direction, slot]]
                parts.append(jnp.where(row == 3, value * live, value))
            out_ref[pl.ds(pl.multiple_of(step * 8, 8), 8), :] = jnp.concatenate(parts, axis=0)
        return 0

    lax.fori_loop(0, slots // 2, fill_messages, 0)

    def place(step, _):
        for turn in range(8):
            cluster = step * 8 + turn
            index_z = lax.bitwise_and(cell_ref[cluster], 127)
            at = pl.ds(cluster, 1)
            sum_ref[at, :] = jnp.where(lane == index_z, sum_ref[at, :], 0.0)
        return 0

    lax.fori_loop(0, clusters // 8, place, 0)
    cell = cell_row_ref[...]
    line = lax.shift_right_logical(cell, CELL_BITS)
    line = (line // cells_y * 2 + lax.shift_right_logical(lax.bitwise_and(cell, 255), 7)) * cells_y
    line = line + lax.shift_right_logical(cell, CELL_BITS) % cells_y
    sums = jnp.concatenate([part.astype(jnp.bfloat16) for part in split3(sum_ref[...])], axis=1)
    block = 128
    for first in range(0, deposit_ref.shape[0], block):
        rows = lax.broadcasted_iota(jnp.int32, (block, clusters), 0) + first
        hot = jnp.where(rows == line, 1.0, 0.0).astype(jnp.bfloat16)
        added = jnp.dot(hot, sums, preferred_element_type=jnp.float32)
        deposit_ref[first : first + block, :] = added[:, :128] + (
            added[:, 128:256] + added[:, 256:]
        )
    for copy in copies[2:]:
        copy.wait()
    inverse_ref[...] = 1.0 / (6.0 + screen_ref[...])
    for index in range(cells_x):
        for half in range(2):
            lanes = slice(128 * half, 128 * half + 128)
            first = (index * 2 + half) * cells_y
            source_ref[index, :, lanes] = (
                ion_ref[index, :, lanes] + deposit_ref[first : first + cells_y, :]
            ) * inverse_ref[index, :, lanes]
    def fill_rows(out_ref, after):
        for index in range(cells_x):
            base = slots * 4 + index * 32
            offset = 0
            for field_ref, width in zip(
                (start_ref, inverse_ref, source_ref, ion_ref), HALO_WIDTHS, strict=True
            ):
                first = cells_y - width if after else 0
                rows = field_ref[index, first : first + width, :]
                for half in range(2):
                    out_ref[base + 16 * half + offset : base + 16 * half + offset + width, :] = (
                        rows[:, 128 * half : 128 * half + 128]
                    )
                offset += width
            for half in range(2):
                out_ref[base + 16 * half + offset : base + 16 * half + 16, :] = jnp.zeros(
                    (16 - offset, 128), jnp.float32
                )

    for up in range(2):

        @pl.when(ups[0] == up)
        def _(up=up):
            fill_rows(out_refs[1], up == 1)
            fill_rows(out_refs[2], up == 0)


def prepare(fill, cell, send_index, send_count, positions, charges, ions, start, screen):
    clusters = charges.shape[0]
    directions, slots = send_index.shape
    cells_x = ions.shape[0]
    smem = pl.BlockSpec(memory_space=pltpu.SMEM)
    vmem = pl.BlockSpec(memory_space=pltpu.VMEM)
    rows = [slots * 4] * directions
    rows[1] = rows[2] = slots * 4 + cells_x * 32
    return pl.pallas_call(
        prepare_kernel,
        out_shape=(
            jax.ShapeDtypeStruct((clusters, 4, 128), jnp.float32),
            jax.ShapeDtypeStruct((clusters, 128), jnp.float32),
            jax.ShapeDtypeStruct(ions.shape, jnp.float32),
            jax.ShapeDtypeStruct(ions.shape, jnp.float32),
            *[jax.ShapeDtypeStruct((count, 128), jnp.float32) for count in rows],
        ),
        in_specs=[smem] * 4 + [vmem] + [pl.BlockSpec(memory_space=pltpu.HBM)] * 5,
        out_specs=(vmem,) * (4 + directions),
        scratch_shapes=[
            pltpu.VMEM((clusters, 128), jnp.float32),
            pltpu.VMEM((ions.size // 128, 128), jnp.float32),
            *[
                pltpu.VMEM(operand.shape, jnp.float32)
                for operand in (positions, charges, ions, start, screen)
            ],
            pltpu.SemaphoreType.DMA((5,)),
        ],
        compiler_params=pltpu.CompilerParams(vmem_limit_bytes=60 * 1024 * 1024),
        name="prepare",
    )(
        fill,
        cell,
        send_index,
        send_count,
        cell.reshape(1, clusters),
        positions,
        charges,
        ions,
        start,
        screen,
    )


def line_rows(cells_y):
    return (cells_y + 2 * DEPTH + 7) // 8 * 8


def collect_rows(rim_ref, first_ref, second_ref, base):
    size = rim_ref.shape[0] // 2
    up = upward()[0]
    rim_ref[pl.ds(pl.multiple_of(up * size, size), size), :] = first_ref[base : base + size, :]
    rim_ref[pl.ds(pl.multiple_of((1 - up) * size, size), size), :] = second_ref[
        base : base + size, :
    ]


def fill_lines(target_ref, plane, field, field_ref, index, rim_ref):
    cells_x, cells_y, _ = field_ref.shape
    width = HALO_WIDTHS[field]
    for half in range(2):
        at = (plane * 2 + half) * line_rows(cells_y) + DEPTH
        first = index * 32 + 16 * half + sum(HALO_WIDTHS[:field])
        target_ref[pl.ds(at - width, width), :] = rim_ref[pl.ds(first, width), :]
        target_ref[pl.ds(at, cells_y), :] = field_ref[index, :, 128 * half : 128 * half + 128]
        first = first + cells_x * 32
        target_ref[pl.ds(at + cells_y, width), :] = rim_ref[pl.ds(first, width), :]


def planes_kernel(base, *refs):
    field_refs, (first_ref, second_ref, *out_refs, rim_ref) = (refs[:4], refs[4:])
    cells_x = field_refs[0].shape[0]
    collect_rows(rim_ref, first_ref, second_ref, base)
    up = upward()[2]
    for field, width in enumerate(HALO_WIDTHS):
        plane = sum(HALO_WIDTHS[:field])

        def fill(step, _, field=field, plane=plane, width=width):
            for phase, out_ref in enumerate(out_refs):
                last = up if phase == 0 else 1 - up
                source = last * (cells_x - width) + step
                fill_lines(out_ref, plane + step, field, field_refs[field], source, rim_ref)
            return 0

        lax.fori_loop(0, width, fill, 0)


def planes(fields, first, second, base):
    vmem = pl.BlockSpec(memory_space=pltpu.VMEM)
    cells_x, cells_y, _ = fields[0].shape
    rows = sum(HALO_WIDTHS) * 2 * line_rows(cells_y)
    shape = jax.ShapeDtypeStruct((rows, 128), jnp.float32)
    return pl.pallas_call(
        functools.partial(planes_kernel, base),
        out_shape=(shape, shape),
        in_specs=[vmem] * 6,
        out_specs=(vmem, vmem),
        scratch_shapes=[pltpu.VMEM((cells_x * 64, 128), jnp.float32)],
        compiler_params=pltpu.CompilerParams(vmem_limit_bytes=32 * 1024 * 1024),
        name="planes",
    )(*fields, first, second)


def face_flux(pot_low, pot_high, ion_low, ion_high):
    speed = -mobility * (pot_high - pot_low)
    return (
        jnp.maximum(speed, 0.0) * ion_low
        + jnp.minimum(speed, 0.0) * ion_high
        - diffusion * (ion_high - ion_low)
    )


def grid_kernel(base, *refs):
    cell_ref, masked_ref = refs[:2]
    field_refs = refs[2:6]
    first_ref, second_ref, *plane_refs = refs[6:10]
    potential_ref, next_ref, force_ref = refs[10:13]
    start_ref, inverse_ref, source_ref, ion_ref = refs[13:17]
    updates, resids, final_ref, pick_refs = (refs[17:20], refs[20:22], refs[22], refs[23:26])
    rim_ref = refs[26]
    cells_x, cells_y, _ = field_refs[0].shape
    rows = line_rows(cells_y)
    inner = cells_y + 2 * DEPTH - 2
    clusters = masked_ref.shape[0]
    up = upward()[2]
    collect_rows(rim_ref, first_ref, second_ref, base)

    for field, target_ref in enumerate((start_ref, inverse_ref, source_ref, ion_ref)):
        width = HALO_WIDTHS[field]
        size = width * 2 * rows
        first = sum(HALO_WIDTHS[:field]) * 2 * rows
        for phase, plane_ref in enumerate(plane_refs):
            higher = up if phase == 0 else 1 - up
            plane = (DEPTH - width) + higher * (cells_x + width)
            at = pl.ds(pl.multiple_of(plane * 2 * rows, 2 * rows), size)
            target_ref[at, :] = plane_ref[first : first + size, :]

    def fill(index, _):
        for field, target_ref in enumerate((start_ref, inverse_ref, source_ref, ion_ref)):
            fill_lines(target_ref, DEPTH + index, field, field_refs[field], index, rim_ref)
        return 0

    lax.fori_loop(0, cells_x, fill, 0, unroll=2)

    def beyond(values):
        lane = lax.broadcasted_iota(jnp.int32, values[0].shape, 1)
        right = [pltpu.roll(value, 127, 1) for value in values]
        left = [pltpu.roll(value, 1, 1) for value in values]
        above = [jnp.where(lane == 127, right[1], right[0]), jnp.where(lane == 127, 0.0, right[1])]
        below = [jnp.where(lane == 0, 0.0, left[0]), jnp.where(lane == 0, left[0], left[1])]
        return (below, above)

    def wide(plane, half, shift=0):
        return pl.ds((plane * 2 + half) * rows + 1 + shift, inner)

    def around(ref, plane):
        here = [ref[wide(plane, half), :] for half in range(2)]
        below, above = beyond(here)
        sums = [
            (ref[wide(plane - 1, half), :] + ref[wide(plane + 1, half), :])
            + (ref[wide(plane, half, -1), :] + ref[wide(plane, half, 1), :])
            + (below[half] + above[half])
            for half in range(2)
        ]
        return (here, sums)

    middle = 0.5 * (highest_eig + lowest_eig)
    spread = 0.5 * (highest_eig - lowest_eig)
    assert middle == 1.0 and SWEEPS == 4

    def sweep_first(plane, _):
        here, sums = around(start_ref, plane)
        for half in range(2):
            at = wide(plane, half)
            updates[0][at, :] = source_ref[at, :] - here[half] + inverse_ref[at, :] * sums[half]
        return 0

    lax.fori_loop(1, cells_x + 2 * DEPTH - 1, sweep_first, 0, unroll=2)

    ratio_ms = middle / spread
    weight_now = 1.0 / ratio_ms
    for turn in range(1, SWEEPS):
        weight_next = 1.0 / (2.0 * ratio_ms - weight_now)
        keep, gain = (weight_next * weight_now, 2.0 * weight_next / spread)
        weight_now = weight_next

        def sweep(plane, _, turn=turn, keep=keep, gain=gain):
            here, sums = around(updates[turn - 1], plane)
            for half in range(2):
                at = wide(plane, half)
                resid = inverse_ref[at, :] * sums[half]
                if turn > 1:
                    resid = resid + (resids[turn - 2][at, :] - here[half])
                update = keep * here[half] + gain * resid
                if turn + 1 < SWEEPS:
                    resids[turn - 1][at, :] = resid
                    updates[turn][at, :] = update
                else:
                    final_ref[at, :] = (start_ref[at, :] + updates[0][at, :]) + (
                        (updates[1][at, :] + here[half]) + update
                    )
            return 0

        first = 1 + turn
        lax.fori_loop(first, cells_x + 2 * DEPTH - first, sweep, 0, unroll=2)

    def local(plane, half, shift=0):
        return pl.ds((plane * 2 + half) * rows + DEPTH + shift, cells_y)

    def advance(index, _):
        plane = index + DEPTH
        pots = [final_ref[local(plane, half), :] for half in range(2)]
        ions = [ion_ref[local(plane, half), :] for half in range(2)]
        pot_below, pot_above = beyond(pots)
        ion_below, ion_above = beyond(ions)
        for half in range(2):
            pot, ion = (pots[half], ions[half])
            steps = [
                (final_ref[at, :], ion_ref[at, :])
                for at in (
                    local(plane - 1, half),
                    local(plane + 1, half),
                    local(plane, half, -1),
                    local(plane, half, 1),
                )
            ]
            steps += [(pot_below[half], ion_below[half]), (pot_above[half], ion_above[half])]
            total = 0.0
            for low, high in zip(steps[0::2], steps[1::2], strict=True):
                total = total + (
                    face_flux(pot, high[0], ion, high[1]) - face_flux(low[0], pot, low[1], ion)
                )
            lanes = slice(128 * half, 128 * half + 128)
            next_ref[index, :, lanes] = ion - time_step * total
            potential_ref[index, :, lanes] = pot
        return 0

    lax.fori_loop(0, cells_x, advance, 0)

    row_lane = lax.broadcasted_iota(jnp.int32, (1, 128), 1)

    def pick(cluster, _):
        cell = cell_ref[cluster]
        index_x = lax.shift_right_logical(cell, CELL_BITS) // cells_y + DEPTH
        index_y = lax.shift_right_logical(cell, CELL_BITS) % cells_y + DEPTH
        index_z = lax.bitwise_and(cell, 255)
        half = lax.shift_right_logical(index_z, 7)
        here = row_lane == lax.bitwise_and(index_z, 127)

        def line(plane, row, part):
            return final_ref[pl.ds((plane * 2 + part) * rows + row, 1), :]

        along_x = line(index_x - 1, index_y, half) - line(index_x + 1, index_y, half)
        along_y = line(index_x, index_y - 1, half) - line(index_x, index_y + 1, half)
        along_z = jnp.zeros((1, 128), jnp.float32)
        for part in range(2):
            value = line(index_x, index_y, part)
            place = row_lane + 128 * part
            along_z = along_z + jnp.where(place == index_z - 1, value, 0.0)
            along_z = along_z - jnp.where(place == index_z + 1, value, 0.0)
        at = pl.ds(cluster, 1)
        pick_refs[0][at, :] = jnp.where(here, along_x, 0.0)
        pick_refs[1][at, :] = jnp.where(here, along_y, 0.0)
        pick_refs[2][at, :] = along_z
        return 0

    lax.fori_loop(0, clusters, pick, 0, unroll=8)

    def spread_out(step, _):
        start = pl.multiple_of(step * 8, 8)
        charge = masked_ref[pl.ds(start, 8), :] * (0.5 * field_scale)
        for part, pick_ref in enumerate(pick_refs):
            total = jnp.sum(pick_ref[pl.ds(start, 8), :], axis=1, keepdims=True)
            force_ref[pl.ds(4 * start + part, 8, stride=4), :] = charge * total
        force_ref[pl.ds(4 * start + 3, 8, stride=4), :] = jnp.zeros((8, 128), jnp.float32)
        return 0

    lax.fori_loop(0, clusters // 8, spread_out, 0, unroll=4)


def grid_step(cell, masked, fields, rims, edges, base):
    smem = pl.BlockSpec(memory_space=pltpu.SMEM)
    vmem = pl.BlockSpec(memory_space=pltpu.VMEM)
    clusters = masked.shape[0]
    cells_x, cells_y, _ = fields[0].shape
    block = ((cells_x + 2 * DEPTH) * 2 * line_rows(cells_y), 128)
    return pl.pallas_call(
        functools.partial(grid_kernel, base),
        out_shape=(
            jax.ShapeDtypeStruct(fields[0].shape, jnp.float32),
            jax.ShapeDtypeStruct(fields[0].shape, jnp.float32),
            jax.ShapeDtypeStruct((clusters * 4, 128), jnp.float32),
        ),
        in_specs=[smem] + [vmem] * 9,
        out_specs=(vmem,) * 3,
        scratch_shapes=[pltpu.VMEM(block, jnp.float32)] * 10
        + [pltpu.VMEM((clusters, 128), jnp.float32)] * 3
        + [pltpu.VMEM((cells_x * 64, 128), jnp.float32)],
        compiler_params=pltpu.CompilerParams(vmem_limit_bytes=40 * 1024 * 1024),
        cost_estimate=pl.CostEstimate(
            flops=block[0] * block[1] * 100, bytes_accessed=8 << 20, transcendentals=0
        ),
        name="grid_step",
    )(cell, masked, *fields, *rims, *edges)


def gather_forces_kernel(send_index_ref, own_ref, field_ref, *refs):
    back_refs, (out_ref, sum_ref) = (refs[:-2], refs[-2:])
    clusters = own_ref.shape[0]
    slots = send_index_ref.shape[1]
    sum_ref[...] = own_ref[...] + field_ref[...]
    ups = upward()

    def visit(slot, _):
        for position, back_ref in enumerate(back_refs):
            cluster = send_index_ref[sent_row(position, ups) if position else 0, slot]
            sum_ref[cluster] += back_ref[slot]
        return 0

    lax.fori_loop(0, slots, visit, 0)

    def write(step, _):
        for turn in range(8):
            cluster = step * 8 + turn
            out_ref[:, pl.ds(pl.multiple_of(cluster * 128, 128), 128)] = sum_ref[cluster][0:3]
        return 0

    lax.fori_loop(0, clusters // 8, write, 0)


def gather_forces(send_index, own, field, backs):
    smem = pl.BlockSpec(memory_space=pltpu.SMEM)
    vmem = pl.BlockSpec(memory_space=pltpu.VMEM)
    clusters = own.shape[0]
    return pl.pallas_call(
        gather_forces_kernel,
        out_shape=jax.ShapeDtypeStruct((3, clusters * 128), jnp.float32),
        in_specs=[smem] + [vmem] * (2 + len(backs)),
        out_specs=vmem,
        scratch_shapes=[pltpu.VMEM(own.shape, jnp.float32)],
        compiler_params=pltpu.CompilerParams(vmem_limit_bytes=32 * 1024 * 1024),
        name="gather_forces",
    )(send_index, own, field, *backs)


def shards(
    positions,
    charges,
    cluster_fill,
    cluster_cell,
    send_index,
    send_count,
    pair_local,
    pair_dir,
    pair_slot,
    ion_density,
    potential_prev,
    screening,
):
    clusters = cluster_fill.shape[0]
    psize = charges.shape[0] // clusters
    slots = send_index.shape[1]
    base = slots * 4
    own, masked, inverse, source, local, *messages = prepare(
        cluster_fill,
        cluster_cell,
        send_index,
        send_count,
        positions,
        charges.reshape(clusters, psize),
        ion_density,
        potential_prev,
        screening,
    )
    arrived = [local] + [
        swapped(message, *swap) for message, swap in zip(messages, SWAPS, strict=True)
    ]
    fields = (potential_prev, inverse, source, ion_density)
    arrived = lax.optimization_barrier(arrived)
    rims = arrived[1:3]
    edges = [
        swapped(edge, "grp", 1, phase) for phase, edge in enumerate(planes(fields, *rims, base))
    ]
    way = lax.shift_right_arithmetic(pair_dir - 1, 1)
    ups = upward()
    flip = jnp.where(way == 0, ups[0], jnp.where(way == 1, ups[1], ups[2]))
    position = 1 + 2 * way + lax.bitwise_xor(lax.bitwise_and(pair_dir - 1, 1), flip)
    own_force, *reactions = pair_forces(
        pair_local,
        jnp.where(pair_dir == 0, 0, position) * slots + pair_slot,
        own.reshape(clusters * 4, psize),
        arrived,
        slots,
    )
    backs = [reactions[0]] + [
        swapped(reaction, *swap) for reaction, swap in zip(reactions[1:], SWAPS, strict=True)
    ]
    potential, ion_next, field_force = grid_step(cluster_cell, masked, fields, rims, edges, base)
    forces = gather_forces(
        send_index,
        own_force.reshape(clusters, 4, psize),
        field_force.reshape(clusters, 4, psize),
        [back.reshape(slots, 4, psize) for back in backs],
    )
    return (forces, potential, ion_next)


def solution(mesh):
    in_specs = (
        P(None, ("grp", "brick")),
        P(("grp", "brick")),
        P(("grp", "brick")),
        P(("grp", "brick")),
        P(("grp", "brick"), None),
        P(("grp", "brick"), None),
        P(("grp", "brick")),
        P(("grp", "brick")),
        P(("grp", "brick")),
        P("grp", "brick", None),
        P("grp", "brick", None),
        P("grp", "brick", None),
    )
    out_specs = (P(None, ("grp", "brick")), P("grp", "brick", None), P("grp", "brick", None))
    return jax.shard_map(shards, mesh=mesh, in_specs=in_specs, out_specs=out_specs, check_vma=False)
```

```python
import functools

import jax
import jax.numpy as jnp
import numpy as np
from jax import lax
from jax.experimental import pallas as pl
from jax.experimental.pallas import tpu as pltpu
from jax.sharding import PartitionSpec as P

SWEEPS = 4
UNROLL = 8
CHUNKS = 4
HALO_WIDTHS = (SWEEPS + 1, SWEEPS, SWEEPS, 1)
DEPTH = SWEEPS + 1
CELL_BITS = 8
SWAPS = tuple(
    (*way, phase) for way in (("brick", 1), ("brick", 2), ("grp", 1)) for phase in (0, 1)
)


coulomb_scale = 0.02
softening = 0.1
field_scale = 0.5
deposit_scale = 0.2
lowest_eig = 0.01
highest_eig = 1.99
mobility = 0.3
diffusion = 0.2
time_step = 0.2


VMEM_LIMIT = 60 * 1024 * 1024


def start_copies(pairs, sems):
    copies = [
        pltpu.make_async_copy(source, target, sems.at[index])
        for index, (source, target) in enumerate(pairs)
    ]
    for copy in copies:
        copy.start()
    return copies


def upward():
    brick, grp = (lax.axis_index("brick"), lax.axis_index("grp"))
    bits = (brick, lax.shift_right_logical(brick, 1), grp)
    return [1 - lax.bitwise_and(bit, 1) for bit in bits]


def sent_row(position, ups):
    way, phase = ((position - 1) // 2, (position - 1) % 2)
    return 1 + 2 * way + (ups[way] if phase else 1 - ups[way])


def swapped(shard, axis, distance, phase):
    devices = lax.axis_size(axis)
    pairs = []
    for index in range(devices):
        step = distance if (index // distance + phase) % 2 == 0 else -distance
        if 0 <= index + step < devices:
            pairs.append((index, index + step))
    return lax.ppermute(shard, axis, pairs)


def split3(value):
    first = value.astype(jnp.bfloat16).astype(jnp.float32)
    rest = value - first
    second = rest.astype(jnp.bfloat16).astype(jnp.float32)
    third = (rest - second).astype(jnp.bfloat16).astype(jnp.float32)
    return (first, second, third)


def moment_pieces(comps, charge):
    rows = [None] * 12
    for part, charged in enumerate((*comps, None)):
        for level, piece in enumerate(split3(charge if charged is None else charge * charged)):
            rows[4 * level + part] = piece
    return rows


def selections():
    near_kinds, far_kinds = ([], [])
    for part in range(3):
        near_kinds += [3 * part + level for level in (0, 0, 0, 1, 1, 2)]
        far_kinds += [3 * part + level for level in (0, 1, 2, 0, 1, 0)]
    near_kinds += [9, 10, 11, 12, 12, 12]
    far_kinds += [12, 12, 12, 9, 10, 11]
    near = np.zeros((128, 1024), np.float32)
    far = np.zeros((256, 128), np.float32)
    moment = np.zeros((128, 128), np.float32)
    for cluster in range(8):
        for index, kind in enumerate(near_kinds):
            near[kind * 8 + cluster, cluster * 128 + index] = 1.0
        for index, kind in enumerate(far_kinds):
            far[cluster * 32 + index, kind * 8 + cluster] = 1.0
        for kind in range(12):
            moment[cluster * 16 + kind, kind * 8 + cluster] = 1.0
    return tuple(jnp.asarray(part, jnp.bfloat16) for part in (near, far, moment))


def pair_kernel(own_rows_ref, other_rows_ref, *refs):
    sources = len(SWAPS) + 1
    fetched = sources + 4
    hbm_refs = refs[:fetched]
    own_out_ref = refs[fetched]
    other_out_refs = refs[fetched + 1 : fetched + 1 + sources]
    refs = refs[fetched + 1 + sources :]
    near_sel_ref, far_sel_ref, moment_sel_ref, own_ref = refs[:4]
    other_refs = refs[4:fetched]
    sems = refs[fetched]
    copies = start_copies(
        [
            (source.at[0 : target.shape[0]], target)
            for source, target in zip(hbm_refs, refs[:fetched], strict=True)
        ],
        sems,
    )
    (
        near_ref,
        far_ref,
        own_moment_ref,
        other_moment_ref,
        own_sum_ref,
        other_sum_ref,
        dist_ref,
        *weight_refs,
    ) = refs[fetched + 1 :]
    clusters = own_ref.shape[0] // 4
    slots = other_out_refs[0].shape[0] // 4
    others = slots * sources
    groups = own_rows_ref.shape[0] // UNROLL
    ones = jnp.ones((8, 128), jnp.float32)
    zeros = jnp.zeros((8, 128), jnp.float32)

    def components(data_ref, start):
        return [data_ref[pl.ds(4 * start + part, 8, stride=4), :] for part in range(4)]

    def place_pieces(comps, factor, offset):
        pieces = []
        square = zeros
        for comp in comps:
            square = square + comp * comp
            pieces += split3(factor * comp)
        pieces += [*split3(square + offset), ones]
        return jnp.concatenate(pieces + [zeros] * (16 - len(pieces)), axis=0)

    def selected(left, right):
        return jnp.dot(
            left.astype(jnp.bfloat16), right, preferred_element_type=jnp.float32
        ).astype(jnp.bfloat16)

    def near_rows(step, _):
        start = pl.multiple_of(step * 8, 8)
        *comps, charge = components(own_ref, start)
        moments = jnp.concatenate(moment_pieces(comps, charge) + [zeros] * 4, axis=0)
        own_moment_ref[pl.ds(pl.multiple_of(start * 16, 128), 128), :] = selected(
            moment_sel_ref[...], moments.astype(jnp.bfloat16)
        )
        tiles = selected(place_pieces(comps, 1.0, 0.0).T, near_sel_ref[...])
        for index in range(8):
            at = pl.ds(pl.multiple_of((start + index) * 128, 128), 128)
            near_ref[at, :] = tiles[:, 128 * index : 128 * index + 128]
        return 0

    def far_rows(source, step, _):
        local = pl.multiple_of(step * 8, 8)
        start = source * slots + local
        *comps, charge = components(other_refs[source], local)
        far_ref[pl.ds(pl.multiple_of(start * 32, 256), 256), :] = selected(
            far_sel_ref[...], place_pieces(comps, -2.0, softening).astype(jnp.bfloat16)
        )
        moments = jnp.concatenate(moment_pieces(comps, charge) + [zeros] * 4, axis=0)
        other_moment_ref[pl.ds(pl.multiple_of(start * 16, 128), 128), :] = selected(
            moment_sel_ref[...], moments.astype(jnp.bfloat16)
        )
        return 0

    own_sum_ref[...] = jnp.zeros_like(own_sum_ref)
    other_sum_ref[...] = jnp.zeros_like(other_sum_ref)
    weight_refs[0][...] = jnp.zeros_like(weight_refs[0])
    for copy in copies[:4]:
        copy.wait()
    lax.fori_loop(0, clusters // 8, near_rows, 0, unroll=4)
    for copy in copies[4:]:
        copy.wait()
    for source in range(sources):
        lax.fori_loop(0, slots // 8, functools.partial(far_rows, source), 0, unroll=4)
    def distances(pair):
        own = own_rows_ref[pair]
        other = other_rows_ref[pair]
        return jnp.dot(
            near_ref[pl.ds(pl.multiple_of(own * 128, 128), 128), 0:32],
            far_ref[pl.ds(pl.multiple_of(other * 32, 32), 32), :],
            preferred_element_type=jnp.float32,
        )

    def weights(dist, index, chunk, weight_ref):
        rows = 128 // CHUNKS
        first = rows * chunk
        root = lax.rsqrt(dist[first : first + rows])
        weight = root * root * root
        high = weight.astype(jnp.bfloat16)
        low = (weight - high.astype(jnp.float32)).astype(jnp.bfloat16)
        at = slice(128 * index + first, 128 * index + first + rows)
        weight_ref[at, :128] = high
        weight_ref[at, 128:] = low

    def row_block(index):
        return pl.ds(pl.multiple_of(index * 16, 16), 16)

    def own_product(other, weight_ref, index):
        both = weight_ref[128 * index : 128 * index + 128]
        return lax.dot_general(
            other_moment_ref[row_block(other), :],
            jnp.concatenate([both[:, :128], both[:, 128:]], axis=0),
            (((1,), (1,)), ((), ())),
            preferred_element_type=jnp.float32,
        )

    def other_product(own, weight_ref, index):
        return jnp.dot(
            own_moment_ref[row_block(own), :],
            weight_ref[128 * index : 128 * index + 128],
            preferred_element_type=jnp.float32,
        )

    def add_rows(own, other, to_own, to_other):
        own_sum_ref[row_block(own), :] += to_own[:, :128] + to_own[:, 128:]
        other_sum_ref[row_block(other), :] += to_other[:, :128] + to_other[:, 128:]

    def half_step(step, side, dist):
        last = jnp.maximum(step - 1, 0) * UNROLL
        waiting = []
        for index in range(UNROLL):
            own = own_rows_ref[last + index]
            other = other_rows_ref[last + index]
            later = distances(jnp.minimum(step * UNROLL + index + 1, groups * UNROLL - 1))
            weights(dist, index, 0, weight_refs[1 - side])
            to_own = own_product(other, weight_refs[side], index)
            weights(dist, index, 1, weight_refs[1 - side])
            weights(dist, index, 2, weight_refs[1 - side])
            to_other = other_product(own, weight_refs[side], index)
            weights(dist, index, 3, weight_refs[1 - side])
            dist = later
            waiting.append((own, other, to_own, to_other))
            if len(waiting) > 2:
                add_rows(*waiting.pop(0))
        for entry in waiting:
            add_rows(*entry)
        return dist

    def visit(step, _):
        dist = dist_ref[...]
        for side in range(2):
            dist = half_step(step * 2 + side, side, dist)
        dist_ref[...] = dist
        return 0

    dist_ref[...] = distances(0)
    lax.fori_loop(0, groups // 2, visit, 0)
    half_step(groups, 0, dist_ref[...])

    def finish(data_ref, out_ref, sum_ref, base, step, _):
        start = pl.multiple_of(step * 8, 8)
        *comps, charge = components(data_ref, start)

        def total(part):
            terms = [
                sum_ref[pl.ds(base + start * 16 + 4 * level + part, 8, stride=16), :]
                for level in range(3)
            ]
            return terms[0] + (terms[1] + terms[2])

        weight = total(3)
        scale = coulomb_scale * charge
        for part, comp in enumerate(comps):
            out_ref[pl.ds(4 * start + part, 8, stride=4), :] = scale * (comp * weight - total(part))
        out_ref[pl.ds(4 * start + 3, 8, stride=4), :] = zeros
        return 0

    lax.fori_loop(
        0, clusters // 8, functools.partial(finish, own_ref, own_out_ref, own_sum_ref, 0), 0, unroll=4
    )
    for source in range(sources):
        body = functools.partial(
            finish,
            other_refs[source],
            other_out_refs[source],
            other_sum_ref,
            source * slots * 16,
        )
        lax.fori_loop(0, slots // 8, body, 0, unroll=4)


def pair_forces(own_rows, other_rows, own, arrived, slots):
    clusters = own.shape[0] // 4
    others = slots * len(arrived)
    pairs = own_rows.shape[0]
    smem = pl.BlockSpec(memory_space=pltpu.SMEM)
    vmem = pl.BlockSpec(memory_space=pltpu.VMEM)
    hbm = pl.BlockSpec(memory_space=pltpu.HBM)
    operands = (*selections(), own)
    return pl.pallas_call(
        pair_kernel,
        out_shape=(
            jax.ShapeDtypeStruct(own.shape, jnp.float32),
            *[jax.ShapeDtypeStruct((slots * 4, 128), jnp.float32)] * len(arrived),
        ),
        in_specs=[smem, smem] + [hbm] * (4 + len(arrived)),
        out_specs=(vmem,) * (len(arrived) + 1),
        scratch_shapes=[
            *[pltpu.VMEM(operand.shape, operand.dtype) for operand in operands],
            *[pltpu.VMEM((slots * 4, 128), jnp.float32)] * len(arrived),
            pltpu.SemaphoreType.DMA((len(operands) + len(arrived),)),
            pltpu.VMEM((clusters * 128, 128), jnp.bfloat16),
            pltpu.VMEM((others * 32, 128), jnp.bfloat16),
            pltpu.VMEM((clusters * 16, 128), jnp.bfloat16),
            pltpu.VMEM((others * 16, 128), jnp.bfloat16),
            pltpu.VMEM((clusters * 16, 128), jnp.float32),
            pltpu.VMEM((others * 16, 128), jnp.float32),
            pltpu.VMEM((128, 128), jnp.float32),
            *[pltpu.VMEM((128 * UNROLL, 256), jnp.bfloat16)] * 2,
        ],
        compiler_params=pltpu.CompilerParams(vmem_limit_bytes=VMEM_LIMIT),
        cost_estimate=pl.CostEstimate(
            flops=pairs * 128 * 128 * 20, bytes_accessed=4 * 1024 * 1024, transcendentals=0
        ),
        name="pair_forces",
    )(own_rows, other_rows, *operands, *arrived)


def prepare_kernel(
    fill_ref,
    cell_ref,
    send_index_ref,
    send_count_ref,
    cell_row_ref,
    pair_dir_ref,
    pair_slot_ref,
    position_hbm,
    charge_hbm,
    ion_hbm,
    start_hbm,
    screen_hbm,
    row_ref,
    own_ref,
    masked_ref,
    inverse_ref,
    source_ref,
    *refs,
):
    out_refs, scratch = (refs[:-8], refs[-8:])
    sum_ref, deposit_ref, position_ref, charge_ref, ion_ref, start_ref, screen_ref, sems = scratch
    copies = start_copies(
        (
            (position_hbm, position_ref),
            (charge_hbm, charge_ref),
            (ion_hbm, ion_ref),
            (start_hbm, start_ref),
            (screen_hbm, screen_ref),
        ),
        sems,
    )
    copies[0].wait()
    copies[1].wait()
    clusters = charge_ref.shape[0]
    cells_x, cells_y, _ = ion_ref.shape
    slots = send_index_ref.shape[1]
    lane = lax.broadcasted_iota(jnp.int32, (1, 128), 1)
    row = lax.broadcasted_iota(jnp.int32, (4, 128), 0)

    def collect(step, _):
        for turn in range(8):
            cluster = step * 8 + turn
            masked = jnp.where(lane < fill_ref[cluster], charge_ref[pl.ds(cluster, 1), :], 0.0)
            masked_ref[pl.ds(cluster, 1), :] = masked
            place = position_ref[:, pl.ds(pl.multiple_of(cluster * 128, 128), 128)]
            own_ref[cluster, 0:3, :] = place
            own_ref[cluster, 3:4, :] = masked
        at = pl.ds(pl.multiple_of(step * 8, 8), 8)
        total = jnp.sum(masked_ref[at, :], axis=1, keepdims=True)
        sum_ref[at, :] = jnp.broadcast_to(deposit_scale * total, (8, 128))
        return 0

    lax.fori_loop(0, clusters // 8, collect, 0, unroll=4)

    ups = upward()
    direction = pair_dir_ref[...]
    way = lax.shift_right_arithmetic(direction - 1, 1)
    flip = jnp.where(way == 0, ups[0], jnp.where(way == 1, ups[1], ups[2]))
    position = 1 + 2 * way + lax.bitwise_xor(lax.bitwise_and(direction - 1, 1), flip)
    row_ref[...] = jnp.where(direction == 0, 0, position) * slots + pair_slot_ref[...]

    def fill_messages(step, _):
        for position, out_ref in enumerate(out_refs):
            direction = sent_row(position, ups) if position else 0
            parts = []
            for turn in range(2):
                slot = step * 2 + turn
                live = jnp.where(slot < send_count_ref[0, direction], 1.0, 0.0)
                value = own_ref[send_index_ref[direction, slot]]
                parts.append(jnp.where(row == 3, value * live, value))
            out_ref[pl.ds(pl.multiple_of(step * 8, 8), 8), :] = jnp.concatenate(parts, axis=0)
        return 0

    lax.fori_loop(0, slots // 2, fill_messages, 0)

    def place(step, _):
        for turn in range(8):
            cluster = step * 8 + turn
            index_z = lax.bitwise_and(cell_ref[cluster], 127)
            at = pl.ds(cluster, 1)
            sum_ref[at, :] = jnp.where(lane == index_z, sum_ref[at, :], 0.0)
        return 0

    lax.fori_loop(0, clusters // 8, place, 0)
    cell = cell_row_ref[...]
    line = lax.shift_right_logical(cell, CELL_BITS)
    line = (line // cells_y * 2 + lax.shift_right_logical(lax.bitwise_and(cell, 255), 7)) * cells_y
    line = line + lax.shift_right_logical(cell, CELL_BITS) % cells_y
    sums = jnp.concatenate([part.astype(jnp.bfloat16) for part in split3(sum_ref[...])], axis=1)
    block = 128
    for first in range(0, deposit_ref.shape[0], block):
        rows = lax.broadcasted_iota(jnp.int32, (block, clusters), 0) + first
        hot = jnp.where(rows == line, 1.0, 0.0).astype(jnp.bfloat16)
        added = jnp.dot(hot, sums, preferred_element_type=jnp.float32)
        deposit_ref[first : first + block, :] = added[:, :128] + (
            added[:, 128:256] + added[:, 256:]
        )
    for copy in copies[2:]:
        copy.wait()
    inverse_ref[...] = 1.0 / (6.0 + screen_ref[...])
    for index in range(cells_x):
        for half in range(2):
            lanes = slice(128 * half, 128 * half + 128)
            first = (index * 2 + half) * cells_y
            source_ref[index, :, lanes] = (
                ion_ref[index, :, lanes] + deposit_ref[first : first + cells_y, :]
            ) * inverse_ref[index, :, lanes]
    def fill_rows(out_ref, after):
        for index in range(cells_x):
            base = slots * 4 + index * 32
            offset = 0
            for field_ref, width in zip(
                (start_ref, inverse_ref, source_ref, ion_ref), HALO_WIDTHS, strict=True
            ):
                first = cells_y - width if after else 0
                rows = field_ref[index, first : first + width, :]
                for half in range(2):
                    out_ref[base + 16 * half + offset : base + 16 * half + offset + width, :] = (
                        rows[:, 128 * half : 128 * half + 128]
                    )
                offset += width
            for half in range(2):
                out_ref[base + 16 * half + offset : base + 16 * half + 16, :] = jnp.zeros(
                    (16 - offset, 128), jnp.float32
                )

    for up in range(2):

        @pl.when(ups[0] == up)
        def _(up=up):
            fill_rows(out_refs[1], up == 1)
            fill_rows(out_refs[2], up == 0)


def prepare(
    fill,
    cell,
    send_index,
    send_count,
    pair_dir,
    pair_slot,
    positions,
    charges,
    ions,
    start,
    screen,
):
    clusters = charges.shape[0]
    directions, slots = send_index.shape
    cells_x = ions.shape[0]
    smem = pl.BlockSpec(memory_space=pltpu.SMEM)
    vmem = pl.BlockSpec(memory_space=pltpu.VMEM)
    rows = [slots * 4] * directions
    rows[1] = rows[2] = slots * 4 + cells_x * 32
    return pl.pallas_call(
        prepare_kernel,
        out_shape=(
            jax.ShapeDtypeStruct(pair_dir.shape, jnp.int32),
            jax.ShapeDtypeStruct((clusters, 4, 128), jnp.float32),
            jax.ShapeDtypeStruct((clusters, 128), jnp.float32),
            jax.ShapeDtypeStruct(ions.shape, jnp.float32),
            jax.ShapeDtypeStruct(ions.shape, jnp.float32),
            *[jax.ShapeDtypeStruct((count, 128), jnp.float32) for count in rows],
        ),
        in_specs=[smem] * 4 + [vmem] * 3 + [pl.BlockSpec(memory_space=pltpu.HBM)] * 5,
        out_specs=(vmem,) * (5 + directions),
        scratch_shapes=[
            pltpu.VMEM((clusters, 128), jnp.float32),
            pltpu.VMEM((ions.size // 128, 128), jnp.float32),
            *[
                pltpu.VMEM(operand.shape, jnp.float32)
                for operand in (positions, charges, ions, start, screen)
            ],
            pltpu.SemaphoreType.DMA((5,)),
        ],
        compiler_params=pltpu.CompilerParams(vmem_limit_bytes=VMEM_LIMIT),
        name="prepare",
    )(
        fill,
        cell,
        send_index,
        send_count,
        cell.reshape(1, clusters),
        pair_dir,
        pair_slot,
        positions,
        charges,
        ions,
        start,
        screen,
    )


def line_rows(cells_y):
    return (cells_y + 2 * DEPTH + 7) // 8 * 8


def fill_lines(target_ref, plane, field, field_ref, index, rim_ref, source):
    cells_y = field_ref.shape[1]
    width = HALO_WIDTHS[field]
    for half in range(2):
        at = (plane * 2 + half) * line_rows(cells_y) + DEPTH
        first = source * 32 + 16 * half + sum(HALO_WIDTHS[:field])
        target_ref[pl.ds(at - width, width), :] = rim_ref[pl.ds(first, width), :]
        target_ref[pl.ds(at, cells_y), :] = field_ref[index, :, 128 * half : 128 * half + 128]
        first = first + rim_ref.shape[0] // 2
        target_ref[pl.ds(at + cells_y, width), :] = rim_ref[pl.ds(first, width), :]


def planes_kernel(base, *refs):
    field_refs, rims, out_refs = (refs[:4], refs[4:6], refs[6:8])
    edge_refs, rim_ref, sems = (refs[8:12], refs[12], refs[13])
    cells_x = field_refs[0].shape[0]
    size = cells_x * 32
    ups = upward()
    moves = [
        (rim.at[base : base + size], rim_ref.at[pl.ds(pl.multiple_of(side * size, size), size)])
        for rim, side in zip(rims, (ups[0], 1 - ups[0]), strict=True)
    ]
    for field_ref, edge_ref, width in zip(field_refs, edge_refs, HALO_WIDTHS, strict=True):
        moves.append((field_ref.at[0:width], edge_ref.at[0:width]))
        moves.append((field_ref.at[cells_x - width : cells_x], edge_ref.at[width : 2 * width]))
    for copy in start_copies(moves, sems):
        copy.wait()
    for field, width in enumerate(HALO_WIDTHS):
        plane = sum(HALO_WIDTHS[:field])

        def fill(step, _, field=field, plane=plane, width=width):
            for phase, out_ref in enumerate(out_refs):
                last = ups[2] if phase == 0 else 1 - ups[2]
                source = last * (cells_x - width) + step
                fill_lines(
                    out_ref,
                    plane + step,
                    field,
                    edge_refs[field],
                    last * width + step,
                    rim_ref,
                    source,
                )
            return 0

        lax.fori_loop(0, width, fill, 0)


def planes(fields, first, second, base):
    vmem = pl.BlockSpec(memory_space=pltpu.VMEM)
    cells_x, cells_y, cells_z = fields[0].shape
    rows = sum(HALO_WIDTHS) * 2 * line_rows(cells_y)
    shape = jax.ShapeDtypeStruct((rows, 128), jnp.float32)
    return pl.pallas_call(
        functools.partial(planes_kernel, base),
        out_shape=(shape, shape),
        in_specs=[pl.BlockSpec(memory_space=pltpu.HBM)] * 6,
        out_specs=(vmem, vmem),
        scratch_shapes=[
            *[pltpu.VMEM((2 * width, cells_y, cells_z), jnp.float32) for width in HALO_WIDTHS],
            pltpu.VMEM((cells_x * 64, 128), jnp.float32),
            pltpu.SemaphoreType.DMA((2 + 2 * len(HALO_WIDTHS),)),
        ],
        compiler_params=pltpu.CompilerParams(vmem_limit_bytes=VMEM_LIMIT),
        name="planes",
    )(*fields, first, second)


def face_flux(pot_low, pot_high, ion_low, ion_high):
    speed = -mobility * (pot_high - pot_low)
    return (
        jnp.maximum(speed, 0.0) * ion_low
        + jnp.minimum(speed, 0.0) * ion_high
        - diffusion * (ion_high - ion_low)
    )


def grid_kernel(base, *refs):
    cell_ref, masked_hbm = refs[:2]
    hbm_refs, plane_hbms = (refs[2:6], refs[8:10])
    potential_ref, next_ref, force_ref = refs[10:13]
    start_ref, inverse_ref, source_ref, ion_ref = refs[13:17]
    updates, resids, final_ref, pick_refs = (refs[17:20], refs[20:22], refs[22], refs[23:26])
    rim_ref, field_refs, masked_ref, sems = (refs[26], refs[27:31], refs[31], refs[32])
    cells_x, cells_y, _ = field_refs[0].shape
    rows = line_rows(cells_y)
    inner = cells_y + 2 * DEPTH - 2
    clusters = masked_ref.shape[0]
    ups = upward()
    size = cells_x * 32
    moves = [
        (rim.at[base : base + size], rim_ref.at[pl.ds(pl.multiple_of(side * size, size), size)])
        for rim, side in zip(refs[6:8], (ups[0], 1 - ups[0]), strict=True)
    ]
    moves += zip(hbm_refs, field_refs, strict=True)
    moves.append((masked_hbm, masked_ref))
    near = len(moves)
    for field, target_ref in enumerate((start_ref, inverse_ref, source_ref, ion_ref)):
        width = HALO_WIDTHS[field]
        size = width * 2 * rows
        first = sum(HALO_WIDTHS[:field]) * 2 * rows
        for phase, plane_ref in enumerate(plane_hbms):
            higher = ups[2] if phase == 0 else 1 - ups[2]
            plane = (DEPTH - width) + higher * (cells_x + width)
            at = pl.ds(pl.multiple_of(plane * 2 * rows, 2 * rows), size)
            moves.append((plane_ref.at[first : first + size], target_ref.at[at]))
    copies = start_copies(moves, sems)
    for copy in copies[:near]:
        copy.wait()

    def fill(index, _):
        for field, target_ref in enumerate((start_ref, inverse_ref, source_ref, ion_ref)):
            fill_lines(target_ref, DEPTH + index, field, field_refs[field], index, rim_ref, index)
        return 0

    lax.fori_loop(0, cells_x, fill, 0, unroll=2)
    for copy in copies[near:]:
        copy.wait()

    def beyond(values):
        lane = lax.broadcasted_iota(jnp.int32, values[0].shape, 1)
        right = [pltpu.roll(value, 127, 1) for value in values]
        left = [pltpu.roll(value, 1, 1) for value in values]
        above = [jnp.where(lane == 127, right[1], right[0]), jnp.where(lane == 127, 0.0, right[1])]
        below = [jnp.where(lane == 0, 0.0, left[0]), jnp.where(lane == 0, left[0], left[1])]
        return (below, above)

    def wide(plane, half, shift=0):
        return pl.ds((plane * 2 + half) * rows + 1 + shift, inner)

    def around(ref, plane):
        here = [ref[wide(plane, half), :] for half in range(2)]
        below, above = beyond(here)
        sums = [
            (ref[wide(plane - 1, half), :] + ref[wide(plane + 1, half), :])
            + (ref[wide(plane, half, -1), :] + ref[wide(plane, half, 1), :])
            + (below[half] + above[half])
            for half in range(2)
        ]
        return (here, sums)

    middle = 0.5 * (highest_eig + lowest_eig)
    spread = 0.5 * (highest_eig - lowest_eig)
    assert middle == 1.0 and SWEEPS == 4

    def sweep_first(plane, _):
        here, sums = around(start_ref, plane)
        for half in range(2):
            at = wide(plane, half)
            updates[0][at, :] = source_ref[at, :] - here[half] + inverse_ref[at, :] * sums[half]
        return 0

    lax.fori_loop(1, cells_x + 2 * DEPTH - 1, sweep_first, 0, unroll=2)

    ratio_ms = middle / spread
    weight_now = 1.0 / ratio_ms
    for turn in range(1, SWEEPS):
        weight_next = 1.0 / (2.0 * ratio_ms - weight_now)
        keep, gain = (weight_next * weight_now, 2.0 * weight_next / spread)
        weight_now = weight_next

        def sweep(plane, _, turn=turn, keep=keep, gain=gain):
            here, sums = around(updates[turn - 1], plane)
            for half in range(2):
                at = wide(plane, half)
                resid = inverse_ref[at, :] * sums[half]
                if turn > 1:
                    resid = resid + (resids[turn - 2][at, :] - here[half])
                update = keep * here[half] + gain * resid
                if turn + 1 < SWEEPS:
                    resids[turn - 1][at, :] = resid
                    updates[turn][at, :] = update
                else:
                    final_ref[at, :] = (start_ref[at, :] + updates[0][at, :]) + (
                        (updates[1][at, :] + here[half]) + update
                    )
            return 0

        first = 1 + turn
        lax.fori_loop(first, cells_x + 2 * DEPTH - first, sweep, 0, unroll=2)

    def local(plane, half, shift=0):
        return pl.ds((plane * 2 + half) * rows + DEPTH + shift, cells_y)

    def advance(index, _):
        plane = index + DEPTH
        pots = [final_ref[local(plane, half), :] for half in range(2)]
        ions = [ion_ref[local(plane, half), :] for half in range(2)]
        pot_below, pot_above = beyond(pots)
        ion_below, ion_above = beyond(ions)
        for half in range(2):
            pot, ion = (pots[half], ions[half])
            steps = [
                (final_ref[at, :], ion_ref[at, :])
                for at in (
                    local(plane - 1, half),
                    local(plane + 1, half),
                    local(plane, half, -1),
                    local(plane, half, 1),
                )
            ]
            steps += [(pot_below[half], ion_below[half]), (pot_above[half], ion_above[half])]
            total = 0.0
            for low, high in zip(steps[0::2], steps[1::2], strict=True):
                total = total + (
                    face_flux(pot, high[0], ion, high[1]) - face_flux(low[0], pot, low[1], ion)
                )
            lanes = slice(128 * half, 128 * half + 128)
            next_ref[index, :, lanes] = ion - time_step * total
            potential_ref[index, :, lanes] = pot
        return 0

    lax.fori_loop(0, cells_x, advance, 0)

    row_lane = lax.broadcasted_iota(jnp.int32, (1, 128), 1)

    def pick(cluster, _):
        cell = cell_ref[cluster]
        index_x = lax.shift_right_logical(cell, CELL_BITS) // cells_y + DEPTH
        index_y = lax.shift_right_logical(cell, CELL_BITS) % cells_y + DEPTH
        index_z = lax.bitwise_and(cell, 255)
        half = lax.shift_right_logical(index_z, 7)
        here = row_lane == lax.bitwise_and(index_z, 127)

        def line(plane, row, part):
            return final_ref[pl.ds((plane * 2 + part) * rows + row, 1), :]

        along_x = line(index_x - 1, index_y, half) - line(index_x + 1, index_y, half)
        along_y = line(index_x, index_y - 1, half) - line(index_x, index_y + 1, half)
        along_z = jnp.zeros((1, 128), jnp.float32)
        for part in range(2):
            value = line(index_x, index_y, part)
            place = row_lane + 128 * part
            along_z = along_z + jnp.where(place == index_z - 1, value, 0.0)
            along_z = along_z - jnp.where(place == index_z + 1, value, 0.0)
        at = pl.ds(cluster, 1)
        pick_refs[0][at, :] = jnp.where(here, along_x, 0.0)
        pick_refs[1][at, :] = jnp.where(here, along_y, 0.0)
        pick_refs[2][at, :] = along_z
        return 0

    lax.fori_loop(0, clusters, pick, 0, unroll=8)

    def spread_out(step, _):
        start = pl.multiple_of(step * 8, 8)
        charge = masked_ref[pl.ds(start, 8), :] * (0.5 * field_scale)
        for part, pick_ref in enumerate(pick_refs):
            total = jnp.sum(pick_ref[pl.ds(start, 8), :], axis=1, keepdims=True)
            force_ref[pl.ds(4 * start + part, 8, stride=4), :] = charge * total
        force_ref[pl.ds(4 * start + 3, 8, stride=4), :] = jnp.zeros((8, 128), jnp.float32)
        return 0

    lax.fori_loop(0, clusters // 8, spread_out, 0, unroll=4)


def grid_step(cell, masked, fields, rims, edges, base):
    smem = pl.BlockSpec(memory_space=pltpu.SMEM)
    vmem = pl.BlockSpec(memory_space=pltpu.VMEM)
    clusters = masked.shape[0]
    cells_x, cells_y, _ = fields[0].shape
    block = ((cells_x + 2 * DEPTH) * 2 * line_rows(cells_y), 128)
    return pl.pallas_call(
        functools.partial(grid_kernel, base),
        out_shape=(
            jax.ShapeDtypeStruct(fields[0].shape, jnp.float32),
            jax.ShapeDtypeStruct(fields[0].shape, jnp.float32),
            jax.ShapeDtypeStruct((clusters * 4, 128), jnp.float32),
        ),
        in_specs=[smem] + [pl.BlockSpec(memory_space=pltpu.HBM)] * 9,
        out_specs=(vmem,) * 3,
        scratch_shapes=[pltpu.VMEM(block, jnp.float32)] * 10
        + [pltpu.VMEM((clusters, 128), jnp.float32)] * 3
        + [pltpu.VMEM((cells_x * 64, 128), jnp.float32)]
        + [pltpu.VMEM(field.shape, jnp.float32) for field in fields]
        + [pltpu.VMEM(masked.shape, jnp.float32), pltpu.SemaphoreType.DMA((15,))],
        compiler_params=pltpu.CompilerParams(vmem_limit_bytes=VMEM_LIMIT),
        cost_estimate=pl.CostEstimate(
            flops=block[0] * block[1] * 100, bytes_accessed=8 << 20, transcendentals=0
        ),
        name="grid_step",
    )(cell, masked, *fields, *rims, *edges)


def gather_forces_kernel(send_index_ref, *refs):
    fetched = len(SWAPS) + 3
    out_ref, sum_ref = refs[fetched : fetched + 2]
    own_ref, field_ref, *back_refs = refs[fetched + 2 : -1]
    copies = start_copies(zip(refs[:fetched], refs[fetched + 2 : -1], strict=True), refs[-1])
    for copy in copies:
        copy.wait()
    clusters = own_ref.shape[0]
    slots = send_index_ref.shape[1]
    sum_ref[...] = own_ref[...] + field_ref[...]
    ups = upward()

    def visit(slot, _):
        for position, back_ref in enumerate(back_refs):
            cluster = send_index_ref[sent_row(position, ups) if position else 0, slot]
            sum_ref[cluster] += back_ref[slot]
        return 0

    lax.fori_loop(0, slots, visit, 0)

    def write(step, _):
        for turn in range(8):
            cluster = step * 8 + turn
            out_ref[:, pl.ds(pl.multiple_of(cluster * 128, 128), 128)] = sum_ref[cluster][0:3]
        return 0

    lax.fori_loop(0, clusters // 8, write, 0)


def gather_forces(send_index, own, field, backs):
    smem = pl.BlockSpec(memory_space=pltpu.SMEM)
    vmem = pl.BlockSpec(memory_space=pltpu.VMEM)
    clusters = own.shape[0]
    return pl.pallas_call(
        gather_forces_kernel,
        out_shape=jax.ShapeDtypeStruct((3, clusters * 128), jnp.float32),
        in_specs=[smem] + [pl.BlockSpec(memory_space=pltpu.HBM)] * (2 + len(backs)),
        out_specs=vmem,
        scratch_shapes=[
            *[pltpu.VMEM(part.shape, jnp.float32) for part in (own, own, field, *backs)],
            pltpu.SemaphoreType.DMA((2 + len(backs),)),
        ],
        compiler_params=pltpu.CompilerParams(vmem_limit_bytes=VMEM_LIMIT),
        name="gather_forces",
    )(send_index, own, field, *backs)


def shards(
    positions,
    charges,
    cluster_fill,
    cluster_cell,
    send_index,
    send_count,
    pair_local,
    pair_dir,
    pair_slot,
    ion_density,
    potential_prev,
    screening,
):
    clusters = cluster_fill.shape[0]
    psize = charges.shape[0] // clusters
    slots = send_index.shape[1]
    base = slots * 4
    other_rows, own, masked, inverse, source, local, *messages = prepare(
        cluster_fill,
        cluster_cell,
        send_index,
        send_count,
        pair_dir.reshape(-1, 128),
        pair_slot.reshape(-1, 128),
        positions,
        charges.reshape(clusters, psize),
        ion_density,
        potential_prev,
        screening,
    )
    arrived = [local] + [
        swapped(message, *swap) for message, swap in zip(messages, SWAPS, strict=True)
    ]
    fields = (potential_prev, inverse, source, ion_density)
    arrived = lax.optimization_barrier(arrived)
    rims = arrived[1:3]
    edges = [
        swapped(edge, "grp", 1, phase) for phase, edge in enumerate(planes(fields, *rims, base))
    ]
    own_force, *reactions = pair_forces(
        pair_local,
        other_rows.reshape(-1),
        own.reshape(clusters * 4, psize),
        arrived,
        slots,
    )
    backs = [reactions[0]] + [
        swapped(reaction, *swap) for reaction, swap in zip(reactions[1:], SWAPS, strict=True)
    ]
    potential, ion_next, field_force = grid_step(cluster_cell, masked, fields, rims, edges, base)
    forces = gather_forces(
        send_index,
        own_force.reshape(clusters, 4, psize),
        field_force.reshape(clusters, 4, psize),
        [back.reshape(slots, 4, psize) for back in backs],
    )
    return (forces, potential, ion_next)


def solution(mesh):
    in_specs = (
        P(None, ("grp", "brick")),
        P(("grp", "brick")),
        P(("grp", "brick")),
        P(("grp", "brick")),
        P(("grp", "brick"), None),
        P(("grp", "brick"), None),
        P(("grp", "brick")),
        P(("grp", "brick")),
        P(("grp", "brick")),
        P("grp", "brick", None),
        P("grp", "brick", None),
        P("grp", "brick", None),
    )
    out_specs = (P(None, ("grp", "brick")), P("grp", "brick", None), P("grp", "brick", None))
    return jax.shard_map(shards, mesh=mesh, in_specs=in_specs, out_specs=out_specs, check_vma=False)
```

```python
import functools

import jax
import jax.numpy as jnp
import numpy as np
from jax import lax
from jax.experimental import pallas as pl
from jax.experimental.pallas import tpu as pltpu
from jax.sharding import PartitionSpec as P

SWEEPS = 4
UNROLL = 8
CHUNKS = 4
HALO_WIDTHS = (SWEEPS + 1, SWEEPS, SWEEPS, 1)
DEPTH = SWEEPS + 1
CELL_BITS = 8
SWAPS = tuple(
    (*way, phase) for way in (("brick", 1), ("brick", 2), ("grp", 1)) for phase in (0, 1)
)


coulomb_scale = 0.02
softening = 0.1
field_scale = 0.5
deposit_scale = 0.2
lowest_eig = 0.01
highest_eig = 1.99
mobility = 0.3
diffusion = 0.2
time_step = 0.2


VMEM_LIMIT = 60 * 1024 * 1024


def start_copies(pairs, sems):
    copies = [
        pltpu.make_async_copy(source, target, sems.at[index])
        for index, (source, target) in enumerate(pairs)
    ]
    for copy in copies:
        copy.start()
    return copies


def upward():
    brick, grp = (lax.axis_index("brick"), lax.axis_index("grp"))
    bits = (brick, lax.shift_right_logical(brick, 1), grp)
    return [1 - lax.bitwise_and(bit, 1) for bit in bits]


def sent_row(position, ups):
    way, phase = ((position - 1) // 2, (position - 1) % 2)
    return 1 + 2 * way + (ups[way] if phase else 1 - ups[way])


def swapped(shard, axis, distance, phase):
    devices = lax.axis_size(axis)
    pairs = []
    for index in range(devices):
        step = distance if (index // distance + phase) % 2 == 0 else -distance
        if 0 <= index + step < devices:
            pairs.append((index, index + step))
    return lax.ppermute(shard, axis, pairs)


def split3(value):
    first = value.astype(jnp.bfloat16).astype(jnp.float32)
    rest = value - first
    second = rest.astype(jnp.bfloat16).astype(jnp.float32)
    third = (rest - second).astype(jnp.bfloat16).astype(jnp.float32)
    return (first, second, third)


def moment_pieces(comps, charge):
    rows = [None] * 12
    for part, charged in enumerate((*comps, None)):
        for level, piece in enumerate(split3(charge if charged is None else charge * charged)):
            rows[4 * level + part] = piece
    return rows


def selections():
    near_kinds, far_kinds = ([], [])
    for part in range(3):
        near_kinds += [3 * part + level for level in (0, 0, 0, 1, 1, 2)]
        far_kinds += [3 * part + level for level in (0, 1, 2, 0, 1, 0)]
    near_kinds += [9, 10, 11, 12, 12, 12]
    far_kinds += [12, 12, 12, 9, 10, 11]
    near = np.zeros((128, 1024), np.float32)
    far = np.zeros((256, 128), np.float32)
    moment = np.zeros((128, 128), np.float32)
    for cluster in range(8):
        for index, kind in enumerate(near_kinds):
            near[kind * 8 + cluster, cluster * 128 + index] = 1.0
        for index, kind in enumerate(far_kinds):
            far[cluster * 32 + index, kind * 8 + cluster] = 1.0
        for kind in range(12):
            moment[cluster * 16 + kind, kind * 8 + cluster] = 1.0
    return tuple(jnp.asarray(part, jnp.bfloat16) for part in (near, far, moment))


def pair_kernel(own_rows_ref, other_rows_ref, *refs):
    sources = len(SWAPS) + 1
    fetched = sources + 4
    hbm_refs = refs[:fetched]
    own_out_ref = refs[fetched]
    other_out_refs = refs[fetched + 1 : fetched + 1 + sources]
    refs = refs[fetched + 1 + sources :]
    near_sel_ref, far_sel_ref, moment_sel_ref, own_ref = refs[:4]
    other_refs = refs[4:fetched]
    sems = refs[fetched]
    copies = start_copies(
        [
            (source.at[0 : target.shape[0]], target)
            for source, target in zip(hbm_refs, refs[:fetched], strict=True)
        ],
        sems,
    )
    (
        near_ref,
        far_ref,
        own_moment_ref,
        other_moment_ref,
        own_sum_ref,
        other_sum_ref,
        dist_ref,
        *weight_refs,
    ) = refs[fetched + 1 :]
    clusters = own_ref.shape[0] // 4
    slots = other_out_refs[0].shape[0] // 4
    others = slots * sources
    groups = own_rows_ref.shape[0] // UNROLL
    ones = jnp.ones((8, 128), jnp.float32)
    zeros = jnp.zeros((8, 128), jnp.float32)

    def components(data_ref, start):
        return [data_ref[pl.ds(4 * start + part, 8, stride=4), :] for part in range(4)]

    def place_pieces(comps, factor, offset):
        pieces = []
        square = zeros
        for comp in comps:
            square = square + comp * comp
            pieces += split3(factor * comp)
        pieces += [*split3(square + offset), ones]
        return jnp.concatenate(pieces + [zeros] * (16 - len(pieces)), axis=0)

    def selected(left, right):
        return jnp.dot(
            left.astype(jnp.bfloat16), right, preferred_element_type=jnp.float32
        ).astype(jnp.bfloat16)

    def near_rows(step, _):
        start = pl.multiple_of(step * 8, 8)
        *comps, charge = components(own_ref, start)
        moments = jnp.concatenate(moment_pieces(comps, charge) + [zeros] * 4, axis=0)
        own_moment_ref[pl.ds(pl.multiple_of(start * 16, 128), 128), :] = selected(
            moment_sel_ref[...], moments.astype(jnp.bfloat16)
        )
        tiles = selected(place_pieces(comps, 1.0, 0.0).T, near_sel_ref[...])
        for index in range(8):
            at = pl.ds(pl.multiple_of((start + index) * 128, 128), 128)
            near_ref[at, :] = tiles[:, 128 * index : 128 * index + 128]
        return 0

    def far_rows(source, step, _):
        local = pl.multiple_of(step * 8, 8)
        start = source * slots + local
        *comps, charge = components(other_refs[source], local)
        far_ref[pl.ds(pl.multiple_of(start * 32, 256), 256), :] = selected(
            far_sel_ref[...], place_pieces(comps, -2.0, softening).astype(jnp.bfloat16)
        )
        moments = jnp.concatenate(moment_pieces(comps, charge) + [zeros] * 4, axis=0)
        other_moment_ref[pl.ds(pl.multiple_of(start * 16, 128), 128), :] = selected(
            moment_sel_ref[...], moments.astype(jnp.bfloat16)
        )
        return 0

    own_sum_ref[...] = jnp.zeros_like(own_sum_ref)
    other_sum_ref[...] = jnp.zeros_like(other_sum_ref)
    weight_refs[0][...] = jnp.zeros_like(weight_refs[0])
    for copy in copies[:4]:
        copy.wait()
    lax.fori_loop(0, clusters // 8, near_rows, 0, unroll=4)
    for copy in copies[4:]:
        copy.wait()
    for source in range(sources):
        lax.fori_loop(0, slots // 8, functools.partial(far_rows, source), 0, unroll=4)
    def distances(pair):
        own = own_rows_ref[pair]
        other = other_rows_ref[pair]
        return jnp.dot(
            near_ref[pl.ds(pl.multiple_of(own * 128, 128), 128), 0:32],
            far_ref[pl.ds(pl.multiple_of(other * 32, 32), 32), :],
            preferred_element_type=jnp.float32,
        )

    def weights(dist, index, chunk, weight_ref):
        rows = 128 // CHUNKS
        first = rows * chunk
        root = lax.rsqrt(dist[first : first + rows])
        weight = root * root * root
        high = weight.astype(jnp.bfloat16)
        low = (weight - high.astype(jnp.float32)).astype(jnp.bfloat16)
        at = slice(128 * index + first, 128 * index + first + rows)
        weight_ref[at, :128] = high
        weight_ref[at, 128:] = low

    def row_block(index):
        return pl.ds(pl.multiple_of(index * 16, 16), 16)

    def own_product(other, weight_ref, index):
        both = weight_ref[128 * index : 128 * index + 128]
        return lax.dot_general(
            other_moment_ref[row_block(other), :],
            jnp.concatenate([both[:, :128], both[:, 128:]], axis=0),
            (((1,), (1,)), ((), ())),
            preferred_element_type=jnp.float32,
        )

    def other_product(own, weight_ref, index):
        return jnp.dot(
            own_moment_ref[row_block(own), :],
            weight_ref[128 * index : 128 * index + 128],
            preferred_element_type=jnp.float32,
        )

    def add_rows(own, other, to_own, to_other):
        own_sum_ref[row_block(own), :] += to_own[:, :128] + to_own[:, 128:]
        other_sum_ref[row_block(other), :] += to_other[:, :128] + to_other[:, 128:]

    def half_step(step, side, dist):
        last = jnp.maximum(step - 1, 0) * UNROLL
        waiting = []
        for index in range(UNROLL):
            own = own_rows_ref[last + index]
            other = other_rows_ref[last + index]
            later = distances(jnp.minimum(step * UNROLL + index + 1, groups * UNROLL - 1))
            weights(dist, index, 0, weight_refs[1 - side])
            to_own = own_product(other, weight_refs[side], index)
            weights(dist, index, 1, weight_refs[1 - side])
            weights(dist, index, 2, weight_refs[1 - side])
            to_other = other_product(own, weight_refs[side], index)
            weights(dist, index, 3, weight_refs[1 - side])
            dist = later
            waiting.append((own, other, to_own, to_other))
            if len(waiting) > 2:
                add_rows(*waiting.pop(0))
        for entry in waiting:
            add_rows(*entry)
        return dist

    def visit(step, _):
        dist = dist_ref[...]
        for side in range(2):
            dist = half_step(step * 2 + side, side, dist)
        dist_ref[...] = dist
        return 0

    dist_ref[...] = distances(0)
    lax.fori_loop(0, groups // 2, visit, 0)
    half_step(groups, 0, dist_ref[...])

    def finish(data_ref, out_ref, sum_ref, base, step, _):
        start = pl.multiple_of(step * 8, 8)
        *comps, charge = components(data_ref, start)

        def total(part):
            terms = [
                sum_ref[pl.ds(base + start * 16 + 4 * level + part, 8, stride=16), :]
                for level in range(3)
            ]
            return terms[0] + (terms[1] + terms[2])

        weight = total(3)
        scale = coulomb_scale * charge
        for part, comp in enumerate(comps):
            out_ref[pl.ds(4 * start + part, 8, stride=4), :] = scale * (comp * weight - total(part))
        out_ref[pl.ds(4 * start + 3, 8, stride=4), :] = zeros
        return 0

    lax.fori_loop(
        0, clusters // 8, functools.partial(finish, own_ref, own_out_ref, own_sum_ref, 0), 0, unroll=4
    )
    for source in range(sources):
        body = functools.partial(
            finish,
            other_refs[source],
            other_out_refs[source],
            other_sum_ref,
            source * slots * 16,
        )
        lax.fori_loop(0, slots // 8, body, 0, unroll=4)


def pair_forces(own_rows, other_rows, own, arrived, slots):
    clusters = own.shape[0] // 4
    others = slots * len(arrived)
    pairs = own_rows.shape[0]
    smem = pl.BlockSpec(memory_space=pltpu.SMEM)
    vmem = pl.BlockSpec(memory_space=pltpu.VMEM)
    hbm = pl.BlockSpec(memory_space=pltpu.HBM)
    operands = (*selections(), own)
    return pl.pallas_call(
        pair_kernel,
        out_shape=(
            jax.ShapeDtypeStruct(own.shape, jnp.float32),
            *[jax.ShapeDtypeStruct((slots * 4, 128), jnp.float32)] * len(arrived),
        ),
        in_specs=[smem, smem] + [hbm] * (4 + len(arrived)),
        out_specs=(vmem,) * (len(arrived) + 1),
        scratch_shapes=[
            *[pltpu.VMEM(operand.shape, operand.dtype) for operand in operands],
            *[pltpu.VMEM((slots * 4, 128), jnp.float32)] * len(arrived),
            pltpu.SemaphoreType.DMA((len(operands) + len(arrived),)),
            pltpu.VMEM((clusters * 128, 128), jnp.bfloat16),
            pltpu.VMEM((others * 32, 128), jnp.bfloat16),
            pltpu.VMEM((clusters * 16, 128), jnp.bfloat16),
            pltpu.VMEM((others * 16, 128), jnp.bfloat16),
            pltpu.VMEM((clusters * 16, 128), jnp.float32),
            pltpu.VMEM((others * 16, 128), jnp.float32),
            pltpu.VMEM((128, 128), jnp.float32),
            *[pltpu.VMEM((128 * UNROLL, 256), jnp.bfloat16)] * 2,
        ],
        compiler_params=pltpu.CompilerParams(vmem_limit_bytes=VMEM_LIMIT),
        cost_estimate=pl.CostEstimate(
            flops=pairs * 128 * 128 * 20, bytes_accessed=4 * 1024 * 1024, transcendentals=0
        ),
        name="pair_forces",
    )(own_rows, other_rows, *operands, *arrived)


def prepare_kernel(
    fill_ref,
    cell_ref,
    send_index_ref,
    send_count_ref,
    cell_row_ref,
    pair_dir_ref,
    pair_slot_ref,
    position_hbm,
    charge_hbm,
    ion_hbm,
    start_hbm,
    screen_hbm,
    row_ref,
    own_ref,
    masked_ref,
    inverse_ref,
    source_ref,
    *refs,
):
    out_refs, edge_refs, scratch = (refs[:-10], refs[-10:-8], refs[-8:])
    sum_ref, deposit_ref, position_ref, charge_ref, ion_ref, start_ref, screen_ref, sems = scratch
    copies = start_copies(
        (
            (position_hbm, position_ref),
            (charge_hbm, charge_ref),
            (ion_hbm, ion_ref),
            (start_hbm, start_ref),
            (screen_hbm, screen_ref),
        ),
        sems,
    )
    copies[0].wait()
    copies[1].wait()
    clusters = charge_ref.shape[0]
    cells_x, cells_y, _ = ion_ref.shape
    slots = send_index_ref.shape[1]
    lane = lax.broadcasted_iota(jnp.int32, (1, 128), 1)
    row = lax.broadcasted_iota(jnp.int32, (4, 128), 0)

    def collect(step, _):
        for turn in range(8):
            cluster = step * 8 + turn
            masked = jnp.where(lane < fill_ref[cluster], charge_ref[pl.ds(cluster, 1), :], 0.0)
            masked_ref[pl.ds(cluster, 1), :] = masked
            place = position_ref[:, pl.ds(pl.multiple_of(cluster * 128, 128), 128)]
            own_ref[cluster, 0:3, :] = place
            own_ref[cluster, 3:4, :] = masked
        at = pl.ds(pl.multiple_of(step * 8, 8), 8)
        total = jnp.sum(masked_ref[at, :], axis=1, keepdims=True)
        sum_ref[at, :] = jnp.broadcast_to(deposit_scale * total, (8, 128))
        return 0

    lax.fori_loop(0, clusters // 8, collect, 0, unroll=4)

    ups = upward()
    direction = pair_dir_ref[...]
    way = lax.shift_right_arithmetic(direction - 1, 1)
    flip = jnp.where(way == 0, ups[0], jnp.where(way == 1, ups[1], ups[2]))
    position = 1 + 2 * way + lax.bitwise_xor(lax.bitwise_and(direction - 1, 1), flip)
    row_ref[...] = jnp.where(direction == 0, 0, position) * slots + pair_slot_ref[...]

    def fill_messages(step, _):
        for position, out_ref in enumerate(out_refs):
            direction = sent_row(position, ups) if position else 0
            parts = []
            for turn in range(2):
                slot = step * 2 + turn
                live = jnp.where(slot < send_count_ref[0, direction], 1.0, 0.0)
                value = own_ref[send_index_ref[direction, slot]]
                parts.append(jnp.where(row == 3, value * live, value))
            out_ref[pl.ds(pl.multiple_of(step * 8, 8), 8), :] = jnp.concatenate(parts, axis=0)
        return 0

    lax.fori_loop(0, slots // 2, fill_messages, 0)

    def place(step, _):
        for turn in range(8):
            cluster = step * 8 + turn
            index_z = lax.bitwise_and(cell_ref[cluster], 127)
            at = pl.ds(cluster, 1)
            sum_ref[at, :] = jnp.where(lane == index_z, sum_ref[at, :], 0.0)
        return 0

    lax.fori_loop(0, clusters // 8, place, 0)
    cell = cell_row_ref[...]
    line = lax.shift_right_logical(cell, CELL_BITS)
    line = (line // cells_y * 2 + lax.shift_right_logical(lax.bitwise_and(cell, 255), 7)) * cells_y
    line = line + lax.shift_right_logical(cell, CELL_BITS) % cells_y
    sums = jnp.concatenate([part.astype(jnp.bfloat16) for part in split3(sum_ref[...])], axis=1)
    block = 128
    for first in range(0, deposit_ref.shape[0], block):
        rows = lax.broadcasted_iota(jnp.int32, (block, clusters), 0) + first
        hot = jnp.where(rows == line, 1.0, 0.0).astype(jnp.bfloat16)
        added = jnp.dot(hot, sums, preferred_element_type=jnp.float32)
        deposit_ref[first : first + block, :] = added[:, :128] + (
            added[:, 128:256] + added[:, 256:]
        )
    for copy in copies[2:]:
        copy.wait()
    inverse_ref[...] = 1.0 / (6.0 + screen_ref[...])
    for index in range(cells_x):
        for half in range(2):
            lanes = slice(128 * half, 128 * half + 128)
            first = (index * 2 + half) * cells_y
            source_ref[index, :, lanes] = (
                ion_ref[index, :, lanes] + deposit_ref[first : first + cells_y, :]
            ) * inverse_ref[index, :, lanes]
    edge = 0
    for field_ref, width in zip(
        (start_ref, inverse_ref, source_ref, ion_ref), HALO_WIDTHS, strict=True
    ):
        for step in range(width):
            for phase, edge_ref in enumerate(edge_refs):
                last = ups[2] if phase == 0 else 1 - ups[2]
                plane = field_ref[last * (cells_x - width) + step]
                for half in range(2):
                    edge_ref[2 * edge + half] = plane[:, 128 * half : 128 * half + 128]
            edge += 1


def prepare(
    fill,
    cell,
    send_index,
    send_count,
    pair_dir,
    pair_slot,
    positions,
    charges,
    ions,
    start,
    screen,
):
    clusters = charges.shape[0]
    directions, slots = send_index.shape
    cells_y = ions.shape[1]
    smem = pl.BlockSpec(memory_space=pltpu.SMEM)
    vmem = pl.BlockSpec(memory_space=pltpu.VMEM)
    return pl.pallas_call(
        prepare_kernel,
        out_shape=(
            jax.ShapeDtypeStruct(pair_dir.shape, jnp.int32),
            jax.ShapeDtypeStruct((clusters, 4, 128), jnp.float32),
            jax.ShapeDtypeStruct((clusters, 128), jnp.float32),
            jax.ShapeDtypeStruct(ions.shape, jnp.float32),
            jax.ShapeDtypeStruct(ions.shape, jnp.float32),
            *[jax.ShapeDtypeStruct((slots * 4, 128), jnp.float32)] * directions,
            *[jax.ShapeDtypeStruct((2 * sum(HALO_WIDTHS), cells_y, 128), jnp.float32)] * 2,
        ),
        in_specs=[smem] * 4 + [vmem] * 3 + [pl.BlockSpec(memory_space=pltpu.HBM)] * 5,
        out_specs=(vmem,) * (7 + directions),
        scratch_shapes=[
            pltpu.VMEM((clusters, 128), jnp.float32),
            pltpu.VMEM((ions.size // 128, 128), jnp.float32),
            *[
                pltpu.VMEM(operand.shape, jnp.float32)
                for operand in (positions, charges, ions, start, screen)
            ],
            pltpu.SemaphoreType.DMA((5,)),
        ],
        compiler_params=pltpu.CompilerParams(vmem_limit_bytes=VMEM_LIMIT),
        name="prepare",
    )(
        fill,
        cell,
        send_index,
        send_count,
        cell.reshape(1, clusters),
        pair_dir,
        pair_slot,
        positions,
        charges,
        ions,
        start,
        screen,
    )


def line_rows(cells_y):
    return (cells_y + 2 * DEPTH + 7) // 8 * 8


def pack_rows_kernel(*refs):
    field_hbms, edge_hbms, reaction_hbms, out_refs = (refs[:4], refs[4:6], refs[6:8], refs[8:10])
    near_refs, edge_refs, sems = (refs[10:14], refs[14:16], refs[16])
    cells_x, cells_y, _ = field_hbms[0].shape
    base = reaction_hbms[0].shape[0]
    ups = upward()
    moves = [
        (reaction, out_ref.at[0:base])
        for reaction, out_ref in zip(reaction_hbms, out_refs, strict=True)
    ]
    for source, target in zip(field_hbms + edge_hbms, near_refs + edge_refs, strict=True):
        moves.append((source.at[:, 0:8], target.at[0]))
        moves.append((source.at[:, cells_y - 8 : cells_y], target.at[1]))
    for copy in start_copies(moves, sems):
        copy.wait()

    def fill(out_ref, after):
        for field, width in enumerate(HALO_WIDTHS):
            offset = sum(HALO_WIDTHS[:field])
            rows = slice(8 - width, 8) if after else slice(0, width)
            for index in range(cells_x):
                value = near_refs[field][after, index, rows, :]
                for half in range(2):
                    at = base + ((DEPTH + index) * 2 + half) * 16 + offset
                    out_ref[at : at + width, :] = value[:, 128 * half : 128 * half + 128]
            if width == 1:
                continue
            for phase, edge_ref in enumerate(edge_refs):
                higher = ups[2] if phase == 0 else 1 - ups[2]
                for step in range(width):
                    plane = (DEPTH - width) + higher * (cells_x + width) + step
                    for half in range(2):
                        at = pl.ds(base + (plane * 2 + half) * 16 + offset, width)
                        out_ref[at, :] = edge_ref[after, 2 * (offset + step) + half, rows, :]

    for up in range(2):

        @pl.when(ups[0] == up)
        def _(up=up):
            fill(out_refs[0], up)
            fill(out_refs[1], 1 - up)


def pack_rows(fields, edges, reactions):
    vmem = pl.BlockSpec(memory_space=pltpu.VMEM)
    cells_x, _, cells_z = fields[0].shape
    rows = reactions[0].shape[0] + (cells_x + 2 * DEPTH) * 32
    shape = jax.ShapeDtypeStruct((rows, 128), jnp.float32)
    return pl.pallas_call(
        pack_rows_kernel,
        out_shape=(shape, shape),
        in_specs=[pl.BlockSpec(memory_space=pltpu.HBM)] * 8,
        out_specs=(vmem, vmem),
        scratch_shapes=[
            *[pltpu.VMEM((2, cells_x, 8, cells_z), jnp.float32)] * 4,
            *[pltpu.VMEM((2, edges[0].shape[0], 8, 128), jnp.float32)] * 2,
            pltpu.SemaphoreType.DMA((14,)),
        ],
        compiler_params=pltpu.CompilerParams(vmem_limit_bytes=VMEM_LIMIT),
        name="pack_rows",
    )(*fields, *edges, *reactions)


def fill_line(target_ref, plane, half, field, value, rim_ref):
    cells_y = value.shape[0]
    width = HALO_WIDTHS[field]
    at = (plane * 2 + half) * line_rows(cells_y) + DEPTH
    target_ref[pl.ds(at, cells_y), :] = value
    first = (plane * 2 + half) * 16 + sum(HALO_WIDTHS[:field])
    target_ref[pl.ds(at - width, width), :] = rim_ref[pl.ds(first, width), :]
    first = first + rim_ref.shape[0] // 2
    target_ref[pl.ds(at + cells_y, width), :] = rim_ref[pl.ds(first, width), :]


def face_flux(pot_low, pot_high, ion_low, ion_high):
    speed = -mobility * (pot_high - pot_low)
    return (
        jnp.maximum(speed, 0.0) * ion_low
        + jnp.minimum(speed, 0.0) * ion_high
        - diffusion * (ion_high - ion_low)
    )


def grid_kernel(base, *refs):
    cell_ref, masked_hbm = refs[:2]
    hbm_refs, edge_hbms = (refs[2:6], refs[8:10])
    potential_ref, next_ref, force_ref = refs[10:13]
    start_ref, inverse_ref, source_ref, ion_ref = refs[13:17]
    updates, resids, final_ref, pick_refs = (refs[17:20], refs[20:22], refs[22], refs[23:26])
    rim_ref, field_refs, masked_ref, sems = (refs[26], refs[27:31], refs[31], refs[32])
    edge_refs = refs[33:35]
    cells_x, cells_y, _ = field_refs[0].shape
    rows = line_rows(cells_y)
    inner = cells_y + 2 * DEPTH - 2
    clusters = masked_ref.shape[0]
    ups = upward()
    size = (cells_x + 2 * DEPTH) * 32
    moves = [
        (rim.at[base : base + size], rim_ref.at[pl.ds(pl.multiple_of(side * size, size), size)])
        for rim, side in zip(refs[6:8], (ups[0], 1 - ups[0]), strict=True)
    ]
    moves += zip(hbm_refs, field_refs, strict=True)
    moves += zip(edge_hbms, edge_refs, strict=True)
    moves.append((masked_hbm, masked_ref))
    for copy in start_copies(moves, sems):
        copy.wait()
    extended = (start_ref, inverse_ref, source_ref, ion_ref)

    def fill(index, _):
        for field, target_ref in enumerate(extended):
            plane = field_refs[field][index]
            for half in range(2):
                value = plane[:, 128 * half : 128 * half + 128]
                fill_line(target_ref, DEPTH + index, half, field, value, rim_ref)
        return 0

    lax.fori_loop(0, cells_x, fill, 0, unroll=2)
    for field, target_ref in enumerate(extended):
        width = HALO_WIDTHS[field]
        for phase, edge_ref in enumerate(edge_refs):
            higher = ups[2] if phase == 0 else 1 - ups[2]

            def fill_edge(step, _, field=field, target_ref=target_ref, edge_ref=edge_ref):
                width = HALO_WIDTHS[field]
                plane = (DEPTH - width) + higher * (cells_x + width) + step
                for half in range(2):
                    value = edge_ref[2 * (sum(HALO_WIDTHS[:field]) + step) + half]
                    fill_line(target_ref, plane, half, field, value, rim_ref)
                return 0

            lax.fori_loop(0, width, fill_edge, 0, unroll=True)

    def beyond(values):
        lane = lax.broadcasted_iota(jnp.int32, values[0].shape, 1)
        right = [pltpu.roll(value, 127, 1) for value in values]
        left = [pltpu.roll(value, 1, 1) for value in values]
        above = [jnp.where(lane == 127, right[1], right[0]), jnp.where(lane == 127, 0.0, right[1])]
        below = [jnp.where(lane == 0, 0.0, left[0]), jnp.where(lane == 0, left[0], left[1])]
        return (below, above)

    def wide(plane, half, shift=0):
        return pl.ds((plane * 2 + half) * rows + 1 + shift, inner)

    def around(ref, plane):
        here = [ref[wide(plane, half), :] for half in range(2)]
        below, above = beyond(here)
        sums = [
            (ref[wide(plane - 1, half), :] + ref[wide(plane + 1, half), :])
            + (ref[wide(plane, half, -1), :] + ref[wide(plane, half, 1), :])
            + (below[half] + above[half])
            for half in range(2)
        ]
        return (here, sums)

    middle = 0.5 * (highest_eig + lowest_eig)
    spread = 0.5 * (highest_eig - lowest_eig)
    assert middle == 1.0 and SWEEPS == 4

    def sweep_first(plane, _):
        here, sums = around(start_ref, plane)
        for half in range(2):
            at = wide(plane, half)
            updates[0][at, :] = source_ref[at, :] - here[half] + inverse_ref[at, :] * sums[half]
        return 0

    lax.fori_loop(1, cells_x + 2 * DEPTH - 1, sweep_first, 0, unroll=2)

    ratio_ms = middle / spread
    weight_now = 1.0 / ratio_ms
    for turn in range(1, SWEEPS):
        weight_next = 1.0 / (2.0 * ratio_ms - weight_now)
        keep, gain = (weight_next * weight_now, 2.0 * weight_next / spread)
        weight_now = weight_next

        def sweep(plane, _, turn=turn, keep=keep, gain=gain):
            here, sums = around(updates[turn - 1], plane)
            for half in range(2):
                at = wide(plane, half)
                resid = inverse_ref[at, :] * sums[half]
                if turn > 1:
                    resid = resid + (resids[turn - 2][at, :] - here[half])
                update = keep * here[half] + gain * resid
                if turn + 1 < SWEEPS:
                    resids[turn - 1][at, :] = resid
                    updates[turn][at, :] = update
                else:
                    final_ref[at, :] = (start_ref[at, :] + updates[0][at, :]) + (
                        (updates[1][at, :] + here[half]) + update
                    )
            return 0

        first = 1 + turn
        lax.fori_loop(first, cells_x + 2 * DEPTH - first, sweep, 0, unroll=2)

    def local(plane, half, shift=0):
        return pl.ds((plane * 2 + half) * rows + DEPTH + shift, cells_y)

    def advance(index, _):
        plane = index + DEPTH
        pots = [final_ref[local(plane, half), :] for half in range(2)]
        ions = [ion_ref[local(plane, half), :] for half in range(2)]
        pot_below, pot_above = beyond(pots)
        ion_below, ion_above = beyond(ions)
        for half in range(2):
            pot, ion = (pots[half], ions[half])
            steps = [
                (final_ref[at, :], ion_ref[at, :])
                for at in (
                    local(plane - 1, half),
                    local(plane + 1, half),
                    local(plane, half, -1),
                    local(plane, half, 1),
                )
            ]
            steps += [(pot_below[half], ion_below[half]), (pot_above[half], ion_above[half])]
            total = 0.0
            for low, high in zip(steps[0::2], steps[1::2], strict=True):
                total = total + (
                    face_flux(pot, high[0], ion, high[1]) - face_flux(low[0], pot, low[1], ion)
                )
            lanes = slice(128 * half, 128 * half + 128)
            next_ref[index, :, lanes] = ion - time_step * total
            potential_ref[index, :, lanes] = pot
        return 0

    lax.fori_loop(0, cells_x, advance, 0)

    row_lane = lax.broadcasted_iota(jnp.int32, (1, 128), 1)

    def pick(cluster, _):
        cell = cell_ref[cluster]
        index_x = lax.shift_right_logical(cell, CELL_BITS) // cells_y + DEPTH
        index_y = lax.shift_right_logical(cell, CELL_BITS) % cells_y + DEPTH
        index_z = lax.bitwise_and(cell, 255)
        half = lax.shift_right_logical(index_z, 7)
        here = row_lane == lax.bitwise_and(index_z, 127)

        def line(plane, row, part):
            return final_ref[pl.ds((plane * 2 + part) * rows + row, 1), :]

        along_x = line(index_x - 1, index_y, half) - line(index_x + 1, index_y, half)
        along_y = line(index_x, index_y - 1, half) - line(index_x, index_y + 1, half)
        along_z = jnp.zeros((1, 128), jnp.float32)
        for part in range(2):
            value = line(index_x, index_y, part)
            place = row_lane + 128 * part
            along_z = along_z + jnp.where(place == index_z - 1, value, 0.0)
            along_z = along_z - jnp.where(place == index_z + 1, value, 0.0)
        at = pl.ds(cluster, 1)
        pick_refs[0][at, :] = jnp.where(here, along_x, 0.0)
        pick_refs[1][at, :] = jnp.where(here, along_y, 0.0)
        pick_refs[2][at, :] = along_z
        return 0

    lax.fori_loop(0, clusters, pick, 0, unroll=8)

    def spread_out(step, _):
        start = pl.multiple_of(step * 8, 8)
        charge = masked_ref[pl.ds(start, 8), :] * (0.5 * field_scale)
        for part, pick_ref in enumerate(pick_refs):
            total = jnp.sum(pick_ref[pl.ds(start, 8), :], axis=1, keepdims=True)
            force_ref[pl.ds(4 * start + part, 8, stride=4), :] = charge * total
        force_ref[pl.ds(4 * start + 3, 8, stride=4), :] = jnp.zeros((8, 128), jnp.float32)
        return 0

    lax.fori_loop(0, clusters // 8, spread_out, 0, unroll=4)


def grid_step(cell, masked, fields, rims, edges, base):
    smem = pl.BlockSpec(memory_space=pltpu.SMEM)
    vmem = pl.BlockSpec(memory_space=pltpu.VMEM)
    clusters = masked.shape[0]
    cells_x, cells_y, _ = fields[0].shape
    block = ((cells_x + 2 * DEPTH) * 2 * line_rows(cells_y), 128)
    return pl.pallas_call(
        functools.partial(grid_kernel, base),
        out_shape=(
            jax.ShapeDtypeStruct(fields[0].shape, jnp.float32),
            jax.ShapeDtypeStruct(fields[0].shape, jnp.float32),
            jax.ShapeDtypeStruct((clusters * 4, 128), jnp.float32),
        ),
        in_specs=[smem] + [pl.BlockSpec(memory_space=pltpu.HBM)] * 9,
        out_specs=(vmem,) * 3,
        scratch_shapes=[pltpu.VMEM(block, jnp.float32)] * 10
        + [pltpu.VMEM((clusters, 128), jnp.float32)] * 3
        + [pltpu.VMEM(((cells_x + 2 * DEPTH) * 64, 128), jnp.float32)]
        + [pltpu.VMEM(field.shape, jnp.float32) for field in fields]
        + [pltpu.VMEM(masked.shape, jnp.float32), pltpu.SemaphoreType.DMA((9,))]
        + [pltpu.VMEM(edge.shape, jnp.float32) for edge in edges],
        compiler_params=pltpu.CompilerParams(vmem_limit_bytes=VMEM_LIMIT),
        cost_estimate=pl.CostEstimate(
            flops=block[0] * block[1] * 100, bytes_accessed=8 << 20, transcendentals=0
        ),
        name="grid_step",
    )(cell, masked, *fields, *rims, *edges)


def gather_forces_kernel(send_index_ref, *refs):
    fetched = len(SWAPS) + 3
    out_ref, sum_ref = refs[fetched : fetched + 2]
    own_ref, field_ref, *back_refs = refs[fetched + 2 : -1]
    copies = start_copies(
        [
            (source.at[0 : target.shape[0]], target)
            for source, target in zip(refs[:fetched], refs[fetched + 2 : -1], strict=True)
        ],
        refs[-1],
    )
    for copy in copies:
        copy.wait()
    clusters = own_ref.shape[0]
    slots = send_index_ref.shape[1]
    sum_ref[...] = own_ref[...] + field_ref[...]
    ups = upward()

    def visit(slot, _):
        for position, back_ref in enumerate(back_refs):
            cluster = send_index_ref[sent_row(position, ups) if position else 0, slot]
            sum_ref[cluster] += back_ref[slot]
        return 0

    lax.fori_loop(0, slots, visit, 0)

    def write(step, _):
        for turn in range(8):
            cluster = step * 8 + turn
            out_ref[:, pl.ds(pl.multiple_of(cluster * 128, 128), 128)] = sum_ref[cluster][0:3]
        return 0

    lax.fori_loop(0, clusters // 8, write, 0)


def gather_forces(send_index, own, field, backs):
    smem = pl.BlockSpec(memory_space=pltpu.SMEM)
    vmem = pl.BlockSpec(memory_space=pltpu.VMEM)
    clusters = own.shape[0]
    return pl.pallas_call(
        gather_forces_kernel,
        out_shape=jax.ShapeDtypeStruct((3, clusters * 128), jnp.float32),
        in_specs=[smem] + [pl.BlockSpec(memory_space=pltpu.HBM)] * (2 + len(backs)),
        out_specs=vmem,
        scratch_shapes=[
            *[pltpu.VMEM(part.shape, jnp.float32) for part in (own, own, field)],
            *[pltpu.VMEM((send_index.shape[1], 4, 128), jnp.float32)] * len(backs),
            pltpu.SemaphoreType.DMA((2 + len(backs),)),
        ],
        compiler_params=pltpu.CompilerParams(vmem_limit_bytes=VMEM_LIMIT),
        name="gather_forces",
    )(send_index, own, field, *backs)


def shards(
    positions,
    charges,
    cluster_fill,
    cluster_cell,
    send_index,
    send_count,
    pair_local,
    pair_dir,
    pair_slot,
    ion_density,
    potential_prev,
    screening,
):
    clusters = cluster_fill.shape[0]
    psize = charges.shape[0] // clusters
    slots = send_index.shape[1]
    base = slots * 4
    other_rows, own, masked, inverse, source, local, *messages = prepare(
        cluster_fill,
        cluster_cell,
        send_index,
        send_count,
        pair_dir.reshape(-1, 128),
        pair_slot.reshape(-1, 128),
        positions,
        charges.reshape(clusters, psize),
        ion_density,
        potential_prev,
        screening,
    )
    edges = messages[len(SWAPS) :]
    arrived = [local] + [
        swapped(message, *swap)
        for message, swap in zip(messages[: len(SWAPS)], SWAPS, strict=True)
    ]
    fields = (potential_prev, inverse, source, ion_density)
    arrived, edges = lax.optimization_barrier((arrived, edges))
    edges = [swapped(edge, "grp", 1, phase) for phase, edge in enumerate(edges)]
    own_force, *reactions = pair_forces(
        pair_local,
        other_rows.reshape(-1),
        own.reshape(clusters * 4, psize),
        arrived,
        slots,
    )
    local_back, *reactions = reactions
    rims = pack_rows(fields, edges, reactions[:2])
    backs = [
        swapped(reaction, *swap)
        for reaction, swap in zip((*rims, *reactions[2:]), SWAPS, strict=True)
    ]
    potential, ion_next, field_force = grid_step(
        cluster_cell, masked, fields, backs[:2], edges, base
    )
    forces = gather_forces(
        send_index,
        own_force.reshape(clusters, 4, psize),
        field_force.reshape(clusters, 4, psize),
        [back.reshape(-1, 4, psize) for back in (local_back, *backs)],
    )
    return (forces, potential, ion_next)


def solution(mesh):
    in_specs = (
        P(None, ("grp", "brick")),
        P(("grp", "brick")),
        P(("grp", "brick")),
        P(("grp", "brick")),
        P(("grp", "brick"), None),
        P(("grp", "brick"), None),
        P(("grp", "brick")),
        P(("grp", "brick")),
        P(("grp", "brick")),
        P("grp", "brick", None),
        P("grp", "brick", None),
        P("grp", "brick", None),
    )
    out_specs = (P(None, ("grp", "brick")), P("grp", "brick", None), P("grp", "brick", None))
    return jax.shard_map(shards, mesh=mesh, in_specs=in_specs, out_specs=out_specs, check_vma=False)
```

```python
import functools

import jax
import jax.numpy as jnp
import numpy as np
from jax import lax
from jax.experimental import pallas as pl
from jax.experimental.pallas import tpu as pltpu
from jax.sharding import PartitionSpec as P

SWEEPS = 4
UNROLL = 8
CHUNKS = 4
HALO_WIDTHS = (SWEEPS + 1, SWEEPS, SWEEPS, 1)
DEPTH = SWEEPS + 1
CELL_BITS = 8
SWAPS = tuple(
    (*way, phase) for way in (("brick", 1), ("brick", 2), ("grp", 1)) for phase in (0, 1)
)


coulomb_scale = 0.02
softening = 0.1
field_scale = 0.5
deposit_scale = 0.2
lowest_eig = 0.01
highest_eig = 1.99
mobility = 0.3
diffusion = 0.2
time_step = 0.2


VMEM_LIMIT = 60 * 1024 * 1024
ROOMY_LIMIT = 48 * 1024 * 1024


def start_copies(pairs, sems):
    copies = [
        pltpu.make_async_copy(source, target, sems.at[index])
        for index, (source, target) in enumerate(pairs)
    ]
    for copy in copies:
        copy.start()
    return copies


def upward():
    brick, grp = (lax.axis_index("brick"), lax.axis_index("grp"))
    bits = (brick, lax.shift_right_logical(brick, 1), grp)
    return [1 - lax.bitwise_and(bit, 1) for bit in bits]


def sent_row(position, ups):
    way, phase = ((position - 1) // 2, (position - 1) % 2)
    return 1 + 2 * way + (ups[way] if phase else 1 - ups[way])


def swapped(shard, axis, distance, phase):
    devices = lax.axis_size(axis)
    pairs = []
    for index in range(devices):
        step = distance if (index // distance + phase) % 2 == 0 else -distance
        if 0 <= index + step < devices:
            pairs.append((index, index + step))
    return lax.ppermute(shard, axis, pairs)


def split3(value):
    first = value.astype(jnp.bfloat16).astype(jnp.float32)
    rest = value - first
    second = rest.astype(jnp.bfloat16).astype(jnp.float32)
    third = (rest - second).astype(jnp.bfloat16).astype(jnp.float32)
    return (first, second, third)


def moment_pieces(comps, charge):
    rows = [None] * 12
    for part, charged in enumerate((*comps, None)):
        for level, piece in enumerate(split3(charge if charged is None else charge * charged)):
            rows[4 * level + part] = piece
    return rows


def selections():
    near_kinds, far_kinds = ([], [])
    for part in range(3):
        near_kinds += [3 * part + level for level in (0, 0, 0, 1, 1, 2)]
        far_kinds += [3 * part + level for level in (0, 1, 2, 0, 1, 0)]
    near_kinds += [9, 10, 11, 12, 12, 12]
    far_kinds += [12, 12, 12, 9, 10, 11]
    near = np.zeros((128, 1024), np.float32)
    far = np.zeros((256, 128), np.float32)
    moment = np.zeros((128, 128), np.float32)
    for cluster in range(8):
        for index, kind in enumerate(near_kinds):
            near[kind * 8 + cluster, cluster * 128 + index] = 1.0
        for index, kind in enumerate(far_kinds):
            far[cluster * 32 + index, kind * 8 + cluster] = 1.0
        for kind in range(12):
            moment[cluster * 16 + kind, kind * 8 + cluster] = 1.0
    return tuple(jnp.asarray(part, jnp.bfloat16) for part in (near, far, moment))


def pair_kernel(own_rows_ref, other_rows_ref, *refs):
    sources = len(SWAPS) + 1
    fetched = sources + 4
    hbm_refs = refs[:fetched]
    own_out_ref = refs[fetched]
    other_out_refs = refs[fetched + 1 : fetched + 1 + sources]
    refs = refs[fetched + 1 + sources :]
    near_sel_ref, far_sel_ref, moment_sel_ref, own_ref = refs[:4]
    other_refs = refs[4:fetched]
    sems = refs[fetched]
    copies = start_copies(
        [
            (source.at[0 : target.shape[0]], target)
            for source, target in zip(hbm_refs, refs[:fetched], strict=True)
        ],
        sems,
    )
    (
        near_ref,
        far_ref,
        own_moment_ref,
        other_moment_ref,
        own_sum_ref,
        other_sum_ref,
        dist_ref,
        *weight_refs,
    ) = refs[fetched + 1 :]
    clusters = own_ref.shape[0] // 4
    slots = other_out_refs[0].shape[0] // 4
    others = slots * sources
    groups = own_rows_ref.shape[0] // UNROLL
    ones = jnp.ones((8, 128), jnp.float32)
    zeros = jnp.zeros((8, 128), jnp.float32)

    def components(data_ref, start):
        return [data_ref[pl.ds(4 * start + part, 8, stride=4), :] for part in range(4)]

    def place_pieces(comps, factor, offset):
        pieces = []
        square = zeros
        for comp in comps:
            square = square + comp * comp
            pieces += split3(factor * comp)
        pieces += [*split3(square + offset), ones]
        return jnp.concatenate(pieces + [zeros] * (16 - len(pieces)), axis=0)

    def selected(left, right):
        return jnp.dot(
            left.astype(jnp.bfloat16), right, preferred_element_type=jnp.float32
        ).astype(jnp.bfloat16)

    def near_rows(step, _):
        start = pl.multiple_of(step * 8, 8)
        *comps, charge = components(own_ref, start)
        moments = jnp.concatenate(moment_pieces(comps, charge) + [zeros] * 4, axis=0)
        own_moment_ref[pl.ds(pl.multiple_of(start * 16, 128), 128), :] = selected(
            moment_sel_ref[...], moments.astype(jnp.bfloat16)
        )
        tiles = selected(place_pieces(comps, 1.0, 0.0).T, near_sel_ref[...])
        for index in range(8):
            at = pl.ds(pl.multiple_of((start + index) * 128, 128), 128)
            near_ref[at, :] = tiles[:, 128 * index : 128 * index + 128]
        return 0

    def far_rows(source, step, _):
        local = pl.multiple_of(step * 8, 8)
        start = source * slots + local
        *comps, charge = components(other_refs[source], local)
        far_ref[pl.ds(pl.multiple_of(start * 32, 256), 256), :] = selected(
            far_sel_ref[...], place_pieces(comps, -2.0, softening).astype(jnp.bfloat16)
        )
        moments = jnp.concatenate(moment_pieces(comps, charge) + [zeros] * 4, axis=0)
        other_moment_ref[pl.ds(pl.multiple_of(start * 16, 128), 128), :] = selected(
            moment_sel_ref[...], moments.astype(jnp.bfloat16)
        )
        return 0

    own_sum_ref[...] = jnp.zeros_like(own_sum_ref)
    other_sum_ref[...] = jnp.zeros_like(other_sum_ref)
    weight_refs[0][...] = jnp.zeros_like(weight_refs[0])
    for copy in copies[:4]:
        copy.wait()
    lax.fori_loop(0, clusters // 8, near_rows, 0, unroll=4)
    for copy in copies[4:]:
        copy.wait()
    for source in range(sources):
        lax.fori_loop(0, slots // 8, functools.partial(far_rows, source), 0, unroll=4)
    def distances(pair):
        own = own_rows_ref[pair]
        other = other_rows_ref[pair]
        return jnp.dot(
            near_ref[pl.ds(pl.multiple_of(own * 128, 128), 128), 0:32],
            far_ref[pl.ds(pl.multiple_of(other * 32, 32), 32), :],
            preferred_element_type=jnp.float32,
        )

    def weights(dist, index, chunk, weight_ref):
        rows = 128 // CHUNKS
        first = rows * chunk
        root = lax.rsqrt(dist[first : first + rows])
        weight = root * root * root
        high = weight.astype(jnp.bfloat16)
        low = (weight - high.astype(jnp.float32)).astype(jnp.bfloat16)
        at = slice(128 * index + first, 128 * index + first + rows)
        weight_ref[at, :128] = high
        weight_ref[at, 128:] = low

    def row_block(index):
        return pl.ds(pl.multiple_of(index * 16, 16), 16)

    def own_product(other, weight_ref, index):
        both = weight_ref[128 * index : 128 * index + 128]
        return lax.dot_general(
            other_moment_ref[row_block(other), :],
            jnp.concatenate([both[:, :128], both[:, 128:]], axis=0),
            (((1,), (1,)), ((), ())),
            preferred_element_type=jnp.float32,
        )

    def other_product(own, weight_ref, index):
        return jnp.dot(
            own_moment_ref[row_block(own), :],
            weight_ref[128 * index : 128 * index + 128],
            preferred_element_type=jnp.float32,
        )

    def add_rows(own, other, to_own, to_other):
        own_sum_ref[row_block(own), :] += to_own[:, :128] + to_own[:, 128:]
        other_sum_ref[row_block(other), :] += to_other[:, :128] + to_other[:, 128:]

    def half_step(step, side, dist):
        last = jnp.maximum(step - 1, 0) * UNROLL
        waiting = []
        for index in range(UNROLL):
            own = own_rows_ref[last + index]
            other = other_rows_ref[last + index]
            later = distances(jnp.minimum(step * UNROLL + index + 1, groups * UNROLL - 1))
            weights(dist, index, 0, weight_refs[1 - side])
            to_own = own_product(other, weight_refs[side], index)
            weights(dist, index, 1, weight_refs[1 - side])
            weights(dist, index, 2, weight_refs[1 - side])
            to_other = other_product(own, weight_refs[side], index)
            weights(dist, index, 3, weight_refs[1 - side])
            dist = later
            waiting.append((own, other, to_own, to_other))
            if len(waiting) > 2:
                add_rows(*waiting.pop(0))
        for entry in waiting:
            add_rows(*entry)
        return dist

    def visit(step, _):
        dist = dist_ref[...]
        for side in range(2):
            dist = half_step(step * 2 + side, side, dist)
        dist_ref[...] = dist
        return 0

    dist_ref[...] = distances(0)
    lax.fori_loop(0, groups // 2, visit, 0)
    half_step(groups, 0, dist_ref[...])

    def finish(data_ref, out_ref, sum_ref, base, step, _):
        start = pl.multiple_of(step * 8, 8)
        *comps, charge = components(data_ref, start)

        def total(part):
            terms = [
                sum_ref[pl.ds(base + start * 16 + 4 * level + part, 8, stride=16), :]
                for level in range(3)
            ]
            return terms[0] + (terms[1] + terms[2])

        weight = total(3)
        scale = coulomb_scale * charge
        for part, comp in enumerate(comps):
            out_ref[pl.ds(4 * start + part, 8, stride=4), :] = scale * (comp * weight - total(part))
        out_ref[pl.ds(4 * start + 3, 8, stride=4), :] = zeros
        return 0

    lax.fori_loop(
        0, clusters // 8, functools.partial(finish, own_ref, own_out_ref, own_sum_ref, 0), 0, unroll=4
    )
    for source in range(sources):
        body = functools.partial(
            finish,
            other_refs[source],
            other_out_refs[source],
            other_sum_ref,
            source * slots * 16,
        )
        lax.fori_loop(0, slots // 8, body, 0, unroll=4)


def pair_forces(own_rows, other_rows, own, arrived, slots):
    clusters = own.shape[0] // 4
    others = slots * len(arrived)
    pairs = own_rows.shape[0]
    smem = pl.BlockSpec(memory_space=pltpu.SMEM)
    vmem = pl.BlockSpec(memory_space=pltpu.VMEM)
    hbm = pl.BlockSpec(memory_space=pl.ANY)
    operands = (*selections(), own)
    return pl.pallas_call(
        pair_kernel,
        out_shape=(
            jax.ShapeDtypeStruct(own.shape, jnp.float32),
            *[jax.ShapeDtypeStruct((slots * 4, 128), jnp.float32)] * len(arrived),
        ),
        in_specs=[smem, smem] + [hbm] * (4 + len(arrived)),
        out_specs=(vmem,) * (len(arrived) + 1),
        scratch_shapes=[
            *[pltpu.VMEM(operand.shape, operand.dtype) for operand in operands],
            *[pltpu.VMEM((slots * 4, 128), jnp.float32)] * len(arrived),
            pltpu.SemaphoreType.DMA((len(operands) + len(arrived),)),
            pltpu.VMEM((clusters * 128, 128), jnp.bfloat16),
            pltpu.VMEM((others * 32, 128), jnp.bfloat16),
            pltpu.VMEM((clusters * 16, 128), jnp.bfloat16),
            pltpu.VMEM((others * 16, 128), jnp.bfloat16),
            pltpu.VMEM((clusters * 16, 128), jnp.float32),
            pltpu.VMEM((others * 16, 128), jnp.float32),
            pltpu.VMEM((128, 128), jnp.float32),
            *[pltpu.VMEM((128 * UNROLL, 256), jnp.bfloat16)] * 2,
        ],
        compiler_params=pltpu.CompilerParams(vmem_limit_bytes=ROOMY_LIMIT),
        cost_estimate=pl.CostEstimate(
            flops=pairs * 128 * 128 * 20, bytes_accessed=4 * 1024 * 1024, transcendentals=0
        ),
        name="pair_forces",
    )(own_rows, other_rows, *operands, *arrived)


def prepare_kernel(
    fill_ref,
    send_index_ref,
    send_count_ref,
    pair_dir_ref,
    pair_slot_ref,
    position_hbm,
    charge_hbm,
    row_ref,
    own_ref,
    masked_ref,
    *refs,
):
    out_refs, (position_ref, charge_ref, sems) = (refs[:-3], refs[-3:])
    copies = start_copies(((position_hbm, position_ref), (charge_hbm, charge_ref)), sems)
    clusters = charge_ref.shape[0]
    slots = send_index_ref.shape[1]
    lane = lax.broadcasted_iota(jnp.int32, (1, 128), 1)
    row = lax.broadcasted_iota(jnp.int32, (4, 128), 0)
    ups = upward()
    direction = pair_dir_ref[...]
    way = lax.shift_right_arithmetic(direction - 1, 1)
    flip = jnp.where(way == 0, ups[0], jnp.where(way == 1, ups[1], ups[2]))
    position = 1 + 2 * way + lax.bitwise_xor(lax.bitwise_and(direction - 1, 1), flip)
    row_ref[...] = jnp.where(direction == 0, 0, position) * slots + pair_slot_ref[...]
    for copy in copies:
        copy.wait()

    def collect(step, _):
        for turn in range(8):
            cluster = step * 8 + turn
            masked = jnp.where(lane < fill_ref[cluster], charge_ref[pl.ds(cluster, 1), :], 0.0)
            masked_ref[pl.ds(cluster, 1), :] = masked
            place = position_ref[:, pl.ds(pl.multiple_of(cluster * 128, 128), 128)]
            own_ref[cluster, 0:3, :] = place
            own_ref[cluster, 3:4, :] = masked
        return 0

    lax.fori_loop(0, clusters // 8, collect, 0, unroll=2)

    def fill_messages(step, _):
        for position, out_ref in enumerate(out_refs):
            direction = sent_row(position, ups) if position else 0
            parts = []
            for turn in range(2):
                slot = step * 2 + turn
                live = jnp.where(slot < send_count_ref[0, direction], 1.0, 0.0)
                value = own_ref[send_index_ref[direction, slot]]
                parts.append(jnp.where(row == 3, value * live, value))
            out_ref[pl.ds(pl.multiple_of(step * 8, 8), 8), :] = jnp.concatenate(parts, axis=0)
        return 0

    lax.fori_loop(0, slots // 2, fill_messages, 0)


def prepare(fill, send_index, send_count, pair_dir, pair_slot, positions, charges):
    clusters = charges.shape[0]
    directions, slots = send_index.shape
    smem = pl.BlockSpec(memory_space=pltpu.SMEM)
    vmem = pl.BlockSpec(memory_space=pltpu.VMEM)
    return pl.pallas_call(
        prepare_kernel,
        out_shape=(
            jax.ShapeDtypeStruct(pair_dir.shape, jnp.int32),
            jax.ShapeDtypeStruct((clusters, 4, 128), jnp.float32),
            jax.ShapeDtypeStruct((clusters, 128), jnp.float32),
            *[jax.ShapeDtypeStruct((slots * 4, 128), jnp.float32)] * directions,
        ),
        in_specs=[smem] * 3 + [vmem] * 2 + [pl.BlockSpec(memory_space=pltpu.HBM)] * 2,
        out_specs=(vmem,) * (3 + directions),
        scratch_shapes=[
            *[pltpu.VMEM(operand.shape, jnp.float32) for operand in (positions, charges)],
            pltpu.SemaphoreType.DMA((2,)),
        ],
        compiler_params=pltpu.CompilerParams(vmem_limit_bytes=VMEM_LIMIT),
        name="prepare",
    )(fill, send_index, send_count, pair_dir, pair_slot, positions, charges)


def sources_kernel(
    cell_ref,
    cell_row_ref,
    masked_hbm,
    ion_hbm,
    start_hbm,
    screen_hbm,
    inverse_ref,
    source_ref,
    *refs,
):
    edge_refs, refs = (refs[:2], refs[2:])
    sum_ref, deposit_ref, masked_ref, ion_ref, start_ref, screen_ref, sems = refs
    copies = start_copies(
        (
            (masked_hbm, masked_ref),
            (ion_hbm, ion_ref),
            (start_hbm, start_ref),
            (screen_hbm, screen_ref),
        ),
        sems,
    )
    copies[0].wait()
    clusters = masked_ref.shape[0]
    cells_x, cells_y, _ = ion_ref.shape
    lane = lax.broadcasted_iota(jnp.int32, (1, 128), 1)
    ups = upward()

    def add_up(step, _):
        at = pl.ds(pl.multiple_of(step * 8, 8), 8)
        total = jnp.sum(masked_ref[at, :], axis=1, keepdims=True)
        sum_ref[at, :] = jnp.broadcast_to(deposit_scale * total, (8, 128))
        return 0

    lax.fori_loop(0, clusters // 8, add_up, 0, unroll=8)

    def place(step, _):
        for turn in range(8):
            cluster = step * 8 + turn
            index_z = lax.bitwise_and(cell_ref[cluster], 127)
            at = pl.ds(cluster, 1)
            sum_ref[at, :] = jnp.where(lane == index_z, sum_ref[at, :], 0.0)
        return 0

    lax.fori_loop(0, clusters // 8, place, 0)
    cell = cell_row_ref[...]
    line = lax.shift_right_logical(cell, CELL_BITS)
    line = (line // cells_y * 2 + lax.shift_right_logical(lax.bitwise_and(cell, 255), 7)) * cells_y
    line = line + lax.shift_right_logical(cell, CELL_BITS) % cells_y
    sums = jnp.concatenate([part.astype(jnp.bfloat16) for part in split3(sum_ref[...])], axis=1)
    block = 128
    for first in range(0, deposit_ref.shape[0], block):
        rows = lax.broadcasted_iota(jnp.int32, (block, clusters), 0) + first
        hot = jnp.where(rows == line, 1.0, 0.0).astype(jnp.bfloat16)
        added = jnp.dot(hot, sums, preferred_element_type=jnp.float32)
        deposit_ref[first : first + block, :] = added[:, :128] + (
            added[:, 128:256] + added[:, 256:]
        )
    for copy in copies[1:]:
        copy.wait()
    inverse_ref[...] = 1.0 / (6.0 + screen_ref[...])
    for index in range(cells_x):
        for half in range(2):
            lanes = slice(128 * half, 128 * half + 128)
            first = (index * 2 + half) * cells_y
            source_ref[index, :, lanes] = (
                ion_ref[index, :, lanes] + deposit_ref[first : first + cells_y, :]
            ) * inverse_ref[index, :, lanes]
    edge = 0
    for field_ref, width in zip(
        (start_ref, inverse_ref, source_ref, ion_ref), HALO_WIDTHS, strict=True
    ):
        for step in range(width):
            for phase, edge_ref in enumerate(edge_refs):
                last = ups[2] if phase == 0 else 1 - ups[2]
                plane = field_ref[last * (cells_x - width) + step]
                for half in range(2):
                    edge_ref[2 * edge + half] = plane[:, 128 * half : 128 * half + 128]
            edge += 1


def sources_of(cell, masked, ions, start, screen):
    clusters = masked.shape[0]
    cells_y = ions.shape[1]
    smem = pl.BlockSpec(memory_space=pltpu.SMEM)
    vmem = pl.BlockSpec(memory_space=pltpu.VMEM)
    edge = jax.ShapeDtypeStruct((2 * sum(HALO_WIDTHS), cells_y, 128), jnp.float32)
    return pl.pallas_call(
        sources_kernel,
        out_shape=(*[jax.ShapeDtypeStruct(ions.shape, jnp.float32)] * 2, edge, edge),
        in_specs=[smem, vmem] + [pl.BlockSpec(memory_space=pltpu.HBM)] * 4,
        out_specs=(vmem,) * 4,
        scratch_shapes=[
            pltpu.VMEM((clusters, 128), jnp.float32),
            pltpu.VMEM((ions.size // 128, 128), jnp.float32),
            *[pltpu.VMEM(operand.shape, jnp.float32) for operand in (masked, ions, start, screen)],
            pltpu.SemaphoreType.DMA((4,)),
        ],
        compiler_params=pltpu.CompilerParams(vmem_limit_bytes=VMEM_LIMIT),
        cost_estimate=pl.CostEstimate(
            flops=20_000_000, bytes_accessed=4 << 20, transcendentals=0
        ),
        name="sources",
    )(cell, cell.reshape(1, clusters), masked, ions, start, screen)


def line_rows(cells_y):
    return (cells_y + 2 * DEPTH + 7) // 8 * 8


def pack_rows_kernel(*refs):
    field_hbms, edge_hbms, reaction_hbms, out_refs = (refs[:4], refs[4:6], refs[6:8], refs[8:10])
    near_refs, edge_refs, sems = (refs[10:14], refs[14:16], refs[16])
    cells_x, cells_y, _ = field_hbms[0].shape
    base = reaction_hbms[0].shape[0]
    ups = upward()
    moves = [
        (reaction, out_ref.at[0:base])
        for reaction, out_ref in zip(reaction_hbms, out_refs, strict=True)
    ]
    for source, target in zip(field_hbms + edge_hbms, near_refs + edge_refs, strict=True):
        moves.append((source.at[:, 0:8], target.at[0]))
        moves.append((source.at[:, cells_y - 8 : cells_y], target.at[1]))
    for copy in start_copies(moves, sems):
        copy.wait()

    def fill(out_ref, after):
        for field, width in enumerate(HALO_WIDTHS):
            offset = sum(HALO_WIDTHS[:field])
            rows = slice(8 - width, 8) if after else slice(0, width)
            for index in range(cells_x):
                value = near_refs[field][after, index, rows, :]
                for half in range(2):
                    at = base + ((DEPTH + index) * 2 + half) * 16 + offset
                    out_ref[at : at + width, :] = value[:, 128 * half : 128 * half + 128]
            if width == 1:
                continue
            for phase, edge_ref in enumerate(edge_refs):
                higher = ups[2] if phase == 0 else 1 - ups[2]
                for step in range(width):
                    plane = (DEPTH - width) + higher * (cells_x + width) + step
                    for half in range(2):
                        at = pl.ds(base + (plane * 2 + half) * 16 + offset, width)
                        out_ref[at, :] = edge_ref[after, 2 * (offset + step) + half, rows, :]

    for up in range(2):

        @pl.when(ups[0] == up)
        def _(up=up):
            fill(out_refs[0], up)
            fill(out_refs[1], 1 - up)


def pack_rows(fields, edges, reactions):
    vmem = pl.BlockSpec(memory_space=pltpu.VMEM)
    cells_x, _, cells_z = fields[0].shape
    rows = reactions[0].shape[0] + (cells_x + 2 * DEPTH) * 32
    shape = jax.ShapeDtypeStruct((rows, 128), jnp.float32)
    return pl.pallas_call(
        pack_rows_kernel,
        out_shape=(shape, shape),
        in_specs=[pl.BlockSpec(memory_space=pl.ANY)] * 8,
        out_specs=(vmem, vmem),
        scratch_shapes=[
            *[pltpu.VMEM((2, cells_x, 8, cells_z), jnp.float32)] * 4,
            *[pltpu.VMEM((2, edges[0].shape[0], 8, 128), jnp.float32)] * 2,
            pltpu.SemaphoreType.DMA((14,)),
        ],
        compiler_params=pltpu.CompilerParams(vmem_limit_bytes=ROOMY_LIMIT),
        name="pack_rows",
    )(*fields, *edges, *reactions)


def fill_line(target_ref, plane, half, field, value, rim_ref):
    cells_y = value.shape[0]
    width = HALO_WIDTHS[field]
    at = (plane * 2 + half) * line_rows(cells_y) + DEPTH
    target_ref[pl.ds(at, cells_y), :] = value
    first = (plane * 2 + half) * 16 + sum(HALO_WIDTHS[:field])
    target_ref[pl.ds(at - width, width), :] = rim_ref[pl.ds(first, width), :]
    first = first + rim_ref.shape[0] // 2
    target_ref[pl.ds(at + cells_y, width), :] = rim_ref[pl.ds(first, width), :]


def face_flux(pot_low, pot_high, ion_low, ion_high):
    speed = -mobility * (pot_high - pot_low)
    return (
        jnp.maximum(speed, 0.0) * ion_low
        + jnp.minimum(speed, 0.0) * ion_high
        - diffusion * (ion_high - ion_low)
    )


def grid_kernel(base, *refs):
    cell_ref, masked_hbm = refs[:2]
    hbm_refs, edge_hbms = (refs[2:6], refs[8:10])
    potential_ref, next_ref, force_ref = refs[10:13]
    start_ref, inverse_ref, source_ref, ion_ref = refs[13:17]
    updates, resids, final_ref, pick_refs = (refs[17:20], refs[20:22], refs[22], refs[23:26])
    rim_ref, field_refs, masked_ref, sems = (refs[26], refs[27:31], refs[31], refs[32])
    edge_refs = refs[33:35]
    cells_x, cells_y, _ = field_refs[0].shape
    rows = line_rows(cells_y)
    inner = cells_y + 2 * DEPTH - 2
    clusters = masked_ref.shape[0]
    ups = upward()
    size = (cells_x + 2 * DEPTH) * 32
    moves = [
        (rim.at[base : base + size], rim_ref.at[pl.ds(pl.multiple_of(side * size, size), size)])
        for rim, side in zip(refs[6:8], (ups[0], 1 - ups[0]), strict=True)
    ]
    moves += zip(hbm_refs, field_refs, strict=True)
    moves += zip(edge_hbms, edge_refs, strict=True)
    moves.append((masked_hbm, masked_ref))
    copies = start_copies(moves, sems)
    extended = (start_ref, inverse_ref, source_ref, ion_ref)
    for copy in copies[:2]:
        copy.wait()
    for field, target_ref in enumerate(extended):
        copies[2 + field].wait()

        def fill(index, _, field=field, target_ref=target_ref):
            plane = field_refs[field][index]
            for half in range(2):
                value = plane[:, 128 * half : 128 * half + 128]
                fill_line(target_ref, DEPTH + index, half, field, value, rim_ref)
            return 0

        lax.fori_loop(0, cells_x, fill, 0, unroll=4)
    for copy in copies[6:]:
        copy.wait()
    for field, target_ref in enumerate(extended):
        width = HALO_WIDTHS[field]
        for phase, edge_ref in enumerate(edge_refs):
            higher = ups[2] if phase == 0 else 1 - ups[2]

            def fill_edge(step, _, field=field, target_ref=target_ref, edge_ref=edge_ref):
                width = HALO_WIDTHS[field]
                plane = (DEPTH - width) + higher * (cells_x + width) + step
                for half in range(2):
                    value = edge_ref[2 * (sum(HALO_WIDTHS[:field]) + step) + half]
                    fill_line(target_ref, plane, half, field, value, rim_ref)
                return 0

            lax.fori_loop(0, width, fill_edge, 0, unroll=True)

    def beyond(values):
        lane = lax.broadcasted_iota(jnp.int32, values[0].shape, 1)
        right = [pltpu.roll(value, 127, 1) for value in values]
        left = [pltpu.roll(value, 1, 1) for value in values]
        above = [jnp.where(lane == 127, right[1], right[0]), jnp.where(lane == 127, 0.0, right[1])]
        below = [jnp.where(lane == 0, 0.0, left[0]), jnp.where(lane == 0, left[0], left[1])]
        return (below, above)

    def wide(plane, half, shift=0):
        return pl.ds((plane * 2 + half) * rows + 1 + shift, inner)

    def around(ref, plane):
        here = [ref[wide(plane, half), :] for half in range(2)]
        below, above = beyond(here)
        sums = [
            (ref[wide(plane - 1, half), :] + ref[wide(plane + 1, half), :])
            + (ref[wide(plane, half, -1), :] + ref[wide(plane, half, 1), :])
            + (below[half] + above[half])
            for half in range(2)
        ]
        return (here, sums)

    middle = 0.5 * (highest_eig + lowest_eig)
    spread = 0.5 * (highest_eig - lowest_eig)
    assert middle == 1.0 and SWEEPS == 4

    def sweep_first(plane, _):
        here, sums = around(start_ref, plane)
        for half in range(2):
            at = wide(plane, half)
            updates[0][at, :] = source_ref[at, :] - here[half] + inverse_ref[at, :] * sums[half]
        return 0

    lax.fori_loop(1, cells_x + 2 * DEPTH - 1, sweep_first, 0, unroll=2)

    ratio_ms = middle / spread
    weight_now = 1.0 / ratio_ms
    for turn in range(1, SWEEPS):
        weight_next = 1.0 / (2.0 * ratio_ms - weight_now)
        keep, gain = (weight_next * weight_now, 2.0 * weight_next / spread)
        weight_now = weight_next

        def sweep(plane, _, turn=turn, keep=keep, gain=gain):
            here, sums = around(updates[turn - 1], plane)
            for half in range(2):
                at = wide(plane, half)
                resid = inverse_ref[at, :] * sums[half]
                if turn > 1:
                    resid = resid + (resids[turn - 2][at, :] - here[half])
                update = keep * here[half] + gain * resid
                if turn + 1 < SWEEPS:
                    resids[turn - 1][at, :] = resid
                    updates[turn][at, :] = update
                else:
                    final_ref[at, :] = (start_ref[at, :] + updates[0][at, :]) + (
                        (updates[1][at, :] + here[half]) + update
                    )
            return 0

        first = 1 + turn
        lax.fori_loop(first, cells_x + 2 * DEPTH - first, sweep, 0, unroll=2)

    def local(plane, half, shift=0):
        return pl.ds((plane * 2 + half) * rows + DEPTH + shift, cells_y)

    def advance(index, _):
        plane = index + DEPTH
        pots = [final_ref[local(plane, half), :] for half in range(2)]
        ions = [ion_ref[local(plane, half), :] for half in range(2)]
        pot_below, pot_above = beyond(pots)
        ion_below, ion_above = beyond(ions)
        for half in range(2):
            pot, ion = (pots[half], ions[half])
            steps = [
                (final_ref[at, :], ion_ref[at, :])
                for at in (
                    local(plane - 1, half),
                    local(plane + 1, half),
                    local(plane, half, -1),
                    local(plane, half, 1),
                )
            ]
            steps += [(pot_below[half], ion_below[half]), (pot_above[half], ion_above[half])]
            total = 0.0
            for low, high in zip(steps[0::2], steps[1::2], strict=True):
                total = total + (
                    face_flux(pot, high[0], ion, high[1]) - face_flux(low[0], pot, low[1], ion)
                )
            lanes = slice(128 * half, 128 * half + 128)
            next_ref[index, :, lanes] = ion - time_step * total
            potential_ref[index, :, lanes] = pot
        return 0

    lax.fori_loop(0, cells_x, advance, 0)

    row_lane = lax.broadcasted_iota(jnp.int32, (1, 128), 1)

    def pick(cluster, _):
        cell = cell_ref[cluster]
        index_x = lax.shift_right_logical(cell, CELL_BITS) // cells_y + DEPTH
        index_y = lax.shift_right_logical(cell, CELL_BITS) % cells_y + DEPTH
        index_z = lax.bitwise_and(cell, 255)
        half = lax.shift_right_logical(index_z, 7)
        here = row_lane == lax.bitwise_and(index_z, 127)

        def line(plane, row, part):
            return final_ref[pl.ds((plane * 2 + part) * rows + row, 1), :]

        along_x = line(index_x - 1, index_y, half) - line(index_x + 1, index_y, half)
        along_y = line(index_x, index_y - 1, half) - line(index_x, index_y + 1, half)
        along_z = jnp.zeros((1, 128), jnp.float32)
        for part in range(2):
            value = line(index_x, index_y, part)
            place = row_lane + 128 * part
            along_z = along_z + jnp.where(place == index_z - 1, value, 0.0)
            along_z = along_z - jnp.where(place == index_z + 1, value, 0.0)
        at = pl.ds(cluster, 1)
        pick_refs[0][at, :] = jnp.where(here, along_x, 0.0)
        pick_refs[1][at, :] = jnp.where(here, along_y, 0.0)
        pick_refs[2][at, :] = along_z
        return 0

    lax.fori_loop(0, clusters, pick, 0, unroll=8)

    def spread_out(step, _):
        start = pl.multiple_of(step * 8, 8)
        charge = masked_ref[pl.ds(start, 8), :] * (0.5 * field_scale)
        for part, pick_ref in enumerate(pick_refs):
            total = jnp.sum(pick_ref[pl.ds(start, 8), :], axis=1, keepdims=True)
            force_ref[pl.ds(4 * start + part, 8, stride=4), :] = charge * total
        force_ref[pl.ds(4 * start + 3, 8, stride=4), :] = jnp.zeros((8, 128), jnp.float32)
        return 0

    lax.fori_loop(0, clusters // 8, spread_out, 0, unroll=4)


def grid_step(cell, masked, fields, rims, edges, base):
    smem = pl.BlockSpec(memory_space=pltpu.SMEM)
    vmem = pl.BlockSpec(memory_space=pltpu.VMEM)
    clusters = masked.shape[0]
    cells_x, cells_y, _ = fields[0].shape
    block = ((cells_x + 2 * DEPTH) * 2 * line_rows(cells_y), 128)
    return pl.pallas_call(
        functools.partial(grid_kernel, base),
        out_shape=(
            jax.ShapeDtypeStruct(fields[0].shape, jnp.float32),
            jax.ShapeDtypeStruct(fields[0].shape, jnp.float32),
            jax.ShapeDtypeStruct((clusters * 4, 128), jnp.float32),
        ),
        in_specs=[smem] + [pl.BlockSpec(memory_space=pl.ANY)] * 9,
        out_specs=(vmem,) * 3,
        scratch_shapes=[pltpu.VMEM(block, jnp.float32)] * 10
        + [pltpu.VMEM((clusters, 128), jnp.float32)] * 3
        + [pltpu.VMEM(((cells_x + 2 * DEPTH) * 64, 128), jnp.float32)]
        + [pltpu.VMEM(field.shape, jnp.float32) for field in fields]
        + [pltpu.VMEM(masked.shape, jnp.float32), pltpu.SemaphoreType.DMA((9,))]
        + [pltpu.VMEM(edge.shape, jnp.float32) for edge in edges],
        compiler_params=pltpu.CompilerParams(vmem_limit_bytes=ROOMY_LIMIT),
        cost_estimate=pl.CostEstimate(
            flops=block[0] * block[1] * 100, bytes_accessed=8 << 20, transcendentals=0
        ),
        name="grid_step",
    )(cell, masked, *fields, *rims, *edges)


def gather_forces_kernel(send_index_ref, *refs):
    fetched = len(SWAPS) + 3
    out_ref, extra_ref = refs[fetched : fetched + 2]
    sum_ref, field_ref, *back_refs = refs[fetched + 2 : -1]
    copies = start_copies(
        [
            (source.at[0 : target.shape[0]], target)
            for source, target in zip(refs[:fetched], refs[fetched + 2 : -1], strict=True)
        ],
        refs[-1],
    )
    extra_ref[...] = jnp.zeros_like(extra_ref)
    for copy in copies:
        copy.wait()
    clusters = sum_ref.shape[0]
    slots = send_index_ref.shape[1]
    ups = upward()

    def visit(slot, _):
        for position, back_ref in enumerate(back_refs):
            cluster = send_index_ref[sent_row(position, ups) if position else 0, slot]
            target_ref = extra_ref if position % 2 else sum_ref
            target_ref[cluster] += back_ref[slot]
        return 0

    lax.fori_loop(0, slots, visit, 0, unroll=2)

    def write(step, _):
        for turn in range(8):
            cluster = step * 8 + turn
            total = (sum_ref[cluster] + extra_ref[cluster]) + field_ref[cluster]
            out_ref[:, pl.ds(pl.multiple_of(cluster * 128, 128), 128)] = total[0:3]
        return 0

    lax.fori_loop(0, clusters // 8, write, 0)


def gather_forces(send_index, own, field, backs):
    smem = pl.BlockSpec(memory_space=pltpu.SMEM)
    vmem = pl.BlockSpec(memory_space=pltpu.VMEM)
    clusters = own.shape[0]
    return pl.pallas_call(
        gather_forces_kernel,
        out_shape=jax.ShapeDtypeStruct((3, clusters * 128), jnp.float32),
        in_specs=[smem] + [pl.BlockSpec(memory_space=pl.ANY)] * (2 + len(backs)),
        out_specs=vmem,
        scratch_shapes=[
            *[pltpu.VMEM(part.shape, jnp.float32) for part in (own, own, field)],
            *[pltpu.VMEM((send_index.shape[1], 4, 128), jnp.float32)] * len(backs),
            pltpu.SemaphoreType.DMA((2 + len(backs),)),
        ],
        compiler_params=pltpu.CompilerParams(vmem_limit_bytes=ROOMY_LIMIT),
        name="gather_forces",
    )(send_index, own, field, *backs)


def shards(
    positions,
    charges,
    cluster_fill,
    cluster_cell,
    send_index,
    send_count,
    pair_local,
    pair_dir,
    pair_slot,
    ion_density,
    potential_prev,
    screening,
):
    clusters = cluster_fill.shape[0]
    psize = charges.shape[0] // clusters
    slots = send_index.shape[1]
    base = slots * 4
    other_rows, own, masked, local, *messages = prepare(
        cluster_fill,
        send_index,
        send_count,
        pair_dir.reshape(-1, 128),
        pair_slot.reshape(-1, 128),
        positions,
        charges.reshape(clusters, psize),
    )
    inverse, source, *edges = sources_of(
        cluster_cell, masked, ion_density, potential_prev, screening
    )
    arrived = [local] + [
        swapped(message, *swap)
        for message, swap in zip(messages, SWAPS, strict=True)
    ]
    fields = (potential_prev, inverse, source, ion_density)
    arrived, edges = lax.optimization_barrier((arrived, edges))
    edges = [swapped(edge, "grp", 1, phase) for phase, edge in enumerate(edges)]
    own_force, *reactions = pair_forces(
        pair_local,
        other_rows.reshape(-1),
        own.reshape(clusters * 4, psize),
        arrived,
        slots,
    )
    local_back, *reactions = reactions
    rims = pack_rows(fields, edges, reactions[:2])
    backs = [
        swapped(reaction, *swap)
        for reaction, swap in zip((*rims, *reactions[2:]), SWAPS, strict=True)
    ]
    potential, ion_next, field_force = grid_step(
        cluster_cell, masked, fields, backs[:2], edges, base
    )
    forces = gather_forces(
        send_index,
        own_force.reshape(clusters, 4, psize),
        field_force.reshape(clusters, 4, psize),
        [back.reshape(-1, 4, psize) for back in (local_back, *backs)],
    )
    return (forces, potential, ion_next)


def solution(mesh):
    in_specs = (
        P(None, ("grp", "brick")),
        P(("grp", "brick")),
        P(("grp", "brick")),
        P(("grp", "brick")),
        P(("grp", "brick"), None),
        P(("grp", "brick"), None),
        P(("grp", "brick")),
        P(("grp", "brick")),
        P(("grp", "brick")),
        P("grp", "brick", None),
        P("grp", "brick", None),
        P("grp", "brick", None),
    )
    out_specs = (P(None, ("grp", "brick")), P("grp", "brick", None), P("grp", "brick", None))
    return jax.shard_map(shards, mesh=mesh, in_specs=in_specs, out_specs=out_specs, check_vma=False)
```

```python
import functools

import jax
import jax.numpy as jnp
import numpy as np
from jax import lax
from jax.experimental import pallas as pl
from jax.experimental.pallas import tpu as pltpu
from jax.sharding import PartitionSpec as P

SWEEPS = 4
UNROLL = 8
CHUNKS = 4
AHEAD = 2
BEHIND = 4
HALO_WIDTHS = (SWEEPS + 1, SWEEPS, SWEEPS, 1)
DEPTH = SWEEPS + 1
CELL_BITS = 8
SWAPS = tuple(
    (*way, phase) for way in (("brick", 1), ("brick", 2), ("grp", 1)) for phase in (0, 1)
)


coulomb_scale = 0.02
softening = 0.1
field_scale = 0.5
deposit_scale = 0.2
lowest_eig = 0.01
highest_eig = 1.99
mobility = 0.3
diffusion = 0.2
time_step = 0.2


VMEM_LIMIT = 60 * 1024 * 1024
ROOMY_LIMIT = 48 * 1024 * 1024


def start_copies(pairs, sems):
    copies = [
        pltpu.make_async_copy(source, target, sems.at[index])
        for index, (source, target) in enumerate(pairs)
    ]
    for copy in copies:
        copy.start()
    return copies


def upward():
    brick, grp = (lax.axis_index("brick"), lax.axis_index("grp"))
    bits = (brick, lax.shift_right_logical(brick, 1), grp)
    return [1 - lax.bitwise_and(bit, 1) for bit in bits]


def sent_row(position, ups):
    way, phase = ((position - 1) // 2, (position - 1) % 2)
    return 1 + 2 * way + (ups[way] if phase else 1 - ups[way])


def swapped(shard, axis, distance, phase):
    devices = lax.axis_size(axis)
    pairs = []
    for index in range(devices):
        step = distance if (index // distance + phase) % 2 == 0 else -distance
        if 0 <= index + step < devices:
            pairs.append((index, index + step))
    return lax.ppermute(shard, axis, pairs)


def split3(value):
    first = value.astype(jnp.bfloat16).astype(jnp.float32)
    rest = value - first
    second = rest.astype(jnp.bfloat16).astype(jnp.float32)
    third = (rest - second).astype(jnp.bfloat16).astype(jnp.float32)
    return (first, second, third)


def moment_pieces(comps, charge):
    rows = [None] * 12
    for part, charged in enumerate((*comps, None)):
        for level, piece in enumerate(split3(charge if charged is None else charge * charged)):
            rows[4 * level + part] = piece
    return rows


def selections():
    near_kinds, far_kinds = ([], [])
    for part in range(3):
        near_kinds += [3 * part + level for level in (0, 0, 0, 1, 1, 2)]
        far_kinds += [3 * part + level for level in (0, 1, 2, 0, 1, 0)]
    near_kinds += [9, 10, 11, 12, 12, 12]
    far_kinds += [12, 12, 12, 9, 10, 11]
    near = np.zeros((128, 1024), np.float32)
    far = np.zeros((256, 128), np.float32)
    moment = np.zeros((128, 128), np.float32)
    for cluster in range(8):
        for index, kind in enumerate(near_kinds):
            near[kind * 8 + cluster, cluster * 128 + index] = 1.0
        for index, kind in enumerate(far_kinds):
            far[cluster * 32 + index, kind * 8 + cluster] = 1.0
        for kind in range(12):
            moment[cluster * 16 + kind, kind * 8 + cluster] = 1.0
    return tuple(jnp.asarray(part, jnp.bfloat16) for part in (near, far, moment))


def pair_kernel(own_rows_ref, other_rows_ref, *refs):
    sources = len(SWAPS) + 1
    fetched = sources + 4
    hbm_refs = refs[:fetched]
    own_out_ref = refs[fetched]
    other_out_refs = refs[fetched + 1 : fetched + 1 + sources]
    refs = refs[fetched + 1 + sources :]
    near_sel_ref, far_sel_ref, moment_sel_ref, own_ref = refs[:4]
    other_refs = refs[4:fetched]
    sems = refs[fetched]
    copies = start_copies(
        [
            (source.at[0 : target.shape[0]], target)
            for source, target in zip(hbm_refs, refs[:fetched], strict=True)
        ],
        sems,
    )
    (
        near_ref,
        far_ref,
        own_moment_ref,
        other_moment_ref,
        own_sum_ref,
        other_sum_ref,
        dist_ref,
        *weight_refs,
    ) = refs[fetched + 1 :]
    clusters = own_ref.shape[0] // 4
    slots = other_out_refs[0].shape[0] // 4
    others = slots * sources
    groups = own_rows_ref.shape[0] // UNROLL
    ones = jnp.ones((8, 128), jnp.float32)
    zeros = jnp.zeros((8, 128), jnp.float32)

    def components(data_ref, start):
        return [data_ref[pl.ds(4 * start + part, 8, stride=4), :] for part in range(4)]

    def place_pieces(comps, factor, offset):
        pieces = []
        square = zeros
        for comp in comps:
            square = square + comp * comp
            pieces += split3(factor * comp)
        pieces += [*split3(square + offset), ones]
        return jnp.concatenate(pieces + [zeros] * (16 - len(pieces)), axis=0)

    def selected(left, right):
        return jnp.dot(
            left.astype(jnp.bfloat16), right, preferred_element_type=jnp.float32
        ).astype(jnp.bfloat16)

    def near_rows(step, _):
        start = pl.multiple_of(step * 8, 8)
        *comps, charge = components(own_ref, start)
        moments = jnp.concatenate(moment_pieces(comps, charge) + [zeros] * 4, axis=0)
        own_moment_ref[pl.ds(pl.multiple_of(start * 16, 128), 128), :] = selected(
            moment_sel_ref[...], moments.astype(jnp.bfloat16)
        )
        tiles = selected(place_pieces(comps, 1.0, 0.0).T, near_sel_ref[...])
        for index in range(8):
            at = pl.ds(pl.multiple_of((start + index) * 128, 128), 128)
            near_ref[at, :] = tiles[:, 128 * index : 128 * index + 128]
        return 0

    def far_rows(source, step, _):
        local = pl.multiple_of(step * 8, 8)
        start = source * slots + local
        *comps, charge = components(other_refs[source], local)
        far_ref[pl.ds(pl.multiple_of(start * 32, 256), 256), :] = selected(
            far_sel_ref[...], place_pieces(comps, -2.0, softening).astype(jnp.bfloat16)
        )
        moments = jnp.concatenate(moment_pieces(comps, charge) + [zeros] * 4, axis=0)
        other_moment_ref[pl.ds(pl.multiple_of(start * 16, 128), 128), :] = selected(
            moment_sel_ref[...], moments.astype(jnp.bfloat16)
        )
        return 0

    own_sum_ref[...] = jnp.zeros_like(own_sum_ref)
    other_sum_ref[...] = jnp.zeros_like(other_sum_ref)
    weight_refs[0][...] = jnp.zeros_like(weight_refs[0])
    for copy in copies[:4]:
        copy.wait()
    lax.fori_loop(0, clusters // 8, near_rows, 0, unroll=4)
    for copy in copies[4:]:
        copy.wait()
    for source in range(sources):
        lax.fori_loop(0, slots // 8, functools.partial(far_rows, source), 0, unroll=4)
    def distances(pair):
        own = own_rows_ref[pair]
        other = other_rows_ref[pair]
        return jnp.dot(
            near_ref[pl.ds(pl.multiple_of(own * 128, 128), 128), 0:32],
            far_ref[pl.ds(pl.multiple_of(other * 32, 32), 32), :],
            preferred_element_type=jnp.float32,
        )

    def weights(dist, index, chunk, weight_ref):
        rows = 128 // CHUNKS
        first = rows * chunk
        root = lax.rsqrt(dist[first : first + rows])
        weight = root * root * root
        high = weight.astype(jnp.bfloat16)
        low = (weight - high.astype(jnp.float32)).astype(jnp.bfloat16)
        at = slice(128 * index + first, 128 * index + first + rows)
        weight_ref[at, :128] = high
        weight_ref[at, 128:] = low

    def row_block(index):
        return pl.ds(pl.multiple_of(index * 16, 16), 16)

    def own_product(other, weight_ref, index):
        both = weight_ref[128 * index : 128 * index + 128]
        return lax.dot_general(
            other_moment_ref[row_block(other), :],
            jnp.concatenate([both[:, :128], both[:, 128:]], axis=0),
            (((1,), (1,)), ((), ())),
            preferred_element_type=jnp.float32,
        )

    def other_product(own, weight_ref, index):
        return jnp.dot(
            own_moment_ref[row_block(own), :],
            weight_ref[128 * index : 128 * index + 128],
            preferred_element_type=jnp.float32,
        )

    def add_rows(own, other, to_own, to_other):
        own_sum_ref[row_block(own), :] += to_own[:, :128] + to_own[:, 128:]
        other_sum_ref[row_block(other), :] += to_other[:, :128] + to_other[:, 128:]

    def half_step(step, side, dists):
        last = jnp.maximum(step - 1, 0) * UNROLL
        waiting = []
        for index in range(UNROLL):
            own = own_rows_ref[last + index]
            other = other_rows_ref[last + index]
            coming = step * UNROLL + index + AHEAD
            later = distances(jnp.minimum(coming, groups * UNROLL - 1))
            weights(dists[0], index, 0, weight_refs[1 - side])
            to_own = own_product(other, weight_refs[side], index)
            weights(dists[0], index, 1, weight_refs[1 - side])
            weights(dists[0], index, 2, weight_refs[1 - side])
            to_other = other_product(own, weight_refs[side], index)
            weights(dists[0], index, 3, weight_refs[1 - side])
            dists = [*dists[1:], later]
            waiting.append((own, other, to_own, to_other))
            if len(waiting) > BEHIND:
                add_rows(*waiting.pop(0))
        for entry in waiting:
            add_rows(*entry)
        return dists

    def visit(step, _):
        dists = [dist_ref[index] for index in range(AHEAD)]
        for side in range(2):
            dists = half_step(step * 2 + side, side, dists)
        for index in range(AHEAD):
            dist_ref[index] = dists[index]
        return 0

    for index in range(AHEAD):
        dist_ref[index] = distances(index)
    lax.fori_loop(0, groups // 2, visit, 0)
    half_step(groups, 0, [dist_ref[index] for index in range(AHEAD)])

    def finish(data_ref, out_ref, sum_ref, base, step, _):
        start = pl.multiple_of(step * 8, 8)
        *comps, charge = components(data_ref, start)

        def total(part):
            terms = [
                sum_ref[pl.ds(base + start * 16 + 4 * level + part, 8, stride=16), :]
                for level in range(3)
            ]
            return terms[0] + (terms[1] + terms[2])

        weight = total(3)
        scale = coulomb_scale * charge
        for part, comp in enumerate(comps):
            out_ref[pl.ds(4 * start + part, 8, stride=4), :] = scale * (comp * weight - total(part))
        out_ref[pl.ds(4 * start + 3, 8, stride=4), :] = zeros
        return 0

    lax.fori_loop(
        0, clusters // 8, functools.partial(finish, own_ref, own_out_ref, own_sum_ref, 0), 0, unroll=4
    )
    for source in range(sources):
        body = functools.partial(
            finish,
            other_refs[source],
            other_out_refs[source],
            other_sum_ref,
            source * slots * 16,
        )
        lax.fori_loop(0, slots // 8, body, 0, unroll=4)


def pair_forces(own_rows, other_rows, own, arrived, slots):
    clusters = own.shape[0] // 4
    others = slots * len(arrived)
    pairs = own_rows.shape[0]
    smem = pl.BlockSpec(memory_space=pltpu.SMEM)
    vmem = pl.BlockSpec(memory_space=pltpu.VMEM)
    hbm = pl.BlockSpec(memory_space=pl.ANY)
    operands = (*selections(), own)
    return pl.pallas_call(
        pair_kernel,
        out_shape=(
            jax.ShapeDtypeStruct(own.shape, jnp.float32),
            *[jax.ShapeDtypeStruct((slots * 4, 128), jnp.float32)] * len(arrived),
        ),
        in_specs=[smem, smem] + [hbm] * (4 + len(arrived)),
        out_specs=(vmem,) * (len(arrived) + 1),
        scratch_shapes=[
            *[pltpu.VMEM(operand.shape, operand.dtype) for operand in operands],
            *[pltpu.VMEM((slots * 4, 128), jnp.float32)] * len(arrived),
            pltpu.SemaphoreType.DMA((len(operands) + len(arrived),)),
            pltpu.VMEM((clusters * 128, 128), jnp.bfloat16),
            pltpu.VMEM((others * 32, 128), jnp.bfloat16),
            pltpu.VMEM((clusters * 16, 128), jnp.bfloat16),
            pltpu.VMEM((others * 16, 128), jnp.bfloat16),
            pltpu.VMEM((clusters * 16, 128), jnp.float32),
            pltpu.VMEM((others * 16, 128), jnp.float32),
            pltpu.VMEM((AHEAD, 128, 128), jnp.float32),
            *[pltpu.VMEM((128 * UNROLL, 256), jnp.bfloat16)] * 2,
        ],
        compiler_params=pltpu.CompilerParams(vmem_limit_bytes=ROOMY_LIMIT),
        cost_estimate=pl.CostEstimate(
            flops=pairs * 128 * 128 * 20, bytes_accessed=4 * 1024 * 1024, transcendentals=0
        ),
        name="pair_forces",
    )(own_rows, other_rows, *operands, *arrived)


def prepare_kernel(
    fill_ref,
    send_index_ref,
    send_count_ref,
    pair_dir_ref,
    pair_slot_ref,
    position_hbm,
    charge_hbm,
    row_ref,
    own_ref,
    masked_ref,
    *refs,
):
    out_refs, (position_ref, charge_ref, sems) = (refs[:-3], refs[-3:])
    copies = start_copies(((position_hbm, position_ref), (charge_hbm, charge_ref)), sems)
    clusters = charge_ref.shape[0]
    slots = send_index_ref.shape[1]
    lane = lax.broadcasted_iota(jnp.int32, (1, 128), 1)
    row = lax.broadcasted_iota(jnp.int32, (4, 128), 0)
    ups = upward()
    direction = pair_dir_ref[...]
    way = lax.shift_right_arithmetic(direction - 1, 1)
    flip = jnp.where(way == 0, ups[0], jnp.where(way == 1, ups[1], ups[2]))
    position = 1 + 2 * way + lax.bitwise_xor(lax.bitwise_and(direction - 1, 1), flip)
    row_ref[...] = jnp.where(direction == 0, 0, position) * slots + pair_slot_ref[...]
    for copy in copies:
        copy.wait()

    def collect(step, _):
        for turn in range(8):
            cluster = step * 8 + turn
            masked = jnp.where(lane < fill_ref[cluster], charge_ref[pl.ds(cluster, 1), :], 0.0)
            masked_ref[pl.ds(cluster, 1), :] = masked
            place = position_ref[:, pl.ds(pl.multiple_of(cluster * 128, 128), 128)]
            own_ref[cluster, 0:3, :] = place
            own_ref[cluster, 3:4, :] = masked
        return 0

    lax.fori_loop(0, clusters // 8, collect, 0, unroll=2)

    def fill_messages(step, _):
        for position, out_ref in enumerate(out_refs):
            direction = sent_row(position, ups) if position else 0
            parts = []
            for turn in range(2):
                slot = step * 2 + turn
                live = jnp.where(slot < send_count_ref[0, direction], 1.0, 0.0)
                value = own_ref[send_index_ref[direction, slot]]
                parts.append(jnp.where(row == 3, value * live, value))
            out_ref[pl.ds(pl.multiple_of(step * 8, 8), 8), :] = jnp.concatenate(parts, axis=0)
        return 0

    lax.fori_loop(0, slots // 2, fill_messages, 0)


def prepare(fill, send_index, send_count, pair_dir, pair_slot, positions, charges):
    clusters = charges.shape[0]
    directions, slots = send_index.shape
    smem = pl.BlockSpec(memory_space=pltpu.SMEM)
    vmem = pl.BlockSpec(memory_space=pltpu.VMEM)
    return pl.pallas_call(
        prepare_kernel,
        out_shape=(
            jax.ShapeDtypeStruct(pair_dir.shape, jnp.int32),
            jax.ShapeDtypeStruct((clusters, 4, 128), jnp.float32),
            jax.ShapeDtypeStruct((clusters, 128), jnp.float32),
            *[jax.ShapeDtypeStruct((slots * 4, 128), jnp.float32)] * directions,
        ),
        in_specs=[smem] * 3 + [vmem] * 2 + [pl.BlockSpec(memory_space=pltpu.HBM)] * 2,
        out_specs=(vmem,) * (3 + directions),
        scratch_shapes=[
            *[pltpu.VMEM(operand.shape, jnp.float32) for operand in (positions, charges)],
            pltpu.SemaphoreType.DMA((2,)),
        ],
        compiler_params=pltpu.CompilerParams(vmem_limit_bytes=VMEM_LIMIT),
        name="prepare",
    )(fill, send_index, send_count, pair_dir, pair_slot, positions, charges)


def sources_kernel(
    cell_ref,
    cell_row_ref,
    masked_hbm,
    ion_hbm,
    start_hbm,
    screen_hbm,
    inverse_ref,
    source_ref,
    *refs,
):
    edge_refs, refs = (refs[:2], refs[2:])
    sum_ref, deposit_ref, masked_ref, ion_ref, start_ref, screen_ref, sems = refs
    copies = start_copies(
        (
            (masked_hbm, masked_ref),
            (ion_hbm, ion_ref),
            (start_hbm, start_ref),
            (screen_hbm, screen_ref),
        ),
        sems,
    )
    copies[0].wait()
    clusters = masked_ref.shape[0]
    cells_x, cells_y, _ = ion_ref.shape
    lane = lax.broadcasted_iota(jnp.int32, (1, 128), 1)
    ups = upward()

    def add_up(step, _):
        at = pl.ds(pl.multiple_of(step * 8, 8), 8)
        total = jnp.sum(masked_ref[at, :], axis=1, keepdims=True)
        sum_ref[at, :] = jnp.broadcast_to(deposit_scale * total, (8, 128))
        return 0

    lax.fori_loop(0, clusters // 8, add_up, 0, unroll=8)

    def place(step, _):
        for turn in range(8):
            cluster = step * 8 + turn
            index_z = lax.bitwise_and(cell_ref[cluster], 127)
            at = pl.ds(cluster, 1)
            sum_ref[at, :] = jnp.where(lane == index_z, sum_ref[at, :], 0.0)
        return 0

    lax.fori_loop(0, clusters // 8, place, 0)
    cell = cell_row_ref[...]
    line = lax.shift_right_logical(cell, CELL_BITS)
    line = (line // cells_y * 2 + lax.shift_right_logical(lax.bitwise_and(cell, 255), 7)) * cells_y
    line = line + lax.shift_right_logical(cell, CELL_BITS) % cells_y
    sums = jnp.concatenate([part.astype(jnp.bfloat16) for part in split3(sum_ref[...])], axis=1)
    block = 128
    for first in range(0, deposit_ref.shape[0], block):
        rows = lax.broadcasted_iota(jnp.int32, (block, clusters), 0) + first
        hot = jnp.where(rows == line, 1.0, 0.0).astype(jnp.bfloat16)
        added = jnp.dot(hot, sums, preferred_element_type=jnp.float32)
        deposit_ref[first : first + block, :] = added[:, :128] + (
            added[:, 128:256] + added[:, 256:]
        )
    for copy in copies[1:]:
        copy.wait()
    inverse_ref[...] = 1.0 / (6.0 + screen_ref[...])
    for index in range(cells_x):
        for half in range(2):
            lanes = slice(128 * half, 128 * half + 128)
            first = (index * 2 + half) * cells_y
            source_ref[index, :, lanes] = (
                ion_ref[index, :, lanes] + deposit_ref[first : first + cells_y, :]
            ) * inverse_ref[index, :, lanes]
    edge = 0
    for field_ref, width in zip(
        (start_ref, inverse_ref, source_ref, ion_ref), HALO_WIDTHS, strict=True
    ):
        for step in range(width):
            for phase, edge_ref in enumerate(edge_refs):
                last = ups[2] if phase == 0 else 1 - ups[2]
                plane = field_ref[last * (cells_x - width) + step]
                for half in range(2):
                    edge_ref[2 * edge + half] = plane[:, 128 * half : 128 * half + 128]
            edge += 1


def sources_of(cell, masked, ions, start, screen):
    clusters = masked.shape[0]
    cells_y = ions.shape[1]
    smem = pl.BlockSpec(memory_space=pltpu.SMEM)
    vmem = pl.BlockSpec(memory_space=pltpu.VMEM)
    edge = jax.ShapeDtypeStruct((2 * sum(HALO_WIDTHS), cells_y, 128), jnp.float32)
    return pl.pallas_call(
        sources_kernel,
        out_shape=(*[jax.ShapeDtypeStruct(ions.shape, jnp.float32)] * 2, edge, edge),
        in_specs=[smem, vmem] + [pl.BlockSpec(memory_space=pltpu.HBM)] * 4,
        out_specs=(vmem,) * 4,
        scratch_shapes=[
            pltpu.VMEM((clusters, 128), jnp.float32),
            pltpu.VMEM((ions.size // 128, 128), jnp.float32),
            *[pltpu.VMEM(operand.shape, jnp.float32) for operand in (masked, ions, start, screen)],
            pltpu.SemaphoreType.DMA((4,)),
        ],
        compiler_params=pltpu.CompilerParams(vmem_limit_bytes=VMEM_LIMIT),
        cost_estimate=pl.CostEstimate(
            flops=20_000_000, bytes_accessed=4 << 20, transcendentals=0
        ),
        name="sources",
    )(cell, cell.reshape(1, clusters), masked, ions, start, screen)


def line_rows(cells_y):
    return (cells_y + 2 * DEPTH + 7) // 8 * 8


def pack_rows_kernel(*refs):
    field_hbms, edge_hbms, reaction_hbms, out_refs = (refs[:4], refs[4:6], refs[6:8], refs[8:10])
    near_refs, edge_refs, sems = (refs[10:14], refs[14:16], refs[16])
    cells_x, cells_y, _ = field_hbms[0].shape
    base = reaction_hbms[0].shape[0]
    ups = upward()
    moves = [
        (reaction, out_ref.at[0:base])
        for reaction, out_ref in zip(reaction_hbms, out_refs, strict=True)
    ]
    for source, target in zip(field_hbms + edge_hbms, near_refs + edge_refs, strict=True):
        moves.append((source.at[:, 0:8], target.at[0]))
        moves.append((source.at[:, cells_y - 8 : cells_y], target.at[1]))
    for copy in start_copies(moves, sems):
        copy.wait()

    def fill(out_ref, after):
        for field, width in enumerate(HALO_WIDTHS):
            offset = sum(HALO_WIDTHS[:field])
            rows = slice(8 - width, 8) if after else slice(0, width)
            for index in range(cells_x):
                value = near_refs[field][after, index, rows, :]
                for half in range(2):
                    at = base + ((DEPTH + index) * 2 + half) * 16 + offset
                    out_ref[at : at + width, :] = value[:, 128 * half : 128 * half + 128]
            if width == 1:
                continue
            for phase, edge_ref in enumerate(edge_refs):
                higher = ups[2] if phase == 0 else 1 - ups[2]
                for step in range(width):
                    plane = (DEPTH - width) + higher * (cells_x + width) + step
                    for half in range(2):
                        at = pl.ds(base + (plane * 2 + half) * 16 + offset, width)
                        out_ref[at, :] = edge_ref[after, 2 * (offset + step) + half, rows, :]

    for up in range(2):

        @pl.when(ups[0] == up)
        def _(up=up):
            fill(out_refs[0], up)
            fill(out_refs[1], 1 - up)


def pack_rows(fields, edges, reactions):
    vmem = pl.BlockSpec(memory_space=pltpu.VMEM)
    cells_x, _, cells_z = fields[0].shape
    rows = reactions[0].shape[0] + (cells_x + 2 * DEPTH) * 32
    shape = jax.ShapeDtypeStruct((rows, 128), jnp.float32)
    return pl.pallas_call(
        pack_rows_kernel,
        out_shape=(shape, shape),
        in_specs=[pl.BlockSpec(memory_space=pl.ANY)] * 8,
        out_specs=(vmem, vmem),
        scratch_shapes=[
            *[pltpu.VMEM((2, cells_x, 8, cells_z), jnp.float32)] * 4,
            *[pltpu.VMEM((2, edges[0].shape[0], 8, 128), jnp.float32)] * 2,
            pltpu.SemaphoreType.DMA((14,)),
        ],
        compiler_params=pltpu.CompilerParams(vmem_limit_bytes=ROOMY_LIMIT),
        name="pack_rows",
    )(*fields, *edges, *reactions)


def fill_line(target_ref, plane, half, field, value, rim_ref):
    cells_y = value.shape[0]
    width = HALO_WIDTHS[field]
    at = (plane * 2 + half) * line_rows(cells_y) + DEPTH
    target_ref[pl.ds(at, cells_y), :] = value
    first = (plane * 2 + half) * 16 + sum(HALO_WIDTHS[:field])
    target_ref[pl.ds(at - width, width), :] = rim_ref[pl.ds(first, width), :]
    first = first + rim_ref.shape[0] // 2
    target_ref[pl.ds(at + cells_y, width), :] = rim_ref[pl.ds(first, width), :]


def face_flux(pot_low, pot_high, ion_low, ion_high):
    speed = -mobility * (pot_high - pot_low)
    return (
        jnp.maximum(speed, 0.0) * ion_low
        + jnp.minimum(speed, 0.0) * ion_high
        - diffusion * (ion_high - ion_low)
    )


def grid_kernel(base, *refs):
    cell_ref, masked_hbm = refs[:2]
    hbm_refs, edge_hbms = (refs[2:6], refs[8:10])
    potential_ref, next_ref, force_ref = refs[10:13]
    start_ref, inverse_ref, source_ref, ion_ref = refs[13:17]
    updates, resids, final_ref, pick_refs = (refs[17:20], refs[20:22], refs[22], refs[23:26])
    rim_ref, field_refs, masked_ref, sems = (refs[26], refs[27:31], refs[31], refs[32])
    edge_refs = refs[33:35]
    cells_x, cells_y, _ = field_refs[0].shape
    rows = line_rows(cells_y)
    inner = cells_y + 2 * DEPTH - 2
    clusters = masked_ref.shape[0]
    ups = upward()
    size = (cells_x + 2 * DEPTH) * 32
    moves = [
        (rim.at[base : base + size], rim_ref.at[pl.ds(pl.multiple_of(side * size, size), size)])
        for rim, side in zip(refs[6:8], (ups[0], 1 - ups[0]), strict=True)
    ]
    moves += zip(hbm_refs, field_refs, strict=True)
    moves += zip(edge_hbms, edge_refs, strict=True)
    moves.append((masked_hbm, masked_ref))
    copies = start_copies(moves, sems)
    extended = (start_ref, inverse_ref, source_ref, ion_ref)
    for copy in copies[:2]:
        copy.wait()
    for field, target_ref in enumerate(extended):
        copies[2 + field].wait()

        def fill(index, _, field=field, target_ref=target_ref):
            plane = field_refs[field][index]
            for half in range(2):
                value = plane[:, 128 * half : 128 * half + 128]
                fill_line(target_ref, DEPTH + index, half, field, value, rim_ref)
            return 0

        lax.fori_loop(0, cells_x, fill, 0, unroll=4)
    for copy in copies[6:]:
        copy.wait()
    for field, target_ref in enumerate(extended):
        width = HALO_WIDTHS[field]
        for phase, edge_ref in enumerate(edge_refs):
            higher = ups[2] if phase == 0 else 1 - ups[2]

            def fill_edge(step, _, field=field, target_ref=target_ref, edge_ref=edge_ref):
                width = HALO_WIDTHS[field]
                plane = (DEPTH - width) + higher * (cells_x + width) + step
                for half in range(2):
                    value = edge_ref[2 * (sum(HALO_WIDTHS[:field]) + step) + half]
                    fill_line(target_ref, plane, half, field, value, rim_ref)
                return 0

            lax.fori_loop(0, width, fill_edge, 0, unroll=True)

    def beyond(values):
        lane = lax.broadcasted_iota(jnp.int32, values[0].shape, 1)
        right = [pltpu.roll(value, 127, 1) for value in values]
        left = [pltpu.roll(value, 1, 1) for value in values]
        above = [jnp.where(lane == 127, right[1], right[0]), jnp.where(lane == 127, 0.0, right[1])]
        below = [jnp.where(lane == 0, 0.0, left[0]), jnp.where(lane == 0, left[0], left[1])]
        return (below, above)

    def wide(plane, half, shift=0):
        return pl.ds((plane * 2 + half) * rows + 1 + shift, inner)

    def around(ref, plane):
        here = [ref[wide(plane, half), :] for half in range(2)]
        below, above = beyond(here)
        sums = [
            (ref[wide(plane - 1, half), :] + ref[wide(plane + 1, half), :])
            + (ref[wide(plane, half, -1), :] + ref[wide(plane, half, 1), :])
            + (below[half] + above[half])
            for half in range(2)
        ]
        return (here, sums)

    middle = 0.5 * (highest_eig + lowest_eig)
    spread = 0.5 * (highest_eig - lowest_eig)
    assert middle == 1.0 and SWEEPS == 4

    def sweep_first(plane, _):
        here, sums = around(start_ref, plane)
        for half in range(2):
            at = wide(plane, half)
            updates[0][at, :] = source_ref[at, :] - here[half] + inverse_ref[at, :] * sums[half]
        return 0

    lax.fori_loop(1, cells_x + 2 * DEPTH - 1, sweep_first, 0, unroll=2)

    ratio_ms = middle / spread
    weight_now = 1.0 / ratio_ms
    for turn in range(1, SWEEPS):
        weight_next = 1.0 / (2.0 * ratio_ms - weight_now)
        keep, gain = (weight_next * weight_now, 2.0 * weight_next / spread)
        weight_now = weight_next

        def sweep(plane, _, turn=turn, keep=keep, gain=gain):
            here, sums = around(updates[turn - 1], plane)
            for half in range(2):
                at = wide(plane, half)
                resid = inverse_ref[at, :] * sums[half]
                if turn > 1:
                    resid = resid + (resids[turn - 2][at, :] - here[half])
                update = keep * here[half] + gain * resid
                if turn + 1 < SWEEPS:
                    resids[turn - 1][at, :] = resid
                    updates[turn][at, :] = update
                else:
                    final_ref[at, :] = (start_ref[at, :] + updates[0][at, :]) + (
                        (updates[1][at, :] + here[half]) + update
                    )
            return 0

        first = 1 + turn
        lax.fori_loop(first, cells_x + 2 * DEPTH - first, sweep, 0, unroll=2)

    def local(plane, half, shift=0):
        return pl.ds((plane * 2 + half) * rows + DEPTH + shift, cells_y)

    def advance(index, _):
        plane = index + DEPTH
        pots = [final_ref[local(plane, half), :] for half in range(2)]
        ions = [ion_ref[local(plane, half), :] for half in range(2)]
        pot_below, pot_above = beyond(pots)
        ion_below, ion_above = beyond(ions)
        for half in range(2):
            pot, ion = (pots[half], ions[half])
            steps = [
                (final_ref[at, :], ion_ref[at, :])
                for at in (
                    local(plane - 1, half),
                    local(plane + 1, half),
                    local(plane, half, -1),
                    local(plane, half, 1),
                )
            ]
            steps += [(pot_below[half], ion_below[half]), (pot_above[half], ion_above[half])]
            total = 0.0
            for low, high in zip(steps[0::2], steps[1::2], strict=True):
                total = total + (
                    face_flux(pot, high[0], ion, high[1]) - face_flux(low[0], pot, low[1], ion)
                )
            lanes = slice(128 * half, 128 * half + 128)
            next_ref[index, :, lanes] = ion - time_step * total
            potential_ref[index, :, lanes] = pot
        return 0

    lax.fori_loop(0, cells_x, advance, 0)

    row_lane = lax.broadcasted_iota(jnp.int32, (1, 128), 1)

    def pick(cluster, _):
        cell = cell_ref[cluster]
        index_x = lax.shift_right_logical(cell, CELL_BITS) // cells_y + DEPTH
        index_y = lax.shift_right_logical(cell, CELL_BITS) % cells_y + DEPTH
        index_z = lax.bitwise_and(cell, 255)
        half = lax.shift_right_logical(index_z, 7)
        here = row_lane == lax.bitwise_and(index_z, 127)

        def line(plane, row, part):
            return final_ref[pl.ds((plane * 2 + part) * rows + row, 1), :]

        along_x = line(index_x - 1, index_y, half) - line(index_x + 1, index_y, half)
        along_y = line(index_x, index_y - 1, half) - line(index_x, index_y + 1, half)
        along_z = jnp.zeros((1, 128), jnp.float32)
        for part in range(2):
            value = line(index_x, index_y, part)
            place = row_lane + 128 * part
            along_z = along_z + jnp.where(place == index_z - 1, value, 0.0)
            along_z = along_z - jnp.where(place == index_z + 1, value, 0.0)
        at = pl.ds(cluster, 1)
        pick_refs[0][at, :] = jnp.where(here, along_x, 0.0)
        pick_refs[1][at, :] = jnp.where(here, along_y, 0.0)
        pick_refs[2][at, :] = along_z
        return 0

    lax.fori_loop(0, clusters, pick, 0, unroll=8)

    def spread_out(step, _):
        start = pl.multiple_of(step * 8, 8)
        charge = masked_ref[pl.ds(start, 8), :] * (0.5 * field_scale)
        for part, pick_ref in enumerate(pick_refs):
            total = jnp.sum(pick_ref[pl.ds(start, 8), :], axis=1, keepdims=True)
            force_ref[pl.ds(4 * start + part, 8, stride=4), :] = charge * total
        force_ref[pl.ds(4 * start + 3, 8, stride=4), :] = jnp.zeros((8, 128), jnp.float32)
        return 0

    lax.fori_loop(0, clusters // 8, spread_out, 0, unroll=4)


def grid_step(cell, masked, fields, rims, edges, base):
    smem = pl.BlockSpec(memory_space=pltpu.SMEM)
    vmem = pl.BlockSpec(memory_space=pltpu.VMEM)
    clusters = masked.shape[0]
    cells_x, cells_y, _ = fields[0].shape
    block = ((cells_x + 2 * DEPTH) * 2 * line_rows(cells_y), 128)
    return pl.pallas_call(
        functools.partial(grid_kernel, base),
        out_shape=(
            jax.ShapeDtypeStruct(fields[0].shape, jnp.float32),
            jax.ShapeDtypeStruct(fields[0].shape, jnp.float32),
            jax.ShapeDtypeStruct((clusters * 4, 128), jnp.float32),
        ),
        in_specs=[smem] + [pl.BlockSpec(memory_space=pl.ANY)] * 9,
        out_specs=(vmem,) * 3,
        scratch_shapes=[pltpu.VMEM(block, jnp.float32)] * 10
        + [pltpu.VMEM((clusters, 128), jnp.float32)] * 3
        + [pltpu.VMEM(((cells_x + 2 * DEPTH) * 64, 128), jnp.float32)]
        + [pltpu.VMEM(field.shape, jnp.float32) for field in fields]
        + [pltpu.VMEM(masked.shape, jnp.float32), pltpu.SemaphoreType.DMA((9,))]
        + [pltpu.VMEM(edge.shape, jnp.float32) for edge in edges],
        compiler_params=pltpu.CompilerParams(vmem_limit_bytes=ROOMY_LIMIT),
        cost_estimate=pl.CostEstimate(
            flops=block[0] * block[1] * 100, bytes_accessed=8 << 20, transcendentals=0
        ),
        name="grid_step",
    )(cell, masked, *fields, *rims, *edges)


def gather_forces_kernel(send_index_ref, *refs):
    fetched = len(SWAPS) + 3
    out_ref, extra_ref = refs[fetched : fetched + 2]
    sum_ref, field_ref, *back_refs = refs[fetched + 2 : -1]
    copies = start_copies(
        [
            (source.at[0 : target.shape[0]], target)
            for source, target in zip(refs[:fetched], refs[fetched + 2 : -1], strict=True)
        ],
        refs[-1],
    )
    extra_ref[...] = jnp.zeros_like(extra_ref)
    for copy in copies:
        copy.wait()
    clusters = sum_ref.shape[0]
    slots = send_index_ref.shape[1]
    ups = upward()

    def visit(slot, _):
        for position, back_ref in enumerate(back_refs):
            cluster = send_index_ref[sent_row(position, ups) if position else 0, slot]
            target_ref = extra_ref if position % 2 else sum_ref
            target_ref[cluster] += back_ref[slot]
        return 0

    lax.fori_loop(0, slots, visit, 0, unroll=2)

    def write(step, _):
        for turn in range(8):
            cluster = step * 8 + turn
            total = (sum_ref[cluster] + extra_ref[cluster]) + field_ref[cluster]
            out_ref[:, pl.ds(pl.multiple_of(cluster * 128, 128), 128)] = total[0:3]
        return 0

    lax.fori_loop(0, clusters // 8, write, 0)


def gather_forces(send_index, own, field, backs):
    smem = pl.BlockSpec(memory_space=pltpu.SMEM)
    vmem = pl.BlockSpec(memory_space=pltpu.VMEM)
    clusters = own.shape[0]
    return pl.pallas_call(
        gather_forces_kernel,
        out_shape=jax.ShapeDtypeStruct((3, clusters * 128), jnp.float32),
        in_specs=[smem] + [pl.BlockSpec(memory_space=pl.ANY)] * (2 + len(backs)),
        out_specs=vmem,
        scratch_shapes=[
            *[pltpu.VMEM(part.shape, jnp.float32) for part in (own, own, field)],
            *[pltpu.VMEM((send_index.shape[1], 4, 128), jnp.float32)] * len(backs),
            pltpu.SemaphoreType.DMA((2 + len(backs),)),
        ],
        compiler_params=pltpu.CompilerParams(vmem_limit_bytes=ROOMY_LIMIT),
        name="gather_forces",
    )(send_index, own, field, *backs)


def shards(
    positions,
    charges,
    cluster_fill,
    cluster_cell,
    send_index,
    send_count,
    pair_local,
    pair_dir,
    pair_slot,
    ion_density,
    potential_prev,
    screening,
):
    clusters = cluster_fill.shape[0]
    psize = charges.shape[0] // clusters
    slots = send_index.shape[1]
    base = slots * 4
    other_rows, own, masked, local, *messages = prepare(
        cluster_fill,
        send_index,
        send_count,
        pair_dir.reshape(-1, 128),
        pair_slot.reshape(-1, 128),
        positions,
        charges.reshape(clusters, psize),
    )
    inverse, source, *edges = sources_of(
        cluster_cell, masked, ion_density, potential_prev, screening
    )
    arrived = [local] + [
        swapped(message, *swap)
        for message, swap in zip(messages, SWAPS, strict=True)
    ]
    fields = (potential_prev, inverse, source, ion_density)
    arrived, edges = lax.optimization_barrier((arrived, edges))
    edges = [swapped(edge, "grp", 1, phase) for phase, edge in enumerate(edges)]
    own_force, *reactions = pair_forces(
        pair_local,
        other_rows.reshape(-1),
        own.reshape(clusters * 4, psize),
        arrived,
        slots,
    )
    local_back, *reactions = reactions
    rims = pack_rows(fields, edges, reactions[:2])
    backs = [
        swapped(reaction, *swap)
        for reaction, swap in zip((*rims, *reactions[2:]), SWAPS, strict=True)
    ]
    potential, ion_next, field_force = grid_step(
        cluster_cell, masked, fields, backs[:2], edges, base
    )
    forces = gather_forces(
        send_index,
        own_force.reshape(clusters, 4, psize),
        field_force.reshape(clusters, 4, psize),
        [back.reshape(-1, 4, psize) for back in (local_back, *backs)],
    )
    return (forces, potential, ion_next)


def solution(mesh):
    in_specs = (
        P(None, ("grp", "brick")),
        P(("grp", "brick")),
        P(("grp", "brick")),
        P(("grp", "brick")),
        P(("grp", "brick"), None),
        P(("grp", "brick"), None),
        P(("grp", "brick")),
        P(("grp", "brick")),
        P(("grp", "brick")),
        P("grp", "brick", None),
        P("grp", "brick", None),
        P("grp", "brick", None),
    )
    out_specs = (P(None, ("grp", "brick")), P("grp", "brick", None), P("grp", "brick", None))
    return jax.shard_map(shards, mesh=mesh, in_specs=in_specs, out_specs=out_specs, check_vma=False)
```

```python
import functools

import jax
import jax.numpy as jnp
import numpy as np
from jax import lax
from jax.experimental import pallas as pl
from jax.experimental.pallas import tpu as pltpu
from jax.sharding import PartitionSpec as P

SWEEPS = 4
UNROLL = 8
CHUNKS = 4
AHEAD = 2
BEHIND = 4
HALO_WIDTHS = (SWEEPS + 1, SWEEPS, SWEEPS, 1)
DEPTH = SWEEPS + 1
CELL_BITS = 8
SWAPS = tuple(
    (*way, phase) for way in (("brick", 1), ("brick", 2), ("grp", 1)) for phase in (0, 1)
)


coulomb_scale = 0.02
softening = 0.1
field_scale = 0.5
deposit_scale = 0.2
lowest_eig = 0.01
highest_eig = 1.99
mobility = 0.3
diffusion = 0.2
time_step = 0.2


VMEM_LIMIT = 60 * 1024 * 1024
ROOMY_LIMIT = 48 * 1024 * 1024


def start_copies(pairs, sems):
    copies = [
        pltpu.make_async_copy(source, target, sems.at[index])
        for index, (source, target) in enumerate(pairs)
    ]
    for copy in copies:
        copy.start()
    return copies


def upward():
    brick, grp = (lax.axis_index("brick"), lax.axis_index("grp"))
    bits = (brick, lax.shift_right_logical(brick, 1), grp)
    return [1 - lax.bitwise_and(bit, 1) for bit in bits]


def sent_row(position, ups):
    way, phase = ((position - 1) // 2, (position - 1) % 2)
    return 1 + 2 * way + (ups[way] if phase else 1 - ups[way])


def swapped(shard, axis, distance, phase):
    devices = lax.axis_size(axis)
    pairs = []
    for index in range(devices):
        step = distance if (index // distance + phase) % 2 == 0 else -distance
        if 0 <= index + step < devices:
            pairs.append((index, index + step))
    return lax.ppermute(shard, axis, pairs)


def split3(value):
    first = value.astype(jnp.bfloat16).astype(jnp.float32)
    rest = value - first
    second = rest.astype(jnp.bfloat16).astype(jnp.float32)
    third = (rest - second).astype(jnp.bfloat16).astype(jnp.float32)
    return (first, second, third)


def moment_pieces(comps, charge):
    rows = [None] * 12
    for part, charged in enumerate((*comps, None)):
        for level, piece in enumerate(split3(charge if charged is None else charge * charged)):
            rows[4 * level + part] = piece
    return rows


def selections():
    near_kinds, far_kinds = ([], [])
    for part in range(3):
        near_kinds += [3 * part + level for level in (0, 0, 0, 1, 1, 2)]
        far_kinds += [3 * part + level for level in (0, 1, 2, 0, 1, 0)]
    near_kinds += [9, 10, 11, 12, 12, 12]
    far_kinds += [12, 12, 12, 9, 10, 11]
    near = np.zeros((128, 1024), np.float32)
    far = np.zeros((256, 128), np.float32)
    moment = np.zeros((128, 128), np.float32)
    for cluster in range(8):
        for index, kind in enumerate(near_kinds):
            near[kind * 8 + cluster, cluster * 128 + index] = 1.0
        for index, kind in enumerate(far_kinds):
            far[cluster * 32 + index, kind * 8 + cluster] = 1.0
        for kind in range(12):
            moment[cluster * 16 + kind, kind * 8 + cluster] = 1.0
    return tuple(jnp.asarray(part, jnp.bfloat16) for part in (near, far, moment))


def pair_kernel(own_rows_ref, other_rows_ref, *refs):
    sources = len(SWAPS) + 1
    fetched = sources + 4
    hbm_refs = refs[:fetched]
    own_out_ref = refs[fetched]
    other_out_refs = refs[fetched + 1 : fetched + 1 + sources]
    refs = refs[fetched + 1 + sources :]
    near_sel_ref, far_sel_ref, moment_sel_ref, own_ref = refs[:4]
    other_refs = refs[4:fetched]
    sems = refs[fetched]
    copies = start_copies(
        [
            (source.at[0 : target.shape[0]], target)
            for source, target in zip(hbm_refs, refs[:fetched], strict=True)
        ],
        sems,
    )
    (
        near_ref,
        far_ref,
        own_moment_ref,
        other_moment_ref,
        own_sum_ref,
        other_sum_ref,
        dist_ref,
        *weight_refs,
    ) = refs[fetched + 1 :]
    clusters = own_ref.shape[0] // 4
    slots = other_out_refs[0].shape[0] // 4
    others = slots * sources
    groups = own_rows_ref.shape[0] // UNROLL
    ones = jnp.ones((8, 128), jnp.float32)
    zeros = jnp.zeros((8, 128), jnp.float32)

    def components(data_ref, start):
        return [data_ref[pl.ds(4 * start + part, 8, stride=4), :] for part in range(4)]

    def place_pieces(comps, factor, offset):
        pieces = []
        square = zeros
        for comp in comps:
            square = square + comp * comp
            pieces += split3(factor * comp)
        pieces += [*split3(square + offset), ones]
        return jnp.concatenate(pieces + [zeros] * (16 - len(pieces)), axis=0)

    def selected(left, right):
        return jnp.dot(
            left.astype(jnp.bfloat16), right, preferred_element_type=jnp.float32
        ).astype(jnp.bfloat16)

    def near_rows(step, _):
        start = pl.multiple_of(step * 8, 8)
        *comps, charge = components(own_ref, start)
        moments = jnp.concatenate(moment_pieces(comps, charge) + [zeros] * 4, axis=0)
        own_moment_ref[pl.ds(pl.multiple_of(start * 16, 128), 128), :] = selected(
            moment_sel_ref[...], moments.astype(jnp.bfloat16)
        )
        tiles = selected(place_pieces(comps, 1.0, 0.0).T, near_sel_ref[...])
        for index in range(8):
            at = pl.ds(pl.multiple_of((start + index) * 128, 128), 128)
            near_ref[at, :] = tiles[:, 128 * index : 128 * index + 128]
        return 0

    def far_rows(source, step, _):
        local = pl.multiple_of(step * 8, 8)
        start = source * slots + local
        *comps, charge = components(other_refs[source], local)
        far_ref[pl.ds(pl.multiple_of(start * 32, 256), 256), :] = selected(
            far_sel_ref[...], place_pieces(comps, -2.0, softening).astype(jnp.bfloat16)
        )
        moments = jnp.concatenate(moment_pieces(comps, charge) + [zeros] * 4, axis=0)
        other_moment_ref[pl.ds(pl.multiple_of(start * 16, 128), 128), :] = selected(
            moment_sel_ref[...], moments.astype(jnp.bfloat16)
        )
        return 0

    own_sum_ref[...] = jnp.zeros_like(own_sum_ref)
    other_sum_ref[...] = jnp.zeros_like(other_sum_ref)
    weight_refs[0][...] = jnp.zeros_like(weight_refs[0])
    for copy in copies[:4]:
        copy.wait()
    lax.fori_loop(0, clusters // 8, near_rows, 0, unroll=4)
    for copy in copies[4:]:
        copy.wait()
    for source in range(sources):
        lax.fori_loop(0, slots // 8, functools.partial(far_rows, source), 0, unroll=4)
    def distances(pair):
        own = own_rows_ref[pair]
        other = other_rows_ref[pair]
        return jnp.dot(
            near_ref[pl.ds(pl.multiple_of(own * 128, 128), 128), 0:32],
            far_ref[pl.ds(pl.multiple_of(other * 32, 32), 32), :],
            preferred_element_type=jnp.float32,
        )

    def weights(dist, index, chunk, weight_ref):
        rows = 128 // CHUNKS
        first = rows * chunk
        root = lax.rsqrt(dist[first : first + rows])
        weight = root * root * root
        high = weight.astype(jnp.bfloat16)
        low = (weight - high.astype(jnp.float32)).astype(jnp.bfloat16)
        at = slice(128 * index + first, 128 * index + first + rows)
        weight_ref[at, :128] = high
        weight_ref[at, 128:] = low

    def row_block(index):
        return pl.ds(pl.multiple_of(index * 16, 16), 16)

    def own_product(other, weight_ref, index):
        both = weight_ref[128 * index : 128 * index + 128]
        return lax.dot_general(
            other_moment_ref[row_block(other), :],
            jnp.concatenate([both[:, :128], both[:, 128:]], axis=0),
            (((1,), (1,)), ((), ())),
            preferred_element_type=jnp.float32,
        )

    def other_product(own, weight_ref, index):
        return jnp.dot(
            own_moment_ref[row_block(own), :],
            weight_ref[128 * index : 128 * index + 128],
            preferred_element_type=jnp.float32,
        )

    def add_rows(own, other, to_own, to_other):
        own_sum_ref[row_block(own), :] += to_own[:, :128] + to_own[:, 128:]
        other_sum_ref[row_block(other), :] += to_other[:, :128] + to_other[:, 128:]

    def half_step(step, side, dists):
        last = jnp.maximum(step - 1, 0) * UNROLL
        waiting = []
        for index in range(UNROLL):
            own = own_rows_ref[last + index]
            other = other_rows_ref[last + index]
            coming = step * UNROLL + index + AHEAD
            later = distances(jnp.minimum(coming, groups * UNROLL - 1))
            weights(dists[0], index, 0, weight_refs[1 - side])
            to_own = own_product(other, weight_refs[side], index)
            weights(dists[0], index, 1, weight_refs[1 - side])
            weights(dists[0], index, 2, weight_refs[1 - side])
            to_other = other_product(own, weight_refs[side], index)
            weights(dists[0], index, 3, weight_refs[1 - side])
            dists = [*dists[1:], later]
            waiting.append((own, other, to_own, to_other))
            if len(waiting) > BEHIND:
                add_rows(*waiting.pop(0))
        for entry in waiting:
            add_rows(*entry)
        return dists

    def visit(step, _):
        dists = [dist_ref[index] for index in range(AHEAD)]
        for side in range(2):
            dists = half_step(step * 2 + side, side, dists)
        for index in range(AHEAD):
            dist_ref[index] = dists[index]
        return 0

    for index in range(AHEAD):
        dist_ref[index] = distances(index)
    lax.fori_loop(0, groups // 2, visit, 0)
    half_step(groups, 0, [dist_ref[index] for index in range(AHEAD)])

    def finish(data_ref, out_ref, sum_ref, base, step, _):
        start = pl.multiple_of(step * 8, 8)
        *comps, charge = components(data_ref, start)

        def total(part):
            terms = [
                sum_ref[pl.ds(base + start * 16 + 4 * level + part, 8, stride=16), :]
                for level in range(3)
            ]
            return terms[0] + (terms[1] + terms[2])

        weight = total(3)
        scale = coulomb_scale * charge
        for part, comp in enumerate(comps):
            out_ref[pl.ds(4 * start + part, 8, stride=4), :] = scale * (comp * weight - total(part))
        out_ref[pl.ds(4 * start + 3, 8, stride=4), :] = zeros
        return 0

    lax.fori_loop(
        0, clusters // 8, functools.partial(finish, own_ref, own_out_ref, own_sum_ref, 0), 0, unroll=4
    )
    for source in range(sources):
        body = functools.partial(
            finish,
            other_refs[source],
            other_out_refs[source],
            other_sum_ref,
            source * slots * 16,
        )
        lax.fori_loop(0, slots // 8, body, 0, unroll=4)


def pair_forces(own_rows, other_rows, own, arrived, slots):
    clusters = own.shape[0] // 4
    others = slots * len(arrived)
    pairs = own_rows.shape[0]
    smem = pl.BlockSpec(memory_space=pltpu.SMEM)
    vmem = pl.BlockSpec(memory_space=pltpu.VMEM)
    hbm = pl.BlockSpec(memory_space=pl.ANY)
    operands = (*selections(), own)
    return pl.pallas_call(
        pair_kernel,
        out_shape=(
            jax.ShapeDtypeStruct(own.shape, jnp.float32),
            *[jax.ShapeDtypeStruct((slots * 4, 128), jnp.float32)] * len(arrived),
        ),
        in_specs=[smem, smem] + [hbm] * (4 + len(arrived)),
        out_specs=(vmem,) * (len(arrived) + 1),
        scratch_shapes=[
            *[pltpu.VMEM(operand.shape, operand.dtype) for operand in operands],
            *[pltpu.VMEM((slots * 4, 128), jnp.float32)] * len(arrived),
            pltpu.SemaphoreType.DMA((len(operands) + len(arrived),)),
            pltpu.VMEM((clusters * 128, 128), jnp.bfloat16),
            pltpu.VMEM((others * 32, 128), jnp.bfloat16),
            pltpu.VMEM((clusters * 16, 128), jnp.bfloat16),
            pltpu.VMEM((others * 16, 128), jnp.bfloat16),
            pltpu.VMEM((clusters * 16, 128), jnp.float32),
            pltpu.VMEM((others * 16, 128), jnp.float32),
            pltpu.VMEM((AHEAD, 128, 128), jnp.float32),
            *[pltpu.VMEM((128 * UNROLL, 256), jnp.bfloat16)] * 2,
        ],
        compiler_params=pltpu.CompilerParams(vmem_limit_bytes=ROOMY_LIMIT),
        cost_estimate=pl.CostEstimate(
            flops=pairs * 128 * 128 * 20, bytes_accessed=4 * 1024 * 1024, transcendentals=0
        ),
        name="pair_forces",
    )(own_rows, other_rows, *operands, *arrived)


def prepare_kernel(
    fill_ref,
    send_index_ref,
    send_count_ref,
    pair_dir_ref,
    pair_slot_ref,
    position_hbm,
    charge_hbm,
    row_ref,
    own_ref,
    masked_ref,
    *refs,
):
    out_refs, (position_ref, charge_ref, sems) = (refs[:-3], refs[-3:])
    copies = start_copies(((position_hbm, position_ref), (charge_hbm, charge_ref)), sems)
    clusters = charge_ref.shape[0]
    slots = send_index_ref.shape[1]
    lane = lax.broadcasted_iota(jnp.int32, (1, 128), 1)
    row = lax.broadcasted_iota(jnp.int32, (4, 128), 0)
    ups = upward()
    direction = pair_dir_ref[...]
    way = lax.shift_right_arithmetic(direction - 1, 1)
    flip = jnp.where(way == 0, ups[0], jnp.where(way == 1, ups[1], ups[2]))
    position = 1 + 2 * way + lax.bitwise_xor(lax.bitwise_and(direction - 1, 1), flip)
    row_ref[...] = jnp.where(direction == 0, 0, position) * slots + pair_slot_ref[...]
    for copy in copies:
        copy.wait()

    def collect(step, _):
        for turn in range(8):
            cluster = step * 8 + turn
            masked = jnp.where(lane < fill_ref[cluster], charge_ref[pl.ds(cluster, 1), :], 0.0)
            masked_ref[pl.ds(cluster, 1), :] = masked
            place = position_ref[:, pl.ds(pl.multiple_of(cluster * 128, 128), 128)]
            own_ref[cluster, 0:3, :] = place
            own_ref[cluster, 3:4, :] = masked
        return 0

    lax.fori_loop(0, clusters // 8, collect, 0, unroll=2)

    def fill_messages(step, _):
        for position, out_ref in enumerate(out_refs):
            direction = sent_row(position, ups) if position else 0
            parts = []
            for turn in range(2):
                slot = step * 2 + turn
                live = jnp.where(slot < send_count_ref[0, direction], 1.0, 0.0)
                value = own_ref[send_index_ref[direction, slot]]
                parts.append(jnp.where(row == 3, value * live, value))
            out_ref[pl.ds(pl.multiple_of(step * 8, 8), 8), :] = jnp.concatenate(parts, axis=0)
        return 0

    lax.fori_loop(0, slots // 2, fill_messages, 0)


def prepare(fill, send_index, send_count, pair_dir, pair_slot, positions, charges):
    clusters = charges.shape[0]
    directions, slots = send_index.shape
    smem = pl.BlockSpec(memory_space=pltpu.SMEM)
    vmem = pl.BlockSpec(memory_space=pltpu.VMEM)
    return pl.pallas_call(
        prepare_kernel,
        out_shape=(
            jax.ShapeDtypeStruct(pair_dir.shape, jnp.int32),
            jax.ShapeDtypeStruct((clusters, 4, 128), jnp.float32),
            jax.ShapeDtypeStruct((clusters, 128), jnp.float32),
            *[jax.ShapeDtypeStruct((slots * 4, 128), jnp.float32)] * directions,
        ),
        in_specs=[smem] * 3 + [vmem] * 2 + [pl.BlockSpec(memory_space=pltpu.HBM)] * 2,
        out_specs=(vmem,) * (3 + directions),
        scratch_shapes=[
            *[pltpu.VMEM(operand.shape, jnp.float32) for operand in (positions, charges)],
            pltpu.SemaphoreType.DMA((2,)),
        ],
        compiler_params=pltpu.CompilerParams(vmem_limit_bytes=VMEM_LIMIT),
        name="prepare",
    )(fill, send_index, send_count, pair_dir, pair_slot, positions, charges)


def sources_kernel(
    cell_ref,
    cell_row_ref,
    masked_hbm,
    ion_hbm,
    start_hbm,
    screen_hbm,
    inverse_ref,
    source_ref,
    *refs,
):
    edge_refs, refs = (refs[:2], refs[2:])
    sum_ref, deposit_ref, masked_ref, ion_ref, start_ref, screen_ref, sems = refs
    copies = start_copies(
        (
            (masked_hbm, masked_ref),
            (ion_hbm, ion_ref),
            (start_hbm, start_ref),
            (screen_hbm, screen_ref),
        ),
        sems,
    )
    copies[0].wait()
    clusters = masked_ref.shape[0]
    cells_x, cells_y, _ = ion_ref.shape
    lane = lax.broadcasted_iota(jnp.int32, (1, 128), 1)
    ups = upward()

    def add_up(step, _):
        at = pl.ds(pl.multiple_of(step * 8, 8), 8)
        total = jnp.sum(masked_ref[at, :], axis=1, keepdims=True)
        sum_ref[at, :] = jnp.broadcast_to(deposit_scale * total, (8, 128))
        return 0

    lax.fori_loop(0, clusters // 8, add_up, 0, unroll=8)

    def place(step, _):
        for turn in range(8):
            cluster = step * 8 + turn
            index_z = lax.bitwise_and(cell_ref[cluster], 127)
            at = pl.ds(cluster, 1)
            sum_ref[at, :] = jnp.where(lane == index_z, sum_ref[at, :], 0.0)
        return 0

    lax.fori_loop(0, clusters // 8, place, 0)
    cell = cell_row_ref[...]
    line = lax.shift_right_logical(cell, CELL_BITS)
    line = (line // cells_y * 2 + lax.shift_right_logical(lax.bitwise_and(cell, 255), 7)) * cells_y
    line = line + lax.shift_right_logical(cell, CELL_BITS) % cells_y
    sums = jnp.concatenate([part.astype(jnp.bfloat16) for part in split3(sum_ref[...])], axis=1)
    block = 128
    for first in range(0, deposit_ref.shape[0], block):
        rows = lax.broadcasted_iota(jnp.int32, (block, clusters), 0) + first
        hot = jnp.where(rows == line, 1.0, 0.0).astype(jnp.bfloat16)
        added = jnp.dot(hot, sums, preferred_element_type=jnp.float32)
        deposit_ref[first : first + block, :] = added[:, :128] + (
            added[:, 128:256] + added[:, 256:]
        )
    for copy in copies[1:]:
        copy.wait()
    inverse_ref[...] = 1.0 / (6.0 + screen_ref[...])
    for index in range(cells_x):
        for half in range(2):
            lanes = slice(128 * half, 128 * half + 128)
            first = (index * 2 + half) * cells_y
            source_ref[index, :, lanes] = (
                ion_ref[index, :, lanes] + deposit_ref[first : first + cells_y, :]
            ) * inverse_ref[index, :, lanes]
    edge = 0
    for field_ref, width in zip(
        (start_ref, inverse_ref, source_ref, ion_ref), HALO_WIDTHS, strict=True
    ):
        for step in range(width):
            for phase, edge_ref in enumerate(edge_refs):
                last = ups[2] if phase == 0 else 1 - ups[2]
                plane = field_ref[last * (cells_x - width) + step]
                for half in range(2):
                    edge_ref[2 * edge + half] = plane[:, 128 * half : 128 * half + 128]
            edge += 1


def sources_of(cell, masked, ions, start, screen):
    clusters = masked.shape[0]
    cells_y = ions.shape[1]
    smem = pl.BlockSpec(memory_space=pltpu.SMEM)
    vmem = pl.BlockSpec(memory_space=pltpu.VMEM)
    edge = jax.ShapeDtypeStruct((2 * sum(HALO_WIDTHS), cells_y, 128), jnp.float32)
    return pl.pallas_call(
        sources_kernel,
        out_shape=(*[jax.ShapeDtypeStruct(ions.shape, jnp.float32)] * 2, edge, edge),
        in_specs=[smem, vmem] + [pl.BlockSpec(memory_space=pltpu.HBM)] * 4,
        out_specs=(vmem,) * 4,
        scratch_shapes=[
            pltpu.VMEM((clusters, 128), jnp.float32),
            pltpu.VMEM((ions.size // 128, 128), jnp.float32),
            *[pltpu.VMEM(operand.shape, jnp.float32) for operand in (masked, ions, start, screen)],
            pltpu.SemaphoreType.DMA((4,)),
        ],
        compiler_params=pltpu.CompilerParams(vmem_limit_bytes=VMEM_LIMIT),
        cost_estimate=pl.CostEstimate(
            flops=20_000_000, bytes_accessed=4 << 20, transcendentals=0
        ),
        name="sources",
    )(cell, cell.reshape(1, clusters), masked, ions, start, screen)


def line_rows(cells_y):
    return (cells_y + 2 * DEPTH + 7) // 8 * 8


def pack_rows_kernel(*refs):
    field_refs, edge_refs, reaction_refs, out_refs = (refs[:4], refs[4:6], refs[6:8], refs[8:10])
    cells_x, cells_y, _ = field_refs[0].shape
    base = reaction_refs[0].shape[0]
    ups = upward()
    for reaction_ref, out_ref in zip(reaction_refs, out_refs, strict=True):
        out_ref[0:base, :] = reaction_ref[...]

    def fill(out_ref, after):
        for field, width in enumerate(HALO_WIDTHS):
            offset = sum(HALO_WIDTHS[:field])
            rows = slice(cells_y - width, cells_y) if after else slice(0, width)
            for index in range(cells_x):
                value = field_refs[field][index, rows, :]
                for half in range(2):
                    at = base + ((DEPTH + index) * 2 + half) * 16 + offset
                    out_ref[at : at + width, :] = value[:, 128 * half : 128 * half + 128]
            if width == 1:
                continue
            for phase, edge_ref in enumerate(edge_refs):
                higher = ups[2] if phase == 0 else 1 - ups[2]
                for step in range(width):
                    plane = (DEPTH - width) + higher * (cells_x + width) + step
                    for half in range(2):
                        at = pl.ds(base + (plane * 2 + half) * 16 + offset, width)
                        out_ref[at, :] = edge_ref[2 * (offset + step) + half, rows, :]

    for up in range(2):

        @pl.when(ups[0] == up)
        def _(up=up):
            fill(out_refs[0], up)
            fill(out_refs[1], 1 - up)


def pack_rows(fields, edges, reactions):
    vmem = pl.BlockSpec(memory_space=pltpu.VMEM)
    cells_x = fields[0].shape[0]
    rows = reactions[0].shape[0] + (cells_x + 2 * DEPTH) * 32
    shape = jax.ShapeDtypeStruct((rows, 128), jnp.float32)
    return pl.pallas_call(
        pack_rows_kernel,
        out_shape=(shape, shape),
        in_specs=[vmem] * 8,
        out_specs=(vmem, vmem),
        compiler_params=pltpu.CompilerParams(vmem_limit_bytes=ROOMY_LIMIT),
        name="pack_rows",
    )(*fields, *edges, *reactions)


def fill_line(target_ref, plane, half, field, value, rim_ref):
    cells_y = value.shape[0]
    width = HALO_WIDTHS[field]
    at = (plane * 2 + half) * line_rows(cells_y) + DEPTH
    target_ref[pl.ds(at, cells_y), :] = value
    first = (plane * 2 + half) * 16 + sum(HALO_WIDTHS[:field])
    target_ref[pl.ds(at - width, width), :] = rim_ref[pl.ds(first, width), :]
    first = first + rim_ref.shape[0] // 2
    target_ref[pl.ds(at + cells_y, width), :] = rim_ref[pl.ds(first, width), :]


def face_flux(pot_low, pot_high, ion_low, ion_high):
    speed = -mobility * (pot_high - pot_low)
    return (
        jnp.maximum(speed, 0.0) * ion_low
        + jnp.minimum(speed, 0.0) * ion_high
        - diffusion * (ion_high - ion_low)
    )


def grid_kernel(base, *refs):
    cell_ref, masked_ref = refs[:2]
    field_refs, rims, edge_refs = (refs[2:6], refs[6:8], refs[8:10])
    potential_ref, next_ref, force_ref = refs[10:13]
    start_ref, inverse_ref, source_ref, ion_ref = refs[13:17]
    updates, resids, final_ref, pick_refs = (refs[17:20], refs[20:22], refs[22], refs[23:26])
    rim_ref = refs[26]
    cells_x, cells_y, _ = field_refs[0].shape
    rows = line_rows(cells_y)
    clusters = masked_ref.shape[0]
    ups = upward()
    size = (cells_x + 2 * DEPTH) * 32
    for rim, side in zip(rims, (ups[0], 1 - ups[0]), strict=True):
        rim_ref[pl.ds(pl.multiple_of(side * size, size), size), :] = rim[base : base + size, :]
    extended = (start_ref, inverse_ref, source_ref, ion_ref)
    for field, target_ref in enumerate(extended):

        def fill(index, _, field=field, target_ref=target_ref):
            plane = field_refs[field][index]
            for half in range(2):
                value = plane[:, 128 * half : 128 * half + 128]
                fill_line(target_ref, DEPTH + index, half, field, value, rim_ref)
            return 0

        lax.fori_loop(0, cells_x, fill, 0, unroll=4)
    for field, target_ref in enumerate(extended):
        width = HALO_WIDTHS[field]
        for phase, edge_ref in enumerate(edge_refs):
            higher = ups[2] if phase == 0 else 1 - ups[2]

            def fill_edge(step, _, field=field, target_ref=target_ref, edge_ref=edge_ref):
                width = HALO_WIDTHS[field]
                plane = (DEPTH - width) + higher * (cells_x + width) + step
                for half in range(2):
                    value = edge_ref[2 * (sum(HALO_WIDTHS[:field]) + step) + half]
                    fill_line(target_ref, plane, half, field, value, rim_ref)
                return 0

            lax.fori_loop(0, width, fill_edge, 0, unroll=True)

    lane = lax.broadcasted_iota(jnp.int32, (2 * rows, 128), 1)
    blank = jnp.zeros((rows, 128), jnp.float32)

    def beyond(value):
        right = pltpu.roll(value, 127, 1)
        left = pltpu.roll(value, 1, 1)
        above = jnp.where(lane == 127, jnp.concatenate([right[rows:], blank], axis=0), right)
        below = jnp.where(lane == 0, jnp.concatenate([blank, left[:rows]], axis=0), left)
        return (below, above)

    def whole(plane, shift=0):
        return pl.ds(plane * 2 * rows + shift, 2 * rows)

    def around(ref, plane):
        here = ref[whole(plane), :]
        below, above = beyond(here)
        sums = (ref[whole(plane - 1), :] + ref[whole(plane + 1), :]) + (
            ref[whole(plane, -1), :] + ref[whole(plane, 1), :]
        )
        return (here, sums + (below + above))

    middle = 0.5 * (highest_eig + lowest_eig)
    spread = 0.5 * (highest_eig - lowest_eig)
    assert middle == 1.0 and SWEEPS == 4

    def sweep_first(plane, _):
        here, sums = around(start_ref, plane)
        at = whole(plane)
        updates[0][at, :] = source_ref[at, :] - here + inverse_ref[at, :] * sums
        return 0

    lax.fori_loop(1, cells_x + 2 * DEPTH - 1, sweep_first, 0, unroll=2)

    ratio_ms = middle / spread
    weight_now = 1.0 / ratio_ms
    for turn in range(1, SWEEPS):
        weight_next = 1.0 / (2.0 * ratio_ms - weight_now)
        keep, gain = (weight_next * weight_now, 2.0 * weight_next / spread)
        weight_now = weight_next

        def sweep(plane, _, turn=turn, keep=keep, gain=gain):
            here, sums = around(updates[turn - 1], plane)
            at = whole(plane)
            resid = inverse_ref[at, :] * sums
            if turn > 1:
                resid = resid + (resids[turn - 2][at, :] - here)
            update = keep * here + gain * resid
            if turn + 1 < SWEEPS:
                resids[turn - 1][at, :] = resid
                updates[turn][at, :] = update
            else:
                final_ref[at, :] = (start_ref[at, :] + updates[0][at, :]) + (
                    (updates[1][at, :] + here) + update
                )
            return 0

        first = 1 + turn
        lax.fori_loop(first, cells_x + 2 * DEPTH - first, sweep, 0, unroll=2)

    def advance(index, _):
        plane = index + DEPTH
        pot = final_ref[whole(plane, DEPTH), :]
        ion = ion_ref[whole(plane, DEPTH), :]
        steps = [
            (final_ref[at, :], ion_ref[at, :])
            for at in (
                whole(plane - 1, DEPTH),
                whole(plane + 1, DEPTH),
                whole(plane, DEPTH - 1),
                whole(plane, DEPTH + 1),
            )
        ]
        steps += zip(beyond(pot), beyond(ion), strict=True)
        total = 0.0
        for low, high in zip(steps[0::2], steps[1::2], strict=True):
            total = total + (
                face_flux(pot, high[0], ion, high[1]) - face_flux(low[0], pot, low[1], ion)
            )
        result = ion - time_step * total
        for half in range(2):
            lanes = slice(128 * half, 128 * half + 128)
            kept = slice(rows * half, rows * half + cells_y)
            next_ref[index, :, lanes] = result[kept]
            potential_ref[index, :, lanes] = pot[kept]
        return 0

    lax.fori_loop(0, cells_x, advance, 0)

    row_lane = lax.broadcasted_iota(jnp.int32, (1, 128), 1)

    def pick(cluster, _):
        cell = cell_ref[cluster]
        index_x = lax.shift_right_logical(cell, CELL_BITS) // cells_y + DEPTH
        index_y = lax.shift_right_logical(cell, CELL_BITS) % cells_y + DEPTH
        index_z = lax.bitwise_and(cell, 255)
        half = lax.shift_right_logical(index_z, 7)
        here = row_lane == lax.bitwise_and(index_z, 127)

        def line(plane, row, part):
            return final_ref[pl.ds((plane * 2 + part) * rows + row, 1), :]

        along_x = line(index_x - 1, index_y, half) - line(index_x + 1, index_y, half)
        along_y = line(index_x, index_y - 1, half) - line(index_x, index_y + 1, half)
        along_z = jnp.zeros((1, 128), jnp.float32)
        for part in range(2):
            value = line(index_x, index_y, part)
            place = row_lane + 128 * part
            along_z = along_z + jnp.where(place == index_z - 1, value, 0.0)
            along_z = along_z - jnp.where(place == index_z + 1, value, 0.0)
        at = pl.ds(cluster, 1)
        pick_refs[0][at, :] = jnp.where(here, along_x, 0.0)
        pick_refs[1][at, :] = jnp.where(here, along_y, 0.0)
        pick_refs[2][at, :] = along_z
        return 0

    lax.fori_loop(0, clusters, pick, 0, unroll=8)

    def spread_out(step, _):
        start = pl.multiple_of(step * 8, 8)
        charge = masked_ref[pl.ds(start, 8), :] * (0.5 * field_scale)
        for part, pick_ref in enumerate(pick_refs):
            total = jnp.sum(pick_ref[pl.ds(start, 8), :], axis=1, keepdims=True)
            force_ref[pl.ds(4 * start + part, 8, stride=4), :] = charge * total
        force_ref[pl.ds(4 * start + 3, 8, stride=4), :] = jnp.zeros((8, 128), jnp.float32)
        return 0

    lax.fori_loop(0, clusters // 8, spread_out, 0, unroll=4)


def grid_step(cell, masked, fields, rims, edges, base):
    smem = pl.BlockSpec(memory_space=pltpu.SMEM)
    vmem = pl.BlockSpec(memory_space=pltpu.VMEM)
    clusters = masked.shape[0]
    cells_x, cells_y, _ = fields[0].shape
    block = ((cells_x + 2 * DEPTH) * 2 * line_rows(cells_y), 128)
    return pl.pallas_call(
        functools.partial(grid_kernel, base),
        out_shape=(
            jax.ShapeDtypeStruct(fields[0].shape, jnp.float32),
            jax.ShapeDtypeStruct(fields[0].shape, jnp.float32),
            jax.ShapeDtypeStruct((clusters * 4, 128), jnp.float32),
        ),
        in_specs=[smem] + [vmem] * 9,
        out_specs=(vmem,) * 3,
        scratch_shapes=[pltpu.VMEM(block, jnp.float32)] * 10
        + [pltpu.VMEM((clusters, 128), jnp.float32)] * 3
        + [pltpu.VMEM(((cells_x + 2 * DEPTH) * 64, 128), jnp.float32)],
        compiler_params=pltpu.CompilerParams(vmem_limit_bytes=ROOMY_LIMIT),
        cost_estimate=pl.CostEstimate(
            flops=block[0] * block[1] * 100, bytes_accessed=8 << 20, transcendentals=0
        ),
        name="grid_step",
    )(cell, masked, *fields, *rims, *edges)


def gather_forces_kernel(send_index_ref, *refs):
    own_ref, field_ref, *back_refs = refs[:-3]
    out_ref, sum_ref, extra_ref = refs[-3:]
    sum_ref[...] = own_ref[...]
    extra_ref[...] = field_ref[...]
    clusters = sum_ref.shape[0]
    slots = send_index_ref.shape[1]
    ups = upward()

    def visit(slot, _):
        for position, back_ref in enumerate(back_refs):
            cluster = send_index_ref[sent_row(position, ups) if position else 0, slot]
            target_ref = extra_ref if position % 2 else sum_ref
            target_ref[cluster] += back_ref[slot]
        return 0

    lax.fori_loop(0, slots, visit, 0, unroll=2)

    def write(step, _):
        for turn in range(8):
            cluster = step * 8 + turn
            total = sum_ref[cluster] + extra_ref[cluster]
            out_ref[:, pl.ds(pl.multiple_of(cluster * 128, 128), 128)] = total[0:3]
        return 0

    lax.fori_loop(0, clusters // 8, write, 0)


def gather_forces(send_index, own, field, backs):
    smem = pl.BlockSpec(memory_space=pltpu.SMEM)
    vmem = pl.BlockSpec(memory_space=pltpu.VMEM)
    clusters = own.shape[0]
    return pl.pallas_call(
        gather_forces_kernel,
        out_shape=jax.ShapeDtypeStruct((3, clusters * 128), jnp.float32),
        in_specs=[smem] + [vmem] * (2 + len(backs)),
        out_specs=vmem,
        scratch_shapes=[pltpu.VMEM(own.shape, jnp.float32)] * 2,
        compiler_params=pltpu.CompilerParams(vmem_limit_bytes=ROOMY_LIMIT),
        name="gather_forces",
    )(send_index, own, field, *backs)


def shards(
    positions,
    charges,
    cluster_fill,
    cluster_cell,
    send_index,
    send_count,
    pair_local,
    pair_dir,
    pair_slot,
    ion_density,
    potential_prev,
    screening,
):
    clusters = cluster_fill.shape[0]
    psize = charges.shape[0] // clusters
    slots = send_index.shape[1]
    base = slots * 4
    other_rows, own, masked, local, *messages = prepare(
        cluster_fill,
        send_index,
        send_count,
        pair_dir.reshape(-1, 128),
        pair_slot.reshape(-1, 128),
        positions,
        charges.reshape(clusters, psize),
    )
    inverse, source, *edges = sources_of(
        cluster_cell, masked, ion_density, potential_prev, screening
    )
    arrived = [local] + [
        swapped(message, *swap)
        for message, swap in zip(messages, SWAPS, strict=True)
    ]
    fields = (potential_prev, inverse, source, ion_density)
    arrived, edges = lax.optimization_barrier((arrived, edges))
    edges = [swapped(edge, "grp", 1, phase) for phase, edge in enumerate(edges)]
    own_force, *reactions = pair_forces(
        pair_local,
        other_rows.reshape(-1),
        own.reshape(clusters * 4, psize),
        arrived,
        slots,
    )
    local_back, *reactions = reactions
    rims = pack_rows(fields, edges, reactions[:2])
    backs = [
        swapped(reaction, *swap)
        for reaction, swap in zip((*rims, *reactions[2:]), SWAPS, strict=True)
    ]
    potential, ion_next, field_force = grid_step(
        cluster_cell, masked, fields, backs[:2], edges, base
    )
    forces = gather_forces(
        send_index,
        own_force.reshape(clusters, 4, psize),
        field_force.reshape(clusters, 4, psize),
        [back.reshape(-1, 4, psize) for back in (local_back, *backs)],
    )
    return (forces, potential, ion_next)


def solution(mesh):
    in_specs = (
        P(None, ("grp", "brick")),
        P(("grp", "brick")),
        P(("grp", "brick")),
        P(("grp", "brick")),
        P(("grp", "brick"), None),
        P(("grp", "brick"), None),
        P(("grp", "brick")),
        P(("grp", "brick")),
        P(("grp", "brick")),
        P("grp", "brick", None),
        P("grp", "brick", None),
        P("grp", "brick", None),
    )
    out_specs = (P(None, ("grp", "brick")), P("grp", "brick", None), P("grp", "brick", None))
    return jax.shard_map(shards, mesh=mesh, in_specs=in_specs, out_specs=out_specs, check_vma=False)
```

```python
import functools

import jax
import jax.numpy as jnp
import numpy as np
from jax import lax
from jax.experimental import pallas as pl
from jax.experimental.pallas import tpu as pltpu
from jax.sharding import PartitionSpec as P

SWEEPS = 4
QUAD = 4
UNROLL = 8
CHUNKS = 4
AHEAD = 2
BEHIND = 4
HALO_WIDTHS = (SWEEPS + 1, SWEEPS, SWEEPS, 1)
DEPTH = SWEEPS + 1
CELL_BITS = 8
SWAPS = tuple(
    (*way, phase) for way in (("brick", 1), ("brick", 2), ("grp", 1)) for phase in (0, 1)
)


coulomb_scale = 0.02
softening = 0.1
field_scale = 0.5
deposit_scale = 0.2
lowest_eig = 0.01
highest_eig = 1.99
mobility = 0.3
diffusion = 0.2
time_step = 0.2


VMEM_LIMIT = 60 * 1024 * 1024
ROOMY_LIMIT = 48 * 1024 * 1024


def start_copies(pairs, sems):
    copies = [
        pltpu.make_async_copy(source, target, sems.at[index])
        for index, (source, target) in enumerate(pairs)
    ]
    for copy in copies:
        copy.start()
    return copies


def upward():
    brick, grp = (lax.axis_index("brick"), lax.axis_index("grp"))
    bits = (brick, lax.shift_right_logical(brick, 1), grp)
    return [1 - lax.bitwise_and(bit, 1) for bit in bits]


def sent_row(position, ups):
    way, phase = ((position - 1) // 2, (position - 1) % 2)
    return 1 + 2 * way + (ups[way] if phase else 1 - ups[way])


def swapped(shard, axis, distance, phase):
    devices = lax.axis_size(axis)
    pairs = []
    for index in range(devices):
        step = distance if (index // distance + phase) % 2 == 0 else -distance
        if 0 <= index + step < devices:
            pairs.append((index, index + step))
    return lax.ppermute(shard, axis, pairs)


def split3(value):
    first = value.astype(jnp.bfloat16).astype(jnp.float32)
    rest = value - first
    second = rest.astype(jnp.bfloat16).astype(jnp.float32)
    third = (rest - second).astype(jnp.bfloat16).astype(jnp.float32)
    return (first, second, third)


def moment_pieces(comps, charge):
    rows = [None] * 12
    for part, charged in enumerate((*comps, None)):
        for level, piece in enumerate(split3(charge if charged is None else charge * charged)):
            rows[4 * level + part] = piece
    return rows


def selections():
    near_kinds, far_kinds = ([], [])
    for part in range(3):
        near_kinds += [3 * part + level for level in (0, 0, 0, 1, 1, 2)]
        far_kinds += [3 * part + level for level in (0, 1, 2, 0, 1, 0)]
    near_kinds += [9, 10, 11, 12, 12, 12]
    far_kinds += [12, 12, 12, 9, 10, 11]
    near = np.zeros((128, 1024), np.float32)
    far = np.zeros((256, 128), np.float32)
    moment = np.zeros((128, 128), np.float32)
    column = np.zeros((128, QUAD * 256), np.float32)
    for cluster in range(8):
        for index, kind in enumerate(near_kinds):
            near[kind * 8 + cluster, cluster * 128 + index] = 1.0
        for index, kind in enumerate(far_kinds):
            far[cluster * 32 + index, kind * 8 + cluster] = 1.0
        for kind in range(12):
            moment[cluster * 16 + kind, kind * 8 + cluster] = 1.0
            for turn in range(QUAD):
                lane = (cluster % QUAD + turn) % QUAD * 32 + kind
                target = turn * 256 + cluster // QUAD * 128 + lane
                column[kind * 8 + cluster, target] = 1.0
    return tuple(jnp.asarray(part, jnp.bfloat16) for part in (near, far, moment, column))


def pair_kernel(own_rows_ref, other_rows_ref, *refs):
    sources = len(SWAPS) + 1
    fetched = sources + 5
    hbm_refs = refs[:fetched]
    own_out_ref = refs[fetched]
    other_out_refs = refs[fetched + 1 : fetched + 1 + sources]
    refs = refs[fetched + 1 + sources :]
    near_sel_ref, far_sel_ref, moment_sel_ref, column_sel_ref, own_ref = refs[:5]
    other_refs = refs[5:fetched]
    sems = refs[fetched]
    copies = start_copies(
        [
            (source.at[0 : target.shape[0]], target)
            for source, target in zip(hbm_refs, refs[:fetched], strict=True)
        ],
        sems,
    )
    (
        near_ref,
        far_ref,
        own_moment_ref,
        other_moment_ref,
        own_sum_ref,
        other_sum_ref,
        dist_ref,
        *weight_refs,
    ) = refs[fetched + 1 :]
    clusters = own_ref.shape[0] // 4
    slots = other_out_refs[0].shape[0] // 4
    others = slots * sources
    groups = own_rows_ref.shape[0] // UNROLL
    groups_of_other = others // QUAD
    ones = jnp.ones((8, 128), jnp.float32)
    zeros = jnp.zeros((8, 128), jnp.float32)

    def components(data_ref, start):
        return [data_ref[pl.ds(4 * start + part, 8, stride=4), :] for part in range(4)]

    def place_pieces(comps, factor, offset):
        pieces = []
        square = zeros
        for comp in comps:
            square = square + comp * comp
            pieces += split3(factor * comp)
        pieces += [*split3(square + offset), ones]
        return jnp.concatenate(pieces + [zeros] * (16 - len(pieces)), axis=0)

    def selected(left, right):
        return jnp.dot(
            left.astype(jnp.bfloat16), right, preferred_element_type=jnp.float32
        ).astype(jnp.bfloat16)

    def near_rows(step, _):
        start = pl.multiple_of(step * 8, 8)
        *comps, charge = components(own_ref, start)
        moments = jnp.concatenate(moment_pieces(comps, charge) + [zeros] * 4, axis=0)
        own_moment_ref[pl.ds(pl.multiple_of(start * 16, 128), 128), :] = selected(
            moment_sel_ref[...], moments.astype(jnp.bfloat16)
        )
        tiles = selected(place_pieces(comps, 1.0, 0.0).T, near_sel_ref[...])
        for index in range(8):
            at = pl.ds(pl.multiple_of((start + index) * 128, 128), 128)
            near_ref[at, :] = tiles[:, 128 * index : 128 * index + 128]
        return 0

    def far_rows(source, step, _):
        local = pl.multiple_of(step * 8, 8)
        start = source * slots + local
        *comps, charge = components(other_refs[source], local)
        far_ref[pl.ds(pl.multiple_of(start * 32, 256), 256), :] = selected(
            far_sel_ref[...], place_pieces(comps, -2.0, softening).astype(jnp.bfloat16)
        )
        moments = jnp.concatenate(moment_pieces(comps, charge) + [zeros] * 4, axis=0)
        tiles = selected(moments.T, column_sel_ref[...])
        for turn in range(QUAD):
            for half in range(2):
                group = turn * groups_of_other + source * (slots // QUAD) + step * 2 + half
                column = 256 * turn + 128 * half
                other_moment_ref[pl.ds(pl.multiple_of(group * 128, 128), 128), :] = tiles[
                    :, column : column + 128
                ]
        return 0

    own_sum_ref[...] = jnp.zeros_like(own_sum_ref)
    other_sum_ref[...] = jnp.zeros_like(other_sum_ref)
    weight_refs[0][...] = jnp.zeros_like(weight_refs[0])
    for copy in copies[:5]:
        copy.wait()
    lax.fori_loop(0, clusters // 8, near_rows, 0, unroll=4)
    for copy in copies[5:]:
        copy.wait()
    for source in range(sources):
        lax.fori_loop(0, slots // 8, functools.partial(far_rows, source), 0, unroll=4)
    def distances(pair):
        own = own_rows_ref[pair]
        other = other_rows_ref[pair]
        return jnp.dot(
            near_ref[pl.ds(pl.multiple_of(own * 128, 128), 128), 0:32],
            far_ref[pl.ds(pl.multiple_of(other * 32, 32), 32), :],
            preferred_element_type=jnp.float32,
        )

    def weights(dist, index, chunk, weight_ref):
        rows = 128 // CHUNKS
        first = rows * chunk
        root = lax.rsqrt(dist[first : first + rows])
        weight = root * root * root
        high = weight.astype(jnp.bfloat16)
        low = (weight - high.astype(jnp.float32)).astype(jnp.bfloat16)
        at = slice(128 * index + first, 128 * index + first + rows)
        weight_ref[at, :128] = high
        weight_ref[at, 128:] = low

    def row_block(index):
        return pl.ds(pl.multiple_of(index * 16, 16), 16)

    quarter_row = lax.shift_right_logical(lax.broadcasted_iota(jnp.int32, (1, 128), 1), 5)
    masks = [jnp.where(quarter_row == turn, 1.0, 0.0).astype(jnp.bfloat16) for turn in range(QUAD)]

    def turned(index, turn):
        rotation = lax.bitwise_and(turn - index, 3)
        group = rotation * groups_of_other + lax.shift_right_logical(index, 2)
        return other_moment_ref[pl.ds(pl.multiple_of(group * 128, 128), 128), :] * masks[turn]

    def own_products(others, weight_ref, first):
        levels = [
            jnp.concatenate(
                [
                    weight_ref[128 * (first + turn) : 128 * (first + turn) + 128, lanes]
                    for turn in range(QUAD)
                ],
                axis=1,
            )
            for lanes in (slice(0, 128), slice(128, 256))
        ]
        columns = jnp.concatenate([turned(other, turn) for turn, other in enumerate(others)], axis=0)
        both = jnp.dot(
            jnp.concatenate(levels, axis=0), columns, preferred_element_type=jnp.float32
        )
        return (both[:128] + both[128:]).T

    def other_product(own, weight_ref, index):
        return jnp.dot(
            own_moment_ref[row_block(own), :],
            weight_ref[128 * index : 128 * index + 128],
            preferred_element_type=jnp.float32,
        )

    def add_rows(own, other, turn, to_own, to_other):
        own_sum_ref[row_block(own), :] += to_own[32 * turn : 32 * turn + 16]
        other_sum_ref[row_block(other), :] += to_other[:, :128] + to_other[:, 128:]

    def half_step(step, side, dists):
        last = jnp.maximum(step - 1, 0) * UNROLL
        waiting = []
        for index in range(UNROLL):
            own = own_rows_ref[last + index]
            other = other_rows_ref[last + index]
            coming = step * UNROLL + index + AHEAD
            later = distances(jnp.minimum(coming, groups * UNROLL - 1))
            weights(dists[0], index, 0, weight_refs[1 - side])
            turn = index % QUAD
            if turn == 0:
                others_now = [other_rows_ref[last + index + place] for place in range(QUAD)]
                to_own = own_products(others_now, weight_refs[side], index)
            weights(dists[0], index, 1, weight_refs[1 - side])
            weights(dists[0], index, 2, weight_refs[1 - side])
            to_other = other_product(own, weight_refs[side], index)
            weights(dists[0], index, 3, weight_refs[1 - side])
            dists = [*dists[1:], later]
            waiting.append((own, other, turn, to_own, to_other))
            if len(waiting) > BEHIND:
                add_rows(*waiting.pop(0))
        for entry in waiting:
            add_rows(*entry)
        return dists

    def visit(step, _):
        dists = [dist_ref[index] for index in range(AHEAD)]
        for side in range(2):
            dists = half_step(step * 2 + side, side, dists)
        for index in range(AHEAD):
            dist_ref[index] = dists[index]
        return 0

    for index in range(AHEAD):
        dist_ref[index] = distances(index)
    lax.fori_loop(0, groups // 2, visit, 0)
    half_step(groups, 0, [dist_ref[index] for index in range(AHEAD)])

    def finish(data_ref, out_ref, sum_ref, base, step, _):
        start = pl.multiple_of(step * 8, 8)
        *comps, charge = components(data_ref, start)

        def total(part):
            terms = [
                sum_ref[pl.ds(base + start * 16 + 4 * level + part, 8, stride=16), :]
                for level in range(3)
            ]
            return terms[0] + (terms[1] + terms[2])

        weight = total(3)
        scale = coulomb_scale * charge
        for part, comp in enumerate(comps):
            out_ref[pl.ds(4 * start + part, 8, stride=4), :] = scale * (comp * weight - total(part))
        out_ref[pl.ds(4 * start + 3, 8, stride=4), :] = zeros
        return 0

    lax.fori_loop(
        0, clusters // 8, functools.partial(finish, own_ref, own_out_ref, own_sum_ref, 0), 0, unroll=4
    )
    for source in range(sources):
        body = functools.partial(
            finish,
            other_refs[source],
            other_out_refs[source],
            other_sum_ref,
            source * slots * 16,
        )
        lax.fori_loop(0, slots // 8, body, 0, unroll=4)


def pair_forces(own_rows, other_rows, own, arrived, slots):
    clusters = own.shape[0] // 4
    others = slots * len(arrived)
    pairs = own_rows.shape[0]
    smem = pl.BlockSpec(memory_space=pltpu.SMEM)
    vmem = pl.BlockSpec(memory_space=pltpu.VMEM)
    hbm = pl.BlockSpec(memory_space=pl.ANY)
    operands = (*selections(), own)
    return pl.pallas_call(
        pair_kernel,
        out_shape=(
            jax.ShapeDtypeStruct(own.shape, jnp.float32),
            *[jax.ShapeDtypeStruct((slots * 4, 128), jnp.float32)] * len(arrived),
        ),
        in_specs=[smem, smem] + [hbm] * (5 + len(arrived)),
        out_specs=(vmem,) * (len(arrived) + 1),
        scratch_shapes=[
            *[pltpu.VMEM(operand.shape, operand.dtype) for operand in operands],
            *[pltpu.VMEM((slots * 4, 128), jnp.float32)] * len(arrived),
            pltpu.SemaphoreType.DMA((len(operands) + len(arrived),)),
            pltpu.VMEM((clusters * 128, 128), jnp.bfloat16),
            pltpu.VMEM((others * 32, 128), jnp.bfloat16),
            pltpu.VMEM((clusters * 16, 128), jnp.bfloat16),
            pltpu.VMEM((others * 128, 128), jnp.bfloat16),
            pltpu.VMEM((clusters * 16, 128), jnp.float32),
            pltpu.VMEM((others * 16, 128), jnp.float32),
            pltpu.VMEM((AHEAD, 128, 128), jnp.float32),
            *[pltpu.VMEM((128 * UNROLL, 256), jnp.bfloat16)] * 2,
        ],
        compiler_params=pltpu.CompilerParams(vmem_limit_bytes=ROOMY_LIMIT),
        cost_estimate=pl.CostEstimate(
            flops=pairs * 128 * 128 * 20, bytes_accessed=4 * 1024 * 1024, transcendentals=0
        ),
        name="pair_forces",
    )(own_rows, other_rows, *operands, *arrived)


def prepare_kernel(
    fill_ref,
    send_index_ref,
    send_count_ref,
    pair_dir_ref,
    pair_slot_ref,
    position_hbm,
    charge_hbm,
    row_ref,
    own_ref,
    masked_ref,
    *refs,
):
    out_refs, (position_ref, charge_ref, sems) = (refs[:-3], refs[-3:])
    copies = start_copies(((position_hbm, position_ref), (charge_hbm, charge_ref)), sems)
    clusters = charge_ref.shape[0]
    slots = send_index_ref.shape[1]
    lane = lax.broadcasted_iota(jnp.int32, (1, 128), 1)
    row = lax.broadcasted_iota(jnp.int32, (4, 128), 0)
    ups = upward()
    direction = pair_dir_ref[...]
    way = lax.shift_right_arithmetic(direction - 1, 1)
    flip = jnp.where(way == 0, ups[0], jnp.where(way == 1, ups[1], ups[2]))
    position = 1 + 2 * way + lax.bitwise_xor(lax.bitwise_and(direction - 1, 1), flip)
    row_ref[...] = jnp.where(direction == 0, 0, position) * slots + pair_slot_ref[...]
    for copy in copies:
        copy.wait()

    def collect(step, _):
        for turn in range(8):
            cluster = step * 8 + turn
            masked = jnp.where(lane < fill_ref[cluster], charge_ref[pl.ds(cluster, 1), :], 0.0)
            masked_ref[pl.ds(cluster, 1), :] = masked
            place = position_ref[:, pl.ds(pl.multiple_of(cluster * 128, 128), 128)]
            own_ref[cluster, 0:3, :] = place
            own_ref[cluster, 3:4, :] = masked
        return 0

    lax.fori_loop(0, clusters // 8, collect, 0, unroll=2)

    def fill_messages(step, _):
        for position, out_ref in enumerate(out_refs):
            direction = sent_row(position, ups) if position else 0
            parts = []
            for turn in range(2):
                slot = step * 2 + turn
                live = jnp.where(slot < send_count_ref[0, direction], 1.0, 0.0)
                value = own_ref[send_index_ref[direction, slot]]
                parts.append(jnp.where(row == 3, value * live, value))
            out_ref[pl.ds(pl.multiple_of(step * 8, 8), 8), :] = jnp.concatenate(parts, axis=0)
        return 0

    lax.fori_loop(0, slots // 2, fill_messages, 0)


def prepare(fill, send_index, send_count, pair_dir, pair_slot, positions, charges):
    clusters = charges.shape[0]
    directions, slots = send_index.shape
    smem = pl.BlockSpec(memory_space=pltpu.SMEM)
    vmem = pl.BlockSpec(memory_space=pltpu.VMEM)
    return pl.pallas_call(
        prepare_kernel,
        out_shape=(
            jax.ShapeDtypeStruct(pair_dir.shape, jnp.int32),
            jax.ShapeDtypeStruct((clusters, 4, 128), jnp.float32),
            jax.ShapeDtypeStruct((clusters, 128), jnp.float32),
            *[jax.ShapeDtypeStruct((slots * 4, 128), jnp.float32)] * directions,
        ),
        in_specs=[smem] * 3 + [vmem] * 2 + [pl.BlockSpec(memory_space=pltpu.HBM)] * 2,
        out_specs=(vmem,) * (3 + directions),
        scratch_shapes=[
            *[pltpu.VMEM(operand.shape, jnp.float32) for operand in (positions, charges)],
            pltpu.SemaphoreType.DMA((2,)),
        ],
        compiler_params=pltpu.CompilerParams(vmem_limit_bytes=VMEM_LIMIT),
        name="prepare",
    )(fill, send_index, send_count, pair_dir, pair_slot, positions, charges)


def sources_kernel(
    cell_ref,
    cell_row_ref,
    masked_hbm,
    ion_hbm,
    start_hbm,
    screen_hbm,
    inverse_ref,
    source_ref,
    *refs,
):
    edge_refs, refs = (refs[:2], refs[2:])
    sum_ref, deposit_ref, masked_ref, ion_ref, start_ref, screen_ref, sems = refs
    copies = start_copies(
        (
            (masked_hbm, masked_ref),
            (ion_hbm, ion_ref),
            (start_hbm, start_ref),
            (screen_hbm, screen_ref),
        ),
        sems,
    )
    copies[0].wait()
    clusters = masked_ref.shape[0]
    cells_x, cells_y, _ = ion_ref.shape
    lane = lax.broadcasted_iota(jnp.int32, (1, 128), 1)
    ups = upward()

    def add_up(step, _):
        at = pl.ds(pl.multiple_of(step * 8, 8), 8)
        total = jnp.sum(masked_ref[at, :], axis=1, keepdims=True)
        sum_ref[at, :] = jnp.broadcast_to(deposit_scale * total, (8, 128))
        return 0

    lax.fori_loop(0, clusters // 8, add_up, 0, unroll=8)

    def place(step, _):
        for turn in range(8):
            cluster = step * 8 + turn
            index_z = lax.bitwise_and(cell_ref[cluster], 127)
            at = pl.ds(cluster, 1)
            sum_ref[at, :] = jnp.where(lane == index_z, sum_ref[at, :], 0.0)
        return 0

    lax.fori_loop(0, clusters // 8, place, 0)
    cell = cell_row_ref[...]
    line = lax.shift_right_logical(cell, CELL_BITS)
    line = (line // cells_y * 2 + lax.shift_right_logical(lax.bitwise_and(cell, 255), 7)) * cells_y
    line = line + lax.shift_right_logical(cell, CELL_BITS) % cells_y
    sums = jnp.concatenate([part.astype(jnp.bfloat16) for part in split3(sum_ref[...])], axis=1)
    block = 128
    for first in range(0, deposit_ref.shape[0], block):
        rows = lax.broadcasted_iota(jnp.int32, (block, clusters), 0) + first
        hot = jnp.where(rows == line, 1.0, 0.0).astype(jnp.bfloat16)
        added = jnp.dot(hot, sums, preferred_element_type=jnp.float32)
        deposit_ref[first : first + block, :] = added[:, :128] + (
            added[:, 128:256] + added[:, 256:]
        )
    for copy in copies[1:]:
        copy.wait()
    inverse_ref[...] = 1.0 / (6.0 + screen_ref[...])
    for index in range(cells_x):
        for half in range(2):
            lanes = slice(128 * half, 128 * half + 128)
            first = (index * 2 + half) * cells_y
            source_ref[index, :, lanes] = (
                ion_ref[index, :, lanes] + deposit_ref[first : first + cells_y, :]
            ) * inverse_ref[index, :, lanes]
    edge = 0
    for field_ref, width in zip(
        (start_ref, inverse_ref, source_ref, ion_ref), HALO_WIDTHS, strict=True
    ):
        for step in range(width):
            for phase, edge_ref in enumerate(edge_refs):
                last = ups[2] if phase == 0 else 1 - ups[2]
                plane = field_ref[last * (cells_x - width) + step]
                for half in range(2):
                    edge_ref[2 * edge + half] = plane[:, 128 * half : 128 * half + 128]
            edge += 1


def sources_of(cell, masked, ions, start, screen):
    clusters = masked.shape[0]
    cells_y = ions.shape[1]
    smem = pl.BlockSpec(memory_space=pltpu.SMEM)
    vmem = pl.BlockSpec(memory_space=pltpu.VMEM)
    edge = jax.ShapeDtypeStruct((2 * sum(HALO_WIDTHS), cells_y, 128), jnp.float32)
    return pl.pallas_call(
        sources_kernel,
        out_shape=(*[jax.ShapeDtypeStruct(ions.shape, jnp.float32)] * 2, edge, edge),
        in_specs=[smem, vmem] + [pl.BlockSpec(memory_space=pltpu.HBM)] * 4,
        out_specs=(vmem,) * 4,
        scratch_shapes=[
            pltpu.VMEM((clusters, 128), jnp.float32),
            pltpu.VMEM((ions.size // 128, 128), jnp.float32),
            *[pltpu.VMEM(operand.shape, jnp.float32) for operand in (masked, ions, start, screen)],
            pltpu.SemaphoreType.DMA((4,)),
        ],
        compiler_params=pltpu.CompilerParams(vmem_limit_bytes=VMEM_LIMIT),
        cost_estimate=pl.CostEstimate(
            flops=20_000_000, bytes_accessed=4 << 20, transcendentals=0
        ),
        name="sources",
    )(cell, cell.reshape(1, clusters), masked, ions, start, screen)


def line_rows(cells_y):
    return (cells_y + 2 * DEPTH + 7) // 8 * 8


def pack_rows_kernel(*refs):
    field_refs, edge_refs, reaction_refs, out_refs = (refs[:4], refs[4:6], refs[6:8], refs[8:10])
    cells_x, cells_y, _ = field_refs[0].shape
    base = reaction_refs[0].shape[0]
    ups = upward()
    for reaction_ref, out_ref in zip(reaction_refs, out_refs, strict=True):
        out_ref[0:base, :] = reaction_ref[...]

    def fill(out_ref, after):
        for field, width in enumerate(HALO_WIDTHS):
            offset = sum(HALO_WIDTHS[:field])
            rows = slice(cells_y - width, cells_y) if after else slice(0, width)
            for index in range(cells_x):
                value = field_refs[field][index, rows, :]
                for half in range(2):
                    at = base + ((DEPTH + index) * 2 + half) * 16 + offset
                    out_ref[at : at + width, :] = value[:, 128 * half : 128 * half + 128]
            if width == 1:
                continue
            for phase, edge_ref in enumerate(edge_refs):
                higher = ups[2] if phase == 0 else 1 - ups[2]
                for step in range(width):
                    plane = (DEPTH - width) + higher * (cells_x + width) + step
                    for half in range(2):
                        at = pl.ds(base + (plane * 2 + half) * 16 + offset, width)
                        out_ref[at, :] = edge_ref[2 * (offset + step) + half, rows, :]

    for up in range(2):

        @pl.when(ups[0] == up)
        def _(up=up):
            fill(out_refs[0], up)
            fill(out_refs[1], 1 - up)


def pack_rows(fields, edges, reactions):
    vmem = pl.BlockSpec(memory_space=pltpu.VMEM)
    cells_x = fields[0].shape[0]
    rows = reactions[0].shape[0] + (cells_x + 2 * DEPTH) * 32
    shape = jax.ShapeDtypeStruct((rows, 128), jnp.float32)
    return pl.pallas_call(
        pack_rows_kernel,
        out_shape=(shape, shape),
        in_specs=[vmem] * 8,
        out_specs=(vmem, vmem),
        compiler_params=pltpu.CompilerParams(vmem_limit_bytes=ROOMY_LIMIT),
        name="pack_rows",
    )(*fields, *edges, *reactions)


def fill_line(target_ref, plane, half, field, value, rim_ref):
    cells_y = value.shape[0]
    width = HALO_WIDTHS[field]
    at = (plane * 2 + half) * line_rows(cells_y) + DEPTH
    target_ref[pl.ds(at, cells_y), :] = value
    first = (plane * 2 + half) * 16 + sum(HALO_WIDTHS[:field])
    target_ref[pl.ds(at - width, width), :] = rim_ref[pl.ds(first, width), :]
    first = first + rim_ref.shape[0] // 2
    target_ref[pl.ds(at + cells_y, width), :] = rim_ref[pl.ds(first, width), :]


def face_flux(pot_low, pot_high, ion_low, ion_high):
    speed = -mobility * (pot_high - pot_low)
    return (
        jnp.maximum(speed, 0.0) * ion_low
        + jnp.minimum(speed, 0.0) * ion_high
        - diffusion * (ion_high - ion_low)
    )


def grid_kernel(base, *refs):
    cell_ref, masked_ref = refs[:2]
    field_refs, rims, edge_refs = (refs[2:6], refs[6:8], refs[8:10])
    potential_ref, next_ref, force_ref = refs[10:13]
    start_ref, inverse_ref, source_ref, ion_ref = refs[13:17]
    updates, resids, final_ref, pick_refs = (refs[17:20], refs[20:22], refs[22], refs[23:26])
    rim_ref = refs[26]
    cells_x, cells_y, _ = field_refs[0].shape
    rows = line_rows(cells_y)
    clusters = masked_ref.shape[0]
    ups = upward()
    size = (cells_x + 2 * DEPTH) * 32
    for rim, side in zip(rims, (ups[0], 1 - ups[0]), strict=True):
        rim_ref[pl.ds(pl.multiple_of(side * size, size), size), :] = rim[base : base + size, :]
    extended = (start_ref, inverse_ref, source_ref, ion_ref)
    for field, target_ref in enumerate(extended):

        def fill(index, _, field=field, target_ref=target_ref):
            plane = field_refs[field][index]
            for half in range(2):
                value = plane[:, 128 * half : 128 * half + 128]
                fill_line(target_ref, DEPTH + index, half, field, value, rim_ref)
            return 0

        lax.fori_loop(0, cells_x, fill, 0, unroll=4)
    for field, target_ref in enumerate(extended):
        width = HALO_WIDTHS[field]
        for phase, edge_ref in enumerate(edge_refs):
            higher = ups[2] if phase == 0 else 1 - ups[2]

            def fill_edge(step, _, field=field, target_ref=target_ref, edge_ref=edge_ref):
                width = HALO_WIDTHS[field]
                plane = (DEPTH - width) + higher * (cells_x + width) + step
                for half in range(2):
                    value = edge_ref[2 * (sum(HALO_WIDTHS[:field]) + step) + half]
                    fill_line(target_ref, plane, half, field, value, rim_ref)
                return 0

            lax.fori_loop(0, width, fill_edge, 0, unroll=True)

    lane = lax.broadcasted_iota(jnp.int32, (2 * rows, 128), 1)
    blank = jnp.zeros((rows, 128), jnp.float32)

    def beyond(value):
        right = pltpu.roll(value, 127, 1)
        left = pltpu.roll(value, 1, 1)
        above = jnp.where(lane == 127, jnp.concatenate([right[rows:], blank], axis=0), right)
        below = jnp.where(lane == 0, jnp.concatenate([blank, left[:rows]], axis=0), left)
        return (below, above)

    def whole(plane, shift=0):
        return pl.ds(plane * 2 * rows + shift, 2 * rows)

    def around(ref, plane):
        here = ref[whole(plane), :]
        below, above = beyond(here)
        sums = (ref[whole(plane - 1), :] + ref[whole(plane + 1), :]) + (
            ref[whole(plane, -1), :] + ref[whole(plane, 1), :]
        )
        return (here, sums + (below + above))

    middle = 0.5 * (highest_eig + lowest_eig)
    spread = 0.5 * (highest_eig - lowest_eig)
    assert middle == 1.0 and SWEEPS == 4

    def sweep_first(plane, _):
        here, sums = around(start_ref, plane)
        at = whole(plane)
        updates[0][at, :] = source_ref[at, :] - here + inverse_ref[at, :] * sums
        return 0

    lax.fori_loop(1, cells_x + 2 * DEPTH - 1, sweep_first, 0, unroll=2)

    ratio_ms = middle / spread
    weight_now = 1.0 / ratio_ms
    for turn in range(1, SWEEPS):
        weight_next = 1.0 / (2.0 * ratio_ms - weight_now)
        keep, gain = (weight_next * weight_now, 2.0 * weight_next / spread)
        weight_now = weight_next

        def sweep(plane, _, turn=turn, keep=keep, gain=gain):
            here, sums = around(updates[turn - 1], plane)
            at = whole(plane)
            resid = inverse_ref[at, :] * sums
            if turn > 1:
                resid = resid + (resids[turn - 2][at, :] - here)
            update = keep * here + gain * resid
            if turn + 1 < SWEEPS:
                resids[turn - 1][at, :] = resid
                updates[turn][at, :] = update
            else:
                final_ref[at, :] = (start_ref[at, :] + updates[0][at, :]) + (
                    (updates[1][at, :] + here) + update
                )
            return 0

        first = 1 + turn
        lax.fori_loop(first, cells_x + 2 * DEPTH - first, sweep, 0, unroll=2)

    def advance(index, _):
        plane = index + DEPTH
        pot = final_ref[whole(plane, DEPTH), :]
        ion = ion_ref[whole(plane, DEPTH), :]
        steps = [
            (final_ref[at, :], ion_ref[at, :])
            for at in (
                whole(plane - 1, DEPTH),
                whole(plane + 1, DEPTH),
                whole(plane, DEPTH - 1),
                whole(plane, DEPTH + 1),
            )
        ]
        steps += zip(beyond(pot), beyond(ion), strict=True)
        total = 0.0
        for low, high in zip(steps[0::2], steps[1::2], strict=True):
            total = total + (
                face_flux(pot, high[0], ion, high[1]) - face_flux(low[0], pot, low[1], ion)
            )
        result = ion - time_step * total
        for half in range(2):
            lanes = slice(128 * half, 128 * half + 128)
            kept = slice(rows * half, rows * half + cells_y)
            next_ref[index, :, lanes] = result[kept]
            potential_ref[index, :, lanes] = pot[kept]
        return 0

    lax.fori_loop(0, cells_x, advance, 0)

    row_lane = lax.broadcasted_iota(jnp.int32, (1, 128), 1)

    def pick(cluster, _):
        cell = cell_ref[cluster]
        index_x = lax.shift_right_logical(cell, CELL_BITS) // cells_y + DEPTH
        index_y = lax.shift_right_logical(cell, CELL_BITS) % cells_y + DEPTH
        index_z = lax.bitwise_and(cell, 255)
        half = lax.shift_right_logical(index_z, 7)
        here = row_lane == lax.bitwise_and(index_z, 127)

        def line(plane, row, part):
            return final_ref[pl.ds((plane * 2 + part) * rows + row, 1), :]

        along_x = line(index_x - 1, index_y, half) - line(index_x + 1, index_y, half)
        along_y = line(index_x, index_y - 1, half) - line(index_x, index_y + 1, half)
        along_z = jnp.zeros((1, 128), jnp.float32)
        for part in range(2):
            value = line(index_x, index_y, part)
            place = row_lane + 128 * part
            along_z = along_z + jnp.where(place == index_z - 1, value, 0.0)
            along_z = along_z - jnp.where(place == index_z + 1, value, 0.0)
        at = pl.ds(cluster, 1)
        pick_refs[0][at, :] = jnp.where(here, along_x, 0.0)
        pick_refs[1][at, :] = jnp.where(here, along_y, 0.0)
        pick_refs[2][at, :] = along_z
        return 0

    lax.fori_loop(0, clusters, pick, 0, unroll=8)

    def spread_out(step, _):
        start = pl.multiple_of(step * 8, 8)
        charge = masked_ref[pl.ds(start, 8), :] * (0.5 * field_scale)
        for part, pick_ref in enumerate(pick_refs):
            total = jnp.sum(pick_ref[pl.ds(start, 8), :], axis=1, keepdims=True)
            force_ref[pl.ds(4 * start + part, 8, stride=4), :] = charge * total
        force_ref[pl.ds(4 * start + 3, 8, stride=4), :] = jnp.zeros((8, 128), jnp.float32)
        return 0

    lax.fori_loop(0, clusters // 8, spread_out, 0, unroll=4)


def grid_step(cell, masked, fields, rims, edges, base):
    smem = pl.BlockSpec(memory_space=pltpu.SMEM)
    vmem = pl.BlockSpec(memory_space=pltpu.VMEM)
    clusters = masked.shape[0]
    cells_x, cells_y, _ = fields[0].shape
    block = ((cells_x + 2 * DEPTH) * 2 * line_rows(cells_y), 128)
    return pl.pallas_call(
        functools.partial(grid_kernel, base),
        out_shape=(
            jax.ShapeDtypeStruct(fields[0].shape, jnp.float32),
            jax.ShapeDtypeStruct(fields[0].shape, jnp.float32),
            jax.ShapeDtypeStruct((clusters * 4, 128), jnp.float32),
        ),
        in_specs=[smem] + [vmem] * 9,
        out_specs=(vmem,) * 3,
        scratch_shapes=[pltpu.VMEM(block, jnp.float32)] * 10
        + [pltpu.VMEM((clusters, 128), jnp.float32)] * 3
        + [pltpu.VMEM(((cells_x + 2 * DEPTH) * 64, 128), jnp.float32)],
        compiler_params=pltpu.CompilerParams(vmem_limit_bytes=ROOMY_LIMIT),
        cost_estimate=pl.CostEstimate(
            flops=block[0] * block[1] * 100, bytes_accessed=8 << 20, transcendentals=0
        ),
        name="grid_step",
    )(cell, masked, *fields, *rims, *edges)


def gather_forces_kernel(send_index_ref, *refs):
    own_ref, field_ref, *back_refs = refs[:-3]
    out_ref, sum_ref, extra_ref = refs[-3:]
    sum_ref[...] = own_ref[...]
    extra_ref[...] = field_ref[...]
    clusters = sum_ref.shape[0]
    slots = send_index_ref.shape[1]
    ups = upward()

    def visit(slot, _):
        for position, back_ref in enumerate(back_refs):
            cluster = send_index_ref[sent_row(position, ups) if position else 0, slot]
            target_ref = extra_ref if position % 2 else sum_ref
            target_ref[cluster] += back_ref[slot]
        return 0

    lax.fori_loop(0, slots, visit, 0, unroll=2)

    def write(step, _):
        for turn in range(8):
            cluster = step * 8 + turn
            total = sum_ref[cluster] + extra_ref[cluster]
            out_ref[:, pl.ds(pl.multiple_of(cluster * 128, 128), 128)] = total[0:3]
        return 0

    lax.fori_loop(0, clusters // 8, write, 0)


def gather_forces(send_index, own, field, backs):
    smem = pl.BlockSpec(memory_space=pltpu.SMEM)
    vmem = pl.BlockSpec(memory_space=pltpu.VMEM)
    clusters = own.shape[0]
    return pl.pallas_call(
        gather_forces_kernel,
        out_shape=jax.ShapeDtypeStruct((3, clusters * 128), jnp.float32),
        in_specs=[smem] + [vmem] * (2 + len(backs)),
        out_specs=vmem,
        scratch_shapes=[pltpu.VMEM(own.shape, jnp.float32)] * 2,
        compiler_params=pltpu.CompilerParams(vmem_limit_bytes=ROOMY_LIMIT),
        name="gather_forces",
    )(send_index, own, field, *backs)


def shards(
    positions,
    charges,
    cluster_fill,
    cluster_cell,
    send_index,
    send_count,
    pair_local,
    pair_dir,
    pair_slot,
    ion_density,
    potential_prev,
    screening,
):
    clusters = cluster_fill.shape[0]
    psize = charges.shape[0] // clusters
    slots = send_index.shape[1]
    base = slots * 4
    other_rows, own, masked, local, *messages = prepare(
        cluster_fill,
        send_index,
        send_count,
        pair_dir.reshape(-1, 128),
        pair_slot.reshape(-1, 128),
        positions,
        charges.reshape(clusters, psize),
    )
    inverse, source, *edges = sources_of(
        cluster_cell, masked, ion_density, potential_prev, screening
    )
    arrived = [local] + [
        swapped(message, *swap)
        for message, swap in zip(messages, SWAPS, strict=True)
    ]
    fields = (potential_prev, inverse, source, ion_density)
    arrived, edges = lax.optimization_barrier((arrived, edges))
    edges = [swapped(edge, "grp", 1, phase) for phase, edge in enumerate(edges)]
    own_force, *reactions = pair_forces(
        pair_local,
        other_rows.reshape(-1),
        own.reshape(clusters * 4, psize),
        arrived,
        slots,
    )
    local_back, *reactions = reactions
    rims = pack_rows(fields, edges, reactions[:2])
    backs = [
        swapped(reaction, *swap)
        for reaction, swap in zip((*rims, *reactions[2:]), SWAPS, strict=True)
    ]
    potential, ion_next, field_force = grid_step(
        cluster_cell, masked, fields, backs[:2], edges, base
    )
    forces = gather_forces(
        send_index,
        own_force.reshape(clusters, 4, psize),
        field_force.reshape(clusters, 4, psize),
        [back.reshape(-1, 4, psize) for back in (local_back, *backs)],
    )
    return (forces, potential, ion_next)


def solution(mesh):
    in_specs = (
        P(None, ("grp", "brick")),
        P(("grp", "brick")),
        P(("grp", "brick")),
        P(("grp", "brick")),
        P(("grp", "brick"), None),
        P(("grp", "brick"), None),
        P(("grp", "brick")),
        P(("grp", "brick")),
        P(("grp", "brick")),
        P("grp", "brick", None),
        P("grp", "brick", None),
        P("grp", "brick", None),
    )
    out_specs = (P(None, ("grp", "brick")), P("grp", "brick", None), P("grp", "brick", None))
    return jax.shard_map(shards, mesh=mesh, in_specs=in_specs, out_specs=out_specs, check_vma=False)
```

```python
import functools

import jax
import jax.numpy as jnp
import numpy as np
from jax import lax
from jax.experimental import pallas as pl
from jax.experimental.pallas import tpu as pltpu
from jax.sharding import PartitionSpec as P

SWEEPS = 4
UNROLL = 8
CHUNKS = 4
AHEAD = 2
BEHIND = 4
BATCH = 4
HALO_WIDTHS = (SWEEPS + 1, SWEEPS, SWEEPS, 1)
DEPTH = SWEEPS + 1
CELL_BITS = 8
SWAPS = tuple(
    (*way, phase) for way in (("brick", 1), ("brick", 2), ("grp", 1)) for phase in (0, 1)
)


coulomb_scale = 0.02
softening = 0.1
field_scale = 0.5
deposit_scale = 0.2
lowest_eig = 0.01
highest_eig = 1.99
mobility = 0.3
diffusion = 0.2
time_step = 0.2


VMEM_LIMIT = 60 * 1024 * 1024
ROOMY_LIMIT = 48 * 1024 * 1024


def start_copies(pairs, sems):
    copies = [
        pltpu.make_async_copy(source, target, sems.at[index])
        for index, (source, target) in enumerate(pairs)
    ]
    for copy in copies:
        copy.start()
    return copies


def upward():
    brick, grp = (lax.axis_index("brick"), lax.axis_index("grp"))
    bits = (brick, lax.shift_right_logical(brick, 1), grp)
    return [1 - lax.bitwise_and(bit, 1) for bit in bits]


def sent_row(position, ups):
    way, phase = ((position - 1) // 2, (position - 1) % 2)
    return 1 + 2 * way + (ups[way] if phase else 1 - ups[way])


def swapped(shard, axis, distance, phase):
    devices = lax.axis_size(axis)
    pairs = []
    for index in range(devices):
        step = distance if (index // distance + phase) % 2 == 0 else -distance
        if 0 <= index + step < devices:
            pairs.append((index, index + step))
    return lax.ppermute(shard, axis, pairs)


def split3(value):
    first = value.astype(jnp.bfloat16).astype(jnp.float32)
    rest = value - first
    second = rest.astype(jnp.bfloat16).astype(jnp.float32)
    third = (rest - second).astype(jnp.bfloat16).astype(jnp.float32)
    return (first, second, third)


def moment_pieces(comps, charge):
    rows = [None] * 12
    for part, charged in enumerate((*comps, None)):
        for level, piece in enumerate(split3(charge if charged is None else charge * charged)):
            rows[4 * level + part] = piece
    return rows


def selections():
    near_kinds, far_kinds = ([], [])
    for part in range(3):
        near_kinds += [3 * part + level for level in (0, 0, 0, 1, 1, 2)]
        far_kinds += [3 * part + level for level in (0, 1, 2, 0, 1, 0)]
    near_kinds += [9, 10, 11, 12, 12, 12]
    far_kinds += [12, 12, 12, 9, 10, 11]
    near = np.zeros((128, 1024), np.float32)
    far = np.zeros((256, 128), np.float32)
    moment = np.zeros((128, 128), np.float32)
    for cluster in range(8):
        for index, kind in enumerate(near_kinds):
            near[kind * 8 + cluster, cluster * 128 + index] = 1.0
        for index, kind in enumerate(far_kinds):
            far[cluster * 32 + index, kind * 8 + cluster] = 1.0
        for kind in range(12):
            moment[cluster * 16 + kind, kind * 8 + cluster] = 1.0
    return tuple(jnp.asarray(part, jnp.bfloat16) for part in (near, far, moment))


def pair_kernel(own_rows_ref, other_rows_ref, *refs):
    sources = len(SWAPS) + 1
    fetched = sources + 4
    hbm_refs = refs[:fetched]
    own_out_ref = refs[fetched]
    other_out_refs = refs[fetched + 1 : fetched + 1 + sources]
    refs = refs[fetched + 1 + sources :]
    near_sel_ref, far_sel_ref, moment_sel_ref, own_ref = refs[:4]
    other_refs = refs[4:fetched]
    sems = refs[fetched]
    copies = start_copies(
        [
            (source.at[0 : target.shape[0]], target)
            for source, target in zip(hbm_refs, refs[:fetched], strict=True)
        ],
        sems,
    )
    (
        near_ref,
        far_ref,
        own_moment_ref,
        other_moment_ref,
        own_sum_ref,
        other_sum_ref,
        dist_ref,
        *weight_refs,
    ) = refs[fetched + 1 :]
    clusters = own_ref.shape[0] // 4
    slots = other_out_refs[0].shape[0] // 4
    others = slots * sources
    groups = own_rows_ref.shape[0] // UNROLL
    ones = jnp.ones((8, 128), jnp.float32)
    zeros = jnp.zeros((8, 128), jnp.float32)

    def components(data_ref, start):
        return [data_ref[pl.ds(4 * start + part, 8, stride=4), :] for part in range(4)]

    def place_pieces(comps, factor, offset):
        pieces = []
        square = zeros
        for comp in comps:
            square = square + comp * comp
            pieces += split3(factor * comp)
        pieces += [*split3(square + offset), ones]
        return jnp.concatenate(pieces + [zeros] * (16 - len(pieces)), axis=0)

    def selected(left, right):
        return jnp.dot(
            left.astype(jnp.bfloat16), right, preferred_element_type=jnp.float32
        ).astype(jnp.bfloat16)

    def stacked(moments):
        return jnp.concatenate(moments + [zeros] * 4, axis=0).astype(jnp.bfloat16)

    def near_rows(step, _):
        starts = [pl.multiple_of(step * 8 * BATCH + 8 * index, 8) for index in range(BATCH)]
        parts = [components(own_ref, start) for start in starts]
        turned = [place_pieces(part[:3], 1.0, 0.0).T.astype(jnp.bfloat16) for part in parts]
        moments = [stacked(moment_pieces(part[:3], part[3])) for part in parts]
        placed = [selected(moment_sel_ref[...], moment) for moment in moments]
        for start, rows in zip(starts, placed, strict=True):
            own_moment_ref[pl.ds(pl.multiple_of(start * 16, 128), 128), :] = rows
        for start, pieces in zip(starts, turned, strict=True):
            tiles = selected(pieces, near_sel_ref[...])
            for index in range(8):
                at = pl.ds(pl.multiple_of((start + index) * 128, 128), 128)
                near_ref[at, :] = tiles[:, 128 * index : 128 * index + 128]
        return 0

    def far_rows(source):
        locals_ = range(0, slots, 8)
        parts = [components(other_refs[source], local) for local in locals_]
        pieces = [place_pieces(part[:3], -2.0, softening).astype(jnp.bfloat16) for part in parts]
        moments = [stacked(moment_pieces(part[:3], part[3])) for part in parts]
        rows = [selected(far_sel_ref[...], piece) for piece in pieces]
        placed = [selected(moment_sel_ref[...], moment) for moment in moments]
        for local, row, moment in zip(locals_, rows, placed, strict=True):
            start = source * slots + local
            far_ref[start * 32 : start * 32 + 256, :] = row
            other_moment_ref[start * 16 : start * 16 + 128, :] = moment

    own_sum_ref[...] = jnp.zeros_like(own_sum_ref)
    other_sum_ref[...] = jnp.zeros_like(other_sum_ref)
    weight_refs[0][...] = jnp.zeros_like(weight_refs[0])
    for copy in copies[:4]:
        copy.wait()
    lax.fori_loop(0, clusters // (8 * BATCH), near_rows, 0)
    for copy in copies[4:]:
        copy.wait()
    for source in range(sources):
        far_rows(source)
    def distances(pair):
        own = own_rows_ref[pair]
        other = other_rows_ref[pair]
        return jnp.dot(
            near_ref[pl.ds(pl.multiple_of(own * 128, 128), 128), 0:32],
            far_ref[pl.ds(pl.multiple_of(other * 32, 32), 32), :],
            preferred_element_type=jnp.float32,
        )

    def weights(dist, index, chunk, weight_ref):
        rows = 128 // CHUNKS
        first = rows * chunk
        root = lax.rsqrt(dist[first : first + rows])
        weight = root * root * root
        high = weight.astype(jnp.bfloat16)
        low = (weight - high.astype(jnp.float32)).astype(jnp.bfloat16)
        at = slice(128 * index + first, 128 * index + first + rows)
        weight_ref[at, :128] = high
        weight_ref[at, 128:] = low

    def row_block(index):
        return pl.ds(pl.multiple_of(index * 16, 16), 16)

    def own_product(other, weight_ref, index):
        both = weight_ref[128 * index : 128 * index + 128]
        return lax.dot_general(
            other_moment_ref[row_block(other), :],
            jnp.concatenate([both[:, :128], both[:, 128:]], axis=0),
            (((1,), (1,)), ((), ())),
            preferred_element_type=jnp.float32,
        )

    def other_product(own, weight_ref, index):
        return jnp.dot(
            own_moment_ref[row_block(own), :],
            weight_ref[128 * index : 128 * index + 128],
            preferred_element_type=jnp.float32,
        )

    def add_rows(own, other, to_own, to_other):
        own_sum_ref[row_block(own), :] += to_own[:, :128] + to_own[:, 128:]
        other_sum_ref[row_block(other), :] += to_other[:, :128] + to_other[:, 128:]

    def half_step(step, side, dists):
        last = jnp.maximum(step - 1, 0) * UNROLL
        waiting = []
        for index in range(UNROLL):
            own = own_rows_ref[last + index]
            other = other_rows_ref[last + index]
            coming = step * UNROLL + index + AHEAD
            later = distances(jnp.minimum(coming, groups * UNROLL - 1))
            weights(dists[0], index, 0, weight_refs[1 - side])
            to_own = own_product(other, weight_refs[side], index)
            weights(dists[0], index, 1, weight_refs[1 - side])
            weights(dists[0], index, 2, weight_refs[1 - side])
            to_other = other_product(own, weight_refs[side], index)
            weights(dists[0], index, 3, weight_refs[1 - side])
            dists = [*dists[1:], later]
            waiting.append((own, other, to_own, to_other))
            if len(waiting) > BEHIND:
                add_rows(*waiting.pop(0))
        for entry in waiting:
            add_rows(*entry)
        return dists

    def visit(step, _):
        dists = [dist_ref[index] for index in range(AHEAD)]
        for side in range(2):
            dists = half_step(step * 2 + side, side, dists)
        for index in range(AHEAD):
            dist_ref[index] = dists[index]
        return 0

    for index in range(AHEAD):
        dist_ref[index] = distances(index)
    lax.fori_loop(0, groups // 2, visit, 0)
    half_step(groups, 0, [dist_ref[index] for index in range(AHEAD)])

    def finish(data_ref, out_ref, sum_ref, base, step, _):
        starts = [pl.multiple_of(step * 8 * BATCH + 8 * index, 8) for index in range(BATCH)]
        parts = [components(data_ref, start) for start in starts]

        def total(start, part):
            terms = [
                sum_ref[pl.ds(base + start * 16 + 4 * level + part, 8, stride=16), :]
                for level in range(3)
            ]
            return terms[0] + (terms[1] + terms[2])

        totals = [[total(start, part) for part in range(4)] for start in starts]
        for start, (*comps, charge), sums in zip(starts, parts, totals, strict=True):
            scale = coulomb_scale * charge
            for part, comp in enumerate(comps):
                out_ref[pl.ds(4 * start + part, 8, stride=4), :] = scale * (
                    comp * sums[3] - sums[part]
                )
            out_ref[pl.ds(4 * start + 3, 8, stride=4), :] = zeros
        return 0

    lax.fori_loop(
        0,
        clusters // (8 * BATCH),
        functools.partial(finish, own_ref, own_out_ref, own_sum_ref, 0),
        0,
    )
    for source in range(sources):
        body = functools.partial(
            finish, other_refs[source], other_out_refs[source], other_sum_ref, source * slots * 16
        )
        lax.fori_loop(0, slots // (8 * BATCH), body, 0)


def pair_forces(own_rows, other_rows, own, arrived, slots):
    clusters = own.shape[0] // 4
    others = slots * len(arrived)
    pairs = own_rows.shape[0]
    smem = pl.BlockSpec(memory_space=pltpu.SMEM)
    vmem = pl.BlockSpec(memory_space=pltpu.VMEM)
    hbm = pl.BlockSpec(memory_space=pl.ANY)
    operands = (*selections(), own)
    return pl.pallas_call(
        pair_kernel,
        out_shape=(
            jax.ShapeDtypeStruct(own.shape, jnp.float32),
            *[jax.ShapeDtypeStruct((slots * 4, 128), jnp.float32)] * len(arrived),
        ),
        in_specs=[smem, smem] + [hbm] * (4 + len(arrived)),
        out_specs=(vmem,) * (len(arrived) + 1),
        scratch_shapes=[
            *[pltpu.VMEM(operand.shape, operand.dtype) for operand in operands],
            *[pltpu.VMEM((slots * 4, 128), jnp.float32)] * len(arrived),
            pltpu.SemaphoreType.DMA((len(operands) + len(arrived),)),
            pltpu.VMEM((clusters * 128, 128), jnp.bfloat16),
            pltpu.VMEM((others * 32, 128), jnp.bfloat16),
            pltpu.VMEM((clusters * 16, 128), jnp.bfloat16),
            pltpu.VMEM((others * 16, 128), jnp.bfloat16),
            pltpu.VMEM((clusters * 16, 128), jnp.float32),
            pltpu.VMEM((others * 16, 128), jnp.float32),
            pltpu.VMEM((AHEAD, 128, 128), jnp.float32),
            *[pltpu.VMEM((128 * UNROLL, 256), jnp.bfloat16)] * 2,
        ],
        compiler_params=pltpu.CompilerParams(vmem_limit_bytes=ROOMY_LIMIT),
        cost_estimate=pl.CostEstimate(
            flops=pairs * 128 * 128 * 20, bytes_accessed=4 * 1024 * 1024, transcendentals=0
        ),
        name="pair_forces",
    )(own_rows, other_rows, *operands, *arrived)


def prepare_kernel(
    fill_ref,
    send_index_ref,
    send_count_ref,
    pair_dir_ref,
    pair_slot_ref,
    position_hbm,
    charge_hbm,
    row_ref,
    own_ref,
    masked_ref,
    *refs,
):
    out_refs, (position_ref, charge_ref, sems) = (refs[:-3], refs[-3:])
    copies = start_copies(((position_hbm, position_ref), (charge_hbm, charge_ref)), sems)
    clusters = charge_ref.shape[0]
    slots = send_index_ref.shape[1]
    lane = lax.broadcasted_iota(jnp.int32, (1, 128), 1)
    row = lax.broadcasted_iota(jnp.int32, (4, 128), 0)
    ups = upward()
    direction = pair_dir_ref[...]
    way = lax.shift_right_arithmetic(direction - 1, 1)
    flip = jnp.where(way == 0, ups[0], jnp.where(way == 1, ups[1], ups[2]))
    position = 1 + 2 * way + lax.bitwise_xor(lax.bitwise_and(direction - 1, 1), flip)
    row_ref[...] = jnp.where(direction == 0, 0, position) * slots + pair_slot_ref[...]
    for copy in copies:
        copy.wait()

    def collect(step, _):
        for turn in range(8):
            cluster = step * 8 + turn
            masked = jnp.where(lane < fill_ref[cluster], charge_ref[pl.ds(cluster, 1), :], 0.0)
            masked_ref[pl.ds(cluster, 1), :] = masked
            place = position_ref[:, pl.ds(pl.multiple_of(cluster * 128, 128), 128)]
            own_ref[cluster, 0:3, :] = place
            own_ref[cluster, 3:4, :] = masked
        return 0

    lax.fori_loop(0, clusters // 8, collect, 0, unroll=2)

    def fill_messages(step, _):
        for position, out_ref in enumerate(out_refs):
            direction = sent_row(position, ups) if position else 0
            parts = []
            for turn in range(2):
                slot = step * 2 + turn
                live = jnp.where(slot < send_count_ref[0, direction], 1.0, 0.0)
                value = own_ref[send_index_ref[direction, slot]]
                parts.append(jnp.where(row == 3, value * live, value))
            out_ref[pl.ds(pl.multiple_of(step * 8, 8), 8), :] = jnp.concatenate(parts, axis=0)
        return 0

    lax.fori_loop(0, slots // 2, fill_messages, 0)


def prepare(fill, send_index, send_count, pair_dir, pair_slot, positions, charges):
    clusters = charges.shape[0]
    directions, slots = send_index.shape
    smem = pl.BlockSpec(memory_space=pltpu.SMEM)
    vmem = pl.BlockSpec(memory_space=pltpu.VMEM)
    return pl.pallas_call(
        prepare_kernel,
        out_shape=(
            jax.ShapeDtypeStruct(pair_dir.shape, jnp.int32),
            jax.ShapeDtypeStruct((clusters, 4, 128), jnp.float32),
            jax.ShapeDtypeStruct((clusters, 128), jnp.float32),
            *[jax.ShapeDtypeStruct((slots * 4, 128), jnp.float32)] * directions,
        ),
        in_specs=[smem] * 3 + [vmem] * 2 + [pl.BlockSpec(memory_space=pltpu.HBM)] * 2,
        out_specs=(vmem,) * (3 + directions),
        scratch_shapes=[
            *[pltpu.VMEM(operand.shape, jnp.float32) for operand in (positions, charges)],
            pltpu.SemaphoreType.DMA((2,)),
        ],
        compiler_params=pltpu.CompilerParams(vmem_limit_bytes=VMEM_LIMIT),
        name="prepare",
    )(fill, send_index, send_count, pair_dir, pair_slot, positions, charges)


def sources_kernel(
    cell_ref,
    cell_row_ref,
    masked_hbm,
    ion_hbm,
    start_hbm,
    screen_hbm,
    inverse_ref,
    source_ref,
    *refs,
):
    edge_refs, refs = (refs[:2], refs[2:])
    sum_ref, deposit_ref, masked_ref, ion_ref, start_ref, screen_ref, sems = refs
    copies = start_copies(
        (
            (masked_hbm, masked_ref),
            (ion_hbm, ion_ref),
            (start_hbm, start_ref),
            (screen_hbm, screen_ref),
        ),
        sems,
    )
    copies[0].wait()
    clusters = masked_ref.shape[0]
    cells_x, cells_y, _ = ion_ref.shape
    lane = lax.broadcasted_iota(jnp.int32, (1, 128), 1)
    ups = upward()

    def add_up(step, _):
        at = pl.ds(pl.multiple_of(step * 8, 8), 8)
        total = jnp.sum(masked_ref[at, :], axis=1, keepdims=True)
        sum_ref[at, :] = jnp.broadcast_to(deposit_scale * total, (8, 128))
        return 0

    lax.fori_loop(0, clusters // 8, add_up, 0, unroll=8)

    def place(step, _):
        for turn in range(8):
            cluster = step * 8 + turn
            index_z = lax.bitwise_and(cell_ref[cluster], 127)
            at = pl.ds(cluster, 1)
            sum_ref[at, :] = jnp.where(lane == index_z, sum_ref[at, :], 0.0)
        return 0

    lax.fori_loop(0, clusters // 8, place, 0)
    cell = cell_row_ref[...]
    line = lax.shift_right_logical(cell, CELL_BITS)
    line = (line // cells_y * 2 + lax.shift_right_logical(lax.bitwise_and(cell, 255), 7)) * cells_y
    line = line + lax.shift_right_logical(cell, CELL_BITS) % cells_y
    sums = jnp.concatenate([part.astype(jnp.bfloat16) for part in split3(sum_ref[...])], axis=1)
    block = 128
    for first in range(0, deposit_ref.shape[0], block):
        rows = lax.broadcasted_iota(jnp.int32, (block, clusters), 0) + first
        hot = jnp.where(rows == line, 1.0, 0.0).astype(jnp.bfloat16)
        added = jnp.dot(hot, sums, preferred_element_type=jnp.float32)
        deposit_ref[first : first + block, :] = added[:, :128] + (
            added[:, 128:256] + added[:, 256:]
        )
    for copy in copies[1:]:
        copy.wait()
    inverse_ref[...] = 1.0 / (6.0 + screen_ref[...])
    for index in range(cells_x):
        for half in range(2):
            lanes = slice(128 * half, 128 * half + 128)
            first = (index * 2 + half) * cells_y
            source_ref[index, :, lanes] = (
                ion_ref[index, :, lanes] + deposit_ref[first : first + cells_y, :]
            ) * inverse_ref[index, :, lanes]
    edge = 0
    for field_ref, width in zip(
        (start_ref, inverse_ref, source_ref, ion_ref), HALO_WIDTHS, strict=True
    ):
        for step in range(width):
            for phase, edge_ref in enumerate(edge_refs):
                last = ups[2] if phase == 0 else 1 - ups[2]
                plane = field_ref[last * (cells_x - width) + step]
                for half in range(2):
                    edge_ref[2 * edge + half] = plane[:, 128 * half : 128 * half + 128]
            edge += 1


def sources_of(cell, masked, ions, start, screen):
    clusters = masked.shape[0]
    cells_y = ions.shape[1]
    smem = pl.BlockSpec(memory_space=pltpu.SMEM)
    vmem = pl.BlockSpec(memory_space=pltpu.VMEM)
    edge = jax.ShapeDtypeStruct((2 * sum(HALO_WIDTHS), cells_y, 128), jnp.float32)
    return pl.pallas_call(
        sources_kernel,
        out_shape=(*[jax.ShapeDtypeStruct(ions.shape, jnp.float32)] * 2, edge, edge),
        in_specs=[smem, vmem] + [pl.BlockSpec(memory_space=pltpu.HBM)] * 4,
        out_specs=(vmem,) * 4,
        scratch_shapes=[
            pltpu.VMEM((clusters, 128), jnp.float32),
            pltpu.VMEM((ions.size // 128, 128), jnp.float32),
            *[pltpu.VMEM(operand.shape, jnp.float32) for operand in (masked, ions, start, screen)],
            pltpu.SemaphoreType.DMA((4,)),
        ],
        compiler_params=pltpu.CompilerParams(vmem_limit_bytes=VMEM_LIMIT),
        cost_estimate=pl.CostEstimate(
            flops=20_000_000, bytes_accessed=4 << 20, transcendentals=0
        ),
        name="sources",
    )(cell, cell.reshape(1, clusters), masked, ions, start, screen)


def line_rows(cells_y):
    return (cells_y + 2 * DEPTH + 7) // 8 * 8


def pack_rows_kernel(*refs):
    field_refs, edge_refs, reaction_refs, out_refs = (refs[:4], refs[4:6], refs[6:8], refs[8:10])
    cells_x, cells_y, _ = field_refs[0].shape
    base = reaction_refs[0].shape[0]
    ups = upward()
    for reaction_ref, out_ref in zip(reaction_refs, out_refs, strict=True):
        out_ref[0:base, :] = reaction_ref[...]

    def fill(out_ref, after):
        for field, width in enumerate(HALO_WIDTHS):
            offset = sum(HALO_WIDTHS[:field])
            rows = slice(cells_y - width, cells_y) if after else slice(0, width)
            for index in range(cells_x):
                value = field_refs[field][index, rows, :]
                for half in range(2):
                    at = base + ((DEPTH + index) * 2 + half) * 16 + offset
                    out_ref[at : at + width, :] = value[:, 128 * half : 128 * half + 128]
            if width == 1:
                continue
            for phase, edge_ref in enumerate(edge_refs):
                higher = ups[2] if phase == 0 else 1 - ups[2]
                for step in range(width):
                    plane = (DEPTH - width) + higher * (cells_x + width) + step
                    for half in range(2):
                        at = pl.ds(base + (plane * 2 + half) * 16 + offset, width)
                        out_ref[at, :] = edge_ref[2 * (offset + step) + half, rows, :]

    for up in range(2):

        @pl.when(ups[0] == up)
        def _(up=up):
            fill(out_refs[0], up)
            fill(out_refs[1], 1 - up)


def pack_rows(fields, edges, reactions):
    vmem = pl.BlockSpec(memory_space=pltpu.VMEM)
    cells_x = fields[0].shape[0]
    rows = reactions[0].shape[0] + (cells_x + 2 * DEPTH) * 32
    shape = jax.ShapeDtypeStruct((rows, 128), jnp.float32)
    return pl.pallas_call(
        pack_rows_kernel,
        out_shape=(shape, shape),
        in_specs=[vmem] * 8,
        out_specs=(vmem, vmem),
        compiler_params=pltpu.CompilerParams(vmem_limit_bytes=ROOMY_LIMIT),
        name="pack_rows",
    )(*fields, *edges, *reactions)


def fill_line(target_ref, plane, half, field, value, rim_ref):
    cells_y = value.shape[0]
    width = HALO_WIDTHS[field]
    at = (plane * 2 + half) * line_rows(cells_y) + DEPTH
    target_ref[pl.ds(at, cells_y), :] = value
    first = (plane * 2 + half) * 16 + sum(HALO_WIDTHS[:field])
    target_ref[pl.ds(at - width, width), :] = rim_ref[pl.ds(first, width), :]
    first = first + rim_ref.shape[0] // 2
    target_ref[pl.ds(at + cells_y, width), :] = rim_ref[pl.ds(first, width), :]


def face_flux(pot_low, pot_high, ion_low, ion_high):
    speed = -mobility * (pot_high - pot_low)
    return (
        jnp.maximum(speed, 0.0) * ion_low
        + jnp.minimum(speed, 0.0) * ion_high
        - diffusion * (ion_high - ion_low)
    )


def grid_kernel(base, *refs):
    cell_ref, masked_ref = refs[:2]
    field_refs, rims, edge_refs = (refs[2:6], refs[6:8], refs[8:10])
    potential_ref, next_ref, force_ref = refs[10:13]
    start_ref, inverse_ref, source_ref, ion_ref = refs[13:17]
    updates, resids, final_ref, pick_refs = (refs[17:20], refs[20:22], refs[22], refs[23:26])
    rim_ref = refs[26]
    cells_x, cells_y, _ = field_refs[0].shape
    rows = line_rows(cells_y)
    clusters = masked_ref.shape[0]
    ups = upward()
    size = (cells_x + 2 * DEPTH) * 32
    for rim, side in zip(rims, (ups[0], 1 - ups[0]), strict=True):
        rim_ref[pl.ds(pl.multiple_of(side * size, size), size), :] = rim[base : base + size, :]
    extended = (start_ref, inverse_ref, source_ref, ion_ref)
    for field, target_ref in enumerate(extended):

        def fill(index, _, field=field, target_ref=target_ref):
            plane = field_refs[field][index]
            for half in range(2):
                value = plane[:, 128 * half : 128 * half + 128]
                fill_line(target_ref, DEPTH + index, half, field, value, rim_ref)
            return 0

        lax.fori_loop(0, cells_x, fill, 0, unroll=4)
    for field, target_ref in enumerate(extended):
        width = HALO_WIDTHS[field]
        for phase, edge_ref in enumerate(edge_refs):
            higher = ups[2] if phase == 0 else 1 - ups[2]

            def fill_edge(step, _, field=field, target_ref=target_ref, edge_ref=edge_ref):
                width = HALO_WIDTHS[field]
                plane = (DEPTH - width) + higher * (cells_x + width) + step
                for half in range(2):
                    value = edge_ref[2 * (sum(HALO_WIDTHS[:field]) + step) + half]
                    fill_line(target_ref, plane, half, field, value, rim_ref)
                return 0

            lax.fori_loop(0, width, fill_edge, 0, unroll=True)

    lane = lax.broadcasted_iota(jnp.int32, (2 * rows, 128), 1)
    blank = jnp.zeros((rows, 128), jnp.float32)

    def beyond(value):
        right = pltpu.roll(value, 127, 1)
        left = pltpu.roll(value, 1, 1)
        above = jnp.where(lane == 127, jnp.concatenate([right[rows:], blank], axis=0), right)
        below = jnp.where(lane == 0, jnp.concatenate([blank, left[:rows]], axis=0), left)
        return (below, above)

    def whole(plane, shift=0):
        return pl.ds(plane * 2 * rows + shift, 2 * rows)

    def around(ref, plane):
        here = ref[whole(plane), :]
        below, above = beyond(here)
        sums = (ref[whole(plane - 1), :] + ref[whole(plane + 1), :]) + (
            ref[whole(plane, -1), :] + ref[whole(plane, 1), :]
        )
        return (here, sums + (below + above))

    middle = 0.5 * (highest_eig + lowest_eig)
    spread = 0.5 * (highest_eig - lowest_eig)
    assert middle == 1.0 and SWEEPS == 4

    def sweep_first(plane, _):
        here, sums = around(start_ref, plane)
        at = whole(plane)
        updates[0][at, :] = source_ref[at, :] - here + inverse_ref[at, :] * sums
        return 0

    lax.fori_loop(1, cells_x + 2 * DEPTH - 1, sweep_first, 0, unroll=2)

    ratio_ms = middle / spread
    weight_now = 1.0 / ratio_ms
    for turn in range(1, SWEEPS):
        weight_next = 1.0 / (2.0 * ratio_ms - weight_now)
        keep, gain = (weight_next * weight_now, 2.0 * weight_next / spread)
        weight_now = weight_next

        def sweep(plane, _, turn=turn, keep=keep, gain=gain):
            here, sums = around(updates[turn - 1], plane)
            at = whole(plane)
            resid = inverse_ref[at, :] * sums
            if turn > 1:
                resid = resid + (resids[turn - 2][at, :] - here)
            update = keep * here + gain * resid
            if turn + 1 < SWEEPS:
                resids[turn - 1][at, :] = resid
                updates[turn][at, :] = update
            else:
                final_ref[at, :] = (start_ref[at, :] + updates[0][at, :]) + (
                    (updates[1][at, :] + here) + update
                )
            return 0

        first = 1 + turn
        lax.fori_loop(first, cells_x + 2 * DEPTH - first, sweep, 0, unroll=2)

    def advance(index, _):
        plane = index + DEPTH
        pot = final_ref[whole(plane, DEPTH), :]
        ion = ion_ref[whole(plane, DEPTH), :]
        steps = [
            (final_ref[at, :], ion_ref[at, :])
            for at in (
                whole(plane - 1, DEPTH),
                whole(plane + 1, DEPTH),
                whole(plane, DEPTH - 1),
                whole(plane, DEPTH + 1),
            )
        ]
        steps += zip(beyond(pot), beyond(ion), strict=True)
        total = 0.0
        for low, high in zip(steps[0::2], steps[1::2], strict=True):
            total = total + (
                face_flux(pot, high[0], ion, high[1]) - face_flux(low[0], pot, low[1], ion)
            )
        result = ion - time_step * total
        for half in range(2):
            lanes = slice(128 * half, 128 * half + 128)
            kept = slice(rows * half, rows * half + cells_y)
            next_ref[index, :, lanes] = result[kept]
            potential_ref[index, :, lanes] = pot[kept]
        return 0

    lax.fori_loop(0, cells_x, advance, 0)

    row_lane = lax.broadcasted_iota(jnp.int32, (1, 128), 1)

    def pick(cluster, _):
        cell = cell_ref[cluster]
        index_x = lax.shift_right_logical(cell, CELL_BITS) // cells_y + DEPTH
        index_y = lax.shift_right_logical(cell, CELL_BITS) % cells_y + DEPTH
        index_z = lax.bitwise_and(cell, 255)
        half = lax.shift_right_logical(index_z, 7)
        here = row_lane == lax.bitwise_and(index_z, 127)

        def line(plane, row, part):
            return final_ref[pl.ds((plane * 2 + part) * rows + row, 1), :]

        along_x = line(index_x - 1, index_y, half) - line(index_x + 1, index_y, half)
        along_y = line(index_x, index_y - 1, half) - line(index_x, index_y + 1, half)
        along_z = jnp.zeros((1, 128), jnp.float32)
        for part in range(2):
            value = line(index_x, index_y, part)
            place = row_lane + 128 * part
            along_z = along_z + jnp.where(place == index_z - 1, value, 0.0)
            along_z = along_z - jnp.where(place == index_z + 1, value, 0.0)
        at = pl.ds(cluster, 1)
        pick_refs[0][at, :] = jnp.where(here, along_x, 0.0)
        pick_refs[1][at, :] = jnp.where(here, along_y, 0.0)
        pick_refs[2][at, :] = along_z
        return 0

    lax.fori_loop(0, clusters, pick, 0, unroll=16)

    def spread_out(step, _):
        start = pl.multiple_of(step * 8, 8)
        charge = masked_ref[pl.ds(start, 8), :] * (0.5 * field_scale)
        for part, pick_ref in enumerate(pick_refs):
            total = jnp.sum(pick_ref[pl.ds(start, 8), :], axis=1, keepdims=True)
            force_ref[pl.ds(4 * start + part, 8, stride=4), :] = charge * total
        force_ref[pl.ds(4 * start + 3, 8, stride=4), :] = jnp.zeros((8, 128), jnp.float32)
        return 0

    lax.fori_loop(0, clusters // 8, spread_out, 0, unroll=4)


def grid_step(cell, masked, fields, rims, edges, base):
    smem = pl.BlockSpec(memory_space=pltpu.SMEM)
    vmem = pl.BlockSpec(memory_space=pltpu.VMEM)
    clusters = masked.shape[0]
    cells_x, cells_y, _ = fields[0].shape
    block = ((cells_x + 2 * DEPTH) * 2 * line_rows(cells_y), 128)
    return pl.pallas_call(
        functools.partial(grid_kernel, base),
        out_shape=(
            jax.ShapeDtypeStruct(fields[0].shape, jnp.float32),
            jax.ShapeDtypeStruct(fields[0].shape, jnp.float32),
            jax.ShapeDtypeStruct((clusters * 4, 128), jnp.float32),
        ),
        in_specs=[smem] + [vmem] * 9,
        out_specs=(vmem,) * 3,
        scratch_shapes=[pltpu.VMEM(block, jnp.float32)] * 10
        + [pltpu.VMEM((clusters, 128), jnp.float32)] * 3
        + [pltpu.VMEM(((cells_x + 2 * DEPTH) * 64, 128), jnp.float32)],
        compiler_params=pltpu.CompilerParams(vmem_limit_bytes=ROOMY_LIMIT),
        cost_estimate=pl.CostEstimate(
            flops=block[0] * block[1] * 100, bytes_accessed=8 << 20, transcendentals=0
        ),
        name="grid_step",
    )(cell, masked, *fields, *rims, *edges)


def gather_forces_kernel(send_index_ref, *refs):
    own_ref, field_ref, *back_refs = refs[:-3]
    out_ref, sum_ref, extra_ref = refs[-3:]
    sum_ref[...] = own_ref[...]
    extra_ref[...] = field_ref[...]
    clusters = sum_ref.shape[0]
    slots = send_index_ref.shape[1]
    ups = upward()

    def visit(slot, _):
        for position, back_ref in enumerate(back_refs):
            cluster = send_index_ref[sent_row(position, ups) if position else 0, slot]
            target_ref = extra_ref if position % 2 else sum_ref
            target_ref[cluster] += back_ref[slot]
        return 0

    lax.fori_loop(0, slots, visit, 0, unroll=2)

    def write(step, _):
        for turn in range(8):
            cluster = step * 8 + turn
            total = sum_ref[cluster] + extra_ref[cluster]
            out_ref[:, pl.ds(pl.multiple_of(cluster * 128, 128), 128)] = total[0:3]
        return 0

    lax.fori_loop(0, clusters // 8, write, 0)


def gather_forces(send_index, own, field, backs):
    smem = pl.BlockSpec(memory_space=pltpu.SMEM)
    vmem = pl.BlockSpec(memory_space=pltpu.VMEM)
    clusters = own.shape[0]
    return pl.pallas_call(
        gather_forces_kernel,
        out_shape=jax.ShapeDtypeStruct((3, clusters * 128), jnp.float32),
        in_specs=[smem] + [vmem] * (2 + len(backs)),
        out_specs=vmem,
        scratch_shapes=[pltpu.VMEM(own.shape, jnp.float32)] * 2,
        compiler_params=pltpu.CompilerParams(vmem_limit_bytes=ROOMY_LIMIT),
        name="gather_forces",
    )(send_index, own, field, *backs)


def shards(
    positions,
    charges,
    cluster_fill,
    cluster_cell,
    send_index,
    send_count,
    pair_local,
    pair_dir,
    pair_slot,
    ion_density,
    potential_prev,
    screening,
):
    clusters = cluster_fill.shape[0]
    psize = charges.shape[0] // clusters
    slots = send_index.shape[1]
    base = slots * 4
    other_rows, own, masked, local, *messages = prepare(
        cluster_fill,
        send_index,
        send_count,
        pair_dir.reshape(-1, 128),
        pair_slot.reshape(-1, 128),
        positions,
        charges.reshape(clusters, psize),
    )
    inverse, source, *edges = sources_of(
        cluster_cell, masked, ion_density, potential_prev, screening
    )
    arrived = [local] + [
        swapped(message, *swap)
        for message, swap in zip(messages, SWAPS, strict=True)
    ]
    fields = (potential_prev, inverse, source, ion_density)
    arrived, edges = lax.optimization_barrier((arrived, edges))
    edges = [swapped(edge, "grp", 1, phase) for phase, edge in enumerate(edges)]
    own_force, *reactions = pair_forces(
        pair_local,
        other_rows.reshape(-1),
        own.reshape(clusters * 4, psize),
        arrived,
        slots,
    )
    local_back, *reactions = reactions
    rims = pack_rows(fields, edges, reactions[:2])
    backs = [
        swapped(reaction, *swap)
        for reaction, swap in zip((*rims, *reactions[2:]), SWAPS, strict=True)
    ]
    potential, ion_next, field_force = grid_step(
        cluster_cell, masked, fields, backs[:2], edges, base
    )
    forces = gather_forces(
        send_index,
        own_force.reshape(clusters, 4, psize),
        field_force.reshape(clusters, 4, psize),
        [back.reshape(-1, 4, psize) for back in (local_back, *backs)],
    )
    return (forces, potential, ion_next)


def solution(mesh):
    in_specs = (
        P(None, ("grp", "brick")),
        P(("grp", "brick")),
        P(("grp", "brick")),
        P(("grp", "brick")),
        P(("grp", "brick"), None),
        P(("grp", "brick"), None),
        P(("grp", "brick")),
        P(("grp", "brick")),
        P(("grp", "brick")),
        P("grp", "brick", None),
        P("grp", "brick", None),
        P("grp", "brick", None),
    )
    out_specs = (P(None, ("grp", "brick")), P("grp", "brick", None), P("grp", "brick", None))
    return jax.shard_map(shards, mesh=mesh, in_specs=in_specs, out_specs=out_specs, check_vma=False)
```

```python
import functools

import jax
import jax.numpy as jnp
import numpy as np
from jax import lax
from jax.experimental import pallas as pl
from jax.experimental.pallas import tpu as pltpu
from jax.sharding import PartitionSpec as P

SWEEPS = 4
UNROLL = 16
CHUNKS = 4
AHEAD = 2
BEHIND = 4
BATCH = 4
HALO_WIDTHS = (SWEEPS + 1, SWEEPS, SWEEPS, 1)
DEPTH = SWEEPS + 1
CELL_BITS = 8
SWAPS = tuple(
    (*way, phase) for way in (("brick", 1), ("brick", 2), ("grp", 1)) for phase in (0, 1)
)


coulomb_scale = 0.02
softening = 0.1
field_scale = 0.5
deposit_scale = 0.2
lowest_eig = 0.01
highest_eig = 1.99
mobility = 0.3
diffusion = 0.2
time_step = 0.2


VMEM_LIMIT = 60 * 1024 * 1024
ROOMY_LIMIT = 48 * 1024 * 1024


def start_copies(pairs, sems):
    copies = [
        pltpu.make_async_copy(source, target, sems.at[index])
        for index, (source, target) in enumerate(pairs)
    ]
    for copy in copies:
        copy.start()
    return copies


def upward():
    brick, grp = (lax.axis_index("brick"), lax.axis_index("grp"))
    bits = (brick, lax.shift_right_logical(brick, 1), grp)
    return [1 - lax.bitwise_and(bit, 1) for bit in bits]


def sent_row(position, ups):
    way, phase = ((position - 1) // 2, (position - 1) % 2)
    return 1 + 2 * way + (ups[way] if phase else 1 - ups[way])


def swapped(shard, axis, distance, phase):
    devices = lax.axis_size(axis)
    pairs = []
    for index in range(devices):
        step = distance if (index // distance + phase) % 2 == 0 else -distance
        if 0 <= index + step < devices:
            pairs.append((index, index + step))
    return lax.ppermute(shard, axis, pairs)


def split3(value):
    first = value.astype(jnp.bfloat16).astype(jnp.float32)
    rest = value - first
    second = rest.astype(jnp.bfloat16).astype(jnp.float32)
    third = (rest - second).astype(jnp.bfloat16).astype(jnp.float32)
    return (first, second, third)


def moment_pieces(comps, charge):
    rows = [None] * 12
    for part, charged in enumerate((*comps, None)):
        for level, piece in enumerate(split3(charge if charged is None else charge * charged)):
            rows[4 * level + part] = piece
    return rows


def selections():
    near_kinds, far_kinds = ([], [])
    for part in range(3):
        near_kinds += [3 * part + level for level in (0, 0, 0, 1, 1, 2)]
        far_kinds += [3 * part + level for level in (0, 1, 2, 0, 1, 0)]
    near_kinds += [9, 10, 11, 12, 12, 12]
    far_kinds += [12, 12, 12, 9, 10, 11]
    near = np.zeros((128, 1024), np.float32)
    far = np.zeros((256, 128), np.float32)
    moment = np.zeros((128, 128), np.float32)
    for cluster in range(8):
        for index, kind in enumerate(near_kinds):
            near[kind * 8 + cluster, cluster * 128 + index] = 1.0
        for index, kind in enumerate(far_kinds):
            far[cluster * 32 + index, kind * 8 + cluster] = 1.0
        for kind in range(12):
            moment[cluster * 16 + kind, kind * 8 + cluster] = 1.0
    return tuple(jnp.asarray(part, jnp.bfloat16) for part in (near, far, moment))


def pair_kernel(own_rows_ref, other_rows_ref, *refs):
    sources = len(SWAPS) + 1
    fetched = sources + 4
    hbm_refs = refs[:fetched]
    own_out_ref = refs[fetched]
    other_out_refs = refs[fetched + 1 : fetched + 1 + sources]
    refs = refs[fetched + 1 + sources :]
    near_sel_ref, far_sel_ref, moment_sel_ref, own_ref = refs[:4]
    other_refs = refs[4:fetched]
    sems = refs[fetched]
    copies = start_copies(
        [
            (source.at[0 : target.shape[0]], target)
            for source, target in zip(hbm_refs, refs[:fetched], strict=True)
        ],
        sems,
    )
    (
        near_ref,
        far_ref,
        own_moment_ref,
        other_moment_ref,
        own_sum_ref,
        other_sum_ref,
        dist_ref,
        *weight_refs,
    ) = refs[fetched + 1 :]
    clusters = own_ref.shape[0] // 4
    slots = other_out_refs[0].shape[0] // 4
    others = slots * sources
    groups = own_rows_ref.shape[0] // UNROLL
    ones = jnp.ones((8, 128), jnp.float32)
    zeros = jnp.zeros((8, 128), jnp.float32)

    def components(data_ref, start):
        return [data_ref[pl.ds(4 * start + part, 8, stride=4), :] for part in range(4)]

    def place_pieces(comps, factor, offset):
        pieces = []
        square = zeros
        for comp in comps:
            square = square + comp * comp
            pieces += split3(factor * comp)
        pieces += [*split3(square + offset), ones]
        return jnp.concatenate(pieces + [zeros] * (16 - len(pieces)), axis=0)

    def selected(left, right):
        return jnp.dot(
            left.astype(jnp.bfloat16), right, preferred_element_type=jnp.float32
        ).astype(jnp.bfloat16)

    def stacked(moments):
        return jnp.concatenate(moments + [zeros] * 4, axis=0).astype(jnp.bfloat16)

    def near_rows(step, _):
        starts = [pl.multiple_of(step * 8 * BATCH + 8 * index, 8) for index in range(BATCH)]
        parts = [components(own_ref, start) for start in starts]
        turned = [place_pieces(part[:3], 1.0, 0.0).T.astype(jnp.bfloat16) for part in parts]
        moments = [stacked(moment_pieces(part[:3], part[3])) for part in parts]
        placed = [selected(moment_sel_ref[...], moment) for moment in moments]
        for start, rows in zip(starts, placed, strict=True):
            own_moment_ref[pl.ds(pl.multiple_of(start * 16, 128), 128), :] = rows
        for start, pieces in zip(starts, turned, strict=True):
            tiles = selected(pieces, near_sel_ref[...])
            for index in range(8):
                at = pl.ds(pl.multiple_of((start + index) * 128, 128), 128)
                near_ref[at, :] = tiles[:, 128 * index : 128 * index + 128]
        return 0

    def far_rows(source):
        locals_ = range(0, slots, 8)
        parts = [components(other_refs[source], local) for local in locals_]
        pieces = [place_pieces(part[:3], -2.0, softening).astype(jnp.bfloat16) for part in parts]
        moments = [stacked(moment_pieces(part[:3], part[3])) for part in parts]
        rows = [selected(far_sel_ref[...], piece) for piece in pieces]
        placed = [selected(moment_sel_ref[...], moment) for moment in moments]
        for local, row, moment in zip(locals_, rows, placed, strict=True):
            start = source * slots + local
            far_ref[start * 32 : start * 32 + 256, :] = row
            other_moment_ref[start * 16 : start * 16 + 128, :] = moment

    own_sum_ref[...] = jnp.zeros_like(own_sum_ref)
    other_sum_ref[...] = jnp.zeros_like(other_sum_ref)
    weight_refs[0][...] = jnp.zeros_like(weight_refs[0])
    for copy in copies[:4]:
        copy.wait()
    lax.fori_loop(0, clusters // (8 * BATCH), near_rows, 0)
    for copy in copies[4:]:
        copy.wait()
    for source in range(sources):
        far_rows(source)
    def distances(pair):
        own = own_rows_ref[pair]
        other = other_rows_ref[pair]
        return jnp.dot(
            near_ref[pl.ds(pl.multiple_of(own * 128, 128), 128), 0:32],
            far_ref[pl.ds(pl.multiple_of(other * 32, 32), 32), :],
            preferred_element_type=jnp.float32,
        )

    def weights(dist, index, chunk, weight_ref):
        rows = 128 // CHUNKS
        first = rows * chunk
        root = lax.rsqrt(dist[first : first + rows])
        weight = root * root * root
        high = weight.astype(jnp.bfloat16)
        low = (weight - high.astype(jnp.float32)).astype(jnp.bfloat16)
        at = slice(128 * index + first, 128 * index + first + rows)
        weight_ref[at, :128] = high
        weight_ref[at, 128:] = low

    def row_block(index):
        return pl.ds(pl.multiple_of(index * 16, 16), 16)

    def own_product(other, weight_ref, index):
        both = weight_ref[128 * index : 128 * index + 128]
        return lax.dot_general(
            other_moment_ref[row_block(other), :],
            jnp.concatenate([both[:, :128], both[:, 128:]], axis=0),
            (((1,), (1,)), ((), ())),
            preferred_element_type=jnp.float32,
        )

    def other_product(own, weight_ref, index):
        return jnp.dot(
            own_moment_ref[row_block(own), :],
            weight_ref[128 * index : 128 * index + 128],
            preferred_element_type=jnp.float32,
        )

    def add_rows(own, other, to_own, to_other):
        own_sum_ref[row_block(own), :] += to_own[:, :128] + to_own[:, 128:]
        other_sum_ref[row_block(other), :] += to_other[:, :128] + to_other[:, 128:]

    def half_step(step, side, dists):
        last = jnp.maximum(step - 1, 0) * UNROLL
        waiting = []
        for index in range(UNROLL):
            own = own_rows_ref[last + index]
            other = other_rows_ref[last + index]
            coming = step * UNROLL + index + AHEAD
            later = distances(jnp.minimum(coming, groups * UNROLL - 1))
            weights(dists[0], index, 0, weight_refs[1 - side])
            to_own = own_product(other, weight_refs[side], index)
            weights(dists[0], index, 1, weight_refs[1 - side])
            weights(dists[0], index, 2, weight_refs[1 - side])
            to_other = other_product(own, weight_refs[side], index)
            weights(dists[0], index, 3, weight_refs[1 - side])
            dists = [*dists[1:], later]
            waiting.append((own, other, to_own, to_other))
            if len(waiting) > BEHIND:
                add_rows(*waiting.pop(0))
        for entry in waiting:
            add_rows(*entry)
        return dists

    def visit(step, _):
        dists = [dist_ref[index] for index in range(AHEAD)]
        for side in range(2):
            dists = half_step(step * 2 + side, side, dists)
        for index in range(AHEAD):
            dist_ref[index] = dists[index]
        return 0

    for index in range(AHEAD):
        dist_ref[index] = distances(index)
    lax.fori_loop(0, groups // 2, visit, 0)
    half_step(groups, 0, [dist_ref[index] for index in range(AHEAD)])

    def finish(data_ref, out_ref, sum_ref, base, step, _):
        starts = [pl.multiple_of(step * 8 * BATCH + 8 * index, 8) for index in range(BATCH)]
        parts = [components(data_ref, start) for start in starts]

        def total(start, part):
            terms = [
                sum_ref[pl.ds(base + start * 16 + 4 * level + part, 8, stride=16), :]
                for level in range(3)
            ]
            return terms[0] + (terms[1] + terms[2])

        totals = [[total(start, part) for part in range(4)] for start in starts]
        for start, (*comps, charge), sums in zip(starts, parts, totals, strict=True):
            scale = coulomb_scale * charge
            for part, comp in enumerate(comps):
                out_ref[pl.ds(4 * start + part, 8, stride=4), :] = scale * (
                    comp * sums[3] - sums[part]
                )
            out_ref[pl.ds(4 * start + 3, 8, stride=4), :] = zeros
        return 0

    lax.fori_loop(
        0,
        clusters // (8 * BATCH),
        functools.partial(finish, own_ref, own_out_ref, own_sum_ref, 0),
        0,
    )
    for source in range(sources):
        body = functools.partial(
            finish, other_refs[source], other_out_refs[source], other_sum_ref, source * slots * 16
        )
        lax.fori_loop(0, slots // (8 * BATCH), body, 0)


def pair_forces(own_rows, other_rows, own, arrived, slots):
    clusters = own.shape[0] // 4
    others = slots * len(arrived)
    pairs = own_rows.shape[0]
    smem = pl.BlockSpec(memory_space=pltpu.SMEM)
    vmem = pl.BlockSpec(memory_space=pltpu.VMEM)
    hbm = pl.BlockSpec(memory_space=pl.ANY)
    operands = (*selections(), own)
    return pl.pallas_call(
        pair_kernel,
        out_shape=(
            jax.ShapeDtypeStruct(own.shape, jnp.float32),
            *[jax.ShapeDtypeStruct((slots * 4, 128), jnp.float32)] * len(arrived),
        ),
        in_specs=[smem, smem] + [hbm] * (4 + len(arrived)),
        out_specs=(vmem,) * (len(arrived) + 1),
        scratch_shapes=[
            *[pltpu.VMEM(operand.shape, operand.dtype) for operand in operands],
            *[pltpu.VMEM((slots * 4, 128), jnp.float32)] * len(arrived),
            pltpu.SemaphoreType.DMA((len(operands) + len(arrived),)),
            pltpu.VMEM((clusters * 128, 128), jnp.bfloat16),
            pltpu.VMEM((others * 32, 128), jnp.bfloat16),
            pltpu.VMEM((clusters * 16, 128), jnp.bfloat16),
            pltpu.VMEM((others * 16, 128), jnp.bfloat16),
            pltpu.VMEM((clusters * 16, 128), jnp.float32),
            pltpu.VMEM((others * 16, 128), jnp.float32),
            pltpu.VMEM((AHEAD, 128, 128), jnp.float32),
            *[pltpu.VMEM((128 * UNROLL, 256), jnp.bfloat16)] * 2,
        ],
        compiler_params=pltpu.CompilerParams(vmem_limit_bytes=ROOMY_LIMIT),
        cost_estimate=pl.CostEstimate(
            flops=pairs * 128 * 128 * 20, bytes_accessed=4 * 1024 * 1024, transcendentals=0
        ),
        name="pair_forces",
    )(own_rows, other_rows, *operands, *arrived)


def prepare_kernel(
    fill_ref,
    send_index_ref,
    send_count_ref,
    pair_dir_ref,
    pair_slot_ref,
    position_hbm,
    charge_hbm,
    row_ref,
    own_ref,
    masked_ref,
    *refs,
):
    out_refs, (position_ref, charge_ref, sems) = (refs[:-3], refs[-3:])
    copies = start_copies(((position_hbm, position_ref), (charge_hbm, charge_ref)), sems)
    clusters = charge_ref.shape[0]
    slots = send_index_ref.shape[1]
    lane = lax.broadcasted_iota(jnp.int32, (1, 128), 1)
    row = lax.broadcasted_iota(jnp.int32, (4, 128), 0)
    ups = upward()
    direction = pair_dir_ref[...]
    way = lax.shift_right_arithmetic(direction - 1, 1)
    flip = jnp.where(way == 0, ups[0], jnp.where(way == 1, ups[1], ups[2]))
    position = 1 + 2 * way + lax.bitwise_xor(lax.bitwise_and(direction - 1, 1), flip)
    row_ref[...] = jnp.where(direction == 0, 0, position) * slots + pair_slot_ref[...]
    for copy in copies:
        copy.wait()

    def collect(step, _):
        for turn in range(8):
            cluster = step * 8 + turn
            masked = jnp.where(lane < fill_ref[cluster], charge_ref[pl.ds(cluster, 1), :], 0.0)
            masked_ref[pl.ds(cluster, 1), :] = masked
            place = position_ref[:, pl.ds(pl.multiple_of(cluster * 128, 128), 128)]
            own_ref[cluster, 0:3, :] = place
            own_ref[cluster, 3:4, :] = masked
        return 0

    lax.fori_loop(0, clusters // 8, collect, 0, unroll=2)

    def fill_messages(step, _):
        for position, out_ref in enumerate(out_refs):
            direction = sent_row(position, ups) if position else 0
            parts = []
            for turn in range(2):
                slot = step * 2 + turn
                live = jnp.where(slot < send_count_ref[0, direction], 1.0, 0.0)
                value = own_ref[send_index_ref[direction, slot]]
                parts.append(jnp.where(row == 3, value * live, value))
            out_ref[pl.ds(pl.multiple_of(step * 8, 8), 8), :] = jnp.concatenate(parts, axis=0)
        return 0

    lax.fori_loop(0, slots // 2, fill_messages, 0)


def prepare(fill, send_index, send_count, pair_dir, pair_slot, positions, charges):
    clusters = charges.shape[0]
    directions, slots = send_index.shape
    smem = pl.BlockSpec(memory_space=pltpu.SMEM)
    vmem = pl.BlockSpec(memory_space=pltpu.VMEM)
    return pl.pallas_call(
        prepare_kernel,
        out_shape=(
            jax.ShapeDtypeStruct(pair_dir.shape, jnp.int32),
            jax.ShapeDtypeStruct((clusters, 4, 128), jnp.float32),
            jax.ShapeDtypeStruct((clusters, 128), jnp.float32),
            *[jax.ShapeDtypeStruct((slots * 4, 128), jnp.float32)] * directions,
        ),
        in_specs=[smem] * 3 + [vmem] * 2 + [pl.BlockSpec(memory_space=pltpu.HBM)] * 2,
        out_specs=(vmem,) * (3 + directions),
        scratch_shapes=[
            *[pltpu.VMEM(operand.shape, jnp.float32) for operand in (positions, charges)],
            pltpu.SemaphoreType.DMA((2,)),
        ],
        compiler_params=pltpu.CompilerParams(vmem_limit_bytes=VMEM_LIMIT),
        name="prepare",
    )(fill, send_index, send_count, pair_dir, pair_slot, positions, charges)


def sources_kernel(
    cell_ref,
    cell_row_ref,
    masked_hbm,
    ion_hbm,
    start_hbm,
    screen_hbm,
    inverse_ref,
    source_ref,
    *refs,
):
    edge_refs, refs = (refs[:2], refs[2:])
    sum_ref, deposit_ref, masked_ref, ion_ref, start_ref, screen_ref, sems = refs
    copies = start_copies(
        (
            (masked_hbm, masked_ref),
            (ion_hbm, ion_ref),
            (start_hbm, start_ref),
            (screen_hbm, screen_ref),
        ),
        sems,
    )
    copies[0].wait()
    clusters = masked_ref.shape[0]
    cells_x, cells_y, _ = ion_ref.shape
    lane = lax.broadcasted_iota(jnp.int32, (1, 128), 1)
    ups = upward()

    def add_up(step, _):
        at = pl.ds(pl.multiple_of(step * 8, 8), 8)
        total = jnp.sum(masked_ref[at, :], axis=1, keepdims=True)
        sum_ref[at, :] = jnp.broadcast_to(deposit_scale * total, (8, 128))
        return 0

    lax.fori_loop(0, clusters // 8, add_up, 0, unroll=8)

    def place(step, _):
        for turn in range(8):
            cluster = step * 8 + turn
            index_z = lax.bitwise_and(cell_ref[cluster], 127)
            at = pl.ds(cluster, 1)
            sum_ref[at, :] = jnp.where(lane == index_z, sum_ref[at, :], 0.0)
        return 0

    lax.fori_loop(0, clusters // 8, place, 0)
    cell = cell_row_ref[...]
    line = lax.shift_right_logical(cell, CELL_BITS)
    line = (line // cells_y * 2 + lax.shift_right_logical(lax.bitwise_and(cell, 255), 7)) * cells_y
    line = line + lax.shift_right_logical(cell, CELL_BITS) % cells_y
    sums = jnp.concatenate([part.astype(jnp.bfloat16) for part in split3(sum_ref[...])], axis=1)
    block = 128
    for first in range(0, deposit_ref.shape[0], block):
        rows = lax.broadcasted_iota(jnp.int32, (block, clusters), 0) + first
        hot = jnp.where(rows == line, 1.0, 0.0).astype(jnp.bfloat16)
        added = jnp.dot(hot, sums, preferred_element_type=jnp.float32)
        deposit_ref[first : first + block, :] = added[:, :128] + (
            added[:, 128:256] + added[:, 256:]
        )
    for copy in copies[1:]:
        copy.wait()
    inverse_ref[...] = 1.0 / (6.0 + screen_ref[...])
    for index in range(cells_x):
        for half in range(2):
            lanes = slice(128 * half, 128 * half + 128)
            first = (index * 2 + half) * cells_y
            source_ref[index, :, lanes] = (
                ion_ref[index, :, lanes] + deposit_ref[first : first + cells_y, :]
            ) * inverse_ref[index, :, lanes]
    edge = 0
    for field_ref, width in zip(
        (start_ref, inverse_ref, source_ref, ion_ref), HALO_WIDTHS, strict=True
    ):
        for step in range(width):
            for phase, edge_ref in enumerate(edge_refs):
                last = ups[2] if phase == 0 else 1 - ups[2]
                plane = field_ref[last * (cells_x - width) + step]
                for half in range(2):
                    edge_ref[2 * edge + half] = plane[:, 128 * half : 128 * half + 128]
            edge += 1


def sources_of(cell, masked, ions, start, screen):
    clusters = masked.shape[0]
    cells_y = ions.shape[1]
    smem = pl.BlockSpec(memory_space=pltpu.SMEM)
    vmem = pl.BlockSpec(memory_space=pltpu.VMEM)
    edge = jax.ShapeDtypeStruct((2 * sum(HALO_WIDTHS), cells_y, 128), jnp.float32)
    return pl.pallas_call(
        sources_kernel,
        out_shape=(*[jax.ShapeDtypeStruct(ions.shape, jnp.float32)] * 2, edge, edge),
        in_specs=[smem, vmem] + [pl.BlockSpec(memory_space=pltpu.HBM)] * 4,
        out_specs=(vmem,) * 4,
        scratch_shapes=[
            pltpu.VMEM((clusters, 128), jnp.float32),
            pltpu.VMEM((ions.size // 128, 128), jnp.float32),
            *[pltpu.VMEM(operand.shape, jnp.float32) for operand in (masked, ions, start, screen)],
            pltpu.SemaphoreType.DMA((4,)),
        ],
        compiler_params=pltpu.CompilerParams(vmem_limit_bytes=VMEM_LIMIT),
        cost_estimate=pl.CostEstimate(
            flops=20_000_000, bytes_accessed=4 << 20, transcendentals=0
        ),
        name="sources",
    )(cell, cell.reshape(1, clusters), masked, ions, start, screen)


def line_rows(cells_y):
    return (cells_y + 2 * DEPTH + 7) // 8 * 8


def pack_rows_kernel(*refs):
    field_refs, edge_refs, reaction_refs, out_refs = (refs[:4], refs[4:6], refs[6:8], refs[8:10])
    cells_x, cells_y, _ = field_refs[0].shape
    base = reaction_refs[0].shape[0]
    ups = upward()
    for reaction_ref, out_ref in zip(reaction_refs, out_refs, strict=True):
        out_ref[0:base, :] = reaction_ref[...]

    def fill(out_ref, after):
        for field, width in enumerate(HALO_WIDTHS):
            offset = sum(HALO_WIDTHS[:field])
            rows = slice(cells_y - width, cells_y) if after else slice(0, width)
            for index in range(cells_x):
                value = field_refs[field][index, rows, :]
                for half in range(2):
                    at = base + ((DEPTH + index) * 2 + half) * 16 + offset
                    out_ref[at : at + width, :] = value[:, 128 * half : 128 * half + 128]
            if width == 1:
                continue
            for phase, edge_ref in enumerate(edge_refs):
                higher = ups[2] if phase == 0 else 1 - ups[2]
                for step in range(width):
                    plane = (DEPTH - width) + higher * (cells_x + width) + step
                    for half in range(2):
                        at = pl.ds(base + (plane * 2 + half) * 16 + offset, width)
                        out_ref[at, :] = edge_ref[2 * (offset + step) + half, rows, :]

    for up in range(2):

        @pl.when(ups[0] == up)
        def _(up=up):
            fill(out_refs[0], up)
            fill(out_refs[1], 1 - up)


def pack_rows(fields, edges, reactions):
    vmem = pl.BlockSpec(memory_space=pltpu.VMEM)
    cells_x = fields[0].shape[0]
    rows = reactions[0].shape[0] + (cells_x + 2 * DEPTH) * 32
    shape = jax.ShapeDtypeStruct((rows, 128), jnp.float32)
    return pl.pallas_call(
        pack_rows_kernel,
        out_shape=(shape, shape),
        in_specs=[vmem] * 8,
        out_specs=(vmem, vmem),
        compiler_params=pltpu.CompilerParams(vmem_limit_bytes=ROOMY_LIMIT),
        name="pack_rows",
    )(*fields, *edges, *reactions)


def fill_line(target_ref, plane, half, field, value, rim_ref):
    cells_y = value.shape[0]
    width = HALO_WIDTHS[field]
    at = (plane * 2 + half) * line_rows(cells_y) + DEPTH
    target_ref[pl.ds(at, cells_y), :] = value
    first = (plane * 2 + half) * 16 + sum(HALO_WIDTHS[:field])
    target_ref[pl.ds(at - width, width), :] = rim_ref[pl.ds(first, width), :]
    first = first + rim_ref.shape[0] // 2
    target_ref[pl.ds(at + cells_y, width), :] = rim_ref[pl.ds(first, width), :]


def face_flux(pot_low, pot_high, ion_low, ion_high):
    speed = -mobility * (pot_high - pot_low)
    return (
        jnp.maximum(speed, 0.0) * ion_low
        + jnp.minimum(speed, 0.0) * ion_high
        - diffusion * (ion_high - ion_low)
    )


def grid_kernel(base, *refs):
    cell_ref, masked_ref = refs[:2]
    field_refs, rims, edge_refs = (refs[2:6], refs[6:8], refs[8:10])
    potential_ref, next_ref, force_ref = refs[10:13]
    start_ref, inverse_ref, source_ref, ion_ref = refs[13:17]
    updates, resids, final_ref, pick_refs = (refs[17:20], refs[20:22], refs[22], refs[23:26])
    rim_ref = refs[26]
    cells_x, cells_y, _ = field_refs[0].shape
    rows = line_rows(cells_y)
    clusters = masked_ref.shape[0]
    ups = upward()
    size = (cells_x + 2 * DEPTH) * 32
    for rim, side in zip(rims, (ups[0], 1 - ups[0]), strict=True):
        rim_ref[pl.ds(pl.multiple_of(side * size, size), size), :] = rim[base : base + size, :]
    extended = (start_ref, inverse_ref, source_ref, ion_ref)
    for field, target_ref in enumerate(extended):

        def fill(index, _, field=field, target_ref=target_ref):
            plane = field_refs[field][index]
            for half in range(2):
                value = plane[:, 128 * half : 128 * half + 128]
                fill_line(target_ref, DEPTH + index, half, field, value, rim_ref)
            return 0

        lax.fori_loop(0, cells_x, fill, 0, unroll=4)
    for field, target_ref in enumerate(extended):
        width = HALO_WIDTHS[field]
        for phase, edge_ref in enumerate(edge_refs):
            higher = ups[2] if phase == 0 else 1 - ups[2]

            def fill_edge(step, _, field=field, target_ref=target_ref, edge_ref=edge_ref):
                width = HALO_WIDTHS[field]
                plane = (DEPTH - width) + higher * (cells_x + width) + step
                for half in range(2):
                    value = edge_ref[2 * (sum(HALO_WIDTHS[:field]) + step) + half]
                    fill_line(target_ref, plane, half, field, value, rim_ref)
                return 0

            lax.fori_loop(0, width, fill_edge, 0, unroll=True)

    lane = lax.broadcasted_iota(jnp.int32, (2 * rows, 128), 1)
    blank = jnp.zeros((rows, 128), jnp.float32)

    def beyond(value):
        right = pltpu.roll(value, 127, 1)
        left = pltpu.roll(value, 1, 1)
        above = jnp.where(lane == 127, jnp.concatenate([right[rows:], blank], axis=0), right)
        below = jnp.where(lane == 0, jnp.concatenate([blank, left[:rows]], axis=0), left)
        return (below, above)

    def whole(plane, shift=0):
        return pl.ds(plane * 2 * rows + shift, 2 * rows)

    def around(ref, plane):
        here = ref[whole(plane), :]
        below, above = beyond(here)
        sums = (ref[whole(plane - 1), :] + ref[whole(plane + 1), :]) + (
            ref[whole(plane, -1), :] + ref[whole(plane, 1), :]
        )
        return (here, sums + (below + above))

    middle = 0.5 * (highest_eig + lowest_eig)
    spread = 0.5 * (highest_eig - lowest_eig)
    assert middle == 1.0 and SWEEPS == 4

    def sweep_first(plane, _):
        here, sums = around(start_ref, plane)
        at = whole(plane)
        updates[0][at, :] = source_ref[at, :] - here + inverse_ref[at, :] * sums
        return 0

    lax.fori_loop(1, cells_x + 2 * DEPTH - 1, sweep_first, 0, unroll=2)

    ratio_ms = middle / spread
    weight_now = 1.0 / ratio_ms
    for turn in range(1, SWEEPS):
        weight_next = 1.0 / (2.0 * ratio_ms - weight_now)
        keep, gain = (weight_next * weight_now, 2.0 * weight_next / spread)
        weight_now = weight_next

        def sweep(plane, _, turn=turn, keep=keep, gain=gain):
            here, sums = around(updates[turn - 1], plane)
            at = whole(plane)
            resid = inverse_ref[at, :] * sums
            if turn > 1:
                resid = resid + (resids[turn - 2][at, :] - here)
            update = keep * here + gain * resid
            if turn + 1 < SWEEPS:
                resids[turn - 1][at, :] = resid
                updates[turn][at, :] = update
            else:
                final_ref[at, :] = (start_ref[at, :] + updates[0][at, :]) + (
                    (updates[1][at, :] + here) + update
                )
            return 0

        first = 1 + turn
        lax.fori_loop(first, cells_x + 2 * DEPTH - first, sweep, 0, unroll=2)

    def advance(index, _):
        plane = index + DEPTH
        pot = final_ref[whole(plane, DEPTH), :]
        ion = ion_ref[whole(plane, DEPTH), :]
        steps = [
            (final_ref[at, :], ion_ref[at, :])
            for at in (
                whole(plane - 1, DEPTH),
                whole(plane + 1, DEPTH),
                whole(plane, DEPTH - 1),
                whole(plane, DEPTH + 1),
            )
        ]
        steps += zip(beyond(pot), beyond(ion), strict=True)
        total = 0.0
        for low, high in zip(steps[0::2], steps[1::2], strict=True):
            total = total + (
                face_flux(pot, high[0], ion, high[1]) - face_flux(low[0], pot, low[1], ion)
            )
        result = ion - time_step * total
        for half in range(2):
            lanes = slice(128 * half, 128 * half + 128)
            kept = slice(rows * half, rows * half + cells_y)
            next_ref[index, :, lanes] = result[kept]
            potential_ref[index, :, lanes] = pot[kept]
        return 0

    lax.fori_loop(0, cells_x, advance, 0)

    row_lane = lax.broadcasted_iota(jnp.int32, (1, 128), 1)

    def pick(cluster, _):
        cell = cell_ref[cluster]
        index_x = lax.shift_right_logical(cell, CELL_BITS) // cells_y + DEPTH
        index_y = lax.shift_right_logical(cell, CELL_BITS) % cells_y + DEPTH
        index_z = lax.bitwise_and(cell, 255)
        half = lax.shift_right_logical(index_z, 7)
        here = row_lane == lax.bitwise_and(index_z, 127)

        def line(plane, row, part):
            return final_ref[pl.ds((plane * 2 + part) * rows + row, 1), :]

        along_x = line(index_x - 1, index_y, half) - line(index_x + 1, index_y, half)
        along_y = line(index_x, index_y - 1, half) - line(index_x, index_y + 1, half)
        along_z = jnp.zeros((1, 128), jnp.float32)
        for part in range(2):
            value = line(index_x, index_y, part)
            place = row_lane + 128 * part
            along_z = along_z + jnp.where(place == index_z - 1, value, 0.0)
            along_z = along_z - jnp.where(place == index_z + 1, value, 0.0)
        at = pl.ds(cluster, 1)
        pick_refs[0][at, :] = jnp.where(here, along_x, 0.0)
        pick_refs[1][at, :] = jnp.where(here, along_y, 0.0)
        pick_refs[2][at, :] = along_z
        return 0

    lax.fori_loop(0, clusters, pick, 0, unroll=16)

    def spread_out(step, _):
        start = pl.multiple_of(step * 8, 8)
        charge = masked_ref[pl.ds(start, 8), :] * (0.5 * field_scale)
        for part, pick_ref in enumerate(pick_refs):
            total = jnp.sum(pick_ref[pl.ds(start, 8), :], axis=1, keepdims=True)
            force_ref[pl.ds(4 * start + part, 8, stride=4), :] = charge * total
        force_ref[pl.ds(4 * start + 3, 8, stride=4), :] = jnp.zeros((8, 128), jnp.float32)
        return 0

    lax.fori_loop(0, clusters // 8, spread_out, 0, unroll=4)


def grid_step(cell, masked, fields, rims, edges, base):
    smem = pl.BlockSpec(memory_space=pltpu.SMEM)
    vmem = pl.BlockSpec(memory_space=pltpu.VMEM)
    clusters = masked.shape[0]
    cells_x, cells_y, _ = fields[0].shape
    block = ((cells_x + 2 * DEPTH) * 2 * line_rows(cells_y), 128)
    return pl.pallas_call(
        functools.partial(grid_kernel, base),
        out_shape=(
            jax.ShapeDtypeStruct(fields[0].shape, jnp.float32),
            jax.ShapeDtypeStruct(fields[0].shape, jnp.float32),
            jax.ShapeDtypeStruct((clusters * 4, 128), jnp.float32),
        ),
        in_specs=[smem] + [vmem] * 9,
        out_specs=(vmem,) * 3,
        scratch_shapes=[pltpu.VMEM(block, jnp.float32)] * 10
        + [pltpu.VMEM((clusters, 128), jnp.float32)] * 3
        + [pltpu.VMEM(((cells_x + 2 * DEPTH) * 64, 128), jnp.float32)],
        compiler_params=pltpu.CompilerParams(vmem_limit_bytes=ROOMY_LIMIT),
        cost_estimate=pl.CostEstimate(
            flops=block[0] * block[1] * 100, bytes_accessed=8 << 20, transcendentals=0
        ),
        name="grid_step",
    )(cell, masked, *fields, *rims, *edges)


def gather_forces_kernel(send_index_ref, *refs):
    own_ref, field_ref, *back_refs = refs[:-3]
    out_ref, sum_ref, extra_ref = refs[-3:]
    sum_ref[...] = own_ref[...]
    extra_ref[...] = field_ref[...]
    clusters = sum_ref.shape[0]
    slots = send_index_ref.shape[1]
    ups = upward()

    def visit(slot, _):
        for position, back_ref in enumerate(back_refs):
            cluster = send_index_ref[sent_row(position, ups) if position else 0, slot]
            target_ref = extra_ref if position % 2 else sum_ref
            target_ref[cluster] += back_ref[slot]
        return 0

    lax.fori_loop(0, slots, visit, 0, unroll=2)

    def write(step, _):
        for turn in range(8):
            cluster = step * 8 + turn
            total = sum_ref[cluster] + extra_ref[cluster]
            out_ref[:, pl.ds(pl.multiple_of(cluster * 128, 128), 128)] = total[0:3]
        return 0

    lax.fori_loop(0, clusters // 8, write, 0)


def gather_forces(send_index, own, field, backs):
    smem = pl.BlockSpec(memory_space=pltpu.SMEM)
    vmem = pl.BlockSpec(memory_space=pltpu.VMEM)
    clusters = own.shape[0]
    return pl.pallas_call(
        gather_forces_kernel,
        out_shape=jax.ShapeDtypeStruct((3, clusters * 128), jnp.float32),
        in_specs=[smem] + [vmem] * (2 + len(backs)),
        out_specs=vmem,
        scratch_shapes=[pltpu.VMEM(own.shape, jnp.float32)] * 2,
        compiler_params=pltpu.CompilerParams(vmem_limit_bytes=ROOMY_LIMIT),
        name="gather_forces",
    )(send_index, own, field, *backs)


def shards(
    positions,
    charges,
    cluster_fill,
    cluster_cell,
    send_index,
    send_count,
    pair_local,
    pair_dir,
    pair_slot,
    ion_density,
    potential_prev,
    screening,
):
    clusters = cluster_fill.shape[0]
    psize = charges.shape[0] // clusters
    slots = send_index.shape[1]
    base = slots * 4
    other_rows, own, masked, local, *messages = prepare(
        cluster_fill,
        send_index,
        send_count,
        pair_dir.reshape(-1, 128),
        pair_slot.reshape(-1, 128),
        positions,
        charges.reshape(clusters, psize),
    )
    inverse, source, *edges = sources_of(
        cluster_cell, masked, ion_density, potential_prev, screening
    )
    arrived = [local] + [
        swapped(message, *swap)
        for message, swap in zip(messages, SWAPS, strict=True)
    ]
    fields = (potential_prev, inverse, source, ion_density)
    arrived, edges = lax.optimization_barrier((arrived, edges))
    edges = [swapped(edge, "grp", 1, phase) for phase, edge in enumerate(edges)]
    own_force, *reactions = pair_forces(
        pair_local,
        other_rows.reshape(-1),
        own.reshape(clusters * 4, psize),
        arrived,
        slots,
    )
    local_back, *reactions = reactions
    rims = pack_rows(fields, edges, reactions[:2])
    backs = [
        swapped(reaction, *swap)
        for reaction, swap in zip((*rims, *reactions[2:]), SWAPS, strict=True)
    ]
    potential, ion_next, field_force = grid_step(
        cluster_cell, masked, fields, backs[:2], edges, base
    )
    forces = gather_forces(
        send_index,
        own_force.reshape(clusters, 4, psize),
        field_force.reshape(clusters, 4, psize),
        [back.reshape(-1, 4, psize) for back in (local_back, *backs)],
    )
    return (forces, potential, ion_next)


def solution(mesh):
    in_specs = (
        P(None, ("grp", "brick")),
        P(("grp", "brick")),
        P(("grp", "brick")),
        P(("grp", "brick")),
        P(("grp", "brick"), None),
        P(("grp", "brick"), None),
        P(("grp", "brick")),
        P(("grp", "brick")),
        P(("grp", "brick")),
        P("grp", "brick", None),
        P("grp", "brick", None),
        P("grp", "brick", None),
    )
    out_specs = (P(None, ("grp", "brick")), P("grp", "brick", None), P("grp", "brick", None))
    return jax.shard_map(shards, mesh=mesh, in_specs=in_specs, out_specs=out_specs, check_vma=False)
```
